32 devices in a mesh: ep: 8 (over y, x, core), hs: 4 (over z).
Axes of the slice: x: 2, y: 2, z: 4, core: 2. Of those that a mesh axis runs over, the one named last changes fastest.
Arguments:
- tokens: bfloat16 [4096, 1280], P('ep'), may hold values from -6 to 6
- attn_gain: float32 [1280], replicated, may hold values from 0.5 to 1.5
- attn_query: bfloat16 [1280, 1280], P(None, 'hs'), may hold values from -0.15625 to 0.15625
- attn_key: bfloat16 [1280, 1280], P(None, 'hs'), may hold values from -0.15625 to 0.15625
- attn_value: bfloat16 [1280, 1280], P(None, 'hs'), may hold values from -0.15625 to 0.15625
- attn_out: bfloat16 [1280, 1280], P(None, 'hs'), may hold values from -0.625 to 0.625
- ffn_gain: float32 [1280], replicated, may hold values from 0.5 to 1.5
- router: bfloat16 [1280, 64], replicated, may hold values from -0.078125 to 0.078125
- shared_gate: bfloat16 [1280, 1792], P(None, 'hs'), may hold values from -0.15625 to 0.15625
- shared_up: bfloat16 [1280, 1792], P(None, 'hs'), may hold values from -0.15625 to 0.15625
- shared_down: bfloat16 [1792, 1280], P('hs'), may hold values from -0.125 to 0.125
- expert_gate: bfloat16 [64, 1280, 896], P('ep', None, 'hs'), may hold values from -0.15625 to 0.15625
- expert_up: bfloat16 [64, 1280, 896], P('ep', None, 'hs'), may hold values from -0.15625 to 0.15625
- expert_down: bfloat16 [64, 896, 1280], P('ep', 'hs'), may hold values from -6 to 6
- routes: int32 [4096, 7], P('ep'), may hold values from 0 to 63, all different within a row; in each aligned block of 512 rows (0 to 511, 512 to 1023, ...) at most 112 rows name the same one
- documents: int32 [8, 512], P('ep'), may hold values from 0 to 3, never falling along the last dimension, each value on 1 to 256 neighbouring positions
- out_grad: bfloat16 [4096, 1280], P('ep', 'hs'), may hold values from -6 to 6
Outputs:
- output: bfloat16 [4096, 1280], P('ep', 'hs')
- grad_tokens: float32 [4096, 1280], P('ep', 'hs')
- grad_attn_gain: float32 [1280], replicated
- grad_attn_query: float32 [1280, 1280], P(None, 'hs')
- grad_attn_key: float32 [1280, 1280], P(None, 'hs')
- grad_attn_value: float32 [1280, 1280], P(None, 'hs')
- grad_attn_out: float32 [1280, 1280], P(None, 'hs')
- grad_ffn_gain: float32 [1280], replicated
- grad_router: float32 [1280, 64], replicated
- grad_shared_gate: float32 [1280, 1792], P(None, 'hs')
- grad_shared_up: float32 [1280, 1792], P(None, 'hs')
- grad_shared_down: float32 [1792, 1280], P('hs')
- grad_expert_gate: float32 [64, 1280, 896], P('ep', None, 'hs')
- grad_expert_up: float32 [64, 1280, 896], P('ep', None, 'hs')
- grad_expert_down: float32 [64, 896, 1280], P('ep', 'hs')
The draws below stay inside these ranges and needn't reach their ends.
Inputs may be any that keep to these rules, and one draw needn't show every extreme that they name: `routes`: each row names 7 different experts and every expert is named by some row; the 512 rows of one sequence name any one expert at most 112 times, and in every draw the rows of some sequence name some expert exactly 112 times. `documents`: within each sequence the document number never falls; each document spans 1 to half of 512 positions.
All inputs are finite; a program needn't handle non-finite values.
Results may differ from the reference program's by a relative error of at most 0.02.
Values may be sent and summed in bfloat16 or wider, within the bound.
A program may use at most 448 MiB of HBM per device.

```python
import math
import jax
import jax.numpy as jnp
import numpy as np
from jax import lax

D = 1280
HEADS = 10
HEAD_DIM = 128
SHARED_FF = 1792
EXPERT_FF = 896
EXPERTS = 64
TOPK = 7
TOK_DEV = 512
DOCS = 4
SEQS = 8
TOKENS = 4096
CAP = 112


def shard_levels(stream_key, extent, split, low, top_value):
    def one(axis_at, parts):
        draws = jax.random.uniform(jax.random.fold_in(jax.random.fold_in(stream_key, 6), axis_at), (parts,), jnp.float32, low / len(split), top_value / len(split))
        return jnp.repeat(jnp.exp(draws), extent[axis_at] // parts).reshape((-1,) + (1,) * (len(extent) - axis_at - 1))

    loudness = one(*split[0])
    for cut in split[1:]:
        loudness = loudness * one(*cut)
    return loudness


def length_profile(number_of, total, most, skew):
    weights = [(1 << 20) // math.isqrt(rank ** skew) + 1 for rank in range(2, number_of + 1)]
    surplus, counts = total - most - (number_of - 1), [1] * (number_of - 1)
    while surplus > 0:
        free = [i for i in range(number_of - 1) if counts[i] < most]
        whole, remaining = sum([weights[i] for i in free]), surplus
        for i in free:
            extra = min(most - counts[i], max(1, remaining * weights[i] // whole), surplus)
            counts[i] = counts[i] + extra
            surplus = surplus - extra
    return np.array([most] + counts)


def ragged(stream_key, number_of, total, most, lean):
    if number_of == 2:
        one = jax.random.randint(stream_key, (), max(1, total - most), min(most, total - 1) + 1)
        return jnp.stack([one, total - one])
    tallies = jnp.asarray(length_profile(number_of, total, most, lean), jnp.int32)
    pairs = (number_of - 1) // 2
    giver, receiver = tallies[1:1 + 2 * pairs:2], tallies[2:2 + 2 * pairs:2]
    room = jnp.minimum(giver - 1, most - receiver)
    moved = jax.random.randint(jax.random.fold_in(stream_key, 1), (pairs,), 0, 1 << 20) % (room + 1)
    tallies = tallies.at[1:1 + 2 * pairs:2].set(giver - moved).at[2:2 + 2 * pairs:2].set(receiver + moved)
    return tallies[jax.random.permutation(jax.random.fold_in(stream_key, 2), number_of)]


def deal_out(key, own, number, rows, amount, top, most, lean):
    sequence = jax.random.permutation(key, amount)
    packed, common = shares(amount, rows * top, most, lean, True), shares(amount, rows * top, most, lean, False)
    places = jnp.arange(amount)

    def named(lengths, turn):
        used = int((lengths > 0).sum())
        fixed = max(1, used // 4)
        moved = fixed + (places - fixed + turn * (used - fixed)) % max(1, amount - fixed)
        return jnp.zeros((amount,), jnp.int32).at[sequence[jnp.where(places < fixed, places, moved)]].set(jnp.asarray(lengths, jnp.int32))

    lengths = jnp.where(number % 4 == 0, named(packed, number // 4), named(common, number - number // 4 - 1))
    mixed = jax.random.permutation(jax.random.fold_in(own, 3), amount)
    donor, receiver = mixed[0:amount // 2 * 2:2], mixed[1:amount // 2 * 2:2]
    margin = jnp.minimum(lengths[donor] - 1, most - lengths[receiver]) // 2
    margin = jnp.where((donor == sequence[0]) | (receiver == sequence[0]) | (lengths[receiver] == 0), 0, jnp.maximum(margin, 0))
    moved = jax.random.randint(jax.random.fold_in(own, 4), (amount // 2,), 0, 1 << 20) % (margin + 1)
    lengths = lengths.at[donor].add(-moved).at[receiver].add(moved)
    labels = jnp.searchsorted(jnp.cumsum(lengths), jnp.arange(rows * top), side="right").astype(jnp.int32)
    table = labels.reshape(top, rows).T
    table = table[jax.random.permutation(jax.random.fold_in(own, 1), rows)]
    turn = jax.random.randint(jax.random.fold_in(own, 2), (rows, 1), 0, top)
    return jnp.take_along_axis(table, (jnp.arange(top)[None, :] + turn) % top, axis=1)


def shares(number_of, total, most, lean, full):
    portions = [(1 << 20) // math.isqrt(rank ** lean) + 1 for rank in range(1, number_of + 1)]
    largest = most if full else min(most, max(-(-total // number_of), total * portions[0] // sum(portions)))
    least = 1 if total - largest >= number_of - 1 else 0
    counts, rest = [largest] + [least] * (number_of - 1), total - largest - least * (number_of - 1)
    while rest > 0:
        movable = [i for i in range(1, number_of) if counts[i] < largest] or [i for i in range(1, number_of) if counts[i] < most]
        mass, left = sum([portions[i] for i in movable]), rest
        for i in movable:
            addition = min(most - counts[i], max(1, left * portions[i] // mass), rest)
            counts[i] = counts[i] + addition
            rest = rest - addition
    return np.array(counts)


def noise(rng, extent, deviation, limit, cuts=(), kind=jnp.bfloat16):
    loudness = shard_levels(rng, extent, cuts, -0.22, 0.18) if cuts else 1.0
    drawn = jax.random.normal(rng, extent, jnp.float32) * deviation * loudness
    return jnp.minimum(jnp.maximum(drawn, -limit), limit).astype(kind)


def setup_inputs(seed: int = 0) -> dict:
    keys = jax.random.split(jax.random.key(seed), 18)
    tokens = noise(keys[0], (TOKENS, D), 1.0, 6.0, ((0, 8),))
    attn_gain = jnp.clip(1.0 + 0.1 * jax.random.normal(keys[1], (D,), jnp.float32), 0.5, 1.5)
    attn_query = noise(keys[2], (D, D), D ** -0.5, 0.15625, ((1, 4),))
    attn_key = noise(keys[3], (D, D), D ** -0.5, 0.15625, ((1, 4),))
    attn_value = noise(keys[4], (D, D), D ** -0.5, 0.15625, ((1, 4),))
    attn_out = noise(keys[5], (D, D), (D // 16) ** -0.5, 0.625, ((1, 4),))
    ffn_gain = jnp.clip(1.0 + 0.1 * jax.random.normal(keys[6], (D,), jnp.float32), 0.5, 1.5)
    router = noise(keys[7], (D, EXPERTS), (4 * D) ** -0.5, 0.078125)
    shared_gate = noise(keys[8], (D, SHARED_FF), D ** -0.5, 0.15625, ((1, 4),))
    shared_up = noise(keys[9], (D, SHARED_FF), D ** -0.5, 0.15625, ((1, 4),))
    shared_down = noise(keys[10], (SHARED_FF, D), SHARED_FF ** -0.5, 0.125, ((0, 4),))
    expert_gate = noise(keys[11], (EXPERTS, D, EXPERT_FF), D ** -0.5, 0.15625, ((0, 8), (2, 4)))
    expert_up = noise(keys[12], (EXPERTS, D, EXPERT_FF), D ** -0.5, 0.15625, ((0, 8), (2, 4)))
    expert_down = noise(keys[13], (EXPERTS, EXPERT_FF, D), 1 ** -0.5, 6.0, ((0, 8), (1, 4)))
    routes_keys = jax.random.split(jax.random.fold_in(keys[14], 1), TOKENS // TOK_DEV)
    routes_turns = jax.random.permutation(jax.random.fold_in(keys[14], 3), TOKENS // TOK_DEV)
    routes = jax.vmap(lambda own, number: deal_out(jax.random.fold_in(keys[14], 2), own, number, TOK_DEV, EXPERTS, TOPK, CAP, 2))(routes_keys, routes_turns).reshape((TOKENS, TOPK))
    documents = jax.vmap(lambda own: jnp.searchsorted(jnp.cumsum(ragged(own, DOCS, TOK_DEV, TOK_DEV // 2, 2)), jnp.arange(TOK_DEV), side="right"))(jax.random.split(keys[15], SEQS)).reshape((SEQS, TOK_DEV)).astype(jnp.int32)
    out_grad = noise(keys[16], (TOKENS, D), 1.0, 6.0, ((0, 8), (1, 4)))
    return {"tokens": tokens, "attn_gain": attn_gain, "attn_query": attn_query, "attn_key": attn_key, "attn_value": attn_value, "attn_out": attn_out, "ffn_gain": ffn_gain, "router": router, "shared_gate": shared_gate, "shared_up": shared_up, "shared_down": shared_down, "expert_gate": expert_gate, "expert_up": expert_up, "expert_down": expert_down, "routes": routes, "documents": documents, "out_grad": out_grad}


@jax.custom_vjp
def low(v):
    return lax.optimization_barrier(v.astype(jnp.bfloat16)).astype(jnp.float32)

@jax.custom_vjp
def low_back(v):
    return v

def low_keep(v):
    return (low(v), None)

def low_pass(kept, grad):
    return (grad,)

def back_keep(v):
    return (v, None)

def back_low(kept, grad):
    return (low(grad),)
low.defvjp(low_keep, low_pass)
low_back.defvjp(back_keep, back_low)
epsilon = 1e-06
highest = lax.Precision.HIGHEST

def rms_norm(values, gain_vec):
    inverse_rms = lax.rsqrt(lax.optimization_barrier(jnp.mean(values * values, axis=-1, keepdims=True)) + epsilon)
    return values * inverse_rms * gain_vec

def rotary(head_values):
    half_dim = HEAD_DIM // 2
    frequency = 10000.0 ** (-jnp.arange(half_dim, dtype=jnp.float32) * 2.0 / HEAD_DIM)
    angles = jnp.arange(TOK_DEV, dtype=jnp.float32)[:, None] * frequency[None, :]
    cosine = jnp.cos(angles)[:, None, :]
    sine_table = jnp.sin(angles)[:, None, :]
    lower_half = head_values[..., :half_dim]
    upper_half = head_values[..., half_dim:]
    return jnp.concatenate([lower_half * cosine - upper_half * sine_table, upper_half * cosine + lower_half * sine_table], axis=-1)

def attend(pieces):
    queries, keys_in, values_in, doc_ids = pieces
    scores = low_back(jnp.einsum('qhd,khd->hqk', queries, keys_in, precision=highest) / math.sqrt(HEAD_DIM))
    positions = jnp.arange(TOK_DEV, dtype=jnp.int32)
    allowed = (positions[:, None] >= positions[None, :]) & (doc_ids[:, None] == doc_ids[None, :])
    scores = jnp.where(allowed[None], scores, -1e+30)
    probs = jax.nn.softmax(scores, axis=-1)
    return jnp.einsum('hqk,khd->qhd', low(probs), values_in, precision=highest)

def expert_rows(pieces):
    rows_in, gate_w, up_w, down_w = pieces
    ex_gate = low_back(jnp.dot(rows_in, gate_w, precision=highest))
    ex_up = low_back(jnp.dot(rows_in, up_w, precision=highest))
    ex_hidden = low(jax.nn.silu(ex_gate) * ex_up)
    return low_back(low(jnp.dot(ex_hidden, down_w, precision=highest)))

def destinations(routes):
    flat_routes = routes.reshape(SEQS, TOK_DEV * TOPK)
    onehot = (flat_routes[:, :, None] == jnp.arange(EXPERTS, dtype=jnp.int32)[None, None, :]).astype(jnp.int32)
    before = jnp.cumsum(onehot, axis=1) - onehot
    slot_index = lax.optimization_barrier(jnp.sum(before * onehot, axis=2))
    source = jnp.arange(SEQS, dtype=jnp.int32)[:, None]
    dest_rows = flat_routes * (SEQS * CAP) + source * CAP + slot_index
    return dest_rows.reshape(TOKENS * TOPK).astype(jnp.int32)

def block_forward(tokens, attn_gain, attn_query, attn_key, attn_value, attn_out, ffn_gain, router, shared_gate, shared_up, shared_down, expert_gate, expert_up, expert_down, routes, documents, dest_rows):
    normed1 = low(rms_norm(tokens, attn_gain))
    head_shape = (SEQS, TOK_DEV, HEADS, HEAD_DIM)
    query_pre = low_back(jnp.dot(normed1, attn_query, precision=highest))
    key_pre = low_back(jnp.dot(normed1, attn_key, precision=highest))
    value_low = low_back(low(jnp.dot(normed1, attn_value, precision=highest)))
    queries = low(rotary(query_pre.reshape(head_shape)))
    keys_all = low(rotary(key_pre.reshape(head_shape)))
    attended = lax.map(jax.checkpoint(attend), (queries, keys_all, value_low.reshape(head_shape), documents))
    attended = low_back(low(attended.reshape(TOKENS, D)))
    residual = tokens + low_back(jnp.dot(attended, attn_out, precision=highest))
    normed2 = low(rms_norm(residual, ffn_gain))
    logits = low_back(jnp.dot(normed2, router, precision=highest))
    gate_probs = jax.nn.softmax(logits, axis=-1)
    weight = jnp.take_along_axis(gate_probs, routes, axis=1)
    sh_gate = low_back(jnp.dot(normed2, shared_gate, precision=highest))
    sh_up = low_back(jnp.dot(normed2, shared_up, precision=highest))
    sh_hidden = low(jax.nn.silu(sh_gate) * sh_up)
    shared_result = jnp.dot(sh_hidden, shared_down, precision=highest)
    token_rows = jnp.broadcast_to(normed2[:, None, :], (TOKENS, TOPK, D)).reshape(TOKENS * TOPK, D)
    buffer = jnp.zeros((EXPERTS * SEQS * CAP, D), jnp.float32).at[dest_rows].add(token_rows)
    buffer = buffer.reshape(EXPERTS, SEQS * CAP, D)
    ex_result = lax.map(jax.checkpoint(expert_rows), (buffer, expert_gate, expert_up, expert_down))
    picked = ex_result.reshape(EXPERTS * SEQS * CAP, D)[dest_rows].reshape(TOKENS, TOPK, D)
    routed = lax.optimization_barrier(jnp.sum(weight[:, :, None] * picked, axis=1))
    return residual + shared_result + routed

def reference(tokens, attn_gain, attn_query, attn_key, attn_value, attn_out, ffn_gain, router, shared_gate, shared_up, shared_down, expert_gate, expert_up, expert_down, routes, documents, out_grad):
    dest_rows = destinations(routes)
    floats = (tokens.astype(jnp.float32), attn_gain.astype(jnp.float32), attn_query.astype(jnp.float32), attn_key.astype(jnp.float32), attn_value.astype(jnp.float32), attn_out.astype(jnp.float32), ffn_gain.astype(jnp.float32), router.astype(jnp.float32), shared_gate.astype(jnp.float32), shared_up.astype(jnp.float32), shared_down.astype(jnp.float32), expert_gate.astype(jnp.float32), expert_up.astype(jnp.float32), expert_down.astype(jnp.float32))

    def layer_fn(*values):
        return block_forward(*values, routes, documents, dest_rows)
    result, pullback = jax.vjp(layer_fn, *floats)
    gradients = pullback(out_grad.astype(jnp.float32))
    return (result.astype(jnp.bfloat16), gradients[0], gradients[1], gradients[2], gradients[3], gradients[4], gradients[5], gradients[6], gradients[7], gradients[8], gradients[9], gradients[10], gradients[11], gradients[12], gradients[13])
```

```python
import math

import jax
import jax.numpy as jnp
from jax import lax
from jax.sharding import Mesh
from jax.sharding import PartitionSpec as P

HEADS = 10
HEAD_DIM = 128
CAP = 112
EPS = 1e-06
EP = ("xy", "core")
bf16 = jnp.bfloat16
f32 = jnp.float32


def dot(a, b):
    return jnp.dot(a, b, preferred_element_type=f32)


def ein(spec, a, b):
    return jnp.einsum(spec, a, b, preferred_element_type=f32)


def rope_tables(rows):
    half = HEAD_DIM // 2
    frequency = 10000.0 ** (-jnp.arange(half, dtype=f32) * 2.0 / HEAD_DIM)
    angles = jnp.arange(rows, dtype=f32)[:, None] * frequency[None, :]
    return jnp.cos(angles)[:, None, :], jnp.sin(angles)[:, None, :]


def rope(v, cosine, sine):
    half = HEAD_DIM // 2
    a, b = v[..., :half], v[..., half:]
    return jnp.concatenate([a * cosine - b * sine, b * cosine + a * sine], axis=-1)


def rope_back(v, cosine, sine):
    half = HEAD_DIM // 2
    a, b = v[..., :half], v[..., half:]
    return jnp.concatenate([a * cosine + b * sine, b * cosine - a * sine], axis=-1)


def shards(
    tokens,
    attn_gain,
    attn_query,
    attn_key,
    attn_value,
    attn_out,
    ffn_gain,
    router,
    shared_gate,
    shared_up,
    shared_down,
    expert_gate,
    expert_up,
    expert_down,
    routes,
    documents,
    out_grad,
):
    rows, width = tokens.shape
    quarter = out_grad.shape[1]
    hs = lax.axis_index("hs")
    hs_count = lax.axis_size("hs")
    odd = (hs % 2) == 1
    ep_count = lax.axis_size("xy") * lax.axis_size("core")
    ep = lax.axis_index("xy") * lax.axis_size("core") + lax.axis_index("core")
    local = expert_gate.shape[0]
    experts = router.shape[1]
    spare = HEAD_DIM * (-(-quarter // HEAD_DIM)) - quarter
    held = quarter + spare
    heads = held // HEAD_DIM
    col0 = hs * quarter

    def outer(w):
        return jnp.where(odd, w[:, :spare], w[:, quarter - spare :])

    pairs = [(i, i ^ 1) for i in range(hs_count)]
    sent = jnp.concatenate([outer(attn_query), outer(attn_key), outer(attn_value)], axis=1)
    got = lax.ppermute(sent, "hs", pairs)

    def widened(w, extra):
        return jnp.where(
            odd, jnp.concatenate([extra, w], axis=1), jnp.concatenate([w, extra], axis=1)
        )

    def own(v):
        return jnp.where(odd, v[:, spare:], v[:, :quarter])

    w_query = widened(attn_query, got[:, :spare])
    w_key = widened(attn_key, got[:, spare : 2 * spare])
    w_value = widened(attn_value, got[:, 2 * spare :])
    out_full = lax.all_gather(attn_out, "hs", axis=1, tiled=True)
    grad_full = lax.all_gather(out_grad, "hs", axis=1, tiled=True)
    grad_all = lax.all_gather(grad_full, EP, axis=0, tiled=True)
    routes_all = lax.all_gather(routes, EP, axis=0, tiled=True)

    x = tokens.astype(f32)
    rms1 = lax.rsqrt(jnp.mean(x * x, axis=-1, keepdims=True) + EPS)
    normed1 = (x * rms1 * attn_gain).astype(bf16)
    cosine, sine = rope_tables(rows)
    shape3 = (rows, heads, HEAD_DIM)
    q = rope(dot(normed1, w_query).reshape(shape3), cosine, sine).astype(bf16)
    k = rope(dot(normed1, w_key).reshape(shape3), cosine, sine).astype(bf16)
    v = dot(normed1, w_value).astype(bf16).reshape(shape3)
    scale = 1.0 / math.sqrt(HEAD_DIM)
    positions = jnp.arange(rows, dtype=jnp.int32)
    doc = documents[0]
    allowed = (positions[:, None] >= positions[None, :]) & (doc[:, None] == doc[None, :])
    scores = jnp.where(allowed[None], ein("qhd,khd->hqk", q, k) * scale, -1e30)
    top = jnp.max(scores, axis=-1, keepdims=True)
    raised = jnp.exp(scores - top)
    probs = raised / jnp.sum(raised, axis=-1, keepdims=True)
    probs_low = probs.astype(bf16)
    attended3 = ein("hqk,khd->qhd", probs_low, v).reshape(rows, held).astype(bf16)
    attended = lax.all_gather(own(attended3), "hs", axis=1, tiled=True)
    residual = x + dot(attended, out_full)
    rms2 = lax.rsqrt(jnp.mean(residual * residual, axis=-1, keepdims=True) + EPS)
    normed2 = (residual * rms2 * ffn_gain).astype(bf16)
    normed_all = lax.all_gather(normed2, EP, axis=0, tiled=True)

    sh_gate = dot(normed2, shared_gate)
    sh_up = dot(normed2, shared_up)
    sh_sig = jax.nn.sigmoid(sh_gate)
    sh_act = sh_gate * sh_sig
    sh_hidden = (sh_act * sh_up).astype(bf16)
    shared_part = dot(sh_hidden, shared_down)
    grad_sh = ein("td,fd->tf", grad_full, shared_down)
    grad_sh_gate = (grad_sh * sh_up * sh_sig * (1 + sh_gate * (1 - sh_sig))).astype(bf16)
    grad_sh_up = (grad_sh * sh_act).astype(bf16)
    grad_shared_down = ein("tf,td->fd", sh_hidden, grad_full)
    grad_shared_gate = ein("td,tf->df", normed2, grad_sh_gate)
    grad_shared_up = ein("td,tf->df", normed2, grad_sh_up)
    shared_back = ein("tf,df->td", grad_sh_gate, shared_gate) + ein(
        "tf,df->td", grad_sh_up, shared_up
    )

    gate_all = jax.nn.softmax(dot(normed_all, router), axis=-1)
    first = ep * local
    weight_all = lax.dynamic_slice_in_dim(gate_all, first, local, 1).reshape(ep_count, rows, local)
    mine = first + jnp.arange(local, dtype=jnp.int32)
    chosen = jnp.any(
        routes_all.reshape(ep_count, rows, -1)[:, :, :, None] == mine[None, None, None, :], axis=2
    )
    below = (positions[:, None] > positions[None, :]).astype(bf16)
    rank = ein("tu,sue->ste", below, chosen.astype(bf16)).astype(jnp.int32)
    slot = jnp.where(chosen, rank, -1).transpose(0, 2, 1)
    pick_f = (slot[:, :, None, :] == jnp.arange(CAP, dtype=jnp.int32)[None, None, :, None]).astype(f32)
    pick = pick_f.astype(bf16).reshape(ep_count, local * CAP, rows)
    slot_weight = jnp.sum(pick_f * weight_all.transpose(0, 2, 1)[:, :, None, :], axis=-1)
    slot_weight = slot_weight.transpose(1, 0, 2).reshape(local, ep_count * CAP, 1)

    def spread(all_rows):
        picked = ein("srt,std->srd", pick, all_rows.reshape(ep_count, rows, width)).astype(bf16)
        return (
            picked.reshape(ep_count, local, CAP, width)
            .transpose(1, 0, 2, 3)
            .reshape(local, ep_count * CAP, width)
        )

    def gathered(slots):
        slots = (
            slots.astype(bf16)
            .reshape(local, ep_count, CAP, -1)
            .transpose(1, 0, 2, 3)
            .reshape(ep_count, local * CAP, -1)
        )
        return ein("srt,srd->std", pick, slots).astype(bf16).reshape(ep_count * rows, -1)

    ex_in = spread(normed_all)
    ex_grad = spread(grad_all)
    ex_gate = ein("erd,edf->erf", ex_in, expert_gate)
    ex_up = ein("erd,edf->erf", ex_in, expert_up)
    sig = jax.nn.sigmoid(ex_gate)
    act = ex_gate * sig
    hidden = (act * ex_up).astype(bf16)
    hidden_w = (hidden.astype(f32) * slot_weight).astype(bf16)
    out_part = gathered(ein("erf,efd->erd", hidden_w, expert_down))
    grad_hidden = ein("erd,efd->erf", ex_grad, expert_down)
    grad_slot_weight = jnp.sum(grad_hidden * hidden.astype(f32), axis=-1)
    grad_hidden = grad_hidden * slot_weight
    grad_ex_gate = (grad_hidden * ex_up * sig * (1 + ex_gate * (1 - sig))).astype(bf16)
    grad_ex_up = (grad_hidden * act).astype(bf16)
    grad_expert_down = ein("erf,erd->efd", hidden_w, ex_grad)
    grad_expert_gate = ein("erd,erf->edf", ex_in, grad_ex_gate)
    grad_expert_up = ein("erd,erf->edf", ex_in, grad_ex_up)
    back = ein("erf,edf->erd", grad_ex_gate, expert_gate) + ein(
        "erf,edf->erd", grad_ex_up, expert_up
    )
    back_part = gathered(back)
    grad_probs_local = jnp.sum(
        pick_f * grad_slot_weight.reshape(local, ep_count, CAP).transpose(1, 0, 2)[..., None], axis=2
    ).transpose(0, 2, 1)
    grad_probs_part = lax.dynamic_update_slice_in_dim(
        jnp.zeros((ep_count * rows, experts), f32), grad_probs_local.reshape(-1, local), first, 1
    ).astype(bf16)
    back_part = jnp.concatenate([back_part, grad_probs_part], axis=1)

    out_rows = lax.psum_scatter(out_part, EP, scatter_dimension=0, tiled=True)
    out_rows = (out_rows.astype(f32) + shared_part).astype(bf16)
    out_quarter = lax.psum_scatter(out_rows, "hs", scatter_dimension=1, tiled=True)

    def quarter_of(a):
        return lax.dynamic_slice_in_dim(a, col0, quarter, 1)

    output = (quarter_of(residual) + out_quarter.astype(f32)).astype(bf16)

    back_rows = lax.psum_scatter(back_part, EP, scatter_dimension=0, tiled=True).astype(f32)
    back_rows = jnp.concatenate([back_rows[:, :width] + shared_back, back_rows[:, width:]], axis=1)
    back_rows = lax.psum(back_rows.astype(bf16), "hs").astype(f32)
    gate_own = jax.nn.softmax(dot(normed2, router), axis=-1)
    grad_probs = back_rows[:, width:]
    grad_logits = (
        gate_own * (grad_probs - jnp.sum(grad_probs * gate_own, axis=-1, keepdims=True))
    ).astype(bf16)
    grad_router = ein("td,te->de", normed2, grad_logits)
    grad_normed2 = back_rows[:, :width] + ein("te,de->td", grad_logits, router)
    grad_ffn_gain = jnp.sum(grad_normed2 * residual * rms2, axis=0)
    u = grad_normed2 * ffn_gain
    grad_residual = (
        grad_full.astype(f32)
        + rms2 * u
        - residual * rms2**3 * jnp.mean(u * residual, axis=-1, keepdims=True)
    )
    grad_low = grad_residual.astype(bf16)
    grad_attn_out = ein("td,tc->dc", attended, quarter_of(grad_low))
    out_held = lax.dynamic_slice_in_dim(out_full, jnp.where(odd, col0 - spare, col0), held, 0)
    grad_attended = ein("tc,dc->td", grad_low, out_held).astype(bf16).reshape(shape3)
    grad_p = ein("qhd,khd->hqk", grad_attended, v)
    grad_v = ein("hqk,qhd->khd", probs_low, grad_attended).astype(bf16)
    grad_s = (probs * (grad_p - jnp.sum(probs * grad_p, axis=-1, keepdims=True))).astype(bf16)
    grad_q = ein("hqk,khd->qhd", grad_s, k) * scale
    grad_k = ein("hqk,qhd->khd", grad_s, q) * scale
    grad_q = own(rope_back(grad_q, cosine, sine).astype(bf16).reshape(rows, held))
    grad_k = own(rope_back(grad_k, cosine, sine).astype(bf16).reshape(rows, held))
    grad_v = own(grad_v.reshape(rows, held))
    normed1_part = (
        ein("tc,dc->td", grad_q, attn_query)
        + ein("tc,dc->td", grad_k, attn_key)
        + ein("tc,dc->td", grad_v, attn_value)
    )
    grad_query = ein("td,tc->dc", normed1, grad_q)
    grad_key = ein("td,tc->dc", normed1, grad_k)
    grad_value = ein("td,tc->dc", normed1, grad_v)
    grad_n1 = lax.psum_scatter(
        normed1_part.astype(bf16), "hs", scatter_dimension=1, tiled=True
    ).astype(f32)
    x_own = quarter_of(x)
    w1 = grad_n1 * lax.dynamic_slice_in_dim(attn_gain, col0, quarter, 0)
    mean1 = lax.psum(jnp.sum(w1 * x_own, axis=-1, keepdims=True), "hs") / width
    grad_tokens = quarter_of(grad_residual) + rms1 * w1 - x_own * rms1**3 * mean1
    gain_own = jnp.sum(grad_n1 * x_own * rms1, axis=0)
    gain_part = lax.dynamic_update_slice_in_dim(jnp.zeros((width,), f32), gain_own, col0, 0)
    grad_attn_gain = lax.psum(gain_part, (*EP, "hs"))

    def over_ep(a):
        return lax.psum(a.astype(bf16), EP).astype(f32)

    return (
        output,
        grad_tokens,
        grad_attn_gain,
        over_ep(grad_query),
        over_ep(grad_key),
        over_ep(grad_value),
        over_ep(grad_attn_out),
        lax.psum(grad_ffn_gain, EP),
        over_ep(grad_router),
        over_ep(grad_shared_gate),
        over_ep(grad_shared_up),
        over_ep(grad_shared_down),
        grad_expert_gate,
        grad_expert_up,
        grad_expert_down,
    )


def solution(mesh):
    ep_count, hs_count = mesh.devices.shape
    cut = Mesh(mesh.devices.reshape(ep_count // 2, 2, hs_count), ("xy", "core", "hs"))
    return jax.shard_map(
        shards,
        mesh=cut,
        in_specs=(
            P(EP, None),
            P(),
            P(None, "hs"),
            P(None, "hs"),
            P(None, "hs"),
            P(None, "hs"),
            P(),
            P(),
            P(None, "hs"),
            P(None, "hs"),
            P("hs", None),
            P(EP, None, "hs"),
            P(EP, None, "hs"),
            P(EP, "hs", None),
            P(EP, None),
            P(EP, None),
            P(EP, "hs"),
        ),
        out_specs=(
            P(EP, "hs"),
            P(EP, "hs"),
            P(),
            P(None, "hs"),
            P(None, "hs"),
            P(None, "hs"),
            P(None, "hs"),
            P(),
            P(),
            P(None, "hs"),
            P(None, "hs"),
            P("hs", None),
            P(EP, None, "hs"),
            P(EP, None, "hs"),
            P(EP, "hs", None),
        ),
        check_vma=False,
    )
```

```python
import functools
import math

import jax
import jax.numpy as jnp
from jax import lax
from jax.experimental import pallas as pl
from jax.experimental.pallas import tpu as pltpu
from jax.sharding import Mesh
from jax.sharding import PartitionSpec as P

HEADS = 10
HEAD_DIM = 128
CAP = 112
EPS = 1e-06
EP = ("xy", "core")
bf16 = jnp.bfloat16
f32 = jnp.float32


def dot(a, b):
    return jnp.dot(a, b, preferred_element_type=f32)


def ein(spec, a, b):
    return jnp.einsum(spec, a, b, preferred_element_type=f32)


def rope_tables(rows):
    half = HEAD_DIM // 2
    frequency = 10000.0 ** (-jnp.arange(half, dtype=f32) * 2.0 / HEAD_DIM)
    angles = jnp.arange(rows, dtype=f32)[:, None] * frequency[None, :]
    return jnp.cos(angles)[:, None, :], jnp.sin(angles)[:, None, :]


def rope(v, cosine, sine):
    half = HEAD_DIM // 2
    a, b = v[..., :half], v[..., half:]
    return jnp.concatenate([a * cosine - b * sine, b * cosine + a * sine], axis=-1)


def rope_back(v, cosine, sine):
    half = HEAD_DIM // 2
    a, b = v[..., :half], v[..., half:]
    return jnp.concatenate([a * cosine + b * sine, b * cosine - a * sine], axis=-1)


VMEM_LIMIT = 60 * 1024 * 1024
PAD = 256


def nn(a, b):
    return lax.dot_general(a, b, (((1,), (0,)), ((), ())), preferred_element_type=f32)


def nt(a, b):
    return lax.dot_general(a, b, (((1,), (1,)), ((), ())), preferred_element_type=f32)


def tn(a, b):
    return lax.dot_general(a, b, (((0,), (0,)), ((), ())), preferred_element_type=f32)


def slot_masks(slot_ref, at):
    local, rows = slot_ref.shape[-2:]
    number = lax.broadcasted_iota(jnp.int32, (CAP, rows), 0)
    return [slot_ref[at, e : e + 1, :] == number for e in range(local)]


def spread_kernel(weighted, *refs):
    if weighted:
        rows_ref, slot_ref, router_ref, x_ref, sw_ref, pick = refs
    else:
        rows_ref, slot_ref, x_ref, pick = refs
    local = slot_ref.shape[1]
    rows = rows_ref[...]
    masks = slot_masks(slot_ref, 0)
    if weighted:
        logits = nt(router_ref[...], rows)
        raised = jnp.exp(logits - jnp.max(logits, axis=0, keepdims=True))
        gates = raised / jnp.sum(raised, axis=0, keepdims=True)
    for e in range(local):
        pick[e * CAP : (e + 1) * CAP, :] = masks[e].astype(f32).astype(bf16)
        if weighted:
            sw_ref[e] = jnp.sum(
                jnp.where(masks[e], gates[e : e + 1, :], 0.0), axis=1, keepdims=True
            )
    x_ref[...] = nn(pick[...], rows).astype(bf16).reshape(x_ref.shape)


def spread(all_rows, slot, router_t=None):
    s, local, rows = slot.shape
    width = all_rows.shape[1]
    weighted = router_t is not None
    in_specs = [
        pl.BlockSpec((rows, width), lambda i: (i, 0)),
        pl.BlockSpec((1, local, rows), lambda i: (i, 0, 0)),
    ]
    out_specs = [pl.BlockSpec((1, local, CAP, width), lambda i: (i, 0, 0, 0))]
    out_shape = [jax.ShapeDtypeStruct((s, local, CAP, width), bf16)]
    args = [all_rows, slot]
    if weighted:
        in_specs.append(pl.BlockSpec(router_t.shape, lambda i: (0, 0)))
        out_specs.append(pl.BlockSpec((local, CAP, 1), lambda i: (0, i, 0)))
        out_shape.append(jax.ShapeDtypeStruct((local, s * CAP, 1), f32))
        args.append(router_t)
    out = pl.pallas_call(
        functools.partial(spread_kernel, weighted),
        grid=(s,),
        in_specs=in_specs,
        out_specs=out_specs,
        out_shape=out_shape,
        scratch_shapes=[pltpu.VMEM((local * CAP, rows), bf16)],
        compiler_params=pltpu.CompilerParams(vmem_limit_bytes=VMEM_LIMIT),
        name="spread",
    )(*args)
    return out if weighted else out[0]


def padded(ref, out):
    ff = ref.shape[1]
    out[:ff, :] = ref[0]
    out[ff:, :] = jnp.zeros((out.shape[0] - ff, out.shape[1]), out.dtype)


def experts_forward_kernel(
    x_ref, sw_ref, wg_ref, wu_ref, wd_ref, y_ref, gate_ref, up_ref, wg, wu, wd
):
    padded(wg_ref, wg)
    padded(wu_ref, wu)
    padded(wd_ref, wd)
    rows, width = gate_ref.shape[1], x_ref.shape[3]
    x = x_ref[...].reshape(rows, width)
    gate = nt(x, wg[...])
    up = nt(x, wu[...])
    gate_ref[0] = gate
    up_ref[0] = up
    act = gate / (1.0 + jnp.exp(-gate))
    hidden = (act * up).astype(bf16).astype(f32)
    hidden_w = (hidden * sw_ref[0]).astype(bf16)
    y_ref[...] = nn(hidden_w, wd[...]).astype(bf16).reshape(y_ref.shape)


def experts_backward_kernel(
    groups,
    x_ref,
    gx_ref,
    gate_ref,
    up_ref,
    sw_ref,
    wg_ref,
    wu_ref,
    wd_ref,
    dx_ref,
    dg_ref,
    du_ref,
    dd_ref,
    gsw_ref,
    wg,
    wu,
    wd,
):
    padded(wg_ref, wg)
    padded(wu_ref, wu)
    padded(wd_ref, wd)
    rows, width = gate_ref.shape[1], x_ref.shape[3]
    ff = wg_ref.shape[1]
    x = x_ref[...].reshape(rows, width)
    gx = gx_ref[...].reshape(rows, width)
    gate, up, sw = gate_ref[0], up_ref[0], sw_ref[0]
    sig = 1.0 / (1.0 + jnp.exp(-gate))
    act = gate * sig
    hidden = (act * up).astype(bf16).astype(f32)
    gh = nt(gx, wd[...])
    gsw_ref[0] = jnp.sum(gh * hidden, axis=-1, keepdims=True)
    gh = gh * sw
    gg = (gh * up * sig * (1.0 + gate * (1.0 - sig))).astype(bf16)
    gu = (gh * act).astype(bf16)
    sums = (
        (dd_ref, tn((hidden * sw).astype(bf16), gx)[:ff]),
        (dg_ref, tn(gg, x)[:ff]),
        (du_ref, tn(gu, x)[:ff]),
    )
    if groups == 1:
        for ref, value in sums:
            ref[0] = value
    else:

        @pl.when(pl.program_id(1) == 0)
        def _():
            for ref, value in sums:
                ref[0] = value

        @pl.when(pl.program_id(1) > 0)
        def _():
            for ref, value in sums:
                ref[0] += value

    dx_ref[...] = (nn(gg, wg[...]) + nn(gu, wu[...])).astype(bf16).reshape(dx_ref.shape)


def expert_specs(s, width):
    group = min(s, 8)
    slots = pl.BlockSpec((group, 1, CAP, width), lambda i, j: (j, i, 0, 0))
    lines = lambda columns: pl.BlockSpec((1, group * CAP, columns), lambda i, j: (i, j, 0))
    per = lambda *shape: pl.BlockSpec((1, *shape), lambda i, j: (i, 0, 0))
    return s // group, slots, lines, per


def experts_forward(x, sw, wg, wu, wd):
    s, local, cap, width = x.shape
    ff = wg.shape[1]
    rows = s * cap
    groups, slots, lines, per = expert_specs(s, width)
    middle = jax.ShapeDtypeStruct((local, rows, PAD), f32)
    return pl.pallas_call(
        experts_forward_kernel,
        grid=(local, groups),
        in_specs=[slots, lines(1)] + [per(ff, width)] * 3,
        out_specs=[slots, lines(PAD), lines(PAD)],
        out_shape=[jax.ShapeDtypeStruct(x.shape, bf16), middle, middle],
        scratch_shapes=[pltpu.VMEM((PAD, width), bf16)] * 3,
        compiler_params=pltpu.CompilerParams(vmem_limit_bytes=VMEM_LIMIT),
        name="experts_forward",
    )(x, sw, wg, wu, wd)


def experts_backward(x, gx, gate, up, sw, wg, wu, wd):
    s, local, cap, width = x.shape
    ff = wg.shape[1]
    rows = s * cap
    groups, slots, lines, per = expert_specs(s, width)
    return pl.pallas_call(
        functools.partial(experts_backward_kernel, groups),
        grid=(local, groups),
        in_specs=[slots, slots, lines(PAD), lines(PAD), lines(1)]
        + [per(ff, width)] * 3,
        out_specs=[slots] + [per(ff, width)] * 3 + [lines(1)],
        out_shape=[jax.ShapeDtypeStruct(x.shape, bf16)]
        + [jax.ShapeDtypeStruct((local, ff, width), f32)] * 3
        + [jax.ShapeDtypeStruct((local, rows, 1), f32)],
        scratch_shapes=[pltpu.VMEM((PAD, width), bf16)] * 3,
        compiler_params=pltpu.CompilerParams(vmem_limit_bytes=VMEM_LIMIT),
        name="experts_backward",
    )(x, gx, gate, up, sw, wg, wu, wd)


def collect_kernel(y_ref, slot_ref, out_ref, pick):
    local = slot_ref.shape[1]
    masks = slot_masks(slot_ref, 0)
    for e in range(local):
        pick[e * CAP : (e + 1) * CAP, :] = masks[e].astype(f32).astype(bf16)
    out_ref[0] = tn(pick[...], y_ref[...].reshape(pick.shape[0], -1)).astype(bf16)


def collect_back_kernel(experts, y_ref, slot_ref, gsw_ref, first_ref, out_ref, pick):
    local, rows = slot_ref.shape[1:]
    first = first_ref[0]
    masks = slot_masks(slot_ref, 0)
    number = lax.broadcasted_iota(jnp.int32, (experts, rows), 0)
    probs = jnp.zeros((experts, rows), f32)
    for e in range(local):
        pick[e * CAP : (e + 1) * CAP, :] = masks[e].astype(f32).astype(bf16)
        line = jnp.sum(jnp.where(masks[e], gsw_ref[e], 0.0), axis=0, keepdims=True)
        probs = jnp.where(number == first + e, line, probs)
    out_ref[0, :rows] = tn(pick[...], y_ref[...].reshape(pick.shape[0], -1)).astype(bf16)
    half = experts // 2
    out_ref[0, rows:] = jnp.zeros((half, out_ref.shape[2]), bf16)
    out_ref[0, rows:, :rows] = probs[:half].astype(bf16)
    out_ref[0, rows:, rows : 2 * rows] = probs[half:].astype(bf16)


def collect(y, slot, gsw=None, first=None, experts=0):
    s, local, cap, width = y.shape
    rows = slot.shape[2]
    in_specs = [
        pl.BlockSpec((1, local, cap, width), lambda i: (i, 0, 0, 0)),
        pl.BlockSpec((1, local, rows), lambda i: (i, 0, 0)),
    ]
    args = [y, slot]
    kernel = collect_kernel
    tall = rows
    if gsw is not None:
        in_specs += [
            pl.BlockSpec((local, cap, 1), lambda i: (0, i, 0)),
            pl.BlockSpec(memory_space=pltpu.SMEM),
        ]
        args += [gsw, first.reshape(1)]
        kernel = functools.partial(collect_back_kernel, experts)
        tall = rows + experts // 2
    return pl.pallas_call(
        kernel,
        grid=(s,),
        in_specs=in_specs,
        out_specs=pl.BlockSpec((1, tall, width), lambda i: (i, 0, 0)),
        out_shape=jax.ShapeDtypeStruct((s, tall, width), bf16),
        scratch_shapes=[pltpu.VMEM((local * cap, rows), bf16)],
        compiler_params=pltpu.CompilerParams(vmem_limit_bytes=VMEM_LIMIT),
        name="collect",
    )(*args)


def shards(
    tokens,
    attn_gain,
    attn_query,
    attn_key,
    attn_value,
    attn_out,
    ffn_gain,
    router,
    shared_gate,
    shared_up,
    shared_down,
    expert_gate,
    expert_up,
    expert_down,
    routes,
    documents,
    out_grad,
):
    rows, width = tokens.shape
    quarter = out_grad.shape[1]
    hs = lax.axis_index("hs")
    hs_count = lax.axis_size("hs")
    odd = (hs % 2) == 1
    ep_count = lax.axis_size("xy") * lax.axis_size("core")
    ep = lax.axis_index("xy") * lax.axis_size("core") + lax.axis_index("core")
    local = expert_gate.shape[0]
    experts = router.shape[1]
    spare = HEAD_DIM * (-(-quarter // HEAD_DIM)) - quarter
    held = quarter + spare
    heads = held // HEAD_DIM
    col0 = hs * quarter

    def outer(w):
        return jnp.where(odd, w[:, :spare], w[:, quarter - spare :])

    pairs = [(i, i ^ 1) for i in range(hs_count)]
    sent = jnp.concatenate([outer(attn_query), outer(attn_key), outer(attn_value)], axis=1)
    got = lax.ppermute(sent, "hs", pairs)

    def widened(w, extra):
        return jnp.where(
            odd, jnp.concatenate([extra, w], axis=1), jnp.concatenate([w, extra], axis=1)
        )

    def own(v):
        return jnp.where(odd, v[:, spare:], v[:, :quarter])

    w_query = widened(attn_query, got[:, :spare])
    w_key = widened(attn_key, got[:, spare : 2 * spare])
    w_value = widened(attn_value, got[:, 2 * spare :])
    out_full = lax.all_gather(attn_out, "hs", axis=1, tiled=True)
    grad_full = lax.all_gather(out_grad, "hs", axis=1, tiled=True)
    grad_all = lax.all_gather(grad_full, EP, axis=0, tiled=True)
    routes_all = lax.all_gather(routes, EP, axis=0, tiled=True)

    x = tokens.astype(f32)
    rms1 = lax.rsqrt(jnp.mean(x * x, axis=-1, keepdims=True) + EPS)
    normed1 = (x * rms1 * attn_gain).astype(bf16)
    cosine, sine = rope_tables(rows)
    shape3 = (rows, heads, HEAD_DIM)
    q = rope(dot(normed1, w_query).reshape(shape3), cosine, sine).astype(bf16)
    k = rope(dot(normed1, w_key).reshape(shape3), cosine, sine).astype(bf16)
    v = dot(normed1, w_value).astype(bf16).reshape(shape3)
    scale = 1.0 / math.sqrt(HEAD_DIM)
    positions = jnp.arange(rows, dtype=jnp.int32)
    doc = documents[0]
    allowed = (positions[:, None] >= positions[None, :]) & (doc[:, None] == doc[None, :])
    scores = jnp.where(allowed[None], ein("qhd,khd->hqk", q, k) * scale, -1e30)
    top = jnp.max(scores, axis=-1, keepdims=True)
    raised = jnp.exp(scores - top)
    probs = raised / jnp.sum(raised, axis=-1, keepdims=True)
    probs_low = probs.astype(bf16)
    attended3 = ein("hqk,khd->qhd", probs_low, v).reshape(rows, held).astype(bf16)
    attended = lax.all_gather(own(attended3), "hs", axis=1, tiled=True)
    residual = x + dot(attended, out_full)
    rms2 = lax.rsqrt(jnp.mean(residual * residual, axis=-1, keepdims=True) + EPS)
    normed2 = (residual * rms2 * ffn_gain).astype(bf16)
    normed_all = lax.all_gather(normed2, EP, axis=0, tiled=True)

    sh_gate = dot(normed2, shared_gate)
    sh_up = dot(normed2, shared_up)
    sh_sig = jax.nn.sigmoid(sh_gate)
    sh_act = sh_gate * sh_sig
    sh_hidden = (sh_act * sh_up).astype(bf16)
    shared_part = dot(sh_hidden, shared_down)
    grad_sh = ein("td,fd->tf", grad_full, shared_down)
    grad_sh_gate = (grad_sh * sh_up * sh_sig * (1 + sh_gate * (1 - sh_sig))).astype(bf16)
    grad_sh_up = (grad_sh * sh_act).astype(bf16)
    grad_shared_down = ein("tf,td->fd", sh_hidden, grad_full)
    grad_shared_gate = ein("td,tf->df", normed2, grad_sh_gate)
    grad_shared_up = ein("td,tf->df", normed2, grad_sh_up)
    shared_back = ein("tf,df->td", grad_sh_gate, shared_gate) + ein(
        "tf,df->td", grad_sh_up, shared_up
    )

    first = ep * local
    mine = first + jnp.arange(local, dtype=jnp.int32)
    chosen = jnp.any(
        routes_all.reshape(ep_count, rows, -1)[:, :, :, None] == mine[None, None, None, :], axis=2
    )
    below = (positions[:, None] > positions[None, :]).astype(bf16)
    rank = ein("tu,sue->ste", below, chosen.astype(bf16)).astype(jnp.int32)
    slot = jnp.where(chosen, rank, -1).transpose(0, 2, 1)
    router_t = jnp.roll(router.T, -first, axis=0)

    gate_t, up_t = expert_gate.swapaxes(1, 2), expert_up.swapaxes(1, 2)
    ex_grad = spread(grad_all, slot)
    ex_in, slot_weight = spread(normed_all, slot, router_t)
    ex_out, ex_gate, ex_up = experts_forward(ex_in, slot_weight, gate_t, up_t, expert_down)
    out_part = collect(ex_out, slot).reshape(ep_count * rows, width)
    ex_back, grad_gate_t, grad_up_t, grad_expert_down, grad_slot_weight = experts_backward(
        ex_in, ex_grad, ex_gate, ex_up, slot_weight, gate_t, up_t, expert_down
    )
    grad_expert_gate, grad_expert_up = grad_gate_t.swapaxes(1, 2), grad_up_t.swapaxes(1, 2)
    back_part = collect(ex_back, slot, grad_slot_weight, first, experts)
    back_part = back_part.reshape(-1, width)

    out_rows = lax.psum_scatter(out_part, EP, scatter_dimension=0, tiled=True)
    out_rows = (out_rows.astype(f32) + shared_part).astype(bf16)
    out_quarter = lax.psum_scatter(out_rows, "hs", scatter_dimension=1, tiled=True)

    def quarter_of(a):
        return lax.dynamic_slice_in_dim(a, col0, quarter, 1)

    output = (quarter_of(residual) + out_quarter.astype(f32)).astype(bf16)

    back_rows = lax.psum_scatter(back_part, EP, scatter_dimension=0, tiled=True).astype(f32)
    back_rows = jnp.concatenate([back_rows[:rows] + shared_back, back_rows[rows:]], axis=0)
    back_rows = lax.psum(back_rows.astype(bf16), "hs").astype(f32)
    gate_own = jax.nn.softmax(dot(normed2, router), axis=-1)
    grad_probs = jnp.concatenate(
        [back_rows[rows:, :rows], back_rows[rows:, rows : 2 * rows]], axis=0
    ).T
    grad_logits = (
        gate_own * (grad_probs - jnp.sum(grad_probs * gate_own, axis=-1, keepdims=True))
    ).astype(bf16)
    grad_router = ein("td,te->de", normed2, grad_logits)
    grad_normed2 = back_rows[:rows] + ein("te,de->td", grad_logits, router)
    grad_ffn_gain = jnp.sum(grad_normed2 * residual * rms2, axis=0)
    u = grad_normed2 * ffn_gain
    grad_residual = (
        grad_full.astype(f32)
        + rms2 * u
        - residual * rms2**3 * jnp.mean(u * residual, axis=-1, keepdims=True)
    )
    grad_low = grad_residual.astype(bf16)
    grad_attn_out = ein("td,tc->dc", attended, quarter_of(grad_low))
    out_held = lax.dynamic_slice_in_dim(out_full, jnp.where(odd, col0 - spare, col0), held, 0)
    grad_attended = ein("tc,dc->td", grad_low, out_held).astype(bf16).reshape(shape3)
    grad_p = ein("qhd,khd->hqk", grad_attended, v)
    grad_v = ein("hqk,qhd->khd", probs_low, grad_attended).astype(bf16)
    grad_s = (probs * (grad_p - jnp.sum(probs * grad_p, axis=-1, keepdims=True))).astype(bf16)
    grad_q = ein("hqk,khd->qhd", grad_s, k) * scale
    grad_k = ein("hqk,qhd->khd", grad_s, q) * scale
    grad_q = own(rope_back(grad_q, cosine, sine).astype(bf16).reshape(rows, held))
    grad_k = own(rope_back(grad_k, cosine, sine).astype(bf16).reshape(rows, held))
    grad_v = own(grad_v.reshape(rows, held))
    normed1_part = (
        ein("tc,dc->td", grad_q, attn_query)
        + ein("tc,dc->td", grad_k, attn_key)
        + ein("tc,dc->td", grad_v, attn_value)
    )
    grad_query = ein("td,tc->dc", normed1, grad_q)
    grad_key = ein("td,tc->dc", normed1, grad_k)
    grad_value = ein("td,tc->dc", normed1, grad_v)
    grad_n1 = lax.psum_scatter(
        normed1_part.astype(bf16), "hs", scatter_dimension=1, tiled=True
    ).astype(f32)
    x_own = quarter_of(x)
    w1 = grad_n1 * lax.dynamic_slice_in_dim(attn_gain, col0, quarter, 0)
    mean1 = lax.psum(jnp.sum(w1 * x_own, axis=-1, keepdims=True), "hs") / width
    grad_tokens = quarter_of(grad_residual) + rms1 * w1 - x_own * rms1**3 * mean1
    gain_own = jnp.sum(grad_n1 * x_own * rms1, axis=0)
    gain_part = lax.dynamic_update_slice_in_dim(jnp.zeros((width,), f32), gain_own, col0, 0)
    grad_attn_gain = lax.psum(gain_part, (*EP, "hs"))

    def over_ep(a):
        return lax.psum(a.astype(bf16), EP).astype(f32)

    return (
        output,
        grad_tokens,
        grad_attn_gain,
        over_ep(grad_query),
        over_ep(grad_key),
        over_ep(grad_value),
        over_ep(grad_attn_out),
        lax.psum(grad_ffn_gain, EP),
        over_ep(grad_router),
        over_ep(grad_shared_gate),
        over_ep(grad_shared_up),
        over_ep(grad_shared_down),
        grad_expert_gate,
        grad_expert_up,
        grad_expert_down,
    )


def solution(mesh):
    ep_count, hs_count = mesh.devices.shape
    cut = Mesh(mesh.devices.reshape(ep_count // 2, 2, hs_count), ("xy", "core", "hs"))
    return jax.shard_map(
        shards,
        mesh=cut,
        in_specs=(
            P(EP, None),
            P(),
            P(None, "hs"),
            P(None, "hs"),
            P(None, "hs"),
            P(None, "hs"),
            P(),
            P(),
            P(None, "hs"),
            P(None, "hs"),
            P("hs", None),
            P(EP, None, "hs"),
            P(EP, None, "hs"),
            P(EP, "hs", None),
            P(EP, None),
            P(EP, None),
            P(EP, "hs"),
        ),
        out_specs=(
            P(EP, "hs"),
            P(EP, "hs"),
            P(),
            P(None, "hs"),
            P(None, "hs"),
            P(None, "hs"),
            P(None, "hs"),
            P(),
            P(),
            P(None, "hs"),
            P(None, "hs"),
            P("hs", None),
            P(EP, None, "hs"),
            P(EP, None, "hs"),
            P(EP, "hs", None),
        ),
        check_vma=False,
    )
```

```python
import functools
import math

import jax
import jax.numpy as jnp
from jax import lax
from jax.experimental import pallas as pl
from jax.experimental.pallas import tpu as pltpu
from jax.sharding import Mesh
from jax.sharding import PartitionSpec as P

HEADS = 10
HEAD_DIM = 128
CAP = 112
EPS = 1e-06
EP = ("xy", "core")
bf16 = jnp.bfloat16
f32 = jnp.float32


def dot(a, b):
    return jnp.dot(a, b, preferred_element_type=f32)


def ein(spec, a, b):
    return jnp.einsum(spec, a, b, preferred_element_type=f32)


def rope_tables(rows):
    half = HEAD_DIM // 2
    frequency = 10000.0 ** (-jnp.arange(half, dtype=f32) * 2.0 / HEAD_DIM)
    angles = jnp.arange(rows, dtype=f32)[:, None] * frequency[None, :]
    return jnp.cos(angles)[:, None, :], jnp.sin(angles)[:, None, :]


def rope(v, cosine, sine):
    half = HEAD_DIM // 2
    a, b = v[..., :half], v[..., half:]
    return jnp.concatenate([a * cosine - b * sine, b * cosine + a * sine], axis=-1)


def rope_back(v, cosine, sine):
    half = HEAD_DIM // 2
    a, b = v[..., :half], v[..., half:]
    return jnp.concatenate([a * cosine + b * sine, b * cosine - a * sine], axis=-1)


VMEM_LIMIT = 60 * 1024 * 1024
PAD = 256


def nn(a, b):
    return lax.dot_general(a, b, (((1,), (0,)), ((), ())), preferred_element_type=f32)


def nt(a, b):
    return lax.dot_general(a, b, (((1,), (1,)), ((), ())), preferred_element_type=f32)


def tn(a, b):
    return lax.dot_general(a, b, (((0,), (0,)), ((), ())), preferred_element_type=f32)


def slot_masks(slot_ref, at):
    local, rows = slot_ref.shape[-2:]
    number = lax.broadcasted_iota(jnp.int32, (CAP, rows), 0)
    return [slot_ref[at, e : e + 1, :] == number for e in range(local)]


def spread_kernel(weighted, *refs):
    if weighted:
        rows_ref, slot_ref, router_ref, x_ref, sw_ref, pick = refs
    else:
        rows_ref, slot_ref, x_ref, pick = refs
    local = slot_ref.shape[1]
    rows = rows_ref[...] if weighted else rows_ref[0]
    masks = slot_masks(slot_ref, 0)
    if weighted:
        logits = nt(router_ref[...], rows)
        raised = jnp.exp(logits - jnp.max(logits, axis=0, keepdims=True))
        gates = raised / jnp.sum(raised, axis=0, keepdims=True)
    for e in range(local):
        pick[e * CAP : (e + 1) * CAP, :] = masks[e].astype(f32).astype(bf16)
        if weighted:
            sw_ref[e] = jnp.sum(
                jnp.where(masks[e], gates[e : e + 1, :], 0.0), axis=1, keepdims=True
            )
    product = nn if weighted else nt
    x_ref[...] = product(pick[...], rows).astype(bf16).reshape(x_ref.shape)


def spread(all_rows, slot, router_t=None):
    s, local, rows = slot.shape
    weighted = router_t is not None
    if weighted:
        width = all_rows.shape[1]
        block = pl.BlockSpec((rows, width), lambda i: (i, 0))
    else:
        width = all_rows.shape[1]
        block = pl.BlockSpec((1, width, rows), lambda i: (i, 0, 0))
    in_specs = [
        block,
        pl.BlockSpec((1, local, rows), lambda i: (i, 0, 0)),
    ]
    out_specs = [pl.BlockSpec((1, local, CAP, width), lambda i: (i, 0, 0, 0))]
    out_shape = [jax.ShapeDtypeStruct((s, local, CAP, width), bf16)]
    args = [all_rows, slot]
    if weighted:
        in_specs.append(pl.BlockSpec(router_t.shape, lambda i: (0, 0)))
        out_specs.append(pl.BlockSpec((local, CAP, 1), lambda i: (0, i, 0)))
        out_shape.append(jax.ShapeDtypeStruct((local, s * CAP, 1), f32))
        args.append(router_t)
    out = pl.pallas_call(
        functools.partial(spread_kernel, weighted),
        grid=(s,),
        in_specs=in_specs,
        out_specs=out_specs,
        out_shape=out_shape,
        scratch_shapes=[pltpu.VMEM((local * CAP, rows), bf16)],
        compiler_params=pltpu.CompilerParams(vmem_limit_bytes=VMEM_LIMIT),
        name="spread",
    )(*args)
    return out if weighted else out[0]


def padded(ref, out):
    ff = ref.shape[1]
    out[:ff, :] = ref[0]
    out[ff:, :] = jnp.zeros((out.shape[0] - ff, out.shape[1]), out.dtype)


def experts_forward_kernel(
    x_ref, sw_ref, wg_ref, wu_ref, wd_ref, y_ref, gate_ref, up_ref, wg, wu, wd
):
    padded(wg_ref, wg)
    padded(wu_ref, wu)
    padded(wd_ref, wd)
    rows, width = gate_ref.shape[1], x_ref.shape[3]
    x = x_ref[...].reshape(rows, width)
    gate = nt(x, wg[...])
    up = nt(x, wu[...])
    gate_ref[0] = gate
    up_ref[0] = up
    act = gate / (1.0 + jnp.exp(-gate))
    hidden = (act * up).astype(bf16).astype(f32)
    hidden_w = (hidden * sw_ref[0]).astype(bf16)
    y_ref[...] = nn(hidden_w, wd[...]).astype(bf16).reshape(y_ref.shape)


def experts_backward_kernel(
    groups,
    x_ref,
    gx_ref,
    gate_ref,
    up_ref,
    sw_ref,
    wg_ref,
    wu_ref,
    wd_ref,
    dx_ref,
    dg_ref,
    du_ref,
    dd_ref,
    gsw_ref,
    wg,
    wu,
    wd,
):
    padded(wg_ref, wg)
    padded(wu_ref, wu)
    padded(wd_ref, wd)
    rows, width = gate_ref.shape[1], x_ref.shape[3]
    ff = wg_ref.shape[1]
    x = x_ref[...].reshape(rows, width)
    gx = gx_ref[...].reshape(rows, width)
    gate, up, sw = gate_ref[0], up_ref[0], sw_ref[0]
    sig = 1.0 / (1.0 + jnp.exp(-gate))
    act = gate * sig
    hidden = (act * up).astype(bf16).astype(f32)
    gh = nt(gx, wd[...])
    gsw_ref[0] = jnp.sum(gh * hidden, axis=-1, keepdims=True)
    gh = gh * sw
    gg = (gh * up * sig * (1.0 + gate * (1.0 - sig))).astype(bf16)
    gu = (gh * act).astype(bf16)
    sums = (
        (dd_ref, tn((hidden * sw).astype(bf16), gx)[:ff]),
        (dg_ref, tn(gg, x)[:ff]),
        (du_ref, tn(gu, x)[:ff]),
    )
    if groups == 1:
        for ref, value in sums:
            ref[0] = value
    else:

        @pl.when(pl.program_id(1) == 0)
        def _():
            for ref, value in sums:
                ref[0] = value

        @pl.when(pl.program_id(1) > 0)
        def _():
            for ref, value in sums:
                ref[0] += value

    dx_ref[...] = (nn(gg, wg[...]) + nn(gu, wu[...])).astype(bf16).reshape(dx_ref.shape)


def expert_specs(s, width):
    group = min(s, 8)
    slots = pl.BlockSpec((group, 1, CAP, width), lambda i, j: (j, i, 0, 0))
    lines = lambda columns: pl.BlockSpec((1, group * CAP, columns), lambda i, j: (i, j, 0))
    per = lambda *shape: pl.BlockSpec((1, *shape), lambda i, j: (i, 0, 0))
    return s // group, slots, lines, per


def experts_forward(x, sw, wg, wu, wd):
    s, local, cap, width = x.shape
    ff = wg.shape[1]
    rows = s * cap
    groups, slots, lines, per = expert_specs(s, width)
    middle = jax.ShapeDtypeStruct((local, rows, PAD), f32)
    return pl.pallas_call(
        experts_forward_kernel,
        grid=(local, groups),
        in_specs=[slots, lines(1)] + [per(ff, width)] * 3,
        out_specs=[slots, lines(PAD), lines(PAD)],
        out_shape=[jax.ShapeDtypeStruct(x.shape, bf16), middle, middle],
        scratch_shapes=[pltpu.VMEM((PAD, width), bf16)] * 3,
        compiler_params=pltpu.CompilerParams(vmem_limit_bytes=VMEM_LIMIT),
        name="experts_forward",
    )(x, sw, wg, wu, wd)


def experts_backward(x, gx, gate, up, sw, wg, wu, wd):
    s, local, cap, width = x.shape
    ff = wg.shape[1]
    rows = s * cap
    groups, slots, lines, per = expert_specs(s, width)
    return pl.pallas_call(
        functools.partial(experts_backward_kernel, groups),
        grid=(local, groups),
        in_specs=[slots, slots, lines(PAD), lines(PAD), lines(1)]
        + [per(ff, width)] * 3,
        out_specs=[slots] + [per(ff, width)] * 3 + [lines(1)],
        out_shape=[jax.ShapeDtypeStruct(x.shape, bf16)]
        + [jax.ShapeDtypeStruct((local, ff, width), f32)] * 3
        + [jax.ShapeDtypeStruct((local, rows, 1), f32)],
        scratch_shapes=[pltpu.VMEM((PAD, width), bf16)] * 3,
        compiler_params=pltpu.CompilerParams(vmem_limit_bytes=VMEM_LIMIT),
        name="experts_backward",
    )(x, gx, gate, up, sw, wg, wu, wd)


def collect_kernel(y_ref, slot_ref, out_ref, pick):
    local = slot_ref.shape[1]
    masks = slot_masks(slot_ref, 0)
    for e in range(local):
        pick[e * CAP : (e + 1) * CAP, :] = masks[e].astype(f32).astype(bf16)
    out_ref[0] = tn(pick[...], y_ref[...].reshape(pick.shape[0], -1)).astype(bf16)


def collect_back_kernel(experts, y_ref, slot_ref, gsw_ref, first_ref, out_ref, pick):
    local, rows = slot_ref.shape[1:]
    first = first_ref[0]
    masks = slot_masks(slot_ref, 0)
    number = lax.broadcasted_iota(jnp.int32, (experts, rows), 0)
    probs = jnp.zeros((experts, rows), f32)
    for e in range(local):
        pick[e * CAP : (e + 1) * CAP, :] = masks[e].astype(f32).astype(bf16)
        line = jnp.sum(jnp.where(masks[e], gsw_ref[e], 0.0), axis=0, keepdims=True)
        probs = jnp.where(number == first + e, line, probs)
    out_ref[0, :rows] = tn(pick[...], y_ref[...].reshape(pick.shape[0], -1)).astype(bf16)
    out_ref[0, rows:] = jnp.zeros((experts, out_ref.shape[2]), bf16)
    out_ref[0, rows:, :rows] = probs.astype(bf16)


def collect(y, slot, gsw=None, first=None, experts=0):
    s, local, cap, width = y.shape
    rows = slot.shape[2]
    in_specs = [
        pl.BlockSpec((1, local, cap, width), lambda i: (i, 0, 0, 0)),
        pl.BlockSpec((1, local, rows), lambda i: (i, 0, 0)),
    ]
    args = [y, slot]
    kernel = collect_kernel
    tall = rows
    if gsw is not None:
        in_specs += [
            pl.BlockSpec((local, cap, 1), lambda i: (0, i, 0)),
            pl.BlockSpec(memory_space=pltpu.SMEM),
        ]
        args += [gsw, first.reshape(1)]
        kernel = functools.partial(collect_back_kernel, experts)
        tall = rows + experts
    return pl.pallas_call(
        kernel,
        grid=(s,),
        in_specs=in_specs,
        out_specs=pl.BlockSpec((1, tall, width), lambda i: (i, 0, 0)),
        out_shape=jax.ShapeDtypeStruct((s, tall, width), bf16),
        scratch_shapes=[pltpu.VMEM((local * cap, rows), bf16)],
        compiler_params=pltpu.CompilerParams(vmem_limit_bytes=VMEM_LIMIT),
        name="collect",
    )(*args)


MESH = pl.DeviceIdType.MESH
EXTRA = 64


def places():
    chip, core, z = lax.axis_index("xy"), lax.axis_index("core"), lax.axis_index("hs")
    x, y = chip % 2, chip // 2
    return chip, core, z, y * 2 + (1 - x), (1 - y) * 2 + x, (1 - y) * 2 + (1 - x)


def greet(peers):
    barrier = pltpu.get_barrier_semaphore()
    for peer in peers:
        pl.semaphore_signal(barrier, inc=1, device_id=peer, device_id_type=MESH)
    pl.semaphore_wait(barrier, len(peers))


def remote(src, dst, send, recv, peer):
    return pltpu.make_async_remote_copy(
        src_ref=src, dst_ref=dst, send_sem=send, recv_sem=recv, device_id=peer, device_id_type=MESH
    )


def gather_spread_kernel(
    own_ref, slots_ref, router_ref, x_ref, sw_ref, slot_ref, held, pick, xbuf, send, recv, copied
):
    chip, core, z, cx, cy, cd = places()
    other = 1 - core
    x_peer, y_peer, c_peer = (cx, core, z), (cy, core, z), (chip, other, z)
    tall = held.shape[1]
    half = tall // 2
    local, rows = slot_ref.shape[1:]
    me = chip * 2 + core
    top, low = pl.ds(0, half), pl.ds(half, half)

    def at(c, k):
        return c * 2 + k

    def move(number, src_slot, part, peer):
        return remote(
            held.at[src_slot, part], held.at[src_slot, part], send.at[number], recv.at[number], peer
        )

    whole = pl.ds(0, tall)
    greet([x_peer, y_peer, c_peer])
    held[me, :rows] = own_ref[...]
    held[me, rows:] = jnp.zeros((EXTRA, own_ref.shape[1]), bf16)
    held[me, rows:, :rows] = slots_ref[...]
    x_top, x_low = move(0, me, top, x_peer), move(1, me, low, x_peer)
    y_low, y_top = move(2, me, low, y_peer), move(3, me, top, y_peer)
    to_core = move(4, me, whole, c_peer)
    relay_top, relay_low = move(5, at(cx, core), top, y_peer), move(6, at(cy, core), low, x_peer)
    pass_x, pass_y = move(7, at(cx, core), whole, c_peer), move(8, at(cy, core), whole, c_peer)
    pass_d = move(9, at(cd, core), whole, c_peer)
    for copy in (x_top, y_low, x_low, y_top, to_core):
        copy.start()

    def arrived(number, slot, part):
        move(number, slot, part, c_peer).wait_recv()

    number = lax.broadcasted_iota(jnp.int32, (CAP, rows), 0)
    first = me * local
    line = lax.broadcasted_iota(jnp.int32, (local, EXTRA), 0)
    column = lax.broadcasted_iota(jnp.int32, (local, EXTRA), 1)
    chosen = (column == line + first).astype(f32).astype(bf16)

    def out_copy(t, src):
        return pltpu.make_async_copy(xbuf.at[t % 2], x_ref.at[src], copied.at[t % 2])

    def step(t, carry):
        @pl.when(t == 1)
        def _():
            arrived(4, at(chip, other), whole)

        @pl.when(t == 2)
        def _():
            arrived(0, at(cx, core), top)
            relay_top.start()
            arrived(2, at(cy, core), low)
            relay_low.start()
            arrived(1, at(cx, core), low)
            pass_x.start()

        @pl.when(t == 3)
        def _():
            arrived(3, at(cy, core), top)
            pass_y.start()
            arrived(7, at(cx, other), whole)

        @pl.when(t == 5)
        def _():
            arrived(8, at(cy, other), whole)

        @pl.when(t == 6)
        def _():
            arrived(5, at(cd, core), top)
            arrived(6, at(cd, core), low)
            pass_d.start()

        @pl.when(t == 7)
        def _():
            arrived(9, at(cd, other), whole)

        x, y = (chip % 2 + (t // 2) % 2) % 2, (chip // 2 + t // 4) % 2
        src = (y * 2 + x) * 2 + (core + t % 2) % 2
        slots = nn(chosen, held[src, rows:, :rows]).astype(jnp.int32)
        slot_ref[src] = slots
        logits = nt(router_ref[...], held[src, :rows])
        raised = jnp.exp(logits - jnp.max(logits, axis=0, keepdims=True))
        gates = raised / jnp.sum(raised, axis=0, keepdims=True)
        for e in range(local):
            mask = slots[e : e + 1, :] == number
            pick[e * CAP : (e + 1) * CAP, :] = mask.astype(f32).astype(bf16)
            sw_ref[e, pl.ds(pl.multiple_of(src * CAP, 8), CAP), :] = jnp.sum(
                jnp.where(mask, gates[e : e + 1, :], 0.0), axis=1, keepdims=True
            )

        @pl.when(t >= 2)
        def _():
            out_copy(t, src).wait()

        xbuf[t % 2] = nn(pick[...], held[src, :rows]).astype(bf16).reshape(xbuf.shape[1:])
        out_copy(t, src).start()
        return carry

    lax.fori_loop(0, 8, step, 0)
    out_copy(0, me).wait()
    out_copy(1, me).wait()
    for copy in (x_top, x_low, y_low, y_top, to_core, relay_top, relay_low, pass_x, pass_y, pass_d):
        copy.wait_send()


def gather_spread(own, slots, router_t, local, ep_count):
    rows, width = own.shape
    tall = rows + EXTRA
    vmem = pl.BlockSpec(memory_space=pltpu.VMEM)
    return pl.pallas_call(
        gather_spread_kernel,
        in_specs=[vmem, vmem, vmem],
        out_specs=[pl.BlockSpec(memory_space=pl.ANY), vmem, vmem],
        out_shape=[
            jax.ShapeDtypeStruct((ep_count, local, CAP, width), bf16),
            jax.ShapeDtypeStruct((local, ep_count * CAP, 1), f32),
            jax.ShapeDtypeStruct((ep_count, local, rows), jnp.int32),
        ],
        scratch_shapes=[
            pltpu.VMEM((ep_count, tall, width), bf16),
            pltpu.VMEM((local * CAP, rows), bf16),
            pltpu.VMEM((2, local, CAP, width), bf16),
            pltpu.SemaphoreType.DMA((10,)),
            pltpu.SemaphoreType.DMA((10,)),
            pltpu.SemaphoreType.DMA((2,)),
        ],
        compiler_params=pltpu.CompilerParams(
            vmem_limit_bytes=VMEM_LIMIT, collective_id=0, has_side_effects=True
        ),
        name="gather_spread",
    )(own, slots, router_t)


def line_gather_kernel(own_ref, out_ref, held, send, recv):
    chip, core, z, _, _, _ = places()
    peers = [(chip, core, (z + i) % 4) for i in (1, 2, 3)]
    greet(peers)
    copies = [
        remote(own_ref, held.at[i], send.at[i], recv.at[i], peer) for i, peer in enumerate(peers)
    ]
    for copy in (copies[1], copies[0], copies[2]):
        copy.start()
    out_ref[z] = own_ref[...]
    for i in range(3):
        copies[i].wait_recv()
        out_ref[(z + 3 - i) % 4] = held[i]
    for copy in copies:
        copy.wait_send()


def line_gather(own, collective_id):
    vmem = pl.BlockSpec(memory_space=pltpu.VMEM)
    return pl.pallas_call(
        line_gather_kernel,
        in_specs=[vmem],
        out_specs=vmem,
        out_shape=jax.ShapeDtypeStruct((4, *own.shape), own.dtype),
        scratch_shapes=[
            pltpu.VMEM((3, *own.shape), own.dtype),
            pltpu.SemaphoreType.DMA((3,)),
            pltpu.SemaphoreType.DMA((3,)),
        ],
        compiler_params=pltpu.CompilerParams(
            vmem_limit_bytes=VMEM_LIMIT, collective_id=collective_id, has_side_effects=True
        ),
        name="line_gather",
    )(own)


def collect_sum_kernel(
    y_ref,
    slot_ref,
    gsw_ref,
    mine_ref,
    out_ref,
    pick,
    ybuf,
    stage,
    given,
    sums,
    relay,
    land,
    zland,
    total,
    copied,
    core_send,
    core_recv,
    send,
    recv,
    zsend,
    zrecv,
):
    chip, core, z, cx, cy, cd = places()
    other = 1 - core
    x_peer, y_peer, c_peer = (cx, core, z), (cy, core, z), (chip, other, z)
    z_peers = [(chip, core, (z + i) % 4) for i in (1, 2, 3)]
    local, rows = slot_ref.shape[1:]
    tall = out_ref.shape[0]
    half, part = tall // 2, tall // 4
    me = chip * 2 + core
    top, low = pl.ds(0, half), pl.ds(half, half)
    number = lax.broadcasted_iota(jnp.int32, (CAP, rows), 0)
    row = lax.broadcasted_iota(jnp.int32, (EXTRA, rows), 0)

    greet([x_peer, y_peer, c_peer, *z_peers])

    def sequence(t):
        p = t // 2
        x, y = (chip % 2 + 1 + p // 2) % 2, (chip // 2 + 1 + p % 2) % 2
        return (y * 2 + x) * 2 + (core + 1 + t % 2) % 2

    def in_copy(t):
        return pltpu.make_async_copy(y_ref.at[sequence(t)], ybuf.at[t % 2], copied.at[t % 2])

    def to_core(p):
        return remote(stage.at[p], given.at[p], core_send.at[p], core_recv.at[p], c_peer)

    far_top = remote(sums.at[0, top], relay.at[0], send.at[0], recv.at[0], x_peer)
    far_low = remote(sums.at[0, low], relay.at[1], send.at[1], recv.at[1], y_peer)
    x_top = remote(sums.at[1, top], land.at[0, top], send.at[2], recv.at[2], x_peer)
    x_low = remote(sums.at[1, low], land.at[0, low], send.at[3], recv.at[3], x_peer)
    y_low = remote(sums.at[2, low], land.at[1, low], send.at[4], recv.at[4], y_peer)
    y_top = remote(sums.at[2, top], land.at[1, top], send.at[5], recv.at[5], y_peer)

    in_copy(0).start()

    def step(t, carry):
        @pl.when(t < 7)
        def _():
            in_copy(t + 1).start()

        p, s = t // 2, sequence(t)
        probs = jnp.zeros((EXTRA, rows), f32)
        for e in range(local):
            mask = slot_ref[s, e : e + 1, :] == number
            pick[e * CAP : (e + 1) * CAP, :] = mask.astype(f32).astype(bf16)
            column = gsw_ref[e, pl.ds(pl.multiple_of(s * CAP, 8), CAP), :]
            line = jnp.sum(jnp.where(mask, column, 0.0), axis=0, keepdims=True)
            probs = jnp.where(row == me * local + e, line, probs)
        in_copy(t).wait()
        back = tn(pick[...], ybuf[t % 2].reshape(local * CAP, -1))

        @pl.when(t % 2 == 0)
        def _():
            stage[p, :rows] = back.astype(bf16)
            stage[p, rows:] = jnp.zeros((tall - rows, back.shape[1]), bf16)
            stage[p, rows:, :rows] = probs.astype(bf16)
            to_core(p).start()

        @pl.when(t % 2 == 1)
        def _():
            to_core(p).wait_recv()
            sums[p, :rows] = (back + given[p, :rows].astype(f32)).astype(bf16)
            sums[p, rows:] = given[p, rows:]
            sums[p, rows:, :rows] = (probs + given[p, rows:, :rows].astype(f32)).astype(bf16)

        @pl.when(t == 1)
        def _():
            far_top.start()
            far_low.start()

        @pl.when(t == 3)
        def _():
            x_top.start()

        @pl.when(t == 5)
        def _():
            y_low.start()

        return carry

    lax.fori_loop(0, 8, step, 0)
    far_low.wait_recv()
    sums[1, half:] = (sums[1, half:].astype(f32) + relay[1].astype(f32)).astype(bf16)
    x_low.start()
    far_top.wait_recv()
    sums[2, :half] = (sums[2, :half].astype(f32) + relay[0].astype(f32)).astype(bf16)
    y_top.start()

    def add_up(at):
        return (
            sums[3, at].astype(f32) + land[0, at].astype(f32) + land[1, at].astype(f32)
        )

    x_top.wait_recv()
    y_top.wait_recv()
    total[:half] = (add_up(slice(0, half)) + mine_ref[:half]).astype(bf16)
    x_low.wait_recv()
    y_low.wait_recv()
    total[half:rows] = (add_up(slice(half, rows)) + mine_ref[half:]).astype(bf16)
    total[rows:] = add_up(slice(rows, tall)).astype(bf16)

    def block(q):
        return pl.ds(pl.multiple_of(q * part, 16), part)

    scatter = [
        remote(total.at[block((z + i) % 4)], zland.at[i - 1], zsend.at[i - 1], zrecv.at[i - 1], z_peers[i - 1])
        for i in (1, 2, 3)
    ]
    spread_ = [
        remote(out_ref.at[block(z)], out_ref.at[block(z)], zsend.at[2 + i], zrecv.at[2 + i], z_peers[i - 1])
        for i in (1, 2, 3)
    ]
    for i in (1, 0, 2):
        scatter[i].start()
    done = total[block(z)].astype(f32)
    for i in range(3):
        scatter[i].wait_recv()
        done = done + zland[i].astype(f32)
    out_ref[block(z)] = done.astype(bf16)
    for i in (1, 0, 2):
        spread_[i].start()
    for i in (1, 2, 3):
        theirs = block((z + 4 - i) % 4)
        remote(out_ref.at[theirs], out_ref.at[theirs], zsend.at[2 + i], zrecv.at[2 + i], z_peers[i - 1]).wait_recv()
    for copy in (far_top, far_low, x_top, x_low, y_low, y_top, *scatter, *spread_):
        copy.wait_send()
    for p in range(4):
        to_core(p).wait_send()


def collect_sum(y, slot, gsw, mine):
    s, local, cap, width = y.shape
    rows = slot.shape[2]
    tall = rows + EXTRA
    half = tall // 2
    vmem = pl.BlockSpec(memory_space=pltpu.VMEM)
    return pl.pallas_call(
        collect_sum_kernel,
        in_specs=[pl.BlockSpec(memory_space=pl.ANY), vmem, vmem, vmem],
        out_specs=vmem,
        out_shape=jax.ShapeDtypeStruct((tall, width), bf16),
        scratch_shapes=[
            pltpu.VMEM((local * cap, rows), bf16),
            pltpu.VMEM((2, local, cap, width), bf16),
            pltpu.VMEM((4, tall, width), bf16),
            pltpu.VMEM((4, tall, width), bf16),
            pltpu.VMEM((4, tall, width), bf16),
            pltpu.VMEM((2, half, width), bf16),
            pltpu.VMEM((2, tall, width), bf16),
            pltpu.VMEM((3, tall // 4, width), bf16),
            pltpu.VMEM((tall, width), bf16),
            pltpu.SemaphoreType.DMA((2,)),
            pltpu.SemaphoreType.DMA((4,)),
            pltpu.SemaphoreType.DMA((4,)),
            pltpu.SemaphoreType.DMA((6,)),
            pltpu.SemaphoreType.DMA((6,)),
            pltpu.SemaphoreType.DMA((6,)),
            pltpu.SemaphoreType.DMA((6,)),
        ],
        compiler_params=pltpu.CompilerParams(
            vmem_limit_bytes=VMEM_LIMIT, collective_id=2, has_side_effects=True
        ),
        name="collect_sum",
    )(y, slot, gsw, mine)


def shards(
    tokens,
    attn_gain,
    attn_query,
    attn_key,
    attn_value,
    attn_out,
    ffn_gain,
    router,
    shared_gate,
    shared_up,
    shared_down,
    expert_gate,
    expert_up,
    expert_down,
    routes,
    documents,
    out_grad,
):
    rows, width = tokens.shape
    quarter = out_grad.shape[1]
    hs = lax.axis_index("hs")
    hs_count = lax.axis_size("hs")
    odd = (hs % 2) == 1
    ep_count = lax.axis_size("xy") * lax.axis_size("core")
    ep = lax.axis_index("xy") * lax.axis_size("core") + lax.axis_index("core")
    local = expert_gate.shape[0]
    experts = router.shape[1]
    spare = HEAD_DIM * (-(-quarter // HEAD_DIM)) - quarter
    held = quarter + spare
    heads = held // HEAD_DIM
    col0 = hs * quarter

    def outer(w):
        return jnp.where(odd, w[:, :spare], w[:, quarter - spare :])

    pairs = [(i, i ^ 1) for i in range(hs_count)]
    sent = jnp.concatenate([outer(attn_query), outer(attn_key), outer(attn_value)], axis=1)
    got = lax.ppermute(sent, "hs", pairs)

    def widened(w, extra):
        return jnp.where(
            odd, jnp.concatenate([extra, w], axis=1), jnp.concatenate([w, extra], axis=1)
        )

    def own(v):
        return jnp.where(odd, v[:, spare:], v[:, :quarter])

    w_query = widened(attn_query, got[:, :spare])
    w_key = widened(attn_key, got[:, spare : 2 * spare])
    w_value = widened(attn_value, got[:, 2 * spare :])
    small = ep_count == 8 and hs_count == 4
    out_full = lax.all_gather(attn_out, "hs", axis=1, tiled=True)
    grad_all_t = lax.all_gather(out_grad.T, (*EP, "hs"), axis=0, tiled=True)
    grad_all_t = grad_all_t.reshape(ep_count, width, rows)
    grad_full = lax.dynamic_index_in_dim(grad_all_t, ep, 0, keepdims=False).T
    positions = jnp.arange(rows, dtype=jnp.int32)
    below = (positions[:, None] > positions[None, :]).astype(bf16)
    chosen = jnp.any(
        routes[:, :, None] == jnp.arange(experts, dtype=jnp.int32)[None, None, :], axis=1
    )
    own_slots = jnp.where(chosen, dot(below, chosen.astype(bf16)), -1.0).T.astype(bf16)

    x = tokens.astype(f32)
    rms1 = lax.rsqrt(jnp.mean(x * x, axis=-1, keepdims=True) + EPS)
    normed1 = (x * rms1 * attn_gain).astype(bf16)
    cosine, sine = rope_tables(rows)
    shape3 = (rows, heads, HEAD_DIM)
    q = rope(dot(normed1, w_query).reshape(shape3), cosine, sine).astype(bf16)
    k = rope(dot(normed1, w_key).reshape(shape3), cosine, sine).astype(bf16)
    v = dot(normed1, w_value).astype(bf16).reshape(shape3)
    scale = 1.0 / math.sqrt(HEAD_DIM)
    doc = documents[0]
    allowed = (positions[:, None] >= positions[None, :]) & (doc[:, None] == doc[None, :])
    scores = jnp.where(allowed[None], ein("qhd,khd->hqk", q, k) * scale, -1e30)
    top = jnp.max(scores, axis=-1, keepdims=True)
    raised = jnp.exp(scores - top)
    probs = raised / jnp.sum(raised, axis=-1, keepdims=True)
    probs_low = probs.astype(bf16)
    attended3 = ein("khd,hqk->hdq", v, probs_low).astype(bf16).reshape(held, rows)
    attended3 = jnp.where(odd, attended3[spare:], attended3[:quarter])
    if small:
        attended_t = line_gather(attended3, 1).reshape(width, rows)
    else:
        attended_t = lax.all_gather(attended3, "hs", axis=0, tiled=True)
    residual = x + ein("ct,cd->td", attended_t, out_full)
    rms2 = lax.rsqrt(jnp.mean(residual * residual, axis=-1, keepdims=True) + EPS)
    normed2 = (residual * rms2 * ffn_gain).astype(bf16)

    sh_gate = dot(normed2, shared_gate)
    sh_up = dot(normed2, shared_up)
    sh_sig = jax.nn.sigmoid(sh_gate)
    sh_act = sh_gate * sh_sig
    sh_hidden = (sh_act * sh_up).astype(bf16)
    shared_part = dot(sh_hidden, shared_down)
    grad_sh = ein("td,fd->tf", grad_full, shared_down)
    grad_sh_gate = (grad_sh * sh_up * sh_sig * (1 + sh_gate * (1 - sh_sig))).astype(bf16)
    grad_sh_up = (grad_sh * sh_act).astype(bf16)
    grad_shared_down = ein("tf,td->fd", sh_hidden, grad_full)
    grad_shared_gate = ein("td,tf->df", normed2, grad_sh_gate)
    grad_shared_up = ein("td,tf->df", normed2, grad_sh_up)
    shared_back = ein("tf,df->td", grad_sh_gate, shared_gate) + ein(
        "tf,df->td", grad_sh_up, shared_up
    )

    first = ep * local
    router_t = jnp.roll(router.T, -first, axis=0)
    if small:
        ex_in, slot_weight, slot = gather_spread(normed2, own_slots, router_t, local, ep_count)
    else:
        slot = lax.dynamic_slice_in_dim(
            lax.all_gather(own_slots, EP, axis=0), first, local, 1
        ).astype(jnp.int32)
        normed_all = lax.all_gather(normed2, EP, axis=0, tiled=True)
        ex_in, slot_weight = spread(normed_all, slot, router_t)
    gate_t, up_t = expert_gate.swapaxes(1, 2), expert_up.swapaxes(1, 2)
    ex_grad = spread(grad_all_t, slot)
    ex_out, ex_gate, ex_up = experts_forward(ex_in, slot_weight, gate_t, up_t, expert_down)
    out_part = collect(ex_out, slot).reshape(ep_count * rows, width)
    ex_back, grad_gate_t, grad_up_t, grad_expert_down, grad_slot_weight = experts_backward(
        ex_in, ex_grad, ex_gate, ex_up, slot_weight, gate_t, up_t, expert_down
    )
    grad_expert_gate, grad_expert_up = grad_gate_t.swapaxes(1, 2), grad_up_t.swapaxes(1, 2)

    out_rows = lax.psum_scatter(out_part, EP, scatter_dimension=0, tiled=True)
    out_rows = (out_rows.astype(f32) + shared_part).astype(bf16)
    out_quarter = lax.psum_scatter(out_rows, "hs", scatter_dimension=1, tiled=True)

    def quarter_of(a):
        return lax.dynamic_slice_in_dim(a, col0, quarter, 1)

    output = (quarter_of(residual) + out_quarter.astype(f32)).astype(bf16)

    if small:
        back_rows = collect_sum(ex_back, slot, grad_slot_weight, shared_back).astype(f32)
    else:
        back_part = collect(ex_back, slot, grad_slot_weight, first, experts).reshape(-1, width)
        back_rows = lax.psum_scatter(back_part, EP, scatter_dimension=0, tiled=True).astype(f32)
        back_rows = jnp.concatenate([back_rows[:rows] + shared_back, back_rows[rows:]], axis=0)
        back_rows = lax.psum(back_rows.astype(bf16), "hs").astype(f32)
    gate_own = jax.nn.softmax(dot(normed2, router), axis=-1)
    grad_probs = back_rows[rows:, :rows].T
    grad_logits = (
        gate_own * (grad_probs - jnp.sum(grad_probs * gate_own, axis=-1, keepdims=True))
    ).astype(bf16)
    grad_router = ein("td,te->de", normed2, grad_logits)
    grad_normed2 = back_rows[:rows] + ein("te,de->td", grad_logits, router)
    grad_ffn_gain = jnp.sum(grad_normed2 * residual * rms2, axis=0)
    u = grad_normed2 * ffn_gain
    grad_residual = (
        grad_full.astype(f32)
        + rms2 * u
        - residual * rms2**3 * jnp.mean(u * residual, axis=-1, keepdims=True)
    )
    grad_low = grad_residual.astype(bf16)
    grad_attn_out = dot(attended_t, quarter_of(grad_low))
    out_held = lax.dynamic_slice_in_dim(out_full, jnp.where(odd, col0 - spare, col0), held, 0)
    grad_attended = ein("tc,dc->td", grad_low, out_held).astype(bf16).reshape(shape3)
    grad_p = ein("qhd,khd->hqk", grad_attended, v)
    grad_v = ein("hqk,qhd->khd", probs_low, grad_attended).astype(bf16)
    grad_s = (probs * (grad_p - jnp.sum(probs * grad_p, axis=-1, keepdims=True))).astype(bf16)
    grad_q = ein("hqk,khd->qhd", grad_s, k) * scale
    grad_k = ein("hqk,qhd->khd", grad_s, q) * scale
    grad_q = own(rope_back(grad_q, cosine, sine).astype(bf16).reshape(rows, held))
    grad_k = own(rope_back(grad_k, cosine, sine).astype(bf16).reshape(rows, held))
    grad_v = own(grad_v.reshape(rows, held))
    normed1_part = (
        ein("tc,dc->td", grad_q, attn_query)
        + ein("tc,dc->td", grad_k, attn_key)
        + ein("tc,dc->td", grad_v, attn_value)
    )
    grad_query = ein("td,tc->dc", normed1, grad_q)
    grad_key = ein("td,tc->dc", normed1, grad_k)
    grad_value = ein("td,tc->dc", normed1, grad_v)
    grad_n1 = lax.psum_scatter(
        normed1_part.astype(bf16), "hs", scatter_dimension=1, tiled=True
    ).astype(f32)
    x_own = quarter_of(x)
    w1 = grad_n1 * lax.dynamic_slice_in_dim(attn_gain, col0, quarter, 0)
    mean1 = lax.psum(jnp.sum(w1 * x_own, axis=-1, keepdims=True), "hs") / width
    grad_tokens = quarter_of(grad_residual) + rms1 * w1 - x_own * rms1**3 * mean1
    gain_own = jnp.sum(grad_n1 * x_own * rms1, axis=0)
    gain_part = lax.dynamic_update_slice_in_dim(jnp.zeros((width,), f32), gain_own, col0, 0)
    grad_attn_gain = lax.psum(gain_part, (*EP, "hs"))

    def over_ep(a):
        return lax.psum(a.astype(bf16), EP).astype(f32)

    return (
        output,
        grad_tokens,
        grad_attn_gain,
        over_ep(grad_query),
        over_ep(grad_key),
        over_ep(grad_value),
        over_ep(grad_attn_out),
        lax.psum(grad_ffn_gain, EP),
        over_ep(grad_router),
        over_ep(grad_shared_gate),
        over_ep(grad_shared_up),
        over_ep(grad_shared_down),
        grad_expert_gate,
        grad_expert_up,
        grad_expert_down,
    )


def solution(mesh):
    ep_count, hs_count = mesh.devices.shape
    cut = Mesh(mesh.devices.reshape(ep_count // 2, 2, hs_count), ("xy", "core", "hs"))
    return jax.shard_map(
        shards,
        mesh=cut,
        in_specs=(
            P(EP, None),
            P(),
            P(None, "hs"),
            P(None, "hs"),
            P(None, "hs"),
            P(None, "hs"),
            P(),
            P(),
            P(None, "hs"),
            P(None, "hs"),
            P("hs", None),
            P(EP, None, "hs"),
            P(EP, None, "hs"),
            P(EP, "hs", None),
            P(EP, None),
            P(EP, None),
            P(EP, "hs"),
        ),
        out_specs=(
            P(EP, "hs"),
            P(EP, "hs"),
            P(),
            P(None, "hs"),
            P(None, "hs"),
            P(None, "hs"),
            P(None, "hs"),
            P(),
            P(),
            P(None, "hs"),
            P(None, "hs"),
            P("hs", None),
            P(EP, None, "hs"),
            P(EP, None, "hs"),
            P(EP, "hs", None),
        ),
        check_vma=False,
    )
```

```python
import functools
import math

import jax
import jax.numpy as jnp
from jax import lax
from jax.experimental import pallas as pl
from jax.experimental.layout import Layout, with_layout_constraint
from jax.experimental.pallas import tpu as pltpu
from jax.sharding import Mesh
from jax.sharding import PartitionSpec as P

HEADS = 10
HEAD_DIM = 128
CAP = 112
EPS = 1e-06
EP = ("xy", "core")
bf16 = jnp.bfloat16
f32 = jnp.float32


def dot(a, b):
    return jnp.dot(a, b, preferred_element_type=f32)


def ein(spec, a, b):
    return jnp.einsum(spec, a, b, preferred_element_type=f32)


def rope_tables(rows):
    half = HEAD_DIM // 2
    frequency = 10000.0 ** (-jnp.arange(half, dtype=f32) * 2.0 / HEAD_DIM)
    angles = frequency[:, None] * jnp.arange(rows, dtype=f32)[None, :]
    return jnp.cos(angles), jnp.sin(angles)


def rope(v, cosine, sine):
    half = HEAD_DIM // 2
    a, b = v[:, :half], v[:, half:]
    return jnp.concatenate([a * cosine - b * sine, b * cosine + a * sine], axis=1)


def rope_back(v, cosine, sine):
    half = HEAD_DIM // 2
    a, b = v[:, :half], v[:, half:]
    return jnp.concatenate([a * cosine + b * sine, b * cosine - a * sine], axis=1)


VMEM_LIMIT = 60 * 1024 * 1024
PAD = 256


def nn(a, b):
    return lax.dot_general(a, b, (((1,), (0,)), ((), ())), preferred_element_type=f32)


def nt(a, b):
    return lax.dot_general(a, b, (((1,), (1,)), ((), ())), preferred_element_type=f32)


def tn(a, b):
    return lax.dot_general(a, b, (((0,), (0,)), ((), ())), preferred_element_type=f32)


def takes(microseconds):
    return pl.CostEstimate(flops=0, transcendentals=0, bytes_accessed=microseconds * 3_000_000)


def slot_masks(slot_ref, at):
    local, rows = slot_ref.shape[-2:]
    number = lax.broadcasted_iota(jnp.int32, (CAP, rows), 0)
    return [slot_ref[at, e : e + 1, :] == number for e in range(local)]


def spread_kernel(weighted, *refs):
    if weighted:
        rows_ref, slot_ref, router_ref, x_ref, sw_ref, pick = refs
    else:
        rows_ref, slot_ref, x_ref, pick = refs
    local = slot_ref.shape[1]
    rows = rows_ref[...] if weighted else rows_ref[0]
    masks = slot_masks(slot_ref, 0)
    if weighted:
        logits = nt(router_ref[...], rows)
        raised = jnp.exp(logits - jnp.max(logits, axis=0, keepdims=True))
        gates = raised / jnp.sum(raised, axis=0, keepdims=True)
    for e in range(local):
        pick[e * CAP : (e + 1) * CAP, :] = masks[e].astype(f32).astype(bf16)
        if weighted:
            sw_ref[e] = jnp.sum(
                jnp.where(masks[e], gates[e : e + 1, :], 0.0), axis=1, keepdims=True
            )
    product = nn if weighted else nt
    x_ref[...] = product(pick[...], rows).astype(bf16).reshape(x_ref.shape)


def spread(all_rows, slot, router_t=None):
    s, local, rows = slot.shape
    weighted = router_t is not None
    if weighted:
        width = all_rows.shape[1]
        block = pl.BlockSpec((rows, width), lambda i: (i, 0))
    else:
        width = all_rows.shape[1]
        block = pl.BlockSpec((1, width, rows), lambda i: (i, 0, 0))
    in_specs = [
        block,
        pl.BlockSpec((1, local, rows), lambda i: (i, 0, 0)),
    ]
    out_specs = [pl.BlockSpec((1, local, CAP, width), lambda i: (i, 0, 0, 0))]
    out_shape = [jax.ShapeDtypeStruct((s, local, CAP, width), bf16)]
    args = [all_rows, slot]
    if weighted:
        in_specs.append(pl.BlockSpec(router_t.shape, lambda i: (0, 0)))
        out_specs.append(pl.BlockSpec((local, CAP, 1), lambda i: (0, i, 0)))
        out_shape.append(jax.ShapeDtypeStruct((local, s * CAP, 1), f32))
        args.append(router_t)
    out = pl.pallas_call(
        functools.partial(spread_kernel, weighted),
        grid=(s,),
        in_specs=in_specs,
        out_specs=out_specs,
        out_shape=out_shape,
        scratch_shapes=[pltpu.VMEM((local * CAP, rows), bf16)],
        compiler_params=pltpu.CompilerParams(vmem_limit_bytes=VMEM_LIMIT),
        cost_estimate=takes(17),
        name="spread",
    )(*args)
    return out if weighted else out[0]


def padded(ref, out):
    ff = ref.shape[1]
    out[:ff, :] = ref[0]
    out[ff:, :] = jnp.zeros((out.shape[0] - ff, out.shape[1]), out.dtype)


def experts_forward_kernel(
    x_ref, sw_ref, wg_ref, wu_ref, wd_ref, y_ref, gate_ref, up_ref, wg, wu, wd
):
    padded(wg_ref, wg)
    padded(wu_ref, wu)
    padded(wd_ref, wd)
    rows, width = gate_ref.shape[1], x_ref.shape[3]
    x = x_ref[...].reshape(rows, width)
    gate = nt(x, wg[...])
    up = nt(x, wu[...])
    gate_ref[0] = gate
    up_ref[0] = up
    act = gate / (1.0 + jnp.exp(-gate))
    hidden = (act * up).astype(bf16).astype(f32)
    hidden_w = (hidden * sw_ref[0]).astype(bf16)
    y_ref[...] = nn(hidden_w, wd[...]).astype(bf16).reshape(y_ref.shape)


def experts_backward_kernel(
    groups,
    x_ref,
    gx_ref,
    gate_ref,
    up_ref,
    sw_ref,
    wg_ref,
    wu_ref,
    wd_ref,
    dx_ref,
    dg_ref,
    du_ref,
    dd_ref,
    gsw_ref,
    wg,
    wu,
    wd,
):
    padded(wg_ref, wg)
    padded(wu_ref, wu)
    padded(wd_ref, wd)
    rows, width = gate_ref.shape[1], x_ref.shape[3]
    ff = wg_ref.shape[1]
    x = x_ref[...].reshape(rows, width)
    gx = gx_ref[...].reshape(rows, width)
    gate, up, sw = gate_ref[0], up_ref[0], sw_ref[0]
    sig = 1.0 / (1.0 + jnp.exp(-gate))
    act = gate * sig
    hidden = (act * up).astype(bf16).astype(f32)
    gh = nt(gx, wd[...])
    gsw_ref[0] = jnp.sum(gh * hidden, axis=-1, keepdims=True)
    gh = gh * sw
    gg = (gh * up * sig * (1.0 + gate * (1.0 - sig))).astype(bf16)
    gu = (gh * act).astype(bf16)
    sums = (
        (dd_ref, tn((hidden * sw).astype(bf16), gx)[:ff]),
        (dg_ref, tn(gg, x)[:ff]),
        (du_ref, tn(gu, x)[:ff]),
    )
    if groups == 1:
        for ref, value in sums:
            ref[0] = value
    else:

        @pl.when(pl.program_id(1) == 0)
        def _():
            for ref, value in sums:
                ref[0] = value

        @pl.when(pl.program_id(1) > 0)
        def _():
            for ref, value in sums:
                ref[0] += value

    dx_ref[...] = (nn(gg, wg[...]) + nn(gu, wu[...])).astype(bf16).reshape(dx_ref.shape)


def expert_specs(s, width):
    group = min(s, 8)
    slots = pl.BlockSpec((group, 1, CAP, width), lambda i, j: (j, i, 0, 0))
    lines = lambda columns: pl.BlockSpec((1, group * CAP, columns), lambda i, j: (i, j, 0))
    per = lambda *shape: pl.BlockSpec((1, *shape), lambda i, j: (i, 0, 0))
    return s // group, slots, lines, per


def experts_forward(x, sw, wg, wu, wd):
    s, local, cap, width = x.shape
    ff = wg.shape[1]
    rows = s * cap
    groups, slots, lines, per = expert_specs(s, width)
    middle = jax.ShapeDtypeStruct((local, rows, PAD), f32)
    return pl.pallas_call(
        experts_forward_kernel,
        grid=(local, groups),
        in_specs=[slots, lines(1)] + [per(ff, width)] * 3,
        out_specs=[slots, lines(PAD), lines(PAD)],
        out_shape=[jax.ShapeDtypeStruct(x.shape, bf16), middle, middle],
        scratch_shapes=[pltpu.VMEM((PAD, width), bf16)] * 3,
        compiler_params=pltpu.CompilerParams(vmem_limit_bytes=VMEM_LIMIT),
        cost_estimate=takes(31),
        name="experts_forward",
    )(x, sw, wg, wu, wd)


def experts_backward(x, gx, gate, up, sw, wg, wu, wd):
    s, local, cap, width = x.shape
    ff = wg.shape[1]
    rows = s * cap
    groups, slots, lines, per = expert_specs(s, width)
    return pl.pallas_call(
        functools.partial(experts_backward_kernel, groups),
        grid=(local, groups),
        in_specs=[slots, slots, lines(PAD), lines(PAD), lines(1)]
        + [per(ff, width)] * 3,
        out_specs=[slots] + [per(ff, width)] * 3 + [lines(1)],
        out_shape=[jax.ShapeDtypeStruct(x.shape, bf16)]
        + [jax.ShapeDtypeStruct((local, ff, width), f32)] * 3
        + [jax.ShapeDtypeStruct((local, rows, 1), f32)],
        scratch_shapes=[pltpu.VMEM((PAD, width), bf16)] * 3,
        compiler_params=pltpu.CompilerParams(vmem_limit_bytes=VMEM_LIMIT),
        cost_estimate=takes(47),
        name="experts_backward",
    )(x, gx, gate, up, sw, wg, wu, wd)


def collect_kernel(y_ref, slot_ref, out_ref, pick):
    local = slot_ref.shape[1]
    masks = slot_masks(slot_ref, 0)
    for e in range(local):
        pick[e * CAP : (e + 1) * CAP, :] = masks[e].astype(f32).astype(bf16)
    out_ref[0] = tn(pick[...], y_ref[...].reshape(pick.shape[0], -1)).astype(bf16)


def collect_back_kernel(experts, y_ref, slot_ref, gsw_ref, first_ref, out_ref, pick):
    local, rows = slot_ref.shape[1:]
    first = first_ref[0]
    masks = slot_masks(slot_ref, 0)
    number = lax.broadcasted_iota(jnp.int32, (experts, rows), 0)
    probs = jnp.zeros((experts, rows), f32)
    for e in range(local):
        pick[e * CAP : (e + 1) * CAP, :] = masks[e].astype(f32).astype(bf16)
        line = jnp.sum(jnp.where(masks[e], gsw_ref[e], 0.0), axis=0, keepdims=True)
        probs = jnp.where(number == first + e, line, probs)
    out_ref[0, :rows] = tn(pick[...], y_ref[...].reshape(pick.shape[0], -1)).astype(bf16)
    out_ref[0, rows:] = jnp.zeros((experts, out_ref.shape[2]), bf16)
    out_ref[0, rows:, :rows] = probs.astype(bf16)


def collect(y, slot, gsw=None, first=None, experts=0):
    s, local, cap, width = y.shape
    rows = slot.shape[2]
    in_specs = [
        pl.BlockSpec((1, local, cap, width), lambda i: (i, 0, 0, 0)),
        pl.BlockSpec((1, local, rows), lambda i: (i, 0, 0)),
    ]
    args = [y, slot]
    kernel = collect_kernel
    tall = rows
    if gsw is not None:
        in_specs += [
            pl.BlockSpec((local, cap, 1), lambda i: (0, i, 0)),
            pl.BlockSpec(memory_space=pltpu.SMEM),
        ]
        args += [gsw, first.reshape(1)]
        kernel = functools.partial(collect_back_kernel, experts)
        tall = rows + experts
    return pl.pallas_call(
        kernel,
        grid=(s,),
        in_specs=in_specs,
        out_specs=pl.BlockSpec((1, tall, width), lambda i: (i, 0, 0)),
        out_shape=jax.ShapeDtypeStruct((s, tall, width), bf16),
        scratch_shapes=[pltpu.VMEM((local * cap, rows), bf16)],
        compiler_params=pltpu.CompilerParams(vmem_limit_bytes=VMEM_LIMIT),
        cost_estimate=takes(17),
        name="collect",
    )(*args)


MESH = pl.DeviceIdType.MESH
EXTRA = 64


def places():
    chip, core, z = lax.axis_index("xy"), lax.axis_index("core"), lax.axis_index("hs")
    x, y = chip % 2, chip // 2
    return chip, core, z, y * 2 + (1 - x), (1 - y) * 2 + x, (1 - y) * 2 + (1 - x)


def greet(peers):
    barrier = pltpu.get_barrier_semaphore()
    for peer in peers:
        pl.semaphore_signal(barrier, inc=1, device_id=peer, device_id_type=MESH)
    pl.semaphore_wait(barrier, len(peers))


def remote(src, dst, send, recv, peer):
    return pltpu.make_async_remote_copy(
        src_ref=src, dst_ref=dst, send_sem=send, recv_sem=recv, device_id=peer, device_id_type=MESH
    )


def block(q, size):
    return pl.ds(pl.multiple_of(q * size, 16), size)


def weight_sum(grads, given, half, land, out_ref, csend, crecv, send, recv):
    chip, core, z, cx, cy, cd = places()
    other = 1 - core
    c_peer = (chip, other, z)
    chips = (cx, cy, cd)
    count = grads.shape[0] // 2
    piece = count // 4

    to_core = remote(grads.at[block(other, count)], given, csend.at[0], crecv.at[0], c_peer)
    scatter = [
        remote(half.at[block(c, piece)], land.at[i], send.at[i], recv.at[i], (c, core, z))
        for i, c in enumerate(chips)
    ]

    def share():
        to_core.wait_recv()
        half[...] = (grads[block(core, count)].astype(f32) + given[...].astype(f32)).astype(bf16)
        for i in (2, 0, 1):
            scatter[i].start()

    def place(c, k):
        return pl.ds(pl.multiple_of(k * count + c * piece, 16), piece)

    def give(number, c, k, sems, peer):
        return remote(out_ref.at[place(c, k)], out_ref.at[place(c, k)], *sems(number), peer)

    def chip_sems(i):
        return send.at[3 + i], recv.at[3 + i]

    def core_sems(i):
        return csend.at[1 + i], crecv.at[1 + i]

    gather = [give(i, chip, core, chip_sems, (c, core, z)) for i, c in enumerate(chips)]
    over = [give(i, c, core, core_sems, c_peer) for i, c in enumerate((*chips, chip))]

    def give_back():
        done = half[block(chip, piece)].astype(f32)
        for i in range(3):
            scatter[i].wait_recv()
            done = done + land[i].astype(f32)
        out_ref[place(chip, core)] = done.astype(bf16)
        for i in (2, 0, 1):
            gather[i].start()
        over[3].start()

    def end():
        for i, c in enumerate(chips):
            give(i, c, core, chip_sems, (c, core, z)).wait_recv()
            over[i].start()
        for i, c in enumerate((*chips, chip)):
            give(i, c, other, core_sems, c_peer).wait_recv()
        for copy in (to_core, *scatter, *gather, *over):
            copy.wait_send()

    return to_core.start, share, give_back, end


def weight_sum_scratch(tall, width):
    dma = pltpu.SemaphoreType.DMA
    return [
        pltpu.VMEM((tall, width), bf16),
        pltpu.VMEM((tall // 2, width), bf16),
        pltpu.VMEM((tall // 2, width), bf16),
        pltpu.VMEM((3, tall // 8, width), bf16),
        dma((5,)),
        dma((5,)),
        dma((6,)),
        dma((6,)),
    ]


def gather_spread_kernel(
    own_ref, slots_ref, router_ref, x_ref, sw_ref, slot_ref, held, pick, xbuf, send, recv, copied
):
    chip, core, z, cx, cy, cd = places()
    other = 1 - core
    x_peer, y_peer, c_peer = (cx, core, z), (cy, core, z), (chip, other, z)
    tall = held.shape[1]
    half = tall // 2
    local, rows = slot_ref.shape[1:]
    me = chip * 2 + core
    top, low = pl.ds(0, half), pl.ds(half, half)

    def at(c, k):
        return c * 2 + k

    def move(number, src_slot, part, peer):
        return remote(
            held.at[src_slot, part], held.at[src_slot, part], send.at[number], recv.at[number], peer
        )

    whole = pl.ds(0, tall)
    greet([x_peer, y_peer, c_peer])
    held[me, :rows] = own_ref[...]
    held[me, rows:] = jnp.zeros((EXTRA, own_ref.shape[1]), bf16)
    held[me, rows:, :rows] = slots_ref[...]
    x_top, x_low = move(0, me, top, x_peer), move(1, me, low, x_peer)
    y_low, y_top = move(2, me, low, y_peer), move(3, me, top, y_peer)
    to_core = move(4, me, whole, c_peer)
    relay_top, relay_low = move(5, at(cx, core), top, y_peer), move(6, at(cy, core), low, x_peer)
    pass_x, pass_y = move(7, at(cx, core), whole, c_peer), move(8, at(cy, core), whole, c_peer)
    pass_d = move(9, at(cd, core), whole, c_peer)
    for copy in (x_top, y_low, x_low, y_top, to_core):
        copy.start()

    def arrived(number, slot, part):
        move(number, slot, part, c_peer).wait_recv()

    number = lax.broadcasted_iota(jnp.int32, (CAP, rows), 0)
    first = me * local
    line = lax.broadcasted_iota(jnp.int32, (local, EXTRA), 0)
    column = lax.broadcasted_iota(jnp.int32, (local, EXTRA), 1)
    chosen = (column == line + first).astype(f32).astype(bf16)

    def out_copy(t, src):
        return pltpu.make_async_copy(xbuf.at[t % 2], x_ref.at[src], copied.at[t % 2])

    def step(t, carry):
        @pl.when(t == 1)
        def _():
            arrived(4, at(chip, other), whole)

        @pl.when(t == 2)
        def _():
            arrived(0, at(cx, core), top)
            relay_top.start()
            arrived(2, at(cy, core), low)
            relay_low.start()
            arrived(1, at(cx, core), low)
            pass_x.start()

        @pl.when(t == 3)
        def _():
            arrived(3, at(cy, core), top)
            pass_y.start()
            arrived(7, at(cx, other), whole)

        @pl.when(t == 5)
        def _():
            arrived(8, at(cy, other), whole)

        @pl.when(t == 6)
        def _():
            arrived(5, at(cd, core), top)
            arrived(6, at(cd, core), low)
            pass_d.start()

        @pl.when(t == 7)
        def _():
            arrived(9, at(cd, other), whole)

        x, y = (chip % 2 + (t // 2) % 2) % 2, (chip // 2 + t // 4) % 2
        src = (y * 2 + x) * 2 + (core + t % 2) % 2
        slots = nn(chosen, held[src, rows:, :rows]).astype(jnp.int32)
        slot_ref[src] = slots
        logits = nt(router_ref[...], held[src, :rows])
        raised = jnp.exp(logits - jnp.max(logits, axis=0, keepdims=True))
        gates = raised / jnp.sum(raised, axis=0, keepdims=True)
        for e in range(local):
            mask = slots[e : e + 1, :] == number
            pick[e * CAP : (e + 1) * CAP, :] = mask.astype(f32).astype(bf16)
            sw_ref[e, pl.ds(pl.multiple_of(src * CAP, 8), CAP), :] = jnp.sum(
                jnp.where(mask, gates[e : e + 1, :], 0.0), axis=1, keepdims=True
            )

        @pl.when(t >= 2)
        def _():
            out_copy(t, src).wait()

        xbuf[t % 2] = nn(pick[...], held[src, :rows]).astype(bf16).reshape(xbuf.shape[1:])
        out_copy(t, src).start()
        return carry

    lax.fori_loop(0, 8, step, 0)
    out_copy(0, me).wait()
    out_copy(1, me).wait()
    for copy in (x_top, x_low, y_low, y_top, to_core, relay_top, relay_low, pass_x, pass_y, pass_d):
        copy.wait_send()


def gather_spread(own, slots, router_t, local, ep_count):
    rows, width = own.shape
    tall = rows + EXTRA
    vmem = pl.BlockSpec(memory_space=pltpu.VMEM)
    return pl.pallas_call(
        gather_spread_kernel,
        in_specs=[vmem, vmem, vmem],
        out_specs=[pl.BlockSpec(memory_space=pl.ANY), vmem, vmem],
        out_shape=[
            jax.ShapeDtypeStruct((ep_count, local, CAP, width), bf16),
            jax.ShapeDtypeStruct((local, ep_count * CAP, 1), f32),
            jax.ShapeDtypeStruct((ep_count, local, rows), jnp.int32),
        ],
        scratch_shapes=[
            pltpu.VMEM((ep_count, tall, width), bf16),
            pltpu.VMEM((local * CAP, rows), bf16),
            pltpu.VMEM((2, local, CAP, width), bf16),
            pltpu.SemaphoreType.DMA((10,)),
            pltpu.SemaphoreType.DMA((10,)),
            pltpu.SemaphoreType.DMA((2,)),
        ],
        compiler_params=pltpu.CompilerParams(
            vmem_limit_bytes=VMEM_LIMIT, collective_id=0, has_side_effects=True
        ),
        cost_estimate=takes(62),
        name="gather_spread",
    )(own, slots, router_t)


def line_gather_kernel(own_ref, out_ref, held, send, recv):
    chip, core, z, _, _, _ = places()
    peers = [(chip, core, (z + i) % 4) for i in (1, 2, 3)]
    greet(peers)
    copies = [
        remote(own_ref, held.at[i], send.at[i], recv.at[i], peer) for i, peer in enumerate(peers)
    ]
    for copy in (copies[1], copies[0], copies[2]):
        copy.start()
    out_ref[z] = own_ref[...]
    for i in range(3):
        copies[i].wait_recv()
        out_ref[(z + 3 - i) % 4] = held[i]
    for copy in copies:
        copy.wait_send()


def line_gather(own, collective_id):
    vmem = pl.BlockSpec(memory_space=pltpu.VMEM)
    return pl.pallas_call(
        line_gather_kernel,
        in_specs=[vmem],
        out_specs=vmem,
        out_shape=jax.ShapeDtypeStruct((4, *own.shape), own.dtype),
        scratch_shapes=[
            pltpu.VMEM((3, *own.shape), own.dtype),
            pltpu.SemaphoreType.DMA((3,)),
            pltpu.SemaphoreType.DMA((3,)),
        ],
        compiler_params=pltpu.CompilerParams(
            vmem_limit_bytes=VMEM_LIMIT, collective_id=collective_id, has_side_effects=True
        ),
        cost_estimate=takes(30),
        name="line_gather",
    )(own)


def collect_sum_kernel(
    y_ref,
    slot_ref,
    gsw_ref,
    mine_ref,
    shared_gate_ref,
    shared_up_ref,
    shared_down_ref,
    out_ref,
    sum_ref,
    pick,
    ybuf,
    stage,
    given,
    sums,
    relay,
    land,
    zland,
    total,
    copied,
    core_send,
    core_recv,
    send,
    recv,
    zsend,
    zrecv,
    grads,
    *more,
):
    chip, core, z, cx, cy, cd = places()
    other = 1 - core
    x_peer, y_peer, c_peer = (cx, core, z), (cy, core, z), (chip, other, z)
    z_peers = [(chip, core, (z + i) % 4) for i in (1, 2, 3)]
    local, rows = slot_ref.shape[1:]
    tall = out_ref.shape[0]
    half, part = tall // 2, tall // 4
    me = chip * 2 + core
    top, low = pl.ds(0, half), pl.ds(half, half)
    number = lax.broadcasted_iota(jnp.int32, (CAP, rows), 0)
    row = lax.broadcasted_iota(jnp.int32, (EXTRA, rows), 0)

    greet([x_peer, y_peer, c_peer, (cd, core, z), *z_peers])

    def sequence(t):
        p = t // 2
        x, y = (chip % 2 + 1 + p // 2) % 2, (chip // 2 + 1 + p % 2) % 2
        return (y * 2 + x) * 2 + (core + 1 + t % 2) % 2

    def in_copy(t):
        return pltpu.make_async_copy(y_ref.at[sequence(t)], ybuf.at[t % 2], copied.at[t % 2])

    def to_core(p):
        return remote(stage.at[p], given.at[p], core_send.at[p], core_recv.at[p], c_peer)

    far_top = remote(sums.at[0, top], relay.at[0], send.at[0], recv.at[0], x_peer)
    far_low = remote(sums.at[0, low], relay.at[1], send.at[1], recv.at[1], y_peer)
    x_top = remote(sums.at[1, top], land.at[0, top], send.at[2], recv.at[2], x_peer)
    x_low = remote(sums.at[1, low], land.at[0, low], send.at[3], recv.at[3], x_peer)
    y_low = remote(sums.at[2, low], land.at[1, low], send.at[4], recv.at[4], y_peer)
    y_top = remote(sums.at[2, top], land.at[1, top], send.at[5], recv.at[5], y_peer)

    in_copy(0).start()
    start, share, give_back, end = weight_sum(grads, *more[:3], sum_ref, *more[3:])
    at = 0
    for ref in (shared_gate_ref, shared_up_ref, shared_down_ref):
        grads[at : at + ref.shape[0]] = ref[...]
        at += ref.shape[0]
    grads[at:] = jnp.zeros((grads.shape[0] - at, grads.shape[1]), bf16)
    start()

    def step(t, carry):
        @pl.when(t < 7)
        def _():
            in_copy(t + 1).start()

        p, s = t // 2, sequence(t)
        probs = jnp.zeros((EXTRA, rows), f32)
        for e in range(local):
            mask = slot_ref[s, e : e + 1, :] == number
            pick[e * CAP : (e + 1) * CAP, :] = mask.astype(f32).astype(bf16)
            column = gsw_ref[e, pl.ds(pl.multiple_of(s * CAP, 8), CAP), :]
            line = jnp.sum(jnp.where(mask, column, 0.0), axis=0, keepdims=True)
            probs = jnp.where(row == me * local + e, line, probs)
        in_copy(t).wait()
        back = tn(pick[...], ybuf[t % 2].reshape(local * CAP, -1))

        @pl.when(t % 2 == 0)
        def _():
            stage[p, :rows] = back.astype(bf16)
            stage[p, rows:] = jnp.zeros((tall - rows, back.shape[1]), bf16)
            stage[p, rows:, :rows] = probs.astype(bf16)
            to_core(p).start()

        @pl.when(t % 2 == 1)
        def _():
            to_core(p).wait_recv()
            sums[p, :rows] = (back + given[p, :rows].astype(f32)).astype(bf16)
            sums[p, rows:] = given[p, rows:]
            sums[p, rows:, :rows] = (probs + given[p, rows:, :rows].astype(f32)).astype(bf16)

        @pl.when(t == 1)
        def _():
            far_top.start()
            far_low.start()

        @pl.when(t == 3)
        def _():
            x_top.start()

        @pl.when(t == 5)
        def _():
            y_low.start()

        return carry

    lax.fori_loop(0, 8, step, 0)
    far_low.wait_recv()
    sums[1, half:] = (sums[1, half:].astype(f32) + relay[1].astype(f32)).astype(bf16)
    x_low.start()
    far_top.wait_recv()
    sums[2, :half] = (sums[2, :half].astype(f32) + relay[0].astype(f32)).astype(bf16)
    y_top.start()
    share()

    def add_up(at):
        return (
            sums[3, at].astype(f32) + land[0, at].astype(f32) + land[1, at].astype(f32)
        )

    x_top.wait_recv()
    y_top.wait_recv()
    total[:half] = (add_up(slice(0, half)) + mine_ref[:half]).astype(bf16)
    x_low.wait_recv()
    y_low.wait_recv()
    total[half:rows] = (add_up(slice(half, rows)) + mine_ref[half:]).astype(bf16)
    total[rows:] = add_up(slice(rows, tall)).astype(bf16)

    scatter = [
        remote(total.at[block((z + i) % 4, part)], zland.at[i - 1], zsend.at[i - 1], zrecv.at[i - 1], z_peers[i - 1])
        for i in (1, 2, 3)
    ]
    spread_ = [
        remote(out_ref.at[block(z, part)], out_ref.at[block(z, part)], zsend.at[2 + i], zrecv.at[2 + i], z_peers[i - 1])
        for i in (1, 2, 3)
    ]
    for i in (1, 0, 2):
        scatter[i].start()
    give_back()
    done = total[block(z, part)].astype(f32)
    for i in range(3):
        scatter[i].wait_recv()
        done = done + zland[i].astype(f32)
    out_ref[block(z, part)] = done.astype(bf16)
    for i in (1, 0, 2):
        spread_[i].start()
    end()
    for i in (1, 2, 3):
        theirs = block((z + 4 - i) % 4, part)
        remote(out_ref.at[theirs], out_ref.at[theirs], zsend.at[2 + i], zrecv.at[2 + i], z_peers[i - 1]).wait_recv()
    for copy in (far_top, far_low, x_top, x_low, y_low, y_top, *scatter, *spread_):
        copy.wait_send()
    for p in range(4):
        to_core(p).wait_send()


def collect_sum(y, slot, gsw, mine, *shared):
    s, local, cap, width = y.shape
    rows = slot.shape[2]
    tall = rows + EXTRA
    half = tall // 2
    weights = 128 * (-(-sum(a.shape[0] for a in shared) // 128))
    vmem = pl.BlockSpec(memory_space=pltpu.VMEM)
    return pl.pallas_call(
        collect_sum_kernel,
        in_specs=[pl.BlockSpec(memory_space=pl.ANY)] + [vmem] * 6,
        out_specs=[vmem, vmem],
        out_shape=[
            jax.ShapeDtypeStruct((tall, width), bf16),
            jax.ShapeDtypeStruct((weights, width), bf16),
        ],
        scratch_shapes=[
            pltpu.VMEM((local * cap, rows), bf16),
            pltpu.VMEM((2, local, cap, width), bf16),
            pltpu.VMEM((4, tall, width), bf16),
            pltpu.VMEM((4, tall, width), bf16),
            pltpu.VMEM((4, tall, width), bf16),
            pltpu.VMEM((2, half, width), bf16),
            pltpu.VMEM((2, tall, width), bf16),
            pltpu.VMEM((3, tall // 4, width), bf16),
            pltpu.VMEM((tall, width), bf16),
            pltpu.SemaphoreType.DMA((2,)),
            pltpu.SemaphoreType.DMA((4,)),
            pltpu.SemaphoreType.DMA((4,)),
            pltpu.SemaphoreType.DMA((6,)),
            pltpu.SemaphoreType.DMA((6,)),
            pltpu.SemaphoreType.DMA((6,)),
            pltpu.SemaphoreType.DMA((6,)),
            *weight_sum_scratch(weights, width),
        ],
        compiler_params=pltpu.CompilerParams(
            vmem_limit_bytes=VMEM_LIMIT, collective_id=2, has_side_effects=True
        ),
        cost_estimate=takes(131),
        name="collect_sum",
    )(y, slot, gsw, mine, *shared)


def finish_kernel(
    dq_ref,
    dk_ref,
    dv_ref,
    low_ref,
    wq_ref,
    wk_ref,
    wv_ref,
    normed_ref,
    attended_ref,
    x_ref,
    gain_ref,
    rms_ref,
    back_ref,
    router_ref,
    ffn_ref,
    tokens_ref,
    sum_ref,
    part,
    low_part,
    zland,
    mine,
    theirs,
    zsend,
    zrecv,
    lsend,
    lrecv,
    grads,
    given,
    half,
    land,
    csend,
    crecv,
    send,
    recv,
):
    chip, core, z, cx, cy, cd = places()
    other = 1 - core
    c_peer = (chip, other, z)
    chips = (cx, cy, cd)
    z_peers = [(chip, core, (z + i) % 4) for i in (1, 2, 3)]
    quarter, rows = dq_ref.shape
    width = x_ref.shape[0]
    tall = grads.shape[0]
    experts = router_ref.shape[0]

    greet([c_peer, *[(c, core, z) for c in chips], *z_peers])

    part[...] = tn(wq_ref[...], dq_ref[...])
    part[...] += tn(wk_ref[...], dk_ref[...])
    part[...] += tn(wv_ref[...], dv_ref[...])
    low_part[...] = part[...].astype(bf16)
    to_z = [
        remote(
            low_part.at[block((z + i) % 4, quarter)],
            zland.at[i - 1],
            zsend.at[i - 1],
            zrecv.at[i - 1],
            z_peers[i - 1],
        )
        for i in (1, 2, 3)
    ]
    few_to_z = [
        remote(mine, theirs.at[i], lsend.at[i], lrecv.at[i], peer) for i, peer in enumerate(z_peers)
    ]
    along = part[...] * x_ref[...].astype(f32)
    mine[...] = jnp.zeros(mine.shape, f32)
    mine[0:1, :rows] = jnp.sum(along * gain_ref[...], axis=0, keepdims=True)
    mine[:, rows:] = nt(jnp.ones((8, rows), bf16), (along * rms_ref[...]).astype(bf16))
    for copy in few_to_z:
        copy.start()
    for i in (1, 0, 2):
        to_z[i].start()

    normed = normed_ref[...]
    for i, ref in enumerate((dq_ref, dk_ref, dv_ref)):
        grads[i * quarter : (i + 1) * quarter] = nn(ref[...], normed).astype(bf16)
    grads[3 * quarter : 4 * quarter] = nt(low_ref[...], attended_ref[...]).astype(bf16)
    at = 4 * quarter
    grads[at : at + experts] = router_ref[...].astype(bf16)
    for copy in few_to_z:
        copy.wait_recv()
    few = mine[...] + theirs[0] + theirs[1] + theirs[2]
    grads[at + experts :] = jnp.zeros((tall - at - experts, width), bf16)
    line = lax.broadcasted_iota(jnp.int32, (16, width), 0)
    gains = jnp.where(line == 0, few[0:1, rows:], jnp.where(line == 1, ffn_ref[...], 0.0))
    grads[at + experts : at + experts + 16] = gains.astype(bf16)

    start, share, give_back, end = weight_sum(
        grads, given, half, land, sum_ref, csend, crecv, send, recv
    )
    start()
    share()

    own = block(z, quarter)
    total = part[own]
    for i in range(3):
        to_z[i].wait_recv()
        total = total + zland[i].astype(f32)
    rms = rms_ref[...]
    x = x_ref[own].astype(f32)
    mean = few[0:1, :rows] * (1.0 / width)
    tokens_ref[...] = back_ref[...] + rms * gain_ref[own] * total - x * (rms * rms * rms * mean)

    give_back()
    end()
    for copy in (*to_z, *few_to_z):
        copy.wait_send()


def finish(*args):
    quarter, rows = args[0].shape
    width = args[9].shape[0]
    tall = 4 * quarter + 128
    vmem = pl.BlockSpec(memory_space=pltpu.VMEM)
    dma = pltpu.SemaphoreType.DMA
    return pl.pallas_call(
        finish_kernel,
        in_specs=[vmem] * len(args),
        out_specs=[vmem, vmem],
        out_shape=[
            jax.ShapeDtypeStruct((quarter, rows), f32),
            jax.ShapeDtypeStruct((tall, width), bf16),
        ],
        scratch_shapes=[
            pltpu.VMEM((width, rows), f32),
            pltpu.VMEM((width, rows), bf16),
            pltpu.VMEM((3, quarter, rows), bf16),
            pltpu.VMEM((8, rows + width), f32),
            pltpu.VMEM((3, 8, rows + width), f32),
            dma((3,)),
            dma((3,)),
            dma((3,)),
            dma((3,)),
            *weight_sum_scratch(tall, width),
        ],
        compiler_params=pltpu.CompilerParams(
            vmem_limit_bytes=VMEM_LIMIT, collective_id=3, has_side_effects=True
        ),
        cost_estimate=takes(70),
        name="finish",
    )(*args)


def shards(
    tokens,
    attn_gain,
    attn_query,
    attn_key,
    attn_value,
    attn_out,
    ffn_gain,
    router,
    shared_gate,
    shared_up,
    shared_down,
    expert_gate,
    expert_up,
    expert_down,
    routes,
    documents,
    out_grad,
):
    rows, width = tokens.shape
    quarter = out_grad.shape[1]
    hs = lax.axis_index("hs")
    hs_count = lax.axis_size("hs")
    odd = (hs % 2) == 1
    ep_count = lax.axis_size("xy") * lax.axis_size("core")
    ep = lax.axis_index("xy") * lax.axis_size("core") + lax.axis_index("core")
    local = expert_gate.shape[0]
    experts = router.shape[1]
    spare = HEAD_DIM * (-(-quarter // HEAD_DIM)) - quarter
    held = quarter + spare
    heads = held // HEAD_DIM
    col0 = hs * quarter

    query_t, key_t, value_t = attn_query.T, attn_key.T, attn_value.T

    def outer(w):
        return jnp.where(odd, w[:spare], w[quarter - spare :])

    pairs = [(i, i ^ 1) for i in range(hs_count)]
    sent = jnp.concatenate([outer(query_t), outer(key_t), outer(value_t)], axis=0)
    got = lax.ppermute(sent, "hs", pairs)

    def widened(w, extra):
        return jnp.where(
            odd, jnp.concatenate([extra, w], axis=0), jnp.concatenate([w, extra], axis=0)
        )

    def own(v):
        return jnp.where(odd, v[spare:], v[:quarter])

    w_query = widened(query_t, got[:spare])
    w_key = widened(key_t, got[spare : 2 * spare])
    w_value = widened(value_t, got[2 * spare :])
    small = ep_count == 8 and hs_count == 4
    out_full = lax.all_gather(attn_out, "hs", axis=1, tiled=True)
    grad_all_t = lax.all_gather(out_grad.T, (*EP, "hs"), axis=0, tiled=True)
    grad_all_t = grad_all_t.reshape(ep_count, width, rows)
    grad_full = lax.dynamic_index_in_dim(grad_all_t, ep, 0, keepdims=False).T
    positions = jnp.arange(rows, dtype=jnp.int32)
    below = (positions[:, None] > positions[None, :]).astype(bf16)
    chosen = jnp.any(
        routes[:, :, None] == jnp.arange(experts, dtype=jnp.int32)[None, None, :], axis=1
    )
    own_slots = jnp.where(chosen, dot(below, chosen.astype(bf16)), -1.0).T.astype(bf16)

    x = tokens.astype(f32)
    rms1 = lax.rsqrt(jnp.mean(x * x, axis=-1, keepdims=True) + EPS)
    normed1 = (x * rms1 * attn_gain).astype(bf16)
    cosine, sine = rope_tables(rows)
    shape3 = (heads, HEAD_DIM, rows)
    q = rope(ein("cd,td->ct", w_query, normed1).reshape(shape3), cosine, sine).astype(bf16)
    k = rope(ein("cd,td->ct", w_key, normed1).reshape(shape3), cosine, sine).astype(bf16)
    v = ein("cd,td->ct", w_value, normed1).astype(bf16).reshape(shape3)
    scale = 1.0 / math.sqrt(HEAD_DIM)
    doc = documents[0]
    allowed = (positions[:, None] >= positions[None, :]) & (doc[:, None] == doc[None, :])
    scores = jnp.where(allowed[None], ein("hdq,hdk->hqk", q, k) * scale, -1e30)
    top = jnp.max(scores, axis=-1, keepdims=True)
    raised = jnp.exp(scores - top)
    probs = raised / jnp.sum(raised, axis=-1, keepdims=True)
    probs_low = probs.astype(bf16)
    attended3 = own(ein("hdk,hqk->hdq", v, probs_low).astype(bf16).reshape(held, rows))
    if small:
        attended_t = line_gather(attended3, 1).reshape(width, rows)
    else:
        attended_t = lax.all_gather(attended3, "hs", axis=0, tiled=True)
    residual = x + ein("ct,cd->td", attended_t, out_full)
    rms2 = lax.rsqrt(jnp.mean(residual * residual, axis=-1, keepdims=True) + EPS)
    normed2 = (residual * rms2 * ffn_gain).astype(bf16)

    sh_gate = dot(normed2, shared_gate)
    sh_up = dot(normed2, shared_up)
    sh_sig = jax.nn.sigmoid(sh_gate)
    sh_act = sh_gate * sh_sig
    sh_hidden = (sh_act * sh_up).astype(bf16)
    shared_part = dot(sh_hidden, shared_down)
    grad_sh = ein("td,fd->tf", grad_full, shared_down)
    grad_sh_gate = (grad_sh * sh_up * sh_sig * (1 + sh_gate * (1 - sh_sig))).astype(bf16)
    grad_sh_up = (grad_sh * sh_act).astype(bf16)
    grad_shared_down = ein("tf,td->fd", sh_hidden, grad_full)
    grad_shared_gate = ein("tf,td->fd", grad_sh_gate, normed2)
    grad_shared_up = ein("tf,td->fd", grad_sh_up, normed2)
    shared_back = ein("tf,df->td", grad_sh_gate, shared_gate) + ein(
        "tf,df->td", grad_sh_up, shared_up
    )

    shared_grads = [a.astype(bf16) for a in (grad_shared_gate, grad_shared_up, grad_shared_down)]

    first = ep * local
    router_t = jnp.roll(router.T, -first, axis=0)
    if small:
        ex_in, slot_weight, slot = gather_spread(normed2, own_slots, router_t, local, ep_count)
    else:
        slot = lax.dynamic_slice_in_dim(
            lax.all_gather(own_slots, EP, axis=0), first, local, 1
        ).astype(jnp.int32)
        normed_all = lax.all_gather(normed2, EP, axis=0, tiled=True)
        ex_in, slot_weight = spread(normed_all, slot, router_t)
    gate_t, up_t = expert_gate.swapaxes(1, 2), expert_up.swapaxes(1, 2)
    ex_grad = spread(grad_all_t, slot)
    ex_out, ex_gate, ex_up = experts_forward(ex_in, slot_weight, gate_t, up_t, expert_down)
    out_part = collect(ex_out, slot).reshape(ep_count * rows, width)
    ex_back, grad_gate_t, grad_up_t, grad_expert_down, grad_slot_weight = experts_backward(
        ex_in, ex_grad, ex_gate, ex_up, slot_weight, gate_t, up_t, expert_down
    )
    grad_expert_gate, grad_expert_up = grad_gate_t.swapaxes(1, 2), grad_up_t.swapaxes(1, 2)

    rows_major = Layout(major_to_minor=(0, 1))
    out_part = with_layout_constraint(out_part, rows_major)
    out_rows = lax.psum_scatter(out_part, EP, scatter_dimension=0, tiled=True)
    out_rows = with_layout_constraint(out_rows, rows_major)
    out_rows = (out_rows.astype(f32) + shared_part).astype(bf16)
    out_quarter = lax.psum_scatter(out_rows, "hs", scatter_dimension=1, tiled=True)

    def quarter_of(a):
        return lax.dynamic_slice_in_dim(a, col0, quarter, 1)

    output = (quarter_of(residual) + out_quarter.astype(f32)).astype(bf16)

    if small:
        back_rows, shared_sums = collect_sum(
            ex_back, slot, grad_slot_weight, shared_back, *shared_grads
        )
        back_rows, shared_sums = back_rows.astype(f32), shared_sums.astype(f32)
        hidden_units = shared_down.shape[0]
        shared_sums = [shared_sums[i * hidden_units : (i + 1) * hidden_units] for i in range(3)]
    else:
        back_part = collect(ex_back, slot, grad_slot_weight, first, experts).reshape(-1, width)
        back_rows = lax.psum_scatter(back_part, EP, scatter_dimension=0, tiled=True).astype(f32)
        back_rows = jnp.concatenate([back_rows[:rows] + shared_back, back_rows[rows:]], axis=0)
        back_rows = lax.psum(back_rows.astype(bf16), "hs").astype(f32)
        shared_sums = [lax.psum(a, EP).astype(f32) for a in shared_grads]
    gate_own = jax.nn.softmax(dot(normed2, router), axis=-1)
    grad_probs = back_rows[rows:, :rows].T
    grad_logits = (
        gate_own * (grad_probs - jnp.sum(grad_probs * gate_own, axis=-1, keepdims=True))
    ).astype(bf16)
    grad_router = ein("te,td->ed", grad_logits, normed2)
    grad_normed2 = back_rows[:rows] + ein("te,de->td", grad_logits, router)
    grad_ffn_gain = jnp.sum(grad_normed2 * residual * rms2, axis=0)
    u = grad_normed2 * ffn_gain
    grad_residual = (
        grad_full.astype(f32)
        + rms2 * u
        - residual * rms2**3 * jnp.mean(u * residual, axis=-1, keepdims=True)
    )
    grad_low = grad_residual.astype(bf16)
    out_held = lax.dynamic_slice_in_dim(out_full, jnp.where(odd, col0 - spare, col0), held, 0)
    grad_attended = ein("cd,td->ct", out_held, grad_low).astype(bf16).reshape(shape3)
    grad_p = ein("hdq,hdk->hqk", grad_attended, v)
    grad_v = ein("hdq,hqk->hdk", grad_attended, probs_low).astype(bf16)
    grad_s = (probs * (grad_p - jnp.sum(probs * grad_p, axis=-1, keepdims=True))).astype(bf16)
    grad_q = ein("hdk,hqk->hdq", k, grad_s) * scale
    grad_k = ein("hdq,hqk->hdk", q, grad_s) * scale
    grad_q = own(rope_back(grad_q, cosine, sine).astype(bf16).reshape(held, rows))
    grad_k = own(rope_back(grad_k, cosine, sine).astype(bf16).reshape(held, rows))
    grad_v = own(grad_v.reshape(held, rows))
    low_own = quarter_of(grad_low).T
    back_own = quarter_of(grad_residual).T

    def over_ep(a):
        return lax.psum(a.astype(bf16), EP).astype(f32)

    if small:
        grad_tokens, sums = finish(
            grad_q,
            grad_k,
            grad_v,
            low_own,
            query_t,
            key_t,
            value_t,
            normed1,
            attended_t,
            tokens.T,
            attn_gain[:, None],
            rms1.T,
            back_own,
            grad_router,
            grad_ffn_gain[None, :],
        )
        sums = sums.astype(f32)
        heads_sums = [sums[i * quarter : (i + 1) * quarter].T for i in range(4)]
        rest = sums[4 * quarter :]
        grad_router, grad_attn_gain, grad_ffn_gain = rest[:experts].T, rest[experts], rest[experts + 1]
    else:
        heads_sums = [
            over_ep(dot(grad_q, normed1).T),
            over_ep(dot(grad_k, normed1).T),
            over_ep(dot(grad_v, normed1).T),
            over_ep(ein("ct,dt->dc", low_own, attended_t)),
        ]
        part = (
            ein("cd,ct->dt", query_t, grad_q)
            + ein("cd,ct->dt", key_t, grad_k)
            + ein("cd,ct->dt", value_t, grad_v)
        )
        grad_n1 = lax.psum_scatter(
            part.astype(bf16), "hs", scatter_dimension=0, tiled=True
        ).astype(f32)
        x_own = quarter_of(x).T
        w1 = grad_n1 * lax.dynamic_slice_in_dim(attn_gain, col0, quarter, 0)[:, None]
        mean1 = lax.psum(jnp.sum(w1 * x_own, axis=0, keepdims=True), "hs") / width
        rms_t = rms1.T
        grad_tokens = back_own + rms_t * w1 - x_own * rms_t**3 * mean1
        gain_own = jnp.sum(grad_n1 * x_own * rms_t, axis=1)
        gain_part = lax.dynamic_update_slice_in_dim(jnp.zeros((width,), f32), gain_own, col0, 0)
        grad_attn_gain = lax.psum(gain_part, (*EP, "hs"))
        grad_ffn_gain = lax.psum(grad_ffn_gain, EP)
        grad_router = over_ep(grad_router.T)

    return (
        output,
        grad_tokens.T,
        grad_attn_gain,
        *heads_sums,
        grad_ffn_gain,
        grad_router,
        shared_sums[0].T,
        shared_sums[1].T,
        shared_sums[2],
        grad_expert_gate,
        grad_expert_up,
        grad_expert_down,
    )


def solution(mesh):
    ep_count, hs_count = mesh.devices.shape
    cut = Mesh(mesh.devices.reshape(ep_count // 2, 2, hs_count), ("xy", "core", "hs"))
    return jax.shard_map(
        shards,
        mesh=cut,
        in_specs=(
            P(EP, None),
            P(),
            P(None, "hs"),
            P(None, "hs"),
            P(None, "hs"),
            P(None, "hs"),
            P(),
            P(),
            P(None, "hs"),
            P(None, "hs"),
            P("hs", None),
            P(EP, None, "hs"),
            P(EP, None, "hs"),
            P(EP, "hs", None),
            P(EP, None),
            P(EP, None),
            P(EP, "hs"),
        ),
        out_specs=(
            P(EP, "hs"),
            P(EP, "hs"),
            P(),
            P(None, "hs"),
            P(None, "hs"),
            P(None, "hs"),
            P(None, "hs"),
            P(),
            P(),
            P(None, "hs"),
            P(None, "hs"),
            P("hs", None),
            P(EP, None, "hs"),
            P(EP, None, "hs"),
            P(EP, "hs", None),
        ),
        check_vma=False,
    )
```

```python
import functools
import math

import jax
import jax.numpy as jnp
import numpy as np
from jax import lax
from jax.experimental import pallas as pl
from jax.experimental.layout import Layout, with_layout_constraint
from jax.experimental.pallas import tpu as pltpu
from jax.sharding import Mesh
from jax.sharding import PartitionSpec as P

HEADS = 10
HEAD_DIM = 128
CAP = 112
EPS = 1e-06
EP = ("xy", "core")
bf16 = jnp.bfloat16
f32 = jnp.float32


def dot(a, b):
    return jnp.dot(a, b, preferred_element_type=f32)


def ein(spec, a, b):
    return jnp.einsum(spec, a, b, preferred_element_type=f32)


def rope_tables(rows):
    half = HEAD_DIM // 2
    frequency = 10000.0 ** (-np.arange(half) * 2.0 / HEAD_DIM)
    angles = frequency[:, None] * np.arange(rows)[None, :]
    return jnp.asarray(np.cos(angles), f32), jnp.asarray(np.sin(angles), f32)


def rope(v, cosine, sine):
    half = HEAD_DIM // 2
    a, b = v[:, :half], v[:, half:]
    return jnp.concatenate([a * cosine - b * sine, b * cosine + a * sine], axis=1)


def rope_back(v, cosine, sine):
    half = HEAD_DIM // 2
    a, b = v[:, :half], v[:, half:]
    return jnp.concatenate([a * cosine + b * sine, b * cosine - a * sine], axis=1)


VMEM_LIMIT = 60 * 1024 * 1024
PAD = 256


def nn(a, b):
    return lax.dot_general(a, b, (((1,), (0,)), ((), ())), preferred_element_type=f32)


def nt(a, b):
    return lax.dot_general(a, b, (((1,), (1,)), ((), ())), preferred_element_type=f32)


def tn(a, b):
    return lax.dot_general(a, b, (((0,), (0,)), ((), ())), preferred_element_type=f32)


def takes(microseconds):
    return pl.CostEstimate(flops=0, transcendentals=0, bytes_accessed=microseconds * 3_000_000)


def slot_masks(slot_ref, at):
    local, rows = slot_ref.shape[-2:]
    number = lax.broadcasted_iota(jnp.int32, (CAP, rows), 0)
    return [slot_ref[at, e : e + 1, :] == number for e in range(local)]


def spread_kernel(weighted, *refs):
    if weighted:
        rows_ref, slot_ref, router_ref, x_ref, sw_ref, pick = refs
    else:
        rows_ref, slot_ref, x_ref, pick = refs
    local = slot_ref.shape[1]
    rows = rows_ref[...] if weighted else rows_ref[0]
    masks = slot_masks(slot_ref, 0)
    if weighted:
        logits = nt(router_ref[...], rows)
        raised = jnp.exp(logits - jnp.max(logits, axis=0, keepdims=True))
        gates = raised / jnp.sum(raised, axis=0, keepdims=True)
    for e in range(local):
        pick[e * CAP : (e + 1) * CAP, :] = masks[e].astype(f32).astype(bf16)
        if weighted:
            sw_ref[e] = jnp.sum(
                jnp.where(masks[e], gates[e : e + 1, :], 0.0), axis=1, keepdims=True
            )
    product = nn if weighted else nt
    x_ref[...] = product(pick[...], rows).astype(bf16).reshape(x_ref.shape)


def spread(all_rows, slot, router_t=None):
    s, local, rows = slot.shape
    weighted = router_t is not None
    if weighted:
        width = all_rows.shape[1]
        block = pl.BlockSpec((rows, width), lambda i: (i, 0))
    else:
        width = all_rows.shape[1]
        block = pl.BlockSpec((1, width, rows), lambda i: (i, 0, 0))
    in_specs = [
        block,
        pl.BlockSpec((1, local, rows), lambda i: (i, 0, 0)),
    ]
    out_specs = [pl.BlockSpec((1, local, CAP, width), lambda i: (i, 0, 0, 0))]
    out_shape = [jax.ShapeDtypeStruct((s, local, CAP, width), bf16)]
    args = [all_rows, slot]
    if weighted:
        in_specs.append(pl.BlockSpec(router_t.shape, lambda i: (0, 0)))
        out_specs.append(pl.BlockSpec((local, CAP, 1), lambda i: (0, i, 0)))
        out_shape.append(jax.ShapeDtypeStruct((local, s * CAP, 1), f32))
        args.append(router_t)
    out = pl.pallas_call(
        functools.partial(spread_kernel, weighted),
        grid=(s,),
        in_specs=in_specs,
        out_specs=out_specs,
        out_shape=out_shape,
        scratch_shapes=[pltpu.VMEM((local * CAP, rows), bf16)],
        compiler_params=pltpu.CompilerParams(vmem_limit_bytes=VMEM_LIMIT),
        cost_estimate=takes(17),
        name="spread",
    )(*args)
    return out if weighted else out[0]


def padded(ref, out):
    ff = ref.shape[1]
    out[:ff, :] = ref[0]
    out[ff:, :] = jnp.zeros((out.shape[0] - ff, out.shape[1]), out.dtype)


def experts_forward_kernel(
    x_ref, sw_ref, wg_ref, wu_ref, wd_ref, y_ref, gate_ref, up_ref, wg, wu, wd
):
    padded(wg_ref, wg)
    padded(wu_ref, wu)
    padded(wd_ref, wd)
    rows, width = gate_ref.shape[1], x_ref.shape[3]
    x = x_ref[...].reshape(rows, width)
    gate = nt(x, wg[...])
    up = nt(x, wu[...])
    gate_ref[0] = gate
    up_ref[0] = up
    act = gate / (1.0 + jnp.exp(-gate))
    hidden = (act * up).astype(bf16).astype(f32)
    hidden_w = (hidden * sw_ref[0]).astype(bf16)
    y_ref[...] = nn(hidden_w, wd[...]).astype(bf16).reshape(y_ref.shape)


def experts_backward_kernel(
    groups,
    x_ref,
    gx_ref,
    gate_ref,
    up_ref,
    sw_ref,
    wg_ref,
    wu_ref,
    wd_ref,
    dx_ref,
    dg_ref,
    du_ref,
    dd_ref,
    gsw_ref,
    wg,
    wu,
    wd,
):
    padded(wg_ref, wg)
    padded(wu_ref, wu)
    padded(wd_ref, wd)
    rows, width = gate_ref.shape[1], x_ref.shape[3]
    ff = wg_ref.shape[1]
    x = x_ref[...].reshape(rows, width)
    gx = gx_ref[...].reshape(rows, width)
    gate, up, sw = gate_ref[0], up_ref[0], sw_ref[0]
    sig = 1.0 / (1.0 + jnp.exp(-gate))
    act = gate * sig
    hidden = (act * up).astype(bf16).astype(f32)
    gh = nt(gx, wd[...])
    gsw_ref[0] = jnp.sum(gh * hidden, axis=-1, keepdims=True)
    gh = gh * sw
    gg = (gh * up * sig * (1.0 + gate * (1.0 - sig))).astype(bf16)
    gu = (gh * act).astype(bf16)
    sums = (
        (dd_ref, tn((hidden * sw).astype(bf16), gx)[:ff]),
        (dg_ref, tn(gg, x)[:ff]),
        (du_ref, tn(gu, x)[:ff]),
    )
    if groups == 1:
        for ref, value in sums:
            ref[0] = value
    else:

        @pl.when(pl.program_id(1) == 0)
        def _():
            for ref, value in sums:
                ref[0] = value

        @pl.when(pl.program_id(1) > 0)
        def _():
            for ref, value in sums:
                ref[0] += value

    dx_ref[...] = (nn(gg, wg[...]) + nn(gu, wu[...])).astype(bf16).reshape(dx_ref.shape)


def expert_specs(s, width):
    group = min(s, 8)
    slots = pl.BlockSpec((group, 1, CAP, width), lambda i, j: (j, i, 0, 0))
    lines = lambda columns: pl.BlockSpec((1, group * CAP, columns), lambda i, j: (i, j, 0))
    per = lambda *shape: pl.BlockSpec((1, *shape), lambda i, j: (i, 0, 0))
    return s // group, slots, lines, per


def experts_forward(x, sw, wg, wu, wd):
    s, local, cap, width = x.shape
    ff = wg.shape[1]
    rows = s * cap
    groups, slots, lines, per = expert_specs(s, width)
    middle = jax.ShapeDtypeStruct((local, rows, PAD), f32)
    return pl.pallas_call(
        experts_forward_kernel,
        grid=(local, groups),
        in_specs=[slots, lines(1)] + [per(ff, width)] * 3,
        out_specs=[slots, lines(PAD), lines(PAD)],
        out_shape=[jax.ShapeDtypeStruct(x.shape, bf16), middle, middle],
        scratch_shapes=[pltpu.VMEM((PAD, width), bf16)] * 3,
        compiler_params=pltpu.CompilerParams(vmem_limit_bytes=VMEM_LIMIT),
        cost_estimate=takes(31),
        name="experts_forward",
    )(x, sw, wg, wu, wd)


def experts_backward(x, gx, gate, up, sw, wg, wu, wd):
    s, local, cap, width = x.shape
    ff = wg.shape[1]
    rows = s * cap
    groups, slots, lines, per = expert_specs(s, width)
    return pl.pallas_call(
        functools.partial(experts_backward_kernel, groups),
        grid=(local, groups),
        in_specs=[slots, slots, lines(PAD), lines(PAD), lines(1)]
        + [per(ff, width)] * 3,
        out_specs=[slots] + [per(ff, width)] * 3 + [lines(1)],
        out_shape=[jax.ShapeDtypeStruct(x.shape, bf16)]
        + [jax.ShapeDtypeStruct((local, ff, width), f32)] * 3
        + [jax.ShapeDtypeStruct((local, rows, 1), f32)],
        scratch_shapes=[pltpu.VMEM((PAD, width), bf16)] * 3,
        compiler_params=pltpu.CompilerParams(vmem_limit_bytes=VMEM_LIMIT),
        cost_estimate=takes(47),
        name="experts_backward",
    )(x, gx, gate, up, sw, wg, wu, wd)


def collect_kernel(y_ref, slot_ref, out_ref, pick):
    local = slot_ref.shape[1]
    masks = slot_masks(slot_ref, 0)
    for e in range(local):
        pick[e * CAP : (e + 1) * CAP, :] = masks[e].astype(f32).astype(bf16)
    out_ref[0] = tn(pick[...], y_ref[...].reshape(pick.shape[0], -1)).astype(bf16)


def collect_back_kernel(experts, y_ref, slot_ref, gsw_ref, first_ref, out_ref, pick):
    local, rows = slot_ref.shape[1:]
    first = first_ref[0]
    masks = slot_masks(slot_ref, 0)
    number = lax.broadcasted_iota(jnp.int32, (experts, rows), 0)
    probs = jnp.zeros((experts, rows), f32)
    for e in range(local):
        pick[e * CAP : (e + 1) * CAP, :] = masks[e].astype(f32).astype(bf16)
        line = jnp.sum(jnp.where(masks[e], gsw_ref[e], 0.0), axis=0, keepdims=True)
        probs = jnp.where(number == first + e, line, probs)
    out_ref[0, :rows] = tn(pick[...], y_ref[...].reshape(pick.shape[0], -1)).astype(bf16)
    out_ref[0, rows:] = jnp.zeros((experts, out_ref.shape[2]), bf16)
    out_ref[0, rows:, :rows] = probs.astype(bf16)


def collect(y, slot, gsw=None, first=None, experts=0):
    s, local, cap, width = y.shape
    rows = slot.shape[2]
    in_specs = [
        pl.BlockSpec((1, local, cap, width), lambda i: (i, 0, 0, 0)),
        pl.BlockSpec((1, local, rows), lambda i: (i, 0, 0)),
    ]
    args = [y, slot]
    kernel = collect_kernel
    tall = rows
    if gsw is not None:
        in_specs += [
            pl.BlockSpec((local, cap, 1), lambda i: (0, i, 0)),
            pl.BlockSpec(memory_space=pltpu.SMEM),
        ]
        args += [gsw, first.reshape(1)]
        kernel = functools.partial(collect_back_kernel, experts)
        tall = rows + experts
    return pl.pallas_call(
        kernel,
        grid=(s,),
        in_specs=in_specs,
        out_specs=pl.BlockSpec((1, tall, width), lambda i: (i, 0, 0)),
        out_shape=jax.ShapeDtypeStruct((s, tall, width), bf16),
        scratch_shapes=[pltpu.VMEM((local * cap, rows), bf16)],
        compiler_params=pltpu.CompilerParams(vmem_limit_bytes=VMEM_LIMIT),
        cost_estimate=takes(17),
        name="collect",
    )(*args)


MESH = pl.DeviceIdType.MESH
EXTRA = 64


def places():
    chip, core, z = lax.axis_index("xy"), lax.axis_index("core"), lax.axis_index("hs")
    x, y = chip % 2, chip // 2
    return chip, core, z, y * 2 + (1 - x), (1 - y) * 2 + x, (1 - y) * 2 + (1 - x)


def greet(peers):
    barrier = pltpu.get_barrier_semaphore()
    for peer in peers:
        pl.semaphore_signal(barrier, inc=1, device_id=peer, device_id_type=MESH)
    pl.semaphore_wait(barrier, len(peers))


def remote(src, dst, send, recv, peer):
    return pltpu.make_async_remote_copy(
        src_ref=src, dst_ref=dst, send_sem=send, recv_sem=recv, device_id=peer, device_id_type=MESH
    )


def block(q, size):
    return pl.ds(pl.multiple_of(q * size, 16), size)


def weight_sum(grads, given, half, land, out_ref, csend, crecv, send, recv):
    chip, core, z, cx, cy, cd = places()
    other = 1 - core
    c_peer = (chip, other, z)
    chips = (cx, cy, cd)
    count = grads.shape[0] // 2
    piece = count // 4

    to_core = remote(grads.at[block(other, count)], given, csend.at[0], crecv.at[0], c_peer)
    scatter = [
        remote(half.at[block(c, piece)], land.at[i], send.at[i], recv.at[i], (c, core, z))
        for i, c in enumerate(chips)
    ]

    def share():
        to_core.wait_recv()
        half[...] = (grads[block(core, count)].astype(f32) + given[...].astype(f32)).astype(bf16)
        for i in (2, 0, 1):
            scatter[i].start()

    def place(c, k):
        return pl.ds(pl.multiple_of(k * count + c * piece, 16), piece)

    def give(number, c, k, sems, peer):
        return remote(out_ref.at[place(c, k)], out_ref.at[place(c, k)], *sems(number), peer)

    def chip_sems(i):
        return send.at[3 + i], recv.at[3 + i]

    def core_sems(i):
        return csend.at[1 + i], crecv.at[1 + i]

    gather = [give(i, chip, core, chip_sems, (c, core, z)) for i, c in enumerate(chips)]
    over = [give(i, c, core, core_sems, c_peer) for i, c in enumerate((*chips, chip))]

    def give_back():
        done = half[block(chip, piece)].astype(f32)
        for i in range(3):
            scatter[i].wait_recv()
            done = done + land[i].astype(f32)
        out_ref[place(chip, core)] = done.astype(bf16)
        for i in (2, 0, 1):
            gather[i].start()
        over[3].start()

    def end():
        for i, c in enumerate(chips):
            give(i, c, core, chip_sems, (c, core, z)).wait_recv()
            over[i].start()
        for i, c in enumerate((*chips, chip)):
            give(i, c, other, core_sems, c_peer).wait_recv()
        for copy in (to_core, *scatter, *gather, *over):
            copy.wait_send()

    return to_core.start, share, give_back, end


def weight_sum_scratch(tall, width):
    dma = pltpu.SemaphoreType.DMA
    return [
        pltpu.VMEM((tall, width), bf16),
        pltpu.VMEM((tall // 2, width), bf16),
        pltpu.VMEM((tall // 2, width), bf16),
        pltpu.VMEM((3, tall // 8, width), bf16),
        dma((5,)),
        dma((5,)),
        dma((6,)),
        dma((6,)),
    ]


def gather_spread_kernel(
    own_ref, slots_ref, router_ref, x_ref, sw_ref, slot_ref, held, pick, xbuf, send, recv, copied
):
    chip, core, z, cx, cy, cd = places()
    other = 1 - core
    x_peer, y_peer, c_peer = (cx, core, z), (cy, core, z), (chip, other, z)
    tall = held.shape[1]
    half = tall // 2
    local, rows = slot_ref.shape[1:]
    me = chip * 2 + core
    top, low = pl.ds(0, half), pl.ds(half, half)

    def at(c, k):
        return c * 2 + k

    def move(number, src_slot, part, peer):
        return remote(
            held.at[src_slot, part], held.at[src_slot, part], send.at[number], recv.at[number], peer
        )

    whole = pl.ds(0, tall)
    greet([x_peer, y_peer, c_peer])
    held[me, :rows] = own_ref[...]
    held[me, rows:] = jnp.zeros((EXTRA, own_ref.shape[1]), bf16)
    held[me, rows:, :rows] = slots_ref[...]
    x_top, x_low = move(0, me, top, x_peer), move(1, me, low, x_peer)
    y_low, y_top = move(2, me, low, y_peer), move(3, me, top, y_peer)
    to_core = move(4, me, whole, c_peer)
    relay_top, relay_low = move(5, at(cx, core), top, y_peer), move(6, at(cy, core), low, x_peer)
    pass_x, pass_y = move(7, at(cx, core), whole, c_peer), move(8, at(cy, core), whole, c_peer)
    pass_d = move(9, at(cd, core), whole, c_peer)
    for copy in (x_top, y_low, x_low, y_top, to_core):
        copy.start()

    def arrived(number, slot, part):
        move(number, slot, part, c_peer).wait_recv()

    number = lax.broadcasted_iota(jnp.int32, (CAP, rows), 0)
    first = me * local
    line = lax.broadcasted_iota(jnp.int32, (local, EXTRA), 0)
    column = lax.broadcasted_iota(jnp.int32, (local, EXTRA), 1)
    chosen = (column == line + first).astype(f32).astype(bf16)

    def out_copy(t, src):
        return pltpu.make_async_copy(xbuf.at[t % 2], x_ref.at[src], copied.at[t % 2])

    def step(t, carry):
        @pl.when(t == 1)
        def _():
            arrived(4, at(chip, other), whole)

        @pl.when(t == 2)
        def _():
            arrived(0, at(cx, core), top)
            relay_top.start()
            arrived(2, at(cy, core), low)
            relay_low.start()
            arrived(1, at(cx, core), low)
            pass_x.start()

        @pl.when(t == 3)
        def _():
            arrived(3, at(cy, core), top)
            pass_y.start()
            arrived(7, at(cx, other), whole)

        @pl.when(t == 5)
        def _():
            arrived(8, at(cy, other), whole)

        @pl.when(t == 6)
        def _():
            arrived(5, at(cd, core), top)
            arrived(6, at(cd, core), low)
            pass_d.start()

        @pl.when(t == 7)
        def _():
            arrived(9, at(cd, other), whole)

        x, y = (chip % 2 + (t // 2) % 2) % 2, (chip // 2 + t // 4) % 2
        src = (y * 2 + x) * 2 + (core + t % 2) % 2
        slots = nn(chosen, held[src, rows:, :rows]).astype(jnp.int32)
        slot_ref[src] = slots
        logits = nt(router_ref[...], held[src, :rows])
        raised = jnp.exp(logits - jnp.max(logits, axis=0, keepdims=True))
        gates = raised / jnp.sum(raised, axis=0, keepdims=True)
        for e in range(local):
            mask = slots[e : e + 1, :] == number
            pick[e * CAP : (e + 1) * CAP, :] = mask.astype(f32).astype(bf16)
            sw_ref[e, pl.ds(pl.multiple_of(src * CAP, 8), CAP), :] = jnp.sum(
                jnp.where(mask, gates[e : e + 1, :], 0.0), axis=1, keepdims=True
            )

        @pl.when(t >= 2)
        def _():
            out_copy(t, src).wait()

        xbuf[t % 2] = nn(pick[...], held[src, :rows]).astype(bf16).reshape(xbuf.shape[1:])
        out_copy(t, src).start()
        return carry

    lax.fori_loop(0, 8, step, 0)
    out_copy(0, me).wait()
    out_copy(1, me).wait()
    for copy in (x_top, x_low, y_low, y_top, to_core, relay_top, relay_low, pass_x, pass_y, pass_d):
        copy.wait_send()


def gather_spread(own, slots, router_t, local, ep_count):
    rows, width = own.shape
    tall = rows + EXTRA
    vmem = pl.BlockSpec(memory_space=pltpu.VMEM)
    return pl.pallas_call(
        gather_spread_kernel,
        in_specs=[vmem, vmem, vmem],
        out_specs=[pl.BlockSpec(memory_space=pl.ANY), vmem, vmem],
        out_shape=[
            jax.ShapeDtypeStruct((ep_count, local, CAP, width), bf16),
            jax.ShapeDtypeStruct((local, ep_count * CAP, 1), f32),
            jax.ShapeDtypeStruct((ep_count, local, rows), jnp.int32),
        ],
        scratch_shapes=[
            pltpu.VMEM((ep_count, tall, width), bf16),
            pltpu.VMEM((local * CAP, rows), bf16),
            pltpu.VMEM((2, local, CAP, width), bf16),
            pltpu.SemaphoreType.DMA((10,)),
            pltpu.SemaphoreType.DMA((10,)),
            pltpu.SemaphoreType.DMA((2,)),
        ],
        compiler_params=pltpu.CompilerParams(
            vmem_limit_bytes=VMEM_LIMIT, collective_id=0, has_side_effects=True
        ),
        cost_estimate=takes(62),
        name="gather_spread",
    )(own, slots, router_t)


def front_kernel(
    x_ref,
    gain_ref,
    wq_ref,
    wk_ref,
    wv_ref,
    wo_ref,
    ffn_gain_ref,
    doc_ref,
    doc_column_ref,
    cos_ref,
    sin_ref,
    normed1_ref,
    q_ref,
    k_ref,
    v_ref,
    probs_ref,
    attended_ref,
    out_ref,
    residual_ref,
    normed2_ref,
    shared,
    beside,
    esend,
    erecv,
    asend,
    arecv,
    zsend,
    zrecv,
    send,
    recv,
    csend,
    crecv,
):
    chip, core, z, cx, cy, cd = places()
    other = 1 - core
    odd = z % 2
    c_peer = (chip, other, z)
    chips = (cx, cy, cd)
    z_peers = [(chip, core, (z + i) % 4) for i in (1, 2, 3)]
    pair = (chip, core, z + 1 - 2 * odd)
    rows, width = x_ref.shape
    quarter = wq_ref.shape[0]
    whole = HEAD_DIM * (quarter // HEAD_DIM)
    spare = quarter - whole
    greet([c_peer, *[(c, core, z) for c in chips], *z_peers])

    full_rows = pl.ds(pl.multiple_of(odd * spare, 16), whole)
    half_rows = pl.ds(pl.multiple_of((1 - odd) * whole, 16), spare)
    for i, ref in enumerate((wq_ref, wk_ref, wv_ref)):
        shared[i * spare : (i + 1) * spare] = ref[half_rows]
    trade = remote(shared, beside, esend, erecv, pair)
    trade.start()

    share, lanes = quarter // 4, width // 2
    my_lanes = pl.ds(pl.multiple_of(core * lanes, 128), lanes)

    def piece(c):
        return pl.ds(pl.multiple_of(c * share, 16), share)

    out_z = [
        remote(
            wo_ref.at[piece(chip), my_lanes],
            out_ref.at[z, piece(chip), my_lanes],
            zsend.at[i],
            zrecv.at[i],
            peer,
        )
        for i, peer in enumerate(z_peers)
    ]
    for i in (1, 0, 2):
        out_z[i].start()
    behind = [(z + 3 - i) % 4 for i in range(3)]

    def out_chip(i, j, c):
        at = out_ref.at[behind[i], piece(c), my_lanes]
        return remote(at, at, send.at[3 * i + j], recv.at[3 * i + j], (chips[j], core, z))

    def out_core(i, k):
        half = pl.ds(pl.multiple_of(k * lanes, 128), lanes)
        at = out_ref.at[behind[i], :, half]
        return remote(at, at, csend.at[i], crecv.at[i], c_peer)

    x = x_ref[...].astype(f32)
    rms1 = lax.rsqrt(jnp.sum(x * x, axis=-1, keepdims=True) * (1.0 / width) + EPS)
    normed1_ref[...] = (x * rms1 * gain_ref[...]).astype(bf16)
    out_ref[z] = wo_ref[...]

    cosine, sine = cos_ref[...], sin_ref[...]
    half_dim = HEAD_DIM // 2
    scale = 1.0 / math.sqrt(HEAD_DIM)
    row = lax.broadcasted_iota(jnp.int32, (rows, rows), 0)
    column = lax.broadcasted_iota(jnp.int32, (rows, rows), 1)
    allowed = (row >= column) & (doc_column_ref[...] == doc_ref[...])

    def turn(pre):
        a, b = pre[:half_dim], pre[half_dim:]
        return (
            jnp.concatenate([a * cosine - b * sine, b * cosine + a * sine], axis=0).astype(bf16)
        )

    def attend(h):
        scores = jnp.where(allowed, tn(q_ref[h], k_ref[h]) * scale, -1e30)
        raised = jnp.exp(scores - jnp.max(scores, axis=-1, keepdims=True))
        probs = raised * (1.0 / jnp.sum(raised, axis=-1, keepdims=True))
        probs_ref[h] = probs
        return nt(v_ref[h], probs.astype(bf16)).astype(bf16)

    def project(at):
        return [nt(ref[at], normed1_ref[...]) for ref in (wq_ref, wk_ref, wv_ref)]

    q, k, v = project(full_rows)
    heads = whole // HEAD_DIM
    for h in range(heads):
        at = slice(h * HEAD_DIM, (h + 1) * HEAD_DIM)
        q_ref[h], k_ref[h], v_ref[h] = turn(q[at]), turn(k[at]), v[at].astype(bf16)

    def attended_copy(number, start, size):
        at = attended_ref.at[pl.ds(pl.multiple_of(start, 16), size)]
        return lambda i: remote(
            at, at, asend.at[number, i], arecv.at[number, i], z_peers[i]
        )

    mine = z * quarter
    copies = []
    for h in range(heads):
        start = mine + odd * spare + h * HEAD_DIM
        attended_ref[pl.ds(pl.multiple_of(start, 16), HEAD_DIM)] = attend(h)
        copy = attended_copy(h, start, HEAD_DIM)
        copies += [copy(1), copy(0), copy(2)]
        for one in copies[-3:]:
            one.start()
        if h == 0:
            for i in range(3):
                out_z[i].wait_recv()
                for j in (2, 0, 1):
                    out_chip(i, j, chip).start()

    trade.wait_recv()
    for i, (ref, to) in enumerate(((wq_ref, q_ref), (wk_ref, k_ref), (wv_ref, v_ref))):
        normed1 = normed1_ref[...]
        here = nt(ref[half_rows], normed1)
        there = nt(beside[i * spare : (i + 1) * spare], normed1)
        first = jnp.where(odd == 1, there, here)
        second = jnp.where(odd == 1, here, there)
        both = jnp.concatenate([first, second], axis=0)
        to[heads] = both.astype(bf16) if to is v_ref else turn(both)
    last = attend(heads)
    last = jnp.where(odd == 1, last[spare:], last[:spare])
    start = mine + (1 - odd) * whole
    attended_ref[pl.ds(pl.multiple_of(start, 16), spare)] = last
    copy = attended_copy(heads, start, spare)
    copies += [copy(1), copy(0), copy(2)]
    for one in copies[-3:]:
        one.start()

    for i in range(3):
        for j in range(3):
            out_chip(i, j, chips[j]).wait_recv()
        out_core(i, core).start()
    for i in range(3):
        from_z = (z + 3 - i) % 4
        from_odd = from_z % 2
        for h in range(heads):
            attended_copy(h, from_z * quarter + from_odd * spare + h * HEAD_DIM, HEAD_DIM)(i).wait_recv()
        attended_copy(heads, from_z * quarter + (1 - from_odd) * whole, spare)(i).wait_recv()
        out_core(i, other).wait_recv()
    attended = attended_ref[...].T
    residual = x_ref[...].astype(f32) + nt(attended, out_ref[...].reshape(width, width))
    residual_ref[...] = residual
    rms2 = lax.rsqrt(jnp.sum(residual * residual, axis=-1, keepdims=True) * (1.0 / width) + EPS)
    normed2_ref[...] = (residual * rms2 * ffn_gain_ref[...]).astype(bf16)
    for one in (trade, *out_z, *copies):
        one.wait_send()
    for i in range(3):
        for j in range(3):
            out_chip(i, j, chip).wait_send()
        out_core(i, core).wait_send()


def front(x, gain, wq, wk, wv, wo, ffn_gain, doc, tables):
    rows, width = x.shape
    quarter = wq.shape[0]
    heads = -(-quarter // HEAD_DIM)
    spare = quarter % HEAD_DIM
    vmem = pl.BlockSpec(memory_space=pltpu.VMEM)
    dma = pltpu.SemaphoreType.DMA
    low = lambda *shape: jax.ShapeDtypeStruct(shape, bf16)
    return pl.pallas_call(
        front_kernel,
        in_specs=[vmem] * 11,
        out_specs=[vmem] * 9,
        out_shape=[
            low(rows, width),
            *[low(heads, HEAD_DIM, rows)] * 3,
            jax.ShapeDtypeStruct((heads, rows, rows), f32),
            low(width, rows),
            low(4, quarter, width),
            jax.ShapeDtypeStruct((rows, width), f32),
            low(rows, width),
        ],
        scratch_shapes=[
            pltpu.VMEM((3 * spare, width), bf16),
            pltpu.VMEM((3 * spare, width), bf16),
            dma,
            dma,
            dma((heads, 3)),
            dma((heads, 3)),
            dma((3,)),
            dma((3,)),
            dma((9,)),
            dma((9,)),
            dma((3,)),
            dma((3,)),
        ],
        compiler_params=pltpu.CompilerParams(
            vmem_limit_bytes=VMEM_LIMIT, collective_id=1, has_side_effects=True
        ),
        cost_estimate=takes(50),
        name="front",
    )(x, gain[None, :], wq, wk, wv, wo, ffn_gain[None, :], doc, doc.T, *tables)


def collect_sum_kernel(
    y_ref,
    slot_ref,
    gsw_ref,
    mine_ref,
    shared_gate_ref,
    shared_up_ref,
    shared_down_ref,
    forward_ref,
    out_ref,
    sum_ref,
    passed_ref,
    pick,
    ybuf,
    stage,
    given,
    sums,
    relay,
    land,
    zland,
    total,
    copied,
    core_send,
    core_recv,
    send,
    recv,
    zsend,
    zrecv,
    grads,
    *more,
):
    chip, core, z, cx, cy, cd = places()
    other = 1 - core
    x_peer, y_peer, c_peer = (cx, core, z), (cy, core, z), (chip, other, z)
    z_peers = [(chip, core, (z + i) % 4) for i in (1, 2, 3)]
    local, rows = slot_ref.shape[1:]
    tall = out_ref.shape[0]
    half, part = tall // 2, tall // 4
    me = chip * 2 + core
    top, low = pl.ds(0, half), pl.ds(half, half)
    number = lax.broadcasted_iota(jnp.int32, (CAP, rows), 0)
    row = lax.broadcasted_iota(jnp.int32, (EXTRA, rows), 0)

    greet([x_peer, y_peer, c_peer, (cd, core, z), *z_peers])

    def sequence(t):
        p = t // 2
        x, y = (chip % 2 + 1 + p // 2) % 2, (chip // 2 + 1 + p % 2) % 2
        return (y * 2 + x) * 2 + (core + 1 + t % 2) % 2

    def in_copy(t):
        return pltpu.make_async_copy(y_ref.at[sequence(t)], ybuf.at[t % 2], copied.at[t % 2])

    def to_core(p):
        return remote(stage.at[p], given.at[p], core_send.at[p], core_recv.at[p], c_peer)

    far_top = remote(sums.at[0, top], relay.at[0], send.at[0], recv.at[0], x_peer)
    far_low = remote(sums.at[0, low], relay.at[1], send.at[1], recv.at[1], y_peer)
    x_top = remote(sums.at[1, top], land.at[0, top], send.at[2], recv.at[2], x_peer)
    x_low = remote(sums.at[1, low], land.at[0, low], send.at[3], recv.at[3], x_peer)
    y_low = remote(sums.at[2, low], land.at[1, low], send.at[4], recv.at[4], y_peer)
    y_top = remote(sums.at[2, top], land.at[1, top], send.at[5], recv.at[5], y_peer)

    in_copy(0).start()
    passed_ref[...] = forward_ref[...]
    start, share, give_back, end = weight_sum(grads, *more[:3], sum_ref, *more[3:])
    at = 0
    for ref in (shared_gate_ref, shared_up_ref, shared_down_ref):
        grads[at : at + ref.shape[0]] = ref[...]
        at += ref.shape[0]
    grads[at:] = jnp.zeros((grads.shape[0] - at, grads.shape[1]), bf16)
    start()

    def step(t, carry):
        @pl.when(t < 7)
        def _():
            in_copy(t + 1).start()

        p, s = t // 2, sequence(t)
        probs = jnp.zeros((EXTRA, rows), f32)
        for e in range(local):
            mask = slot_ref[s, e : e + 1, :] == number
            pick[e * CAP : (e + 1) * CAP, :] = mask.astype(f32).astype(bf16)
            column = gsw_ref[e, pl.ds(pl.multiple_of(s * CAP, 8), CAP), :]
            line = jnp.sum(jnp.where(mask, column, 0.0), axis=0, keepdims=True)
            probs = jnp.where(row == me * local + e, line, probs)
        in_copy(t).wait()
        back = tn(pick[...], ybuf[t % 2].reshape(local * CAP, -1))

        @pl.when(t % 2 == 0)
        def _():
            stage[p, :rows] = back.astype(bf16)
            stage[p, rows:] = jnp.zeros((tall - rows, back.shape[1]), bf16)
            stage[p, rows:, :rows] = probs.astype(bf16)
            to_core(p).start()

        @pl.when(t % 2 == 1)
        def _():
            to_core(p).wait_recv()
            sums[p, :rows] = (back + given[p, :rows].astype(f32)).astype(bf16)
            sums[p, rows:] = given[p, rows:]
            sums[p, rows:, :rows] = (probs + given[p, rows:, :rows].astype(f32)).astype(bf16)

        @pl.when(t == 1)
        def _():
            far_top.start()
            far_low.start()

        @pl.when(t == 3)
        def _():
            x_top.start()

        @pl.when(t == 5)
        def _():
            y_low.start()

        return carry

    lax.fori_loop(0, 8, step, 0)
    far_low.wait_recv()
    sums[1, half:] = (sums[1, half:].astype(f32) + relay[1].astype(f32)).astype(bf16)
    x_low.start()
    far_top.wait_recv()
    sums[2, :half] = (sums[2, :half].astype(f32) + relay[0].astype(f32)).astype(bf16)
    y_top.start()
    share()

    def add_up(at):
        return (
            sums[3, at].astype(f32) + land[0, at].astype(f32) + land[1, at].astype(f32)
        )

    x_top.wait_recv()
    y_top.wait_recv()
    total[:half] = (add_up(slice(0, half)) + mine_ref[:half]).astype(bf16)
    x_low.wait_recv()
    y_low.wait_recv()
    total[half:rows] = (add_up(slice(half, rows)) + mine_ref[half:]).astype(bf16)
    total[rows:] = add_up(slice(rows, tall)).astype(bf16)

    scatter = [
        remote(total.at[block((z + i) % 4, part)], zland.at[i - 1], zsend.at[i - 1], zrecv.at[i - 1], z_peers[i - 1])
        for i in (1, 2, 3)
    ]
    spread_ = [
        remote(out_ref.at[block(z, part)], out_ref.at[block(z, part)], zsend.at[2 + i], zrecv.at[2 + i], z_peers[i - 1])
        for i in (1, 2, 3)
    ]
    for i in (1, 0, 2):
        scatter[i].start()
    give_back()
    done = total[block(z, part)].astype(f32)
    for i in range(3):
        scatter[i].wait_recv()
        done = done + zland[i].astype(f32)
    out_ref[block(z, part)] = done.astype(bf16)
    for i in (1, 0, 2):
        spread_[i].start()
    end()
    for i in (1, 2, 3):
        theirs = block((z + 4 - i) % 4, part)
        remote(out_ref.at[theirs], out_ref.at[theirs], zsend.at[2 + i], zrecv.at[2 + i], z_peers[i - 1]).wait_recv()
    for copy in (far_top, far_low, x_top, x_low, y_low, y_top, *scatter, *spread_):
        copy.wait_send()
    for p in range(4):
        to_core(p).wait_send()


def collect_sum(y, slot, gsw, mine, forward, *shared):
    s, local, cap, width = y.shape
    rows = slot.shape[2]
    tall = rows + EXTRA
    half = tall // 2
    weights = 128 * (-(-sum(a.shape[0] for a in shared) // 128))
    vmem = pl.BlockSpec(memory_space=pltpu.VMEM)
    return pl.pallas_call(
        collect_sum_kernel,
        in_specs=[pl.BlockSpec(memory_space=pl.ANY)] + [vmem] * 7,
        out_specs=[vmem, vmem, vmem],
        out_shape=[
            jax.ShapeDtypeStruct((tall, width), bf16),
            jax.ShapeDtypeStruct((weights, width), bf16),
            jax.ShapeDtypeStruct(forward.shape, bf16),
        ],
        scratch_shapes=[
            pltpu.VMEM((local * cap, rows), bf16),
            pltpu.VMEM((2, local, cap, width), bf16),
            pltpu.VMEM((4, tall, width), bf16),
            pltpu.VMEM((4, tall, width), bf16),
            pltpu.VMEM((4, tall, width), bf16),
            pltpu.VMEM((2, half, width), bf16),
            pltpu.VMEM((2, tall, width), bf16),
            pltpu.VMEM((3, tall // 4, width), bf16),
            pltpu.VMEM((tall, width), bf16),
            pltpu.SemaphoreType.DMA((2,)),
            pltpu.SemaphoreType.DMA((4,)),
            pltpu.SemaphoreType.DMA((4,)),
            pltpu.SemaphoreType.DMA((6,)),
            pltpu.SemaphoreType.DMA((6,)),
            pltpu.SemaphoreType.DMA((6,)),
            pltpu.SemaphoreType.DMA((6,)),
            *weight_sum_scratch(weights, width),
        ],
        compiler_params=pltpu.CompilerParams(
            vmem_limit_bytes=VMEM_LIMIT, collective_id=2, has_side_effects=True
        ),
        cost_estimate=takes(131),
        name="collect_sum",
    )(y, slot, gsw, mine, *shared, forward)


def back_kernel(
    sums_ref,
    residual_ref,
    normed2_ref,
    grad_ref,
    router_ref,
    ffn_gain_ref,
    out_ref,
    q_ref,
    k_ref,
    v_ref,
    probs_ref,
    cos_ref,
    sin_ref,
    wq_ref,
    wk_ref,
    wv_ref,
    normed_ref,
    attended_ref,
    x_ref,
    gain_ref,
    tokens_ref,
    sum_ref,
    dq_ref,
    dk_ref,
    dv_ref,
    back_t,
    low_t,
    part,
    low_part,
    zland,
    mine,
    theirs,
    zsend,
    zrecv,
    lsend,
    lrecv,
    grads,
    given,
    half,
    land,
    csend,
    crecv,
    send,
    recv,
):
    chip, core, z, cx, cy, cd = places()
    odd = z % 2
    c_peer = (chip, 1 - core, z)
    z_peers = [(chip, core, (z + i) % 4) for i in (1, 2, 3)]
    quarter, width = wq_ref.shape
    rows = x_ref.shape[1]
    tall = grads.shape[0]
    experts = router_ref.shape[0]
    whole = HEAD_DIM * (quarter // HEAD_DIM)
    spare = quarter - whole
    heads = whole // HEAD_DIM
    greet([c_peer, *[(c, core, z) for c in (cx, cy, cd)], *z_peers])

    logits = nt(router_ref[...], normed2_ref[...])
    raised = jnp.exp(logits - jnp.max(logits, axis=0, keepdims=True))
    gates = raised / jnp.sum(raised, axis=0, keepdims=True)
    grad_probs = sums_ref[rows:, :rows].astype(f32)
    grad_logits = gates * (grad_probs - jnp.sum(grad_probs * gates, axis=0, keepdims=True))
    grad_logits = grad_logits.astype(bf16)
    grad_router = nn(grad_logits, normed2_ref[...])
    grad_normed2 = sums_ref[:rows].astype(f32) + tn(grad_logits, router_ref[...])
    residual = residual_ref[...]
    rms2 = lax.rsqrt(jnp.sum(residual * residual, axis=-1, keepdims=True) * (1.0 / width) + EPS)
    grad_ffn = jnp.sum(grad_normed2 * residual * rms2, axis=0, keepdims=True)
    u = grad_normed2 * ffn_gain_ref[...]
    mean2 = jnp.sum(u * residual, axis=-1, keepdims=True) * (1.0 / width)
    added = rms2 * u - residual * (rms2 * rms2 * rms2 * mean2)
    back_t[...] = added.T + grad_ref[...].astype(f32)
    low_t[...] = back_t[...].astype(bf16)

    cosine, sine = cos_ref[...], sin_ref[...]
    half_dim = HEAD_DIM // 2
    scale = 1.0 / math.sqrt(HEAD_DIM)

    def turn_back(v):
        a, b = v[:half_dim] * scale, v[half_dim:] * scale
        turned = [a * cosine + b * sine, b * cosine - a * sine]
        return jnp.concatenate(turned, axis=0).astype(bf16)

    first_lane = z * quarter + odd * spare
    shared_lane = z * quarter + (1 - odd) * whole - odd * spare
    for h in range(heads + 1):
        lane = first_lane + h * HEAD_DIM if h < heads else shared_lane
        lane = pl.ds(pl.multiple_of(lane, HEAD_DIM), HEAD_DIM)
        grad_attended = tn(out_ref[:, lane], low_t[...]).astype(bf16)
        probs = probs_ref[h]
        grad_p = tn(grad_attended, v_ref[h])
        grad_v = nn(grad_attended, probs.astype(bf16)).astype(bf16)
        delta = jnp.sum(probs * grad_p, axis=-1, keepdims=True)
        grad_s = (probs * (grad_p - delta)).astype(bf16)
        grad_q = turn_back(nt(k_ref[h], grad_s))
        grad_k = turn_back(nn(q_ref[h], grad_s))
        for ref, value in ((dq_ref, grad_q), (dk_ref, grad_k), (dv_ref, grad_v)):
            if h < heads:
                at = pl.ds(pl.multiple_of(odd * spare + h * HEAD_DIM, 16), HEAD_DIM)
                ref[at] = value
            else:
                at = pl.ds(pl.multiple_of((1 - odd) * whole, 16), spare)
                ref[at] = jnp.where(odd == 1, value[spare:], value[:spare])

    own = block(z, quarter)
    x_all = x_ref[...].astype(f32)
    rms1 = lax.rsqrt(jnp.sum(x_all * x_all, axis=0, keepdims=True) * (1.0 / width) + EPS)
    part[...] = tn(wq_ref[...], dq_ref[...])
    part[...] += tn(wk_ref[...], dk_ref[...])
    part[...] += tn(wv_ref[...], dv_ref[...])
    low_part[...] = part[...].astype(bf16)
    to_z = [
        remote(
            low_part.at[block((z + i) % 4, quarter)],
            zland.at[i - 1],
            zsend.at[i - 1],
            zrecv.at[i - 1],
            z_peers[i - 1],
        )
        for i in (1, 2, 3)
    ]
    few_to_z = [
        remote(mine, theirs.at[i], lsend.at[i], lrecv.at[i], peer) for i, peer in enumerate(z_peers)
    ]
    along = part[...] * x_ref[...].astype(f32)
    mine[...] = jnp.zeros(mine.shape, f32)
    mine[0:1, :rows] = jnp.sum(along * gain_ref[...], axis=0, keepdims=True)
    mine[:, rows:] = nt(jnp.ones((8, rows), bf16), (along * rms1).astype(bf16))
    for copy in few_to_z:
        copy.start()
    for i in (1, 0, 2):
        to_z[i].start()

    normed = normed_ref[...]
    for i, ref in enumerate((dq_ref, dk_ref, dv_ref)):
        grads[i * quarter : (i + 1) * quarter] = nn(ref[...], normed).astype(bf16)
    grads[3 * quarter : 4 * quarter] = nt(low_t[own], attended_ref[...]).astype(bf16)
    at = 4 * quarter
    grads[at : at + experts] = grad_router.astype(bf16)
    for copy in few_to_z:
        copy.wait_recv()
    few = mine[...] + theirs[0] + theirs[1] + theirs[2]
    grads[at + experts :] = jnp.zeros((tall - at - experts, width), bf16)
    line = lax.broadcasted_iota(jnp.int32, (16, width), 0)
    gains = jnp.where(line == 0, few[0:1, rows:], jnp.where(line == 1, grad_ffn, 0.0))
    grads[at + experts : at + experts + 16] = gains.astype(bf16)

    start, share, give_back, end = weight_sum(
        grads, given, half, land, sum_ref, csend, crecv, send, recv
    )
    start()
    share()

    total = part[own]
    for i in range(3):
        to_z[i].wait_recv()
        total = total + zland[i].astype(f32)
    x = x_ref[own].astype(f32)
    mean = few[0:1, :rows] * (1.0 / width)
    tokens_ref[...] = back_t[own] + rms1 * gain_ref[own] * total - x * (rms1 * rms1 * rms1 * mean)

    give_back()
    end()
    for copy in (*to_z, *few_to_z):
        copy.wait_send()


def back(*args):
    quarter, width = args[13].shape
    rows = args[1].shape[0]
    tall = 4 * quarter + 128
    vmem = pl.BlockSpec(memory_space=pltpu.VMEM)
    dma = pltpu.SemaphoreType.DMA
    return pl.pallas_call(
        back_kernel,
        in_specs=[vmem] * len(args),
        out_specs=[vmem, vmem],
        out_shape=[
            jax.ShapeDtypeStruct((quarter, rows), f32),
            jax.ShapeDtypeStruct((tall, width), bf16),
        ],
        scratch_shapes=[
            *[pltpu.VMEM((quarter, rows), bf16)] * 3,
            pltpu.VMEM((width, rows), f32),
            pltpu.VMEM((width, rows), bf16),
            pltpu.VMEM((width, rows), f32),
            pltpu.VMEM((width, rows), bf16),
            pltpu.VMEM((3, quarter, rows), bf16),
            pltpu.VMEM((8, rows + width), f32),
            pltpu.VMEM((3, 8, rows + width), f32),
            dma((3,)),
            dma((3,)),
            dma((3,)),
            dma((3,)),
            *weight_sum_scratch(tall, width),
        ],
        compiler_params=pltpu.CompilerParams(
            vmem_limit_bytes=VMEM_LIMIT, collective_id=3, has_side_effects=True
        ),
        cost_estimate=takes(90),
        name="back",
    )(*args)


def plain_front(
    tokens, attn_gain, query_t, key_t, value_t, attn_out, ffn_gain, documents, tables
):
    rows, width = tokens.shape
    quarter = query_t.shape[0]
    hs, hs_count = lax.axis_index("hs"), lax.axis_size("hs")
    odd = (hs % 2) == 1
    spare = -quarter % HEAD_DIM
    heads = (quarter + spare) // HEAD_DIM

    def outer(w):
        return jnp.where(odd, w[:spare], w[quarter - spare :])

    sent = jnp.concatenate([outer(query_t), outer(key_t), outer(value_t)], axis=0)
    got = lax.ppermute(sent, "hs", [(i, i ^ 1) for i in range(hs_count)])

    def widened(w, extra):
        return jnp.where(
            odd, jnp.concatenate([extra, w], axis=0), jnp.concatenate([w, extra], axis=0)
        )

    x = tokens.astype(f32)
    rms1 = lax.rsqrt(jnp.mean(x * x, axis=-1, keepdims=True) + EPS)
    normed1 = (x * rms1 * attn_gain).astype(bf16)
    shape3 = (heads, HEAD_DIM, rows)
    q, k, v = [
        ein("cd,td->ct", widened(w, got[i * spare : (i + 1) * spare]), normed1).reshape(shape3)
        for i, w in enumerate((query_t, key_t, value_t))
    ]
    q, k, v = rope(q, *tables).astype(bf16), rope(k, *tables).astype(bf16), v.astype(bf16)
    positions = jnp.arange(rows, dtype=jnp.int32)
    doc = documents[0]
    allowed = (positions[:, None] >= positions[None, :]) & (doc[:, None] == doc[None, :])
    scale = 1.0 / math.sqrt(HEAD_DIM)
    scores = jnp.where(allowed[None], ein("hdq,hdk->hqk", q, k) * scale, -1e30)
    raised = jnp.exp(scores - jnp.max(scores, axis=-1, keepdims=True))
    probs = raised / jnp.sum(raised, axis=-1, keepdims=True)
    attended = ein("hdk,hqk->hdq", v, probs.astype(bf16)).astype(bf16).reshape(-1, rows)
    attended = jnp.where(odd, attended[spare:], attended[:quarter])
    attended_t = lax.all_gather(attended, "hs", axis=0, tiled=True)
    out_t = lax.all_gather(attn_out.T, "hs", axis=0, tiled=True)
    residual = x + ein("ct,oc->to", attended_t, out_t)
    rms2 = lax.rsqrt(jnp.mean(residual * residual, axis=-1, keepdims=True) + EPS)
    normed2 = (residual * rms2 * ffn_gain).astype(bf16)
    return normed1, q, k, v, probs, attended_t, out_t, residual, normed2


def over_ep(a):
    return lax.psum(a.astype(bf16), EP).astype(f32)


def plain_back(
    sums,
    residual,
    normed2,
    grad_t,
    router_t,
    ffn_gain,
    out_t,
    q,
    k,
    v,
    probs,
    tables,
    query_t,
    key_t,
    value_t,
    normed1,
    attended_t,
    tokens,
    attn_gain,
):
    rows, width = tokens.shape
    quarter = query_t.shape[0]
    hs = lax.axis_index("hs")
    odd = (hs % 2) == 1
    spare = -quarter % HEAD_DIM
    held = quarter + spare
    col0 = hs * quarter

    def own(v):
        v = v.astype(bf16).reshape(held, rows)
        return jnp.where(odd, v[spare:], v[:quarter])

    gates = jax.nn.softmax(nt(normed2, router_t), axis=-1)
    grad_probs = sums[rows:, :rows].T.astype(f32)
    grad_logits = (
        gates * (grad_probs - jnp.sum(grad_probs * gates, axis=-1, keepdims=True))
    ).astype(bf16)
    grad_router = tn(grad_logits, normed2)
    grad_normed2 = sums[:rows].astype(f32) + dot(grad_logits, router_t)
    rms2 = lax.rsqrt(jnp.mean(residual * residual, axis=-1, keepdims=True) + EPS)
    grad_ffn_gain = jnp.sum(grad_normed2 * residual * rms2, axis=0)
    u = grad_normed2 * ffn_gain
    grad_residual = (
        grad_t.T.astype(f32)
        + rms2 * u
        - residual * rms2**3 * jnp.mean(u * residual, axis=-1, keepdims=True)
    )
    back_t = grad_residual.T
    low_t = back_t.astype(bf16)
    out_held = lax.dynamic_slice_in_dim(out_t, jnp.where(odd, col0 - spare, col0), held, 1)
    grad_attended = tn(out_held, low_t).astype(bf16).reshape(-1, HEAD_DIM, rows)
    grad_p = ein("hdq,hdk->hqk", grad_attended, v)
    grad_v = own(ein("hdq,hqk->hdk", grad_attended, probs.astype(bf16)))
    grad_s = (probs * (grad_p - jnp.sum(probs * grad_p, axis=-1, keepdims=True))).astype(bf16)
    scale = 1.0 / math.sqrt(HEAD_DIM)
    grad_q = own(rope_back(ein("hdk,hqk->hdq", k, grad_s) * scale, *tables))
    grad_k = own(rope_back(ein("hdq,hqk->hdk", q, grad_s) * scale, *tables))
    own_rows = lambda a: lax.dynamic_slice_in_dim(a, col0, quarter, 0)
    heads_sums = [
        over_ep(dot(grad_q, normed1)),
        over_ep(dot(grad_k, normed1)),
        over_ep(dot(grad_v, normed1)),
        over_ep(nt(own_rows(low_t), attended_t)),
    ]
    part = tn(query_t, grad_q) + tn(key_t, grad_k) + tn(value_t, grad_v)
    grad_n1 = lax.psum_scatter(part.astype(bf16), "hs", scatter_dimension=0, tiled=True)
    grad_n1 = grad_n1.astype(f32)
    x = tokens.T.astype(f32)
    x_own = own_rows(x)
    rms_t = lax.rsqrt(jnp.mean(x * x, axis=0, keepdims=True) + EPS)
    w1 = grad_n1 * own_rows(attn_gain)[:, None]
    mean1 = lax.psum(jnp.sum(w1 * x_own, axis=0, keepdims=True), "hs") / width
    grad_tokens = own_rows(back_t) + rms_t * w1 - x_own * rms_t**3 * mean1
    gain_own = jnp.sum(grad_n1 * x_own * rms_t, axis=1)
    gain_part = lax.dynamic_update_slice_in_dim(jnp.zeros((width,), f32), gain_own, col0, 0)
    grad_attn_gain = lax.psum(gain_part, (*EP, "hs"))
    return (
        grad_tokens,
        heads_sums,
        over_ep(grad_router),
        grad_attn_gain,
        lax.psum(grad_ffn_gain, EP),
    )


def shards(
    tokens,
    attn_gain,
    attn_query,
    attn_key,
    attn_value,
    attn_out,
    ffn_gain,
    router,
    shared_gate,
    shared_up,
    shared_down,
    expert_gate,
    expert_up,
    expert_down,
    routes,
    documents,
    out_grad,
):
    rows, width = tokens.shape
    quarter = out_grad.shape[1]
    hs = lax.axis_index("hs")
    ep_count = lax.axis_size("xy") * lax.axis_size("core")
    ep = lax.axis_index("xy") * lax.axis_size("core") + lax.axis_index("core")
    local = expert_gate.shape[0]
    experts = router.shape[1]
    small = ep_count == 8 and lax.axis_size("hs") == 4

    query_t, key_t, value_t, router_t = attn_query.T, attn_key.T, attn_value.T, router.T
    grad_all_t = lax.all_gather(out_grad.T, (*EP, "hs"), axis=0, tiled=True)
    grad_all_t = grad_all_t.reshape(ep_count, width, rows)
    grad_t = lax.dynamic_index_in_dim(grad_all_t, ep, 0, keepdims=False)
    positions = jnp.arange(rows, dtype=jnp.int32)
    below = (positions[:, None] > positions[None, :]).astype(bf16)
    chosen = jnp.any(
        routes[:, :, None] == jnp.arange(experts, dtype=jnp.int32)[None, None, :], axis=1
    )
    own_slots = jnp.where(chosen, dot(below, chosen.astype(bf16)), -1.0).T.astype(bf16)
    tables = rope_tables(rows)

    if small:
        ahead = front(
            tokens, attn_gain, query_t, key_t, value_t, attn_out.T, ffn_gain, documents, tables
        )
    else:
        ahead = plain_front(
            tokens, attn_gain, query_t, key_t, value_t, attn_out, ffn_gain, documents, tables
        )
    normed1, q, k, v, probs, attended_t, out_t, residual, normed2 = ahead
    out_t = out_t.reshape(width, width)

    sh_gate = dot(normed2, shared_gate)
    sh_up = dot(normed2, shared_up)
    sh_sig = jax.nn.sigmoid(sh_gate)
    sh_act = sh_gate * sh_sig
    sh_hidden = (sh_act * sh_up).astype(bf16)
    shared_part = dot(sh_hidden, shared_down)
    grad_sh = ein("dt,fd->tf", grad_t, shared_down)
    grad_sh_gate = (grad_sh * sh_up * sh_sig * (1 + sh_gate * (1 - sh_sig))).astype(bf16)
    grad_sh_up = (grad_sh * sh_act).astype(bf16)
    shared_grads = [
        ein("tf,td->fd", grad_sh_gate, normed2).astype(bf16),
        ein("tf,td->fd", grad_sh_up, normed2).astype(bf16),
        ein("tf,dt->fd", sh_hidden, grad_t).astype(bf16),
    ]
    shared_back = ein("tf,df->td", grad_sh_gate, shared_gate) + ein(
        "tf,df->td", grad_sh_up, shared_up
    )

    first = ep * local
    rolled = jnp.roll(router_t, -first, axis=0)
    if small:
        ex_in, slot_weight, slot = gather_spread(normed2, own_slots, rolled, local, ep_count)
    else:
        slot = lax.dynamic_slice_in_dim(
            lax.all_gather(own_slots, EP, axis=0), first, local, 1
        ).astype(jnp.int32)
        normed_all = lax.all_gather(normed2, EP, axis=0, tiled=True)
        ex_in, slot_weight = spread(normed_all, slot, rolled)
    gate_t, up_t = expert_gate.swapaxes(1, 2), expert_up.swapaxes(1, 2)
    ex_grad = spread(grad_all_t, slot)
    ex_out, ex_gate, ex_up = experts_forward(ex_in, slot_weight, gate_t, up_t, expert_down)
    out_part = collect(ex_out, slot).reshape(ep_count * rows, width)
    ex_back, grad_gate_t, grad_up_t, grad_expert_down, grad_slot_weight = experts_backward(
        ex_in, ex_grad, ex_gate, ex_up, slot_weight, gate_t, up_t, expert_down
    )

    if small:
        back_sums, shared_sums, shared_part = collect_sum(
            ex_back, slot, grad_slot_weight, shared_back, shared_part.astype(bf16), *shared_grads
        )
        shared_sums = shared_sums.astype(f32)
        hidden_units = shared_down.shape[0]
        shared_sums = [shared_sums[i * hidden_units : (i + 1) * hidden_units] for i in range(3)]
        grad_tokens, sums = back(
            back_sums,
            residual,
            normed2,
            grad_t,
            router_t,
            ffn_gain[None, :],
            out_t,
            q,
            k,
            v,
            probs,
            *tables,
            query_t,
            key_t,
            value_t,
            normed1,
            attended_t,
            tokens.T,
            attn_gain[:, None],
        )
        sums = sums.astype(f32)
        heads_sums = [sums[i * quarter : (i + 1) * quarter] for i in range(4)]
        sums = sums[4 * quarter :]
        grad_router, grad_attn_gain, grad_ffn_gain = sums[:experts], sums[experts], sums[experts + 1]
    else:
        back_part = collect(ex_back, slot, grad_slot_weight, first, experts).reshape(-1, width)
        back_rows = lax.psum_scatter(back_part, EP, scatter_dimension=0, tiled=True).astype(f32)
        back_rows = jnp.concatenate([back_rows[:rows] + shared_back, back_rows[rows:]], axis=0)
        back_sums = lax.psum(back_rows.astype(bf16), "hs")
        shared_sums = [over_ep(a) for a in shared_grads]
        grad_tokens, heads_sums, grad_router, grad_attn_gain, grad_ffn_gain = plain_back(
            back_sums,
            residual,
            normed2,
            grad_t,
            router_t,
            ffn_gain,
            out_t,
            q,
            k,
            v,
            probs,
            tables,
            query_t,
            key_t,
            value_t,
            normed1,
            attended_t,
            tokens,
            attn_gain,
        )

    rows_major = Layout(major_to_minor=(0, 1))
    out_part = with_layout_constraint(out_part, rows_major)
    out_rows = lax.psum_scatter(out_part, EP, scatter_dimension=0, tiled=True)
    out_rows = with_layout_constraint(out_rows, rows_major)
    out_rows = (out_rows.astype(f32) + shared_part.astype(f32)).astype(bf16)
    out_quarter = lax.psum_scatter(out_rows, "hs", scatter_dimension=1, tiled=True)
    residual_quarter = lax.dynamic_slice_in_dim(residual, hs * quarter, quarter, 1)
    output = (residual_quarter + out_quarter.astype(f32)).astype(bf16)

    return (
        output,
        grad_tokens.T,
        grad_attn_gain,
        *[a.T for a in heads_sums],
        grad_ffn_gain,
        grad_router.T,
        shared_sums[0].T,
        shared_sums[1].T,
        shared_sums[2],
        grad_gate_t.swapaxes(1, 2),
        grad_up_t.swapaxes(1, 2),
        grad_expert_down,
    )


def solution(mesh):
    ep_count, hs_count = mesh.devices.shape
    cut = Mesh(mesh.devices.reshape(ep_count // 2, 2, hs_count), ("xy", "core", "hs"))
    return jax.shard_map(
        shards,
        mesh=cut,
        in_specs=(
            P(EP, None),
            P(),
            P(None, "hs"),
            P(None, "hs"),
            P(None, "hs"),
            P(None, "hs"),
            P(),
            P(),
            P(None, "hs"),
            P(None, "hs"),
            P("hs", None),
            P(EP, None, "hs"),
            P(EP, None, "hs"),
            P(EP, "hs", None),
            P(EP, None),
            P(EP, None),
            P(EP, "hs"),
        ),
        out_specs=(
            P(EP, "hs"),
            P(EP, "hs"),
            P(),
            P(None, "hs"),
            P(None, "hs"),
            P(None, "hs"),
            P(None, "hs"),
            P(),
            P(),
            P(None, "hs"),
            P(None, "hs"),
            P("hs", None),
            P(EP, None, "hs"),
            P(EP, None, "hs"),
            P(EP, "hs", None),
        ),
        check_vma=False,
    )
```

```python
import functools
import math

import jax
import jax.numpy as jnp
import numpy as np
from jax import lax
from jax.experimental import pallas as pl
from jax.experimental.layout import Layout, with_layout_constraint
from jax.experimental.pallas import tpu as pltpu
from jax.sharding import Mesh
from jax.sharding import PartitionSpec as P

HEADS = 10
HEAD_DIM = 128
CAP = 112
EPS = 1e-06
EP = ("xy", "core")
bf16 = jnp.bfloat16
f32 = jnp.float32


def dot(a, b):
    return jnp.dot(a, b, preferred_element_type=f32)


def ein(spec, a, b):
    return jnp.einsum(spec, a, b, preferred_element_type=f32)


def rope_tables(rows):
    half = HEAD_DIM // 2
    frequency = 10000.0 ** (-np.arange(half) * 2.0 / HEAD_DIM)
    angles = frequency[:, None] * np.arange(rows)[None, :]
    return jnp.asarray(np.cos(angles), f32), jnp.asarray(np.sin(angles), f32)


def rope(v, cosine, sine):
    half = HEAD_DIM // 2
    a, b = v[:, :half], v[:, half:]
    return jnp.concatenate([a * cosine - b * sine, b * cosine + a * sine], axis=1)


def rope_back(v, cosine, sine):
    half = HEAD_DIM // 2
    a, b = v[:, :half], v[:, half:]
    return jnp.concatenate([a * cosine + b * sine, b * cosine - a * sine], axis=1)


VMEM_LIMIT = 60 * 1024 * 1024
PAD = 256


def nn(a, b):
    return lax.dot_general(a, b, (((1,), (0,)), ((), ())), preferred_element_type=f32)


def nt(a, b):
    return lax.dot_general(a, b, (((1,), (1,)), ((), ())), preferred_element_type=f32)


def tn(a, b):
    return lax.dot_general(a, b, (((0,), (0,)), ((), ())), preferred_element_type=f32)


def takes(microseconds):
    return pl.CostEstimate(flops=0, transcendentals=0, bytes_accessed=microseconds * 3_000_000)


def slot_masks(slot_ref, at):
    local, rows = slot_ref.shape[-2:]
    number = lax.broadcasted_iota(jnp.int32, (CAP, rows), 0)
    return [slot_ref[at, e : e + 1, :] == number for e in range(local)]


def spread_kernel(weighted, *refs):
    if weighted:
        rows_ref, slot_ref, router_ref, x_ref, sw_ref, pick = refs
    else:
        rows_ref, slot_ref, x_ref, pick = refs
    local = slot_ref.shape[1]
    rows = rows_ref[...] if weighted else rows_ref[0]
    masks = slot_masks(slot_ref, 0)
    if weighted:
        logits = nt(router_ref[...], rows)
        raised = jnp.exp(logits - jnp.max(logits, axis=0, keepdims=True))
        gates = raised / jnp.sum(raised, axis=0, keepdims=True)
    for e in range(local):
        pick[e * CAP : (e + 1) * CAP, :] = masks[e].astype(f32).astype(bf16)
        if weighted:
            sw_ref[e] = jnp.sum(
                jnp.where(masks[e], gates[e : e + 1, :], 0.0), axis=1, keepdims=True
            )
    product = nn if weighted else nt
    x_ref[...] = product(pick[...], rows).astype(bf16).reshape(x_ref.shape)


def spread(all_rows, slot, router_t=None):
    s, local, rows = slot.shape
    weighted = router_t is not None
    if weighted:
        width = all_rows.shape[1]
        block = pl.BlockSpec((rows, width), lambda i: (i, 0))
    else:
        width = all_rows.shape[1]
        block = pl.BlockSpec((1, width, rows), lambda i: (i, 0, 0))
    in_specs = [
        block,
        pl.BlockSpec((1, local, rows), lambda i: (i, 0, 0)),
    ]
    out_specs = [pl.BlockSpec((1, local, CAP, width), lambda i: (i, 0, 0, 0))]
    out_shape = [jax.ShapeDtypeStruct((s, local, CAP, width), bf16)]
    args = [all_rows, slot]
    if weighted:
        in_specs.append(pl.BlockSpec(router_t.shape, lambda i: (0, 0)))
        out_specs.append(pl.BlockSpec((local, CAP, 1), lambda i: (0, i, 0)))
        out_shape.append(jax.ShapeDtypeStruct((local, s * CAP, 1), f32))
        args.append(router_t)
    out = pl.pallas_call(
        functools.partial(spread_kernel, weighted),
        grid=(s,),
        in_specs=in_specs,
        out_specs=out_specs,
        out_shape=out_shape,
        scratch_shapes=[pltpu.VMEM((local * CAP, rows), bf16)],
        compiler_params=pltpu.CompilerParams(vmem_limit_bytes=VMEM_LIMIT),
        cost_estimate=takes(17),
        name="spread",
    )(*args)
    return out if weighted else out[0]


def padded(ref, out):
    ff = ref.shape[1]
    out[:ff, :] = ref[0]
    out[ff:, :] = jnp.zeros((out.shape[0] - ff, out.shape[1]), out.dtype)


def experts_forward_kernel(
    x_ref, sw_ref, wg_ref, wu_ref, wd_ref, y_ref, gate_ref, up_ref, wg, wu, wd
):
    padded(wg_ref, wg)
    padded(wu_ref, wu)
    padded(wd_ref, wd)
    rows, width = gate_ref.shape[1], x_ref.shape[3]
    x = x_ref[...].reshape(rows, width)
    gate = nt(x, wg[...])
    up = nt(x, wu[...])
    gate_ref[0] = gate
    up_ref[0] = up
    act = gate / (1.0 + jnp.exp(-gate))
    hidden = (act * up).astype(bf16).astype(f32)
    hidden_w = (hidden * sw_ref[0]).astype(bf16)
    y_ref[...] = nn(hidden_w, wd[...]).astype(bf16).reshape(y_ref.shape)


def experts_backward_kernel(
    groups,
    x_ref,
    gx_ref,
    gate_ref,
    up_ref,
    sw_ref,
    wg_ref,
    wu_ref,
    wd_ref,
    dx_ref,
    dg_ref,
    du_ref,
    dd_ref,
    gsw_ref,
    wg,
    wu,
    wd,
):
    padded(wg_ref, wg)
    padded(wu_ref, wu)
    padded(wd_ref, wd)
    rows, width = gate_ref.shape[1], x_ref.shape[3]
    ff = wg_ref.shape[1]
    x = x_ref[...].reshape(rows, width)
    gx = gx_ref[...].reshape(rows, width)
    gate, up, sw = gate_ref[0], up_ref[0], sw_ref[0]
    sig = 1.0 / (1.0 + jnp.exp(-gate))
    act = gate * sig
    hidden = (act * up).astype(bf16).astype(f32)
    gh = nt(gx, wd[...])
    gsw_ref[0] = jnp.sum(gh * hidden, axis=-1, keepdims=True)
    gh = gh * sw
    gg = (gh * up * sig * (1.0 + gate * (1.0 - sig))).astype(bf16)
    gu = (gh * act).astype(bf16)
    sums = (
        (dd_ref, tn((hidden * sw).astype(bf16), gx)[:ff]),
        (dg_ref, tn(gg, x)[:ff]),
        (du_ref, tn(gu, x)[:ff]),
    )
    if groups == 1:
        for ref, value in sums:
            ref[0] = value
    else:

        @pl.when(pl.program_id(1) == 0)
        def _():
            for ref, value in sums:
                ref[0] = value

        @pl.when(pl.program_id(1) > 0)
        def _():
            for ref, value in sums:
                ref[0] += value

    dx_ref[...] = (nn(gg, wg[...]) + nn(gu, wu[...])).astype(bf16).reshape(dx_ref.shape)


def expert_specs(s, width):
    group = min(s, 8)
    slots = pl.BlockSpec((group, 1, CAP, width), lambda i, j: (j, i, 0, 0))
    lines = lambda columns: pl.BlockSpec((1, group * CAP, columns), lambda i, j: (i, j, 0))
    per = lambda *shape: pl.BlockSpec((1, *shape), lambda i, j: (i, 0, 0))
    return s // group, slots, lines, per


def experts_forward(x, sw, wg, wu, wd):
    s, local, cap, width = x.shape
    ff = wg.shape[1]
    rows = s * cap
    groups, slots, lines, per = expert_specs(s, width)
    middle = jax.ShapeDtypeStruct((local, rows, PAD), f32)
    return pl.pallas_call(
        experts_forward_kernel,
        grid=(local, groups),
        in_specs=[slots, lines(1)] + [per(ff, width)] * 3,
        out_specs=[slots, lines(PAD), lines(PAD)],
        out_shape=[jax.ShapeDtypeStruct(x.shape, bf16), middle, middle],
        scratch_shapes=[pltpu.VMEM((PAD, width), bf16)] * 3,
        compiler_params=pltpu.CompilerParams(vmem_limit_bytes=VMEM_LIMIT),
        cost_estimate=takes(31),
        name="experts_forward",
    )(x, sw, wg, wu, wd)


def experts_backward(x, gx, gate, up, sw, wg, wu, wd):
    s, local, cap, width = x.shape
    ff = wg.shape[1]
    rows = s * cap
    groups, slots, lines, per = expert_specs(s, width)
    return pl.pallas_call(
        functools.partial(experts_backward_kernel, groups),
        grid=(local, groups),
        in_specs=[slots, slots, lines(PAD), lines(PAD), lines(1)]
        + [per(ff, width)] * 3,
        out_specs=[slots] + [per(ff, width)] * 3 + [lines(1)],
        out_shape=[jax.ShapeDtypeStruct(x.shape, bf16)]
        + [jax.ShapeDtypeStruct((local, ff, width), f32)] * 3
        + [jax.ShapeDtypeStruct((local, rows, 1), f32)],
        scratch_shapes=[pltpu.VMEM((PAD, width), bf16)] * 3,
        compiler_params=pltpu.CompilerParams(vmem_limit_bytes=VMEM_LIMIT),
        cost_estimate=takes(47),
        name="experts_backward",
    )(x, gx, gate, up, sw, wg, wu, wd)


def collect_kernel(y_ref, slot_ref, out_ref, pick):
    local = slot_ref.shape[1]
    masks = slot_masks(slot_ref, 0)
    for e in range(local):
        pick[e * CAP : (e + 1) * CAP, :] = masks[e].astype(f32).astype(bf16)
    out_ref[0] = tn(pick[...], y_ref[...].reshape(pick.shape[0], -1)).astype(bf16)


def collect_back_kernel(experts, y_ref, slot_ref, gsw_ref, first_ref, out_ref, pick):
    local, rows = slot_ref.shape[1:]
    first = first_ref[0]
    masks = slot_masks(slot_ref, 0)
    number = lax.broadcasted_iota(jnp.int32, (experts, rows), 0)
    probs = jnp.zeros((experts, rows), f32)
    for e in range(local):
        pick[e * CAP : (e + 1) * CAP, :] = masks[e].astype(f32).astype(bf16)
        line = jnp.sum(jnp.where(masks[e], gsw_ref[e], 0.0), axis=0, keepdims=True)
        probs = jnp.where(number == first + e, line, probs)
    out_ref[0, :rows] = tn(pick[...], y_ref[...].reshape(pick.shape[0], -1)).astype(bf16)
    out_ref[0, rows:] = jnp.zeros((experts, out_ref.shape[2]), bf16)
    out_ref[0, rows:, :rows] = probs.astype(bf16)


def collect(y, slot, gsw=None, first=None, experts=0):
    s, local, cap, width = y.shape
    rows = slot.shape[2]
    in_specs = [
        pl.BlockSpec((1, local, cap, width), lambda i: (i, 0, 0, 0)),
        pl.BlockSpec((1, local, rows), lambda i: (i, 0, 0)),
    ]
    args = [y, slot]
    kernel = collect_kernel
    tall = rows
    if gsw is not None:
        in_specs += [
            pl.BlockSpec((local, cap, 1), lambda i: (0, i, 0)),
            pl.BlockSpec(memory_space=pltpu.SMEM),
        ]
        args += [gsw, first.reshape(1)]
        kernel = functools.partial(collect_back_kernel, experts)
        tall = rows + experts
    return pl.pallas_call(
        kernel,
        grid=(s,),
        in_specs=in_specs,
        out_specs=pl.BlockSpec((1, tall, width), lambda i: (i, 0, 0)),
        out_shape=jax.ShapeDtypeStruct((s, tall, width), bf16),
        scratch_shapes=[pltpu.VMEM((local * cap, rows), bf16)],
        compiler_params=pltpu.CompilerParams(vmem_limit_bytes=VMEM_LIMIT),
        cost_estimate=takes(17),
        name="collect",
    )(*args)


MESH = pl.DeviceIdType.MESH
EXTRA = 64


def places():
    chip, core, z = lax.axis_index("xy"), lax.axis_index("core"), lax.axis_index("hs")
    x, y = chip % 2, chip // 2
    return chip, core, z, y * 2 + (1 - x), (1 - y) * 2 + x, (1 - y) * 2 + (1 - x)


def greet(peers):
    barrier = pltpu.get_barrier_semaphore()
    for peer in peers:
        pl.semaphore_signal(barrier, inc=1, device_id=peer, device_id_type=MESH)
    pl.semaphore_wait(barrier, len(peers))


def remote(src, dst, send, recv, peer):
    return pltpu.make_async_remote_copy(
        src_ref=src, dst_ref=dst, send_sem=send, recv_sem=recv, device_id=peer, device_id_type=MESH
    )


def block(q, size):
    return pl.ds(pl.multiple_of(q * size, 16), size)


def weight_sum(grads, given, half, land, out_ref, csend, crecv, send, recv):
    chip, core, z, cx, cy, cd = places()
    other = 1 - core
    c_peer = (chip, other, z)
    chips = (cx, cy, cd)
    count = grads.shape[0] // 2
    piece = count // 4

    to_core = remote(grads.at[block(other, count)], given, csend.at[0], crecv.at[0], c_peer)
    scatter = [
        remote(half.at[block(c, piece)], land.at[i], send.at[i], recv.at[i], (c, core, z))
        for i, c in enumerate(chips)
    ]

    def share():
        to_core.wait_recv()
        half[...] = (grads[block(core, count)].astype(f32) + given[...].astype(f32)).astype(bf16)
        for i in (2, 0, 1):
            scatter[i].start()

    def place(c, k):
        return pl.ds(pl.multiple_of(k * count + c * piece, 16), piece)

    def give(number, c, k, sems, peer):
        return remote(out_ref.at[place(c, k)], out_ref.at[place(c, k)], *sems(number), peer)

    def chip_sems(i):
        return send.at[3 + i], recv.at[3 + i]

    def core_sems(i):
        return csend.at[1 + i], crecv.at[1 + i]

    gather = [give(i, chip, core, chip_sems, (c, core, z)) for i, c in enumerate(chips)]
    over = [give(i, c, core, core_sems, c_peer) for i, c in enumerate((*chips, chip))]

    def give_back():
        done = half[block(chip, piece)].astype(f32)
        for i in range(3):
            scatter[i].wait_recv()
            done = done + land[i].astype(f32)
        out_ref[place(chip, core)] = done.astype(bf16)
        for i in (2, 0, 1):
            gather[i].start()
        over[3].start()

    def end():
        for i, c in enumerate(chips):
            give(i, c, core, chip_sems, (c, core, z)).wait_recv()
            over[i].start()
        for i, c in enumerate((*chips, chip)):
            give(i, c, other, core_sems, c_peer).wait_recv()
        for copy in (to_core, *scatter, *gather, *over):
            copy.wait_send()

    return to_core.start, share, give_back, end


def weight_sum_scratch(tall, width):
    dma = pltpu.SemaphoreType.DMA
    return [
        pltpu.VMEM((tall, width), bf16),
        pltpu.VMEM((tall // 2, width), bf16),
        pltpu.VMEM((tall // 2, width), bf16),
        pltpu.VMEM((3, tall // 8, width), bf16),
        dma((5,)),
        dma((5,)),
        dma((6,)),
        dma((6,)),
    ]


def gather_spread_kernel(
    own_ref, slots_ref, router_ref, x_ref, sw_ref, slot_ref, held, pick, xbuf, send, recv, copied
):
    chip, core, z, cx, cy, cd = places()
    other = 1 - core
    x_peer, y_peer, c_peer = (cx, core, z), (cy, core, z), (chip, other, z)
    tall = held.shape[1]
    half = tall // 2
    local, rows = slot_ref.shape[1:]
    me = chip * 2 + core
    top, low = pl.ds(0, half), pl.ds(half, half)

    def at(c, k):
        return c * 2 + k

    def move(number, src_slot, part, peer):
        return remote(
            held.at[src_slot, part], held.at[src_slot, part], send.at[number], recv.at[number], peer
        )

    whole = pl.ds(0, tall)
    greet([x_peer, y_peer, c_peer])
    held[me, :rows] = own_ref[...]
    held[me, rows:] = jnp.zeros((EXTRA, own_ref.shape[1]), bf16)
    held[me, rows:, :rows] = slots_ref[...]
    x_top, x_low = move(0, me, top, x_peer), move(1, me, low, x_peer)
    y_low, y_top = move(2, me, low, y_peer), move(3, me, top, y_peer)
    to_core = move(4, me, whole, c_peer)
    relay_top, relay_low = move(5, at(cx, core), top, y_peer), move(6, at(cy, core), low, x_peer)
    pass_x, pass_y = move(7, at(cx, core), whole, c_peer), move(8, at(cy, core), whole, c_peer)
    pass_d = move(9, at(cd, core), whole, c_peer)
    for copy in (x_top, y_low, x_low, y_top, to_core):
        copy.start()

    def arrived(number, slot, part):
        move(number, slot, part, c_peer).wait_recv()

    number = lax.broadcasted_iota(jnp.int32, (CAP, rows), 0)
    first = me * local
    line = lax.broadcasted_iota(jnp.int32, (local, EXTRA), 0)
    column = lax.broadcasted_iota(jnp.int32, (local, EXTRA), 1)
    chosen = (column == line + first).astype(f32).astype(bf16)

    def out_copy(t, src):
        return pltpu.make_async_copy(xbuf.at[t % 2], x_ref.at[src], copied.at[t % 2])

    def step(t, carry):
        @pl.when(t == 1)
        def _():
            arrived(4, at(chip, other), whole)

        @pl.when(t == 2)
        def _():
            arrived(0, at(cx, core), top)
            relay_top.start()
            arrived(2, at(cy, core), low)
            relay_low.start()
            arrived(1, at(cx, core), low)
            pass_x.start()

        @pl.when(t == 3)
        def _():
            arrived(3, at(cy, core), top)
            pass_y.start()
            arrived(7, at(cx, other), whole)

        @pl.when(t == 5)
        def _():
            arrived(8, at(cy, other), whole)

        @pl.when(t == 6)
        def _():
            arrived(5, at(cd, core), top)
            arrived(6, at(cd, core), low)
            pass_d.start()

        @pl.when(t == 7)
        def _():
            arrived(9, at(cd, other), whole)

        x, y = (chip % 2 + (t // 2) % 2) % 2, (chip // 2 + t // 4) % 2
        src = (y * 2 + x) * 2 + (core + t % 2) % 2
        slots = nn(chosen, held[src, rows:, :rows]).astype(jnp.int32)
        slot_ref[src] = slots
        logits = nt(router_ref[...], held[src, :rows])
        raised = jnp.exp(logits - jnp.max(logits, axis=0, keepdims=True))
        gates = raised / jnp.sum(raised, axis=0, keepdims=True)
        for e in range(local):
            mask = slots[e : e + 1, :] == number
            pick[e * CAP : (e + 1) * CAP, :] = mask.astype(f32).astype(bf16)
            sw_ref[e, pl.ds(pl.multiple_of(src * CAP, 8), CAP), :] = jnp.sum(
                jnp.where(mask, gates[e : e + 1, :], 0.0), axis=1, keepdims=True
            )

        @pl.when(t >= 2)
        def _():
            out_copy(t, src).wait()

        xbuf[t % 2] = nn(pick[...], held[src, :rows]).astype(bf16).reshape(xbuf.shape[1:])
        out_copy(t, src).start()
        return carry

    lax.fori_loop(0, 8, step, 0)
    out_copy(0, me).wait()
    out_copy(1, me).wait()
    for copy in (x_top, x_low, y_low, y_top, to_core, relay_top, relay_low, pass_x, pass_y, pass_d):
        copy.wait_send()


def gather_spread(own, slots, router_t, local, ep_count):
    rows, width = own.shape
    tall = rows + EXTRA
    vmem = pl.BlockSpec(memory_space=pltpu.VMEM)
    return pl.pallas_call(
        gather_spread_kernel,
        in_specs=[vmem, vmem, vmem],
        out_specs=[pl.BlockSpec(memory_space=pl.ANY), vmem, vmem],
        out_shape=[
            jax.ShapeDtypeStruct((ep_count, local, CAP, width), bf16),
            jax.ShapeDtypeStruct((local, ep_count * CAP, 1), f32),
            jax.ShapeDtypeStruct((ep_count, local, rows), jnp.int32),
        ],
        scratch_shapes=[
            pltpu.VMEM((ep_count, tall, width), bf16),
            pltpu.VMEM((local * CAP, rows), bf16),
            pltpu.VMEM((2, local, CAP, width), bf16),
            pltpu.SemaphoreType.DMA((10,)),
            pltpu.SemaphoreType.DMA((10,)),
            pltpu.SemaphoreType.DMA((2,)),
        ],
        compiler_params=pltpu.CompilerParams(
            vmem_limit_bytes=VMEM_LIMIT, collective_id=0, has_side_effects=True
        ),
        cost_estimate=takes(62),
        name="gather_spread",
    )(own, slots, router_t)


def front_kernel(
    x_ref,
    gain_ref,
    wq_ref,
    wk_ref,
    wv_ref,
    wo_ref,
    ffn_gain_ref,
    doc_ref,
    doc_column_ref,
    cos_ref,
    sin_ref,
    normed1_ref,
    q_ref,
    k_ref,
    v_ref,
    probs_ref,
    attended_ref,
    out_ref,
    residual_ref,
    normed2_ref,
    shared,
    beside,
    esend,
    erecv,
    asend,
    arecv,
    zsend,
    zrecv,
    send,
    recv,
    csend,
    crecv,
):
    chip, core, z, cx, cy, cd = places()
    other = 1 - core
    odd = z % 2
    c_peer = (chip, other, z)
    chips = (cx, cy, cd)
    z_peers = [(chip, core, (z + i) % 4) for i in (1, 2, 3)]
    pair = (chip, core, z + 1 - 2 * odd)
    rows, width = x_ref.shape
    quarter = wq_ref.shape[0]
    whole = HEAD_DIM * (quarter // HEAD_DIM)
    spare = quarter - whole
    greet([c_peer, *[(c, core, z) for c in chips], *z_peers])

    full_rows = pl.ds(pl.multiple_of(odd * spare, 16), whole)
    half_rows = pl.ds(pl.multiple_of((1 - odd) * whole, 16), spare)
    for i, ref in enumerate((wq_ref, wk_ref, wv_ref)):
        shared[i * spare : (i + 1) * spare] = ref[half_rows]
    trade = remote(shared, beside, esend, erecv, pair)
    trade.start()

    share, lanes = quarter // 4, width // 2
    my_lanes = pl.ds(pl.multiple_of(core * lanes, 128), lanes)

    def piece(c):
        return pl.ds(pl.multiple_of(c * share, 16), share)

    out_z = [
        remote(
            wo_ref.at[piece(chip), my_lanes],
            out_ref.at[z, piece(chip), my_lanes],
            zsend.at[i],
            zrecv.at[i],
            peer,
        )
        for i, peer in enumerate(z_peers)
    ]
    for i in (1, 0, 2):
        out_z[i].start()
    behind = [(z + 3 - i) % 4 for i in range(3)]

    def out_chip(i, j, c):
        at = out_ref.at[behind[i], piece(c), my_lanes]
        return remote(at, at, send.at[3 * i + j], recv.at[3 * i + j], (chips[j], core, z))

    def out_core(i, k):
        half = pl.ds(pl.multiple_of(k * lanes, 128), lanes)
        at = out_ref.at[behind[i], :, half]
        return remote(at, at, csend.at[i], crecv.at[i], c_peer)

    x = x_ref[...].astype(f32)
    rms1 = lax.rsqrt(jnp.sum(x * x, axis=-1, keepdims=True) * (1.0 / width) + EPS)
    normed1_ref[...] = (x * rms1 * gain_ref[...]).astype(bf16)
    out_ref[z] = wo_ref[...]

    cosine, sine = cos_ref[...], sin_ref[...]
    half_dim = HEAD_DIM // 2
    scale = 1.0 / math.sqrt(HEAD_DIM)
    row = lax.broadcasted_iota(jnp.int32, (rows, rows), 0)
    column = lax.broadcasted_iota(jnp.int32, (rows, rows), 1)
    allowed = (row >= column) & (doc_column_ref[...] == doc_ref[...])

    def turn(pre):
        a, b = pre[:half_dim], pre[half_dim:]
        return (
            jnp.concatenate([a * cosine - b * sine, b * cosine + a * sine], axis=0).astype(bf16)
        )

    def attend(h):
        scores = jnp.where(allowed, tn(q_ref[h], k_ref[h]) * scale, -1e30)
        raised = jnp.exp(scores - jnp.max(scores, axis=-1, keepdims=True))
        probs = raised * (1.0 / jnp.sum(raised, axis=-1, keepdims=True))
        probs_ref[h] = probs
        return nt(v_ref[h], probs.astype(bf16)).astype(bf16)

    def project(at):
        return [nt(ref[at], normed1_ref[...]) for ref in (wq_ref, wk_ref, wv_ref)]

    q, k, v = project(full_rows)
    heads = whole // HEAD_DIM
    for h in range(heads):
        at = slice(h * HEAD_DIM, (h + 1) * HEAD_DIM)
        q_ref[h], k_ref[h], v_ref[h] = turn(q[at]), turn(k[at]), v[at].astype(bf16)

    def attended_copy(number, start, size):
        at = attended_ref.at[pl.ds(pl.multiple_of(start, 16), size)]
        return lambda i: remote(
            at, at, asend.at[number, i], arecv.at[number, i], z_peers[i]
        )

    mine = z * quarter
    copies = []
    for h in range(heads):
        start = mine + odd * spare + h * HEAD_DIM
        attended_ref[pl.ds(pl.multiple_of(start, 16), HEAD_DIM)] = attend(h)
        copy = attended_copy(h, start, HEAD_DIM)
        copies += [copy(1), copy(0), copy(2)]
        for one in copies[-3:]:
            one.start()
        if h == 0:
            for i in range(3):
                out_z[i].wait_recv()
                for j in (2, 0, 1):
                    out_chip(i, j, chip).start()

    trade.wait_recv()
    for i, (ref, to) in enumerate(((wq_ref, q_ref), (wk_ref, k_ref), (wv_ref, v_ref))):
        normed1 = normed1_ref[...]
        here = nt(ref[half_rows], normed1)
        there = nt(beside[i * spare : (i + 1) * spare], normed1)
        first = jnp.where(odd == 1, there, here)
        second = jnp.where(odd == 1, here, there)
        both = jnp.concatenate([first, second], axis=0)
        to[heads] = both.astype(bf16) if to is v_ref else turn(both)
    last = attend(heads)
    last = jnp.where(odd == 1, last[spare:], last[:spare])
    start = mine + (1 - odd) * whole
    attended_ref[pl.ds(pl.multiple_of(start, 16), spare)] = last
    copy = attended_copy(heads, start, spare)
    copies += [copy(1), copy(0), copy(2)]
    for one in copies[-3:]:
        one.start()

    for i in range(3):
        for j in range(3):
            out_chip(i, j, chips[j]).wait_recv()
        out_core(i, core).start()
    for i in range(3):
        from_z = (z + 3 - i) % 4
        from_odd = from_z % 2
        for h in range(heads):
            attended_copy(h, from_z * quarter + from_odd * spare + h * HEAD_DIM, HEAD_DIM)(i).wait_recv()
        attended_copy(heads, from_z * quarter + (1 - from_odd) * whole, spare)(i).wait_recv()
        out_core(i, other).wait_recv()
    attended = attended_ref[...].T
    residual = x_ref[...].astype(f32) + nt(attended, out_ref[...].reshape(width, width))
    residual_ref[...] = residual
    rms2 = lax.rsqrt(jnp.sum(residual * residual, axis=-1, keepdims=True) * (1.0 / width) + EPS)
    normed2_ref[...] = (residual * rms2 * ffn_gain_ref[...]).astype(bf16)
    for one in (trade, *out_z, *copies):
        one.wait_send()
    for i in range(3):
        for j in range(3):
            out_chip(i, j, chip).wait_send()
        out_core(i, core).wait_send()


def front(x, gain, wq, wk, wv, wo, ffn_gain, doc, tables):
    rows, width = x.shape
    quarter = wq.shape[0]
    heads = -(-quarter // HEAD_DIM)
    spare = quarter % HEAD_DIM
    vmem = pl.BlockSpec(memory_space=pltpu.VMEM)
    dma = pltpu.SemaphoreType.DMA
    low = lambda *shape: jax.ShapeDtypeStruct(shape, bf16)
    return pl.pallas_call(
        front_kernel,
        in_specs=[vmem] * 11,
        out_specs=[vmem] * 9,
        out_shape=[
            low(rows, width),
            *[low(heads, HEAD_DIM, rows)] * 3,
            jax.ShapeDtypeStruct((heads, rows, rows), f32),
            low(width, rows),
            low(4, quarter, width),
            jax.ShapeDtypeStruct((rows, width), f32),
            low(rows, width),
        ],
        scratch_shapes=[
            pltpu.VMEM((3 * spare, width), bf16),
            pltpu.VMEM((3 * spare, width), bf16),
            dma,
            dma,
            dma((heads, 3)),
            dma((heads, 3)),
            dma((3,)),
            dma((3,)),
            dma((9,)),
            dma((9,)),
            dma((3,)),
            dma((3,)),
        ],
        compiler_params=pltpu.CompilerParams(
            vmem_limit_bytes=VMEM_LIMIT, collective_id=1, has_side_effects=True
        ),
        cost_estimate=takes(50),
        name="front",
    )(x, gain[None, :], wq, wk, wv, wo, ffn_gain[None, :], doc, doc.T, *tables)


def collect_sum_kernel(
    y_ref,
    slot_ref,
    gsw_ref,
    mine_ref,
    shared_gate_ref,
    shared_up_ref,
    shared_down_ref,
    forward_ref,
    out_ref,
    sum_ref,
    passed_ref,
    pick,
    ybuf,
    stage,
    given,
    sums,
    relay,
    land,
    zland,
    total,
    copied,
    core_send,
    core_recv,
    send,
    recv,
    zsend,
    zrecv,
    grads,
    *more,
):
    chip, core, z, cx, cy, cd = places()
    other = 1 - core
    x_peer, y_peer, c_peer = (cx, core, z), (cy, core, z), (chip, other, z)
    z_peers = [(chip, core, (z + i) % 4) for i in (1, 2, 3)]
    local, rows = slot_ref.shape[1:]
    tall = out_ref.shape[0]
    me = chip * 2 + core
    number = lax.broadcasted_iota(jnp.int32, (CAP, rows), 0)
    row = lax.broadcasted_iota(jnp.int32, (EXTRA, rows), 0)

    greet([x_peer, y_peer, c_peer, (cd, core, z), *z_peers])

    def sequence(t):
        p = t // 2
        x, y = (chip % 2 + 1 + p // 2) % 2, (chip // 2 + 1 + p % 2) % 2
        return (y * 2 + x) * 2 + (core + 1 + t % 2) % 2

    def in_copy(t):
        return pltpu.make_async_copy(y_ref.at[sequence(t)], ybuf.at[t % 2], copied.at[t % 2])

    def to_core(p):
        return remote(stage.at[p], given.at[p], core_send.at[p], core_recv.at[p], c_peer)

    units = 3
    unit = tall // units
    half, part = unit // 2, unit // 4

    def top(u):
        return pl.ds(u * unit, half)

    def low(u):
        return pl.ds(u * unit + half, half)

    def over(u, number, src, dst, peer):
        return remote(src, dst, send.at[u, number], recv.at[u, number], peer)

    far_top = [over(u, 0, sums.at[0, top(u)], relay.at[u, 0], x_peer) for u in range(units)]
    far_low = [over(u, 1, sums.at[0, low(u)], relay.at[u, 1], y_peer) for u in range(units)]
    x_top = [over(u, 2, sums.at[1, top(u)], land.at[0, top(u)], x_peer) for u in range(units)]
    x_low = [over(u, 3, sums.at[1, low(u)], land.at[0, low(u)], x_peer) for u in range(units)]
    y_low = [over(u, 4, sums.at[2, low(u)], land.at[1, low(u)], y_peer) for u in range(units)]
    y_top = [over(u, 5, sums.at[2, top(u)], land.at[1, top(u)], y_peer) for u in range(units)]

    in_copy(0).start()
    passed_ref[...] = forward_ref[...]
    start, share, give_back, end = weight_sum(grads, *more[:3], sum_ref, *more[3:])
    at = 0
    for ref in (shared_gate_ref, shared_up_ref, shared_down_ref):
        grads[at : at + ref.shape[0]] = ref[...]
        at += ref.shape[0]
    grads[at:] = jnp.zeros((grads.shape[0] - at, grads.shape[1]), bf16)
    start()

    def step(t, carry):
        @pl.when(t < 7)
        def _():
            in_copy(t + 1).start()

        p, s = t // 2, sequence(t)
        probs = jnp.zeros((EXTRA, rows), f32)
        for e in range(local):
            mask = slot_ref[s, e : e + 1, :] == number
            pick[e * CAP : (e + 1) * CAP, :] = mask.astype(f32).astype(bf16)
            column = gsw_ref[e, pl.ds(pl.multiple_of(s * CAP, 8), CAP), :]
            line = jnp.sum(jnp.where(mask, column, 0.0), axis=0, keepdims=True)
            probs = jnp.where(row == me * local + e, line, probs)
        in_copy(t).wait()
        back = tn(pick[...], ybuf[t % 2].reshape(local * CAP, -1))

        @pl.when(t % 2 == 0)
        def _():
            stage[p, :rows] = back.astype(bf16)
            stage[p, rows:] = jnp.zeros((tall - rows, back.shape[1]), bf16)
            stage[p, rows:, :rows] = probs.astype(bf16)
            to_core(p).start()

        @pl.when(t % 2 == 1)
        def _():
            to_core(p).wait_recv()
            sums[p, :rows] = (back + given[p, :rows].astype(f32)).astype(bf16)
            sums[p, rows:] = given[p, rows:]
            sums[p, rows:, :rows] = (probs + given[p, rows:, :rows].astype(f32)).astype(bf16)

        @pl.when(t == 1)
        def _():
            far_top[0].start()
            far_low[0].start()

        @pl.when(t == 3)
        def _():
            x_top[0].start()

        @pl.when(t == 5)
        def _():
            y_low[0].start()
            far_top[1].start()
            far_low[1].start()

        return carry

    lax.fori_loop(0, 8, step, 0)
    def relayed(u):
        far_low[u].wait_recv()
        at = slice(u * unit + half, (u + 1) * unit)
        sums[1, at] = (sums[1, at].astype(f32) + relay[u, 1].astype(f32)).astype(bf16)
        x_low[u].start()
        far_top[u].wait_recv()
        at = slice(u * unit, u * unit + half)
        sums[2, at] = (sums[2, at].astype(f32) + relay[u, 0].astype(f32)).astype(bf16)
        y_top[u].start()

    def block_of(u, q):
        return pl.ds(pl.multiple_of(u * unit + q * part, 16), part)

    def z_sems(u, number):
        return zsend.at[u, number], zrecv.at[u, number]

    scatter = [
        [
            remote(
                total.at[block_of(u, (z + i) % 4)],
                zland.at[u, i - 1],
                *z_sems(u, i - 1),
                z_peers[i - 1],
            )
            for i in (1, 2, 3)
        ]
        for u in range(units)
    ]

    def back_copy(u, q, i):
        at = out_ref.at[block_of(u, q)]
        return remote(at, at, *z_sems(u, 2 + i), z_peers[i - 1])

    def landed(u):
        for copy in (x_top[u], y_top[u], x_low[u], y_low[u]):
            copy.wait_recv()
        at = slice(u * unit, (u + 1) * unit)
        added = sums[3, at].astype(f32) + land[0, at].astype(f32) + land[1, at].astype(f32)
        ours = min(rows, (u + 1) * unit) - u * unit
        if ours == unit:
            total[at] = (added + mine_ref[at].astype(f32)).astype(bf16)
        else:
            here = slice(u * unit, u * unit + ours)
            total[here] = (added[:ours] + mine_ref[here].astype(f32)).astype(bf16)
            total[u * unit + ours : (u + 1) * unit] = added[ours:].astype(bf16)
        for i in (1, 0, 2):
            scatter[u][i].start()

    def summed(u):
        done = total[block_of(u, z)].astype(f32)
        for i in range(3):
            scatter[u][i].wait_recv()
            done = done + zland[u, i].astype(f32)
        out_ref[block_of(u, z)] = done.astype(bf16)
        for i in (2, 1, 3):
            back_copy(u, z, i).start()

    relayed(0)
    x_top[1].start()
    y_low[1].start()
    far_top[2].start()
    far_low[2].start()
    relayed(1)
    x_top[2].start()
    y_low[2].start()
    landed(0)
    relayed(2)
    share()
    landed(1)
    summed(0)
    landed(2)
    summed(1)
    give_back()
    summed(2)
    end()
    for u in range(units):
        for i in (1, 2, 3):
            back_copy(u, (z + 4 - i) % 4, i).wait_recv()
    for u in range(units):
        for copy in (far_top[u], far_low[u], x_top[u], x_low[u], y_low[u], y_top[u], *scatter[u]):
            copy.wait_send()
        for i in (1, 2, 3):
            back_copy(u, z, i).wait_send()
    for p in range(4):
        to_core(p).wait_send()


def collect_sum(y, slot, gsw, mine, forward, *shared):
    s, local, cap, width = y.shape
    rows = slot.shape[2]
    tall = rows + EXTRA
    dma = pltpu.SemaphoreType.DMA
    weights = 128 * (-(-sum(a.shape[0] for a in shared) // 128))
    vmem = pl.BlockSpec(memory_space=pltpu.VMEM)
    return pl.pallas_call(
        collect_sum_kernel,
        in_specs=[pl.BlockSpec(memory_space=pl.ANY)] + [vmem] * 7,
        out_specs=[vmem, vmem, vmem],
        out_shape=[
            jax.ShapeDtypeStruct((tall, width), bf16),
            jax.ShapeDtypeStruct((weights, width), bf16),
            jax.ShapeDtypeStruct(forward.shape, bf16),
        ],
        scratch_shapes=[
            pltpu.VMEM((local * cap, rows), bf16),
            pltpu.VMEM((2, local, cap, width), bf16),
            pltpu.VMEM((4, tall, width), bf16),
            pltpu.VMEM((4, tall, width), bf16),
            pltpu.VMEM((4, tall, width), bf16),
            pltpu.VMEM((3, 2, tall // 6, width), bf16),
            pltpu.VMEM((2, tall, width), bf16),
            pltpu.VMEM((3, 3, tall // 12, width), bf16),
            pltpu.VMEM((tall, width), bf16),
            dma((2,)),
            dma((4,)),
            dma((4,)),
            dma((3, 6)),
            dma((3, 6)),
            dma((3, 6)),
            dma((3, 6)),
            *weight_sum_scratch(weights, width),
        ],
        compiler_params=pltpu.CompilerParams(
            vmem_limit_bytes=VMEM_LIMIT, collective_id=2, has_side_effects=True
        ),
        cost_estimate=takes(131),
        name="collect_sum",
    )(y, slot, gsw, mine, *shared, forward)


def back_kernel(
    sums_ref,
    residual_ref,
    normed2_ref,
    grad_ref,
    router_ref,
    ffn_gain_ref,
    out_ref,
    q_ref,
    k_ref,
    v_ref,
    probs_ref,
    cos_ref,
    sin_ref,
    wq_ref,
    wk_ref,
    wv_ref,
    normed_ref,
    attended_ref,
    x_ref,
    gain_ref,
    tokens_ref,
    early_ref,
    late_ref,
    dq_ref,
    dk_ref,
    dv_ref,
    back_t,
    low_t,
    part,
    low_part,
    zland,
    mine,
    theirs,
    zsend,
    zrecv,
    lsend,
    lrecv,
    *more,
):
    chip, core, z, cx, cy, cd = places()
    odd = z % 2
    c_peer = (chip, 1 - core, z)
    z_peers = [(chip, core, (z + i) % 4) for i in (1, 2, 3)]
    quarter, width = wq_ref.shape
    rows = x_ref.shape[1]
    early, late = more[0], more[8]
    experts = router_ref.shape[0]
    whole = HEAD_DIM * (quarter // HEAD_DIM)
    spare = quarter - whole
    heads = whole // HEAD_DIM
    greet([c_peer, *[(c, core, z) for c in (cx, cy, cd)], *z_peers])

    logits = nt(router_ref[...], normed2_ref[...])
    raised = jnp.exp(logits - jnp.max(logits, axis=0, keepdims=True))
    gates = raised / jnp.sum(raised, axis=0, keepdims=True)
    grad_probs = sums_ref[rows:, :rows].astype(f32)
    grad_logits = gates * (grad_probs - jnp.sum(grad_probs * gates, axis=0, keepdims=True))
    grad_logits = grad_logits.astype(bf16)
    grad_router = nn(grad_logits, normed2_ref[...])
    grad_normed2 = sums_ref[:rows].astype(f32) + tn(grad_logits, router_ref[...])
    residual = residual_ref[...]
    rms2 = lax.rsqrt(jnp.sum(residual * residual, axis=-1, keepdims=True) * (1.0 / width) + EPS)
    grad_ffn = jnp.sum(grad_normed2 * residual * rms2, axis=0, keepdims=True)
    u = grad_normed2 * ffn_gain_ref[...]
    mean2 = jnp.sum(u * residual, axis=-1, keepdims=True) * (1.0 / width)
    added = rms2 * u - residual * (rms2 * rms2 * rms2 * mean2)
    back_t[...] = added.T + grad_ref[...].astype(f32)
    low_t[...] = back_t[...].astype(bf16)
    own = block(z, quarter)
    early[:quarter] = nt(low_t[own], attended_ref[...]).astype(bf16)
    early[quarter:] = grad_router.astype(bf16)
    start, share, give_back, end = weight_sum(early, *more[1:4], early_ref, *more[4:8])
    start()

    cosine, sine = cos_ref[...], sin_ref[...]
    half_dim = HEAD_DIM // 2
    scale = 1.0 / math.sqrt(HEAD_DIM)

    def turn_back(v):
        a, b = v[:half_dim] * scale, v[half_dim:] * scale
        turned = [a * cosine + b * sine, b * cosine - a * sine]
        return jnp.concatenate(turned, axis=0).astype(bf16)

    first_lane = z * quarter + odd * spare
    shared_lane = z * quarter + (1 - odd) * whole - odd * spare
    for h in range(heads + 1):
        lane = first_lane + h * HEAD_DIM if h < heads else shared_lane
        lane = pl.ds(pl.multiple_of(lane, HEAD_DIM), HEAD_DIM)
        grad_attended = tn(out_ref[:, lane], low_t[...]).astype(bf16)
        probs = probs_ref[h]
        grad_p = tn(grad_attended, v_ref[h])
        grad_v = nn(grad_attended, probs.astype(bf16)).astype(bf16)
        delta = jnp.sum(probs * grad_p, axis=-1, keepdims=True)
        grad_s = (probs * (grad_p - delta)).astype(bf16)
        grad_q = turn_back(nt(k_ref[h], grad_s))
        grad_k = turn_back(nn(q_ref[h], grad_s))
        for ref, value in ((dq_ref, grad_q), (dk_ref, grad_k), (dv_ref, grad_v)):
            if h < heads:
                at = pl.ds(pl.multiple_of(odd * spare + h * HEAD_DIM, 16), HEAD_DIM)
                ref[at] = value
            else:
                at = pl.ds(pl.multiple_of((1 - odd) * whole, 16), spare)
                ref[at] = jnp.where(odd == 1, value[spare:], value[:spare])
        if h == 0:
            share()

    x_all = x_ref[...].astype(f32)
    rms1 = lax.rsqrt(jnp.sum(x_all * x_all, axis=0, keepdims=True) * (1.0 / width) + EPS)
    part[...] = tn(wq_ref[...], dq_ref[...])
    part[...] += tn(wk_ref[...], dk_ref[...])
    part[...] += tn(wv_ref[...], dv_ref[...])
    low_part[...] = part[...].astype(bf16)
    to_z = [
        remote(
            low_part.at[block((z + i) % 4, quarter)],
            zland.at[i - 1],
            zsend.at[i - 1],
            zrecv.at[i - 1],
            z_peers[i - 1],
        )
        for i in (1, 2, 3)
    ]
    few_to_z = [
        remote(mine, theirs.at[i], lsend.at[i], lrecv.at[i], peer) for i, peer in enumerate(z_peers)
    ]
    along = part[...] * x_ref[...].astype(f32)
    mine[...] = jnp.zeros(mine.shape, f32)
    mine[0:1, :rows] = jnp.sum(along * gain_ref[...], axis=0, keepdims=True)
    mine[:, rows:] = nt(jnp.ones((8, rows), bf16), (along * rms1).astype(bf16))
    for copy in few_to_z:
        copy.start()
    for i in (1, 0, 2):
        to_z[i].start()

    give_back()
    normed = normed_ref[...]
    for i, ref in enumerate((dq_ref, dk_ref, dv_ref)):
        late[i * quarter : (i + 1) * quarter] = nn(ref[...], normed).astype(bf16)
    at = 3 * quarter
    for copy in few_to_z:
        copy.wait_recv()
    few = mine[...] + theirs[0] + theirs[1] + theirs[2]
    late[at:] = jnp.zeros((late.shape[0] - at, width), bf16)
    line = lax.broadcasted_iota(jnp.int32, (16, width), 0)
    gains = jnp.where(line == 0, few[0:1, rows:], jnp.where(line == 1, grad_ffn, 0.0))
    late[at : at + 16] = gains.astype(bf16)

    start, share, give_back, end_late = weight_sum(late, *more[9:12], late_ref, *more[12:16])
    start()
    share()

    total = part[own]
    for i in range(3):
        to_z[i].wait_recv()
        total = total + zland[i].astype(f32)
    x = x_ref[own].astype(f32)
    mean = few[0:1, :rows] * (1.0 / width)
    tokens_ref[...] = back_t[own] + rms1 * gain_ref[own] * total - x * (rms1 * rms1 * rms1 * mean)

    give_back()
    end()
    end_late()
    for copy in (*to_z, *few_to_z):
        copy.wait_send()


def back(*args):
    quarter, width = args[13].shape
    rows = args[1].shape[0]
    early, late = quarter + args[4].shape[0], 128 * (3 * quarter // 128 + 1)
    vmem = pl.BlockSpec(memory_space=pltpu.VMEM)
    dma = pltpu.SemaphoreType.DMA
    return pl.pallas_call(
        back_kernel,
        in_specs=[vmem] * len(args),
        out_specs=[vmem] * 3,
        out_shape=[
            jax.ShapeDtypeStruct((quarter, rows), f32),
            jax.ShapeDtypeStruct((early, width), bf16),
            jax.ShapeDtypeStruct((late, width), bf16),
        ],
        scratch_shapes=[
            *[pltpu.VMEM((quarter, rows), bf16)] * 3,
            pltpu.VMEM((width, rows), f32),
            pltpu.VMEM((width, rows), bf16),
            pltpu.VMEM((width, rows), f32),
            pltpu.VMEM((width, rows), bf16),
            pltpu.VMEM((3, quarter, rows), bf16),
            pltpu.VMEM((8, rows + width), f32),
            pltpu.VMEM((3, 8, rows + width), f32),
            dma((3,)),
            dma((3,)),
            dma((3,)),
            dma((3,)),
            *weight_sum_scratch(early, width),
            *weight_sum_scratch(late, width),
        ],
        compiler_params=pltpu.CompilerParams(
            vmem_limit_bytes=VMEM_LIMIT, collective_id=3, has_side_effects=True
        ),
        cost_estimate=takes(90),
        name="back",
    )(*args)


def widen_kernel(early_ref, late_ref, shared_ref, *out_refs):
    quarter = out_refs[0].shape[0]
    for i in range(3):
        out_refs[i][...] = late_ref[i * quarter : (i + 1) * quarter].astype(f32)
    out_refs[3][...] = early_ref[:quarter].astype(f32)
    out_refs[4][...] = early_ref[quarter:].astype(f32)
    out_refs[5][...] = late_ref[3 * quarter : 3 * quarter + 8].astype(f32)
    size = out_refs[6].shape[0]
    for i in range(3):
        out_refs[6 + i][...] = shared_ref[i * size : (i + 1) * size].astype(f32)


def widen(early, late, shared, quarter, hidden_units):
    width = early.shape[1]
    step = width // 5
    tall = [quarter] * 4 + [early.shape[0] - quarter, 8] + [hidden_units] * 3
    blocks = lambda lines: pl.BlockSpec((lines, step), lambda i: (0, i))
    return pl.pallas_call(
        widen_kernel,
        grid=(width // step,),
        in_specs=[blocks(a.shape[0]) for a in (early, late, shared)],
        out_specs=[blocks(lines) for lines in tall],
        out_shape=[jax.ShapeDtypeStruct((lines, width), f32) for lines in tall],
        compiler_params=pltpu.CompilerParams(vmem_limit_bytes=VMEM_LIMIT),
        cost_estimate=takes(8),
        name="widen",
    )(early, late, shared)


def plain_front(
    tokens, attn_gain, query_t, key_t, value_t, attn_out, ffn_gain, documents, tables
):
    rows, width = tokens.shape
    quarter = query_t.shape[0]
    hs, hs_count = lax.axis_index("hs"), lax.axis_size("hs")
    odd = (hs % 2) == 1
    spare = -quarter % HEAD_DIM
    heads = (quarter + spare) // HEAD_DIM

    def outer(w):
        return jnp.where(odd, w[:spare], w[quarter - spare :])

    sent = jnp.concatenate([outer(query_t), outer(key_t), outer(value_t)], axis=0)
    got = lax.ppermute(sent, "hs", [(i, i ^ 1) for i in range(hs_count)])

    def widened(w, extra):
        return jnp.where(
            odd, jnp.concatenate([extra, w], axis=0), jnp.concatenate([w, extra], axis=0)
        )

    x = tokens.astype(f32)
    rms1 = lax.rsqrt(jnp.mean(x * x, axis=-1, keepdims=True) + EPS)
    normed1 = (x * rms1 * attn_gain).astype(bf16)
    shape3 = (heads, HEAD_DIM, rows)
    q, k, v = [
        ein("cd,td->ct", widened(w, got[i * spare : (i + 1) * spare]), normed1).reshape(shape3)
        for i, w in enumerate((query_t, key_t, value_t))
    ]
    q, k, v = rope(q, *tables).astype(bf16), rope(k, *tables).astype(bf16), v.astype(bf16)
    positions = jnp.arange(rows, dtype=jnp.int32)
    doc = documents[0]
    allowed = (positions[:, None] >= positions[None, :]) & (doc[:, None] == doc[None, :])
    scale = 1.0 / math.sqrt(HEAD_DIM)
    scores = jnp.where(allowed[None], ein("hdq,hdk->hqk", q, k) * scale, -1e30)
    raised = jnp.exp(scores - jnp.max(scores, axis=-1, keepdims=True))
    probs = raised / jnp.sum(raised, axis=-1, keepdims=True)
    attended = ein("hdk,hqk->hdq", v, probs.astype(bf16)).astype(bf16).reshape(-1, rows)
    attended = jnp.where(odd, attended[spare:], attended[:quarter])
    attended_t = lax.all_gather(attended, "hs", axis=0, tiled=True)
    out_t = lax.all_gather(attn_out.T, "hs", axis=0, tiled=True)
    residual = x + ein("ct,oc->to", attended_t, out_t)
    rms2 = lax.rsqrt(jnp.mean(residual * residual, axis=-1, keepdims=True) + EPS)
    normed2 = (residual * rms2 * ffn_gain).astype(bf16)
    return normed1, q, k, v, probs, attended_t, out_t, residual, normed2


def over_ep(a):
    return lax.psum(a.astype(bf16), EP).astype(f32)


def plain_back(
    sums,
    residual,
    normed2,
    grad_t,
    router_t,
    ffn_gain,
    out_t,
    q,
    k,
    v,
    probs,
    tables,
    query_t,
    key_t,
    value_t,
    normed1,
    attended_t,
    tokens,
    attn_gain,
):
    rows, width = tokens.shape
    quarter = query_t.shape[0]
    hs = lax.axis_index("hs")
    odd = (hs % 2) == 1
    spare = -quarter % HEAD_DIM
    held = quarter + spare
    col0 = hs * quarter

    def own(v):
        v = v.astype(bf16).reshape(held, rows)
        return jnp.where(odd, v[spare:], v[:quarter])

    gates = jax.nn.softmax(nt(normed2, router_t), axis=-1)
    grad_probs = sums[rows:, :rows].T.astype(f32)
    grad_logits = (
        gates * (grad_probs - jnp.sum(grad_probs * gates, axis=-1, keepdims=True))
    ).astype(bf16)
    grad_router = tn(grad_logits, normed2)
    grad_normed2 = sums[:rows].astype(f32) + dot(grad_logits, router_t)
    rms2 = lax.rsqrt(jnp.mean(residual * residual, axis=-1, keepdims=True) + EPS)
    grad_ffn_gain = jnp.sum(grad_normed2 * residual * rms2, axis=0)
    u = grad_normed2 * ffn_gain
    grad_residual = (
        grad_t.T.astype(f32)
        + rms2 * u
        - residual * rms2**3 * jnp.mean(u * residual, axis=-1, keepdims=True)
    )
    back_t = grad_residual.T
    low_t = back_t.astype(bf16)
    out_held = lax.dynamic_slice_in_dim(out_t, jnp.where(odd, col0 - spare, col0), held, 1)
    grad_attended = tn(out_held, low_t).astype(bf16).reshape(-1, HEAD_DIM, rows)
    grad_p = ein("hdq,hdk->hqk", grad_attended, v)
    grad_v = own(ein("hdq,hqk->hdk", grad_attended, probs.astype(bf16)))
    grad_s = (probs * (grad_p - jnp.sum(probs * grad_p, axis=-1, keepdims=True))).astype(bf16)
    scale = 1.0 / math.sqrt(HEAD_DIM)
    grad_q = own(rope_back(ein("hdk,hqk->hdq", k, grad_s) * scale, *tables))
    grad_k = own(rope_back(ein("hdq,hqk->hdk", q, grad_s) * scale, *tables))
    own_rows = lambda a: lax.dynamic_slice_in_dim(a, col0, quarter, 0)
    heads_sums = [
        over_ep(dot(grad_q, normed1)),
        over_ep(dot(grad_k, normed1)),
        over_ep(dot(grad_v, normed1)),
        over_ep(nt(own_rows(low_t), attended_t)),
    ]
    part = tn(query_t, grad_q) + tn(key_t, grad_k) + tn(value_t, grad_v)
    grad_n1 = lax.psum_scatter(part.astype(bf16), "hs", scatter_dimension=0, tiled=True)
    grad_n1 = grad_n1.astype(f32)
    x = tokens.T.astype(f32)
    x_own = own_rows(x)
    rms_t = lax.rsqrt(jnp.mean(x * x, axis=0, keepdims=True) + EPS)
    w1 = grad_n1 * own_rows(attn_gain)[:, None]
    mean1 = lax.psum(jnp.sum(w1 * x_own, axis=0, keepdims=True), "hs") / width
    grad_tokens = own_rows(back_t) + rms_t * w1 - x_own * rms_t**3 * mean1
    gain_own = jnp.sum(grad_n1 * x_own * rms_t, axis=1)
    gain_part = lax.dynamic_update_slice_in_dim(jnp.zeros((width,), f32), gain_own, col0, 0)
    grad_attn_gain = lax.psum(gain_part, (*EP, "hs"))
    return (
        grad_tokens,
        heads_sums,
        over_ep(grad_router),
        grad_attn_gain,
        lax.psum(grad_ffn_gain, EP),
    )


def shards(
    tokens,
    attn_gain,
    attn_query,
    attn_key,
    attn_value,
    attn_out,
    ffn_gain,
    router,
    shared_gate,
    shared_up,
    shared_down,
    expert_gate,
    expert_up,
    expert_down,
    routes,
    documents,
    out_grad,
):
    rows, width = tokens.shape
    quarter = out_grad.shape[1]
    hs = lax.axis_index("hs")
    ep_count = lax.axis_size("xy") * lax.axis_size("core")
    ep = lax.axis_index("xy") * lax.axis_size("core") + lax.axis_index("core")
    local = expert_gate.shape[0]
    experts = router.shape[1]
    small = ep_count == 8 and lax.axis_size("hs") == 4

    query_t, key_t, value_t, router_t = attn_query.T, attn_key.T, attn_value.T, router.T
    grad_all_t = lax.all_gather(out_grad.T, (*EP, "hs"), axis=0, tiled=True)
    grad_all_t = grad_all_t.reshape(ep_count, width, rows)
    grad_t = lax.dynamic_index_in_dim(grad_all_t, ep, 0, keepdims=False)
    positions = jnp.arange(rows, dtype=jnp.int32)
    below = (positions[:, None] > positions[None, :]).astype(bf16)
    chosen = jnp.any(
        routes[:, :, None] == jnp.arange(experts, dtype=jnp.int32)[None, None, :], axis=1
    )
    own_slots = jnp.where(chosen, dot(below, chosen.astype(bf16)), -1.0).T.astype(bf16)
    tables = rope_tables(rows)

    if small:
        ahead = front(
            tokens, attn_gain, query_t, key_t, value_t, attn_out.T, ffn_gain, documents, tables
        )
    else:
        ahead = plain_front(
            tokens, attn_gain, query_t, key_t, value_t, attn_out, ffn_gain, documents, tables
        )
    normed1, q, k, v, probs, attended_t, out_t, residual, normed2 = ahead
    out_t = out_t.reshape(width, width)

    sh_gate = dot(normed2, shared_gate)
    sh_up = dot(normed2, shared_up)
    sh_sig = jax.nn.sigmoid(sh_gate)
    sh_act = sh_gate * sh_sig
    sh_hidden = (sh_act * sh_up).astype(bf16)
    shared_part = dot(sh_hidden, shared_down)
    grad_sh = ein("dt,fd->tf", grad_t, shared_down)
    grad_sh_gate = (grad_sh * sh_up * sh_sig * (1 + sh_gate * (1 - sh_sig))).astype(bf16)
    grad_sh_up = (grad_sh * sh_act).astype(bf16)
    shared_grads = [
        ein("tf,td->fd", grad_sh_gate, normed2).astype(bf16),
        ein("tf,td->fd", grad_sh_up, normed2).astype(bf16),
        ein("tf,dt->fd", sh_hidden, grad_t).astype(bf16),
    ]
    shared_back = ein("tf,df->td", grad_sh_gate, shared_gate) + ein(
        "tf,df->td", grad_sh_up, shared_up
    )

    first = ep * local
    rolled = jnp.roll(router_t, -first, axis=0)
    if small:
        ex_in, slot_weight, slot = gather_spread(normed2, own_slots, rolled, local, ep_count)
    else:
        slot = lax.dynamic_slice_in_dim(
            lax.all_gather(own_slots, EP, axis=0), first, local, 1
        ).astype(jnp.int32)
        normed_all = lax.all_gather(normed2, EP, axis=0, tiled=True)
        ex_in, slot_weight = spread(normed_all, slot, rolled)
    gate_t, up_t = expert_gate.swapaxes(1, 2), expert_up.swapaxes(1, 2)
    ex_grad = spread(grad_all_t, slot)
    ex_out, ex_gate, ex_up = experts_forward(ex_in, slot_weight, gate_t, up_t, expert_down)
    out_part = collect(ex_out, slot).reshape(ep_count * rows, width)
    ex_back, grad_gate_t, grad_up_t, grad_expert_down, grad_slot_weight = experts_backward(
        ex_in, ex_grad, ex_gate, ex_up, slot_weight, gate_t, up_t, expert_down
    )

    if small:
        back_sums, shared_sums, shared_part = collect_sum(
            ex_back, slot, grad_slot_weight, shared_back.astype(bf16), shared_part.astype(bf16), *shared_grads
        )
        grad_tokens, early, late = back(
            back_sums,
            residual,
            normed2,
            grad_t,
            router_t,
            ffn_gain[None, :],
            out_t,
            q,
            k,
            v,
            probs,
            *tables,
            query_t,
            key_t,
            value_t,
            normed1,
            attended_t,
            tokens.T,
            attn_gain[:, None],
        )
        *heads_sums, grad_router, gains, sum_gate, sum_up, sum_down = widen(
            early, late, shared_sums, quarter, shared_down.shape[0]
        )
        shared_sums = sum_gate, sum_up, sum_down
        grad_attn_gain, grad_ffn_gain = gains[0], gains[1]
    else:
        back_part = collect(ex_back, slot, grad_slot_weight, first, experts).reshape(-1, width)
        back_rows = lax.psum_scatter(back_part, EP, scatter_dimension=0, tiled=True).astype(f32)
        back_rows = jnp.concatenate([back_rows[:rows] + shared_back, back_rows[rows:]], axis=0)
        back_sums = lax.psum(back_rows.astype(bf16), "hs")
        shared_sums = [over_ep(a) for a in shared_grads]
        grad_tokens, heads_sums, grad_router, grad_attn_gain, grad_ffn_gain = plain_back(
            back_sums,
            residual,
            normed2,
            grad_t,
            router_t,
            ffn_gain,
            out_t,
            q,
            k,
            v,
            probs,
            tables,
            query_t,
            key_t,
            value_t,
            normed1,
            attended_t,
            tokens,
            attn_gain,
        )

    rows_major = Layout(major_to_minor=(0, 1))
    out_part = with_layout_constraint(out_part, rows_major)
    out_rows = lax.psum_scatter(out_part, EP, scatter_dimension=0, tiled=True)
    out_rows = with_layout_constraint(out_rows, rows_major)
    out_rows = (out_rows.astype(f32) + shared_part.astype(f32)).astype(bf16)
    out_quarter = lax.psum_scatter(out_rows, "hs", scatter_dimension=1, tiled=True)
    residual_quarter = lax.dynamic_slice_in_dim(residual, hs * quarter, quarter, 1)
    output = (residual_quarter + out_quarter.astype(f32)).astype(bf16)

    return (
        output,
        grad_tokens.T,
        grad_attn_gain,
        *[a.T for a in heads_sums],
        grad_ffn_gain,
        grad_router.T,
        shared_sums[0].T,
        shared_sums[1].T,
        shared_sums[2],
        grad_gate_t.swapaxes(1, 2),
        grad_up_t.swapaxes(1, 2),
        grad_expert_down,
    )


def solution(mesh):
    ep_count, hs_count = mesh.devices.shape
    cut = Mesh(mesh.devices.reshape(ep_count // 2, 2, hs_count), ("xy", "core", "hs"))
    return jax.shard_map(
        shards,
        mesh=cut,
        in_specs=(
            P(EP, None),
            P(),
            P(None, "hs"),
            P(None, "hs"),
            P(None, "hs"),
            P(None, "hs"),
            P(),
            P(),
            P(None, "hs"),
            P(None, "hs"),
            P("hs", None),
            P(EP, None, "hs"),
            P(EP, None, "hs"),
            P(EP, "hs", None),
            P(EP, None),
            P(EP, None),
            P(EP, "hs"),
        ),
        out_specs=(
            P(EP, "hs"),
            P(EP, "hs"),
            P(),
            P(None, "hs"),
            P(None, "hs"),
            P(None, "hs"),
            P(None, "hs"),
            P(),
            P(),
            P(None, "hs"),
            P(None, "hs"),
            P("hs", None),
            P(EP, None, "hs"),
            P(EP, None, "hs"),
            P(EP, "hs", None),
        ),
        check_vma=False,
    )
```

```python
import functools
import math

import jax
import jax.numpy as jnp
import numpy as np
from jax import lax
from jax.experimental import pallas as pl
from jax.experimental.layout import Layout, with_layout_constraint
from jax.experimental.pallas import tpu as pltpu
from jax.sharding import Mesh
from jax.sharding import PartitionSpec as P

HEADS = 10
HEAD_DIM = 128
CAP = 112
EPS = 1e-06
EP = ("xy", "core")
bf16 = jnp.bfloat16
f32 = jnp.float32


def dot(a, b):
    return jnp.dot(a, b, preferred_element_type=f32)


def ein(spec, a, b):
    return jnp.einsum(spec, a, b, preferred_element_type=f32)


def rope_tables(rows):
    half = HEAD_DIM // 2
    frequency = 10000.0 ** (-np.arange(half) * 2.0 / HEAD_DIM)
    angles = frequency[:, None] * np.arange(rows)[None, :]
    return jnp.asarray(np.cos(angles), f32), jnp.asarray(np.sin(angles), f32)


def rope(v, cosine, sine):
    half = HEAD_DIM // 2
    a, b = v[:, :half], v[:, half:]
    return jnp.concatenate([a * cosine - b * sine, b * cosine + a * sine], axis=1)


def rope_back(v, cosine, sine):
    half = HEAD_DIM // 2
    a, b = v[:, :half], v[:, half:]
    return jnp.concatenate([a * cosine + b * sine, b * cosine - a * sine], axis=1)


VMEM_LIMIT = 60 * 1024 * 1024
PAD = 256


def nn(a, b):
    return lax.dot_general(a, b, (((1,), (0,)), ((), ())), preferred_element_type=f32)


def nt(a, b):
    return lax.dot_general(a, b, (((1,), (1,)), ((), ())), preferred_element_type=f32)


def tn(a, b):
    return lax.dot_general(a, b, (((0,), (0,)), ((), ())), preferred_element_type=f32)


def takes(microseconds):
    return pl.CostEstimate(flops=0, transcendentals=0, bytes_accessed=microseconds * 3_000_000)


def slot_masks(slot_ref, at):
    local, rows = slot_ref.shape[-2:]
    number = lax.broadcasted_iota(jnp.int32, (CAP, rows), 0)
    return [slot_ref[at, e : e + 1, :] == number for e in range(local)]


def spread_kernel(weighted, *refs):
    if weighted:
        rows_ref, slot_ref, router_ref, x_ref, sw_ref, pick = refs
    else:
        rows_ref, slot_ref, x_ref, pick = refs
    local = slot_ref.shape[1]
    rows = rows_ref[...] if weighted else rows_ref[0]
    masks = slot_masks(slot_ref, 0)
    if weighted:
        logits = nt(router_ref[...], rows)
        raised = jnp.exp(logits - jnp.max(logits, axis=0, keepdims=True))
        gates = raised / jnp.sum(raised, axis=0, keepdims=True)
    for e in range(local):
        pick[e * CAP : (e + 1) * CAP, :] = masks[e].astype(f32).astype(bf16)
        if weighted:
            sw_ref[e] = jnp.sum(
                jnp.where(masks[e], gates[e : e + 1, :], 0.0), axis=1, keepdims=True
            )
    product = nn if weighted else nt
    x_ref[...] = product(pick[...], rows).astype(bf16).reshape(x_ref.shape)


def spread(all_rows, slot, router_t=None):
    s, local, rows = slot.shape
    weighted = router_t is not None
    if weighted:
        width = all_rows.shape[1]
        block = pl.BlockSpec((rows, width), lambda i: (i, 0))
    else:
        width = all_rows.shape[1]
        block = pl.BlockSpec((1, width, rows), lambda i: (i, 0, 0))
    in_specs = [
        block,
        pl.BlockSpec((1, local, rows), lambda i: (i, 0, 0)),
    ]
    out_specs = [pl.BlockSpec((1, local, CAP, width), lambda i: (i, 0, 0, 0))]
    out_shape = [jax.ShapeDtypeStruct((s, local, CAP, width), bf16)]
    args = [all_rows, slot]
    if weighted:
        in_specs.append(pl.BlockSpec(router_t.shape, lambda i: (0, 0)))
        out_specs.append(pl.BlockSpec((local, CAP, 1), lambda i: (0, i, 0)))
        out_shape.append(jax.ShapeDtypeStruct((local, s * CAP, 1), f32))
        args.append(router_t)
    out = pl.pallas_call(
        functools.partial(spread_kernel, weighted),
        grid=(s,),
        in_specs=in_specs,
        out_specs=out_specs,
        out_shape=out_shape,
        scratch_shapes=[pltpu.VMEM((local * CAP, rows), bf16)],
        compiler_params=pltpu.CompilerParams(vmem_limit_bytes=VMEM_LIMIT),
        cost_estimate=takes(17),
        name="spread",
    )(*args)
    return out if weighted else out[0]


def padded(ref, out):
    ff = ref.shape[1]
    out[:ff, :] = ref[0]
    out[ff:, :] = jnp.zeros((out.shape[0] - ff, out.shape[1]), out.dtype)


def experts_forward_kernel(
    x_ref, sw_ref, wg_ref, wu_ref, wd_ref, y_ref, gate_ref, up_ref, wg, wu, wd
):
    padded(wg_ref, wg)
    padded(wu_ref, wu)
    padded(wd_ref, wd)
    rows, width = gate_ref.shape[1], x_ref.shape[3]
    x = x_ref[...].reshape(rows, width)
    gate = nt(x, wg[...])
    up = nt(x, wu[...])
    gate_ref[0] = gate
    up_ref[0] = up
    act = gate / (1.0 + jnp.exp(-gate))
    hidden = (act * up).astype(bf16).astype(f32)
    hidden_w = (hidden * sw_ref[0]).astype(bf16)
    y_ref[...] = nn(hidden_w, wd[...]).astype(bf16).reshape(y_ref.shape)


def experts_backward_kernel(
    groups,
    x_ref,
    gx_ref,
    gate_ref,
    up_ref,
    sw_ref,
    wg_ref,
    wu_ref,
    wd_ref,
    dx_ref,
    dg_ref,
    du_ref,
    dd_ref,
    gsw_ref,
    wg,
    wu,
    wd,
):
    padded(wg_ref, wg)
    padded(wu_ref, wu)
    padded(wd_ref, wd)
    rows, width = gate_ref.shape[1], x_ref.shape[3]
    ff = wg_ref.shape[1]
    x = x_ref[...].reshape(rows, width)
    gx = gx_ref[...].reshape(rows, width)
    gate, up, sw = gate_ref[0], up_ref[0], sw_ref[0]
    sig = 1.0 / (1.0 + jnp.exp(-gate))
    act = gate * sig
    hidden = (act * up).astype(bf16).astype(f32)
    gh = nt(gx, wd[...])
    gsw_ref[0] = jnp.sum(gh * hidden, axis=-1, keepdims=True)
    gh = gh * sw
    gg = (gh * up * sig * (1.0 + gate * (1.0 - sig))).astype(bf16)
    gu = (gh * act).astype(bf16)
    sums = (
        (dd_ref, tn((hidden * sw).astype(bf16), gx)[:ff]),
        (dg_ref, tn(gg, x)[:ff]),
        (du_ref, tn(gu, x)[:ff]),
    )
    if groups == 1:
        for ref, value in sums:
            ref[0] = value
    else:

        @pl.when(pl.program_id(1) == 0)
        def _():
            for ref, value in sums:
                ref[0] = value

        @pl.when(pl.program_id(1) > 0)
        def _():
            for ref, value in sums:
                ref[0] += value

    dx_ref[...] = (nn(gg, wg[...]) + nn(gu, wu[...])).astype(bf16).reshape(dx_ref.shape)


def sending(remote_too, collective_id):
    if not remote_too:
        return pltpu.CompilerParams(vmem_limit_bytes=VMEM_LIMIT)
    return pltpu.CompilerParams(
        vmem_limit_bytes=VMEM_LIMIT, collective_id=collective_id, has_side_effects=True
    )


def expert_specs(s, width):
    group = min(s, 8)
    slots = pl.BlockSpec((group, 1, CAP, width), lambda i, j: (j, i, 0, 0))
    lines = lambda columns: pl.BlockSpec((1, group * CAP, columns), lambda i, j: (i, j, 0))
    per = lambda *shape: pl.BlockSpec((1, *shape), lambda i, j: (i, 0, 0))
    return s // group, slots, lines, per


def experts_forward_sending_kernel(
    x_ref,
    sw_ref,
    wg_ref,
    wu_ref,
    wd_ref,
    grad_ref,
    y_ref,
    gate_ref,
    up_ref,
    near_ref,
    wg,
    wu,
    wd,
    send,
    recv,
):
    chip, core, z, cx, cy, cd = places()
    peers = [(cx, core, z), (cy, core, z)]
    copies = [
        remote(grad_ref, near_ref.at[i], send.at[i], recv.at[i], peer) for i, peer in enumerate(peers)
    ]

    @pl.when(pl.program_id(0) == 0)
    def _():
        greet(peers)
        for copy in copies:
            copy.start()

    experts_forward_kernel(
        x_ref, sw_ref, wg_ref, wu_ref, wd_ref, y_ref, gate_ref, up_ref, wg, wu, wd
    )

    @pl.when(pl.program_id(0) == pl.num_programs(0) - 1)
    def _():
        for copy in copies:
            copy.wait()


def experts_forward(x, sw, wg, wu, wd, grad=None):
    s, local, cap, width = x.shape
    ff = wg.shape[1]
    rows = s * cap
    groups, slots, lines, per = expert_specs(s, width)
    middle = jax.ShapeDtypeStruct((local, rows, PAD), f32)
    kernel = experts_forward_kernel
    in_specs = [slots, lines(1)] + [per(ff, width)] * 3
    out_specs = [slots, lines(PAD), lines(PAD)]
    out_shape = [jax.ShapeDtypeStruct(x.shape, bf16), middle, middle]
    scratch = [pltpu.VMEM((PAD, width), bf16)] * 3
    args = [x, sw, wg, wu, wd]
    if grad is not None:
        kernel = experts_forward_sending_kernel
        in_specs.append(pl.BlockSpec(memory_space=pl.ANY))
        out_specs.append(pl.BlockSpec(memory_space=pl.ANY))
        out_shape.append(jax.ShapeDtypeStruct((2, *grad.shape), bf16))
        scratch += [pltpu.SemaphoreType.DMA((2,))] * 2
        args.append(grad)
    return pl.pallas_call(
        kernel,
        grid=(local, groups),
        in_specs=in_specs,
        out_specs=out_specs,
        out_shape=out_shape,
        scratch_shapes=scratch,
        compiler_params=sending(grad is not None, 4),
        cost_estimate=takes(31),
        name="experts_forward",
    )(*args)


def experts_backward(x, gx, gate, up, sw, wg, wu, wd):
    s, local, cap, width = x.shape
    ff = wg.shape[1]
    rows = s * cap
    groups, slots, lines, per = expert_specs(s, width)
    return pl.pallas_call(
        functools.partial(experts_backward_kernel, groups),
        grid=(local, groups),
        in_specs=[slots, slots, lines(PAD), lines(PAD), lines(1)]
        + [per(ff, width)] * 3,
        out_specs=[slots] + [per(ff, width)] * 3 + [lines(1)],
        out_shape=[jax.ShapeDtypeStruct(x.shape, bf16)]
        + [jax.ShapeDtypeStruct((local, ff, width), f32)] * 3
        + [jax.ShapeDtypeStruct((local, rows, 1), f32)],
        scratch_shapes=[pltpu.VMEM((PAD, width), bf16)] * 3,
        compiler_params=pltpu.CompilerParams(vmem_limit_bytes=VMEM_LIMIT),
        cost_estimate=takes(47),
        name="experts_backward",
    )(x, gx, gate, up, sw, wg, wu, wd)


def collect_kernel(y_ref, slot_ref, out_ref, pick):
    local = slot_ref.shape[1]
    masks = slot_masks(slot_ref, 0)
    for e in range(local):
        pick[e * CAP : (e + 1) * CAP, :] = masks[e].astype(f32).astype(bf16)
    out_ref[0] = tn(pick[...], y_ref[...].reshape(pick.shape[0], -1)).astype(bf16)


def collect_sending_kernel(
    y_ref, slot_ref, grad_ref, near_ref, out_ref, far_ref, given_ref, pick, send, recv, csend, crecv
):
    chip, core, z, cx, cy, cd = places()
    x_peer, y_peer, c_peer = (cx, core, z), (cy, core, z), (chip, 1 - core, z)
    half = grad_ref.shape[0] // 2
    top, low = pl.ds(0, half), pl.ds(half, half)
    relays = [
        remote(near_ref.at[0, top], far_ref.at[top], send.at[0], recv.at[0], y_peer),
        remote(near_ref.at[1, low], far_ref.at[low], send.at[1], recv.at[1], x_peer),
    ]
    passes = [
        remote(ref, given_ref.at[i], csend.at[i], crecv.at[i], c_peer)
        for i, ref in enumerate((grad_ref, near_ref.at[0], near_ref.at[1], far_ref))
    ]

    @pl.when(pl.program_id(0) == 0)
    def _():
        greet([x_peer, y_peer, c_peer])
        for copy in (*relays, *passes[:3]):
            copy.start()

    collect_kernel(y_ref, slot_ref, out_ref, pick)

    @pl.when(pl.program_id(0) == pl.num_programs(0) - 1)
    def _():
        for copy in relays:
            copy.wait_recv()
        passes[3].start()
        for copy in passes:
            copy.wait()
        for copy in relays:
            copy.wait_send()


def collect_back_kernel(experts, y_ref, slot_ref, gsw_ref, first_ref, out_ref, pick):
    local, rows = slot_ref.shape[1:]
    first = first_ref[0]
    masks = slot_masks(slot_ref, 0)
    number = lax.broadcasted_iota(jnp.int32, (experts, rows), 0)
    probs = jnp.zeros((experts, rows), f32)
    for e in range(local):
        pick[e * CAP : (e + 1) * CAP, :] = masks[e].astype(f32).astype(bf16)
        line = jnp.sum(jnp.where(masks[e], gsw_ref[e], 0.0), axis=0, keepdims=True)
        probs = jnp.where(number == first + e, line, probs)
    out_ref[0, :rows] = tn(pick[...], y_ref[...].reshape(pick.shape[0], -1)).astype(bf16)
    out_ref[0, rows:] = jnp.zeros((experts, out_ref.shape[2]), bf16)
    out_ref[0, rows:, :rows] = probs.astype(bf16)


def collect_sending(y, slot, grad, near):
    s, local, cap, width = y.shape
    rows = slot.shape[2]
    dma = pltpu.SemaphoreType.DMA
    whole = pl.BlockSpec(memory_space=pl.ANY)
    return pl.pallas_call(
        collect_sending_kernel,
        grid=(s,),
        in_specs=[
            pl.BlockSpec((1, local, cap, width), lambda i: (i, 0, 0, 0)),
            pl.BlockSpec((1, local, rows), lambda i: (i, 0, 0)),
            whole,
            whole,
        ],
        out_specs=[pl.BlockSpec((1, rows, width), lambda i: (i, 0, 0)), whole, whole],
        out_shape=[
            jax.ShapeDtypeStruct((s, rows, width), bf16),
            jax.ShapeDtypeStruct(grad.shape, bf16),
            jax.ShapeDtypeStruct((4, *grad.shape), bf16),
        ],
        scratch_shapes=[
            pltpu.VMEM((local * cap, rows), bf16),
            dma((2,)),
            dma((2,)),
            dma((4,)),
            dma((4,)),
        ],
        compiler_params=sending(True, 5),
        cost_estimate=takes(20),
        name="collect_sending",
    )(y, slot, grad, near)


def spread_grad_kernel(grad_ref, near_ref, far_ref, given_ref, slot_ref, x_ref, pick, gbuf, xbuf, come, gone):
    chip, core = lax.axis_index("xy"), lax.axis_index("core")
    local, rows = slot_ref.shape[1:]
    here = [grad_ref, near_ref.at[0], near_ref.at[1], far_ref]
    sources = [(here[t // 2], given_ref.at[t // 2])[t % 2] for t in range(8)]

    def in_copy(t):
        return pltpu.make_async_copy(sources[t], gbuf.at[t % 2], come.at[t % 2])

    def out_copy(t, src):
        return pltpu.make_async_copy(xbuf.at[t % 2], x_ref.at[src], gone.at[t % 2])

    number = lax.broadcasted_iota(jnp.int32, (CAP, rows), 0)
    in_copy(0).start()
    for t in range(8):
        if t < 7:
            in_copy(t + 1).start()
        x, y = (chip % 2 + (t // 2) % 2) % 2, (chip // 2 + t // 4) % 2
        src = (y * 2 + x) * 2 + (core + t % 2) % 2
        slots = slot_ref[src]
        for e in range(local):
            mask = slots[e : e + 1, :] == number
            pick[e * CAP : (e + 1) * CAP, :] = mask.astype(f32).astype(bf16)
        in_copy(t).wait()
        if t >= 2:
            out_copy(t, src).wait()
        xbuf[t % 2] = nt(pick[...], gbuf[t % 2]).astype(bf16).reshape(xbuf.shape[1:])
        out_copy(t, src).start()
    out_copy(0, 0).wait()
    out_copy(1, 0).wait()


def spread_grad(grad, near, far, given, slot):
    s, local, rows = slot.shape
    width = grad.shape[0]
    whole = pl.BlockSpec(memory_space=pl.ANY)
    dma = pltpu.SemaphoreType.DMA
    return pl.pallas_call(
        spread_grad_kernel,
        in_specs=[whole] * 4 + [pl.BlockSpec(memory_space=pltpu.VMEM)],
        out_specs=whole,
        out_shape=jax.ShapeDtypeStruct((s, local, CAP, width), bf16),
        scratch_shapes=[
            pltpu.VMEM((local * CAP, rows), bf16),
            pltpu.VMEM((2, width, rows), bf16),
            pltpu.VMEM((2, local, CAP, width), bf16),
            dma((2,)),
            dma((2,)),
        ],
        compiler_params=sending(False, 0),
        cost_estimate=takes(16),
        name="spread_grad",
    )(grad, near, far, given, slot)


def collect(y, slot, gsw=None, first=None, experts=0):
    s, local, cap, width = y.shape
    rows = slot.shape[2]
    in_specs = [
        pl.BlockSpec((1, local, cap, width), lambda i: (i, 0, 0, 0)),
        pl.BlockSpec((1, local, rows), lambda i: (i, 0, 0)),
    ]
    args = [y, slot]
    kernel = collect_kernel
    tall = rows
    if gsw is not None:
        in_specs += [
            pl.BlockSpec((local, cap, 1), lambda i: (0, i, 0)),
            pl.BlockSpec(memory_space=pltpu.SMEM),
        ]
        args += [gsw, first.reshape(1)]
        kernel = functools.partial(collect_back_kernel, experts)
        tall = rows + experts
    return pl.pallas_call(
        kernel,
        grid=(s,),
        in_specs=in_specs,
        out_specs=pl.BlockSpec((1, tall, width), lambda i: (i, 0, 0)),
        out_shape=jax.ShapeDtypeStruct((s, tall, width), bf16),
        scratch_shapes=[pltpu.VMEM((local * cap, rows), bf16)],
        compiler_params=pltpu.CompilerParams(vmem_limit_bytes=VMEM_LIMIT),
        cost_estimate=takes(17),
        name="collect",
    )(*args)


MESH = pl.DeviceIdType.MESH
EXTRA = 64


def places():
    chip, core, z = lax.axis_index("xy"), lax.axis_index("core"), lax.axis_index("hs")
    x, y = chip % 2, chip // 2
    return chip, core, z, y * 2 + (1 - x), (1 - y) * 2 + x, (1 - y) * 2 + (1 - x)


def greet(peers):
    barrier = pltpu.get_barrier_semaphore()
    for peer in peers:
        pl.semaphore_signal(barrier, inc=1, device_id=peer, device_id_type=MESH)
    pl.semaphore_wait(barrier, len(peers))


def remote(src, dst, send, recv, peer):
    return pltpu.make_async_remote_copy(
        src_ref=src, dst_ref=dst, send_sem=send, recv_sem=recv, device_id=peer, device_id_type=MESH
    )


def block(q, size):
    return pl.ds(pl.multiple_of(q * size, 16), size)


def weight_sum(grads, given, half, land, out_ref, csend, crecv, send, recv):
    chip, core, z, cx, cy, cd = places()
    other = 1 - core
    c_peer = (chip, other, z)
    chips = (cx, cy, cd)
    count = grads.shape[0] // 2
    piece = count // 4

    to_core = remote(grads.at[block(other, count)], given, csend.at[0], crecv.at[0], c_peer)
    scatter = [
        remote(half.at[block(c, piece)], land.at[i], send.at[i], recv.at[i], (c, core, z))
        for i, c in enumerate(chips)
    ]

    def share():
        to_core.wait_recv()
        half[...] = (grads[block(core, count)].astype(f32) + given[...].astype(f32)).astype(bf16)
        for i in (2, 0, 1):
            scatter[i].start()

    def place(c, k):
        return pl.ds(pl.multiple_of(k * count + c * piece, 16), piece)

    def give(number, c, k, sems, peer):
        return remote(out_ref.at[place(c, k)], out_ref.at[place(c, k)], *sems(number), peer)

    def chip_sems(i):
        return send.at[3 + i], recv.at[3 + i]

    def core_sems(i):
        return csend.at[1 + i], crecv.at[1 + i]

    gather = [give(i, chip, core, chip_sems, (c, core, z)) for i, c in enumerate(chips)]
    over = [give(i, c, core, core_sems, c_peer) for i, c in enumerate((*chips, chip))]

    def give_back():
        done = half[block(chip, piece)].astype(f32)
        for i in range(3):
            scatter[i].wait_recv()
            done = done + land[i].astype(f32)
        out_ref[place(chip, core)] = done.astype(bf16)
        for i in (2, 0, 1):
            gather[i].start()
        over[3].start()

    def end():
        for i, c in enumerate(chips):
            give(i, c, core, chip_sems, (c, core, z)).wait_recv()
            over[i].start()
        for i, c in enumerate((*chips, chip)):
            give(i, c, other, core_sems, c_peer).wait_recv()
        for copy in (to_core, *scatter, *gather, *over):
            copy.wait_send()

    return to_core.start, share, give_back, end


def weight_sum_scratch(tall, width):
    dma = pltpu.SemaphoreType.DMA
    return [
        pltpu.VMEM((tall, width), bf16),
        pltpu.VMEM((tall // 2, width), bf16),
        pltpu.VMEM((tall // 2, width), bf16),
        pltpu.VMEM((3, tall // 8, width), bf16),
        dma((5,)),
        dma((5,)),
        dma((6,)),
        dma((6,)),
    ]


def gather_spread_kernel(
    own_ref,
    slots_ref,
    router_ref,
    grad_ref,
    x_ref,
    sw_ref,
    slot_ref,
    grad_all_ref,
    held,
    pick,
    xbuf,
    send,
    recv,
    copied,
    zsend,
    zrecv,
):
    chip, core, z, cx, cy, cd = places()
    other = 1 - core
    x_peer, y_peer, c_peer = (cx, core, z), (cy, core, z), (chip, other, z)
    tall = held.shape[1]
    half = tall // 2
    local, rows = slot_ref.shape[1:]
    me = chip * 2 + core
    top, low = pl.ds(0, half), pl.ds(half, half)

    def at(c, k):
        return c * 2 + k

    def move(number, src_slot, part, peer):
        return remote(
            held.at[src_slot, part], held.at[src_slot, part], send.at[number], recv.at[number], peer
        )

    whole = pl.ds(0, tall)
    z_peers = [(chip, core, (z + i) % 4) for i in (1, 2, 3)]
    greet([x_peer, y_peer, c_peer, *z_peers])
    quarter = grad_ref.shape[0]

    def grad_copy(i, q):
        return remote(
            grad_ref, grad_all_ref.at[block(q, quarter)], zsend.at[i], zrecv.at[i], z_peers[i]
        )

    held[me, :rows] = own_ref[...]
    held[me, rows:] = jnp.zeros((EXTRA, own_ref.shape[1]), bf16)
    held[me, rows:, :rows] = slots_ref[...]
    x_top, x_low = move(0, me, top, x_peer), move(1, me, low, x_peer)
    y_low, y_top = move(2, me, low, y_peer), move(3, me, top, y_peer)
    to_core = move(4, me, whole, c_peer)
    relay_top, relay_low = move(5, at(cx, core), top, y_peer), move(6, at(cy, core), low, x_peer)
    pass_x, pass_y = move(7, at(cx, core), whole, c_peer), move(8, at(cy, core), whole, c_peer)
    pass_d = move(9, at(cd, core), whole, c_peer)
    for copy in (x_top, y_low, x_low, y_top, to_core, *[grad_copy(i, z) for i in (1, 0, 2)]):
        copy.start()
    grad_all_ref[block(z, quarter)] = grad_ref[...]

    def arrived(number, slot, part):
        move(number, slot, part, c_peer).wait_recv()

    number = lax.broadcasted_iota(jnp.int32, (CAP, rows), 0)
    first = me * local
    line = lax.broadcasted_iota(jnp.int32, (local, EXTRA), 0)
    column = lax.broadcasted_iota(jnp.int32, (local, EXTRA), 1)
    chosen = (column == line + first).astype(f32).astype(bf16)

    def out_copy(t, src):
        return pltpu.make_async_copy(xbuf.at[t % 2], x_ref.at[src], copied.at[t % 2])

    def step(t, carry):
        @pl.when(t == 1)
        def _():
            arrived(4, at(chip, other), whole)

        @pl.when(t == 2)
        def _():
            arrived(0, at(cx, core), top)
            relay_top.start()
            arrived(2, at(cy, core), low)
            relay_low.start()
            arrived(1, at(cx, core), low)
            pass_x.start()

        @pl.when(t == 3)
        def _():
            arrived(3, at(cy, core), top)
            pass_y.start()
            arrived(7, at(cx, other), whole)

        @pl.when(t == 5)
        def _():
            arrived(8, at(cy, other), whole)

        @pl.when(t == 6)
        def _():
            arrived(5, at(cd, core), top)
            arrived(6, at(cd, core), low)
            pass_d.start()

        @pl.when(t == 7)
        def _():
            arrived(9, at(cd, other), whole)

        x, y = (chip % 2 + (t // 2) % 2) % 2, (chip // 2 + t // 4) % 2
        src = (y * 2 + x) * 2 + (core + t % 2) % 2
        slots = nn(chosen, held[src, rows:, :rows]).astype(jnp.int32)
        slot_ref[src] = slots
        logits = nt(router_ref[...], held[src, :rows])
        raised = jnp.exp(logits - jnp.max(logits, axis=0, keepdims=True))
        gates = raised / jnp.sum(raised, axis=0, keepdims=True)
        for e in range(local):
            mask = slots[e : e + 1, :] == number
            pick[e * CAP : (e + 1) * CAP, :] = mask.astype(f32).astype(bf16)
            sw_ref[e, pl.ds(pl.multiple_of(src * CAP, 8), CAP), :] = jnp.sum(
                jnp.where(mask, gates[e : e + 1, :], 0.0), axis=1, keepdims=True
            )

        @pl.when(t >= 2)
        def _():
            out_copy(t, src).wait()

        xbuf[t % 2] = nn(pick[...], held[src, :rows]).astype(bf16).reshape(xbuf.shape[1:])
        out_copy(t, src).start()
        return carry

    lax.fori_loop(0, 8, step, 0)
    out_copy(0, me).wait()
    out_copy(1, me).wait()
    for i in range(3):
        grad_copy(i, (z + 3 - i) % 4).wait_recv()
        grad_copy(i, z).wait_send()
    for copy in (x_top, x_low, y_low, y_top, to_core, relay_top, relay_low, pass_x, pass_y, pass_d):
        copy.wait_send()


def gather_spread(own, slots, router_t, grad_quarter, local, ep_count):
    rows, width = own.shape
    tall = rows + EXTRA
    vmem = pl.BlockSpec(memory_space=pltpu.VMEM)
    return pl.pallas_call(
        gather_spread_kernel,
        in_specs=[vmem] * 4,
        out_specs=[pl.BlockSpec(memory_space=pl.ANY), vmem, vmem, vmem],
        out_shape=[
            jax.ShapeDtypeStruct((ep_count, local, CAP, width), bf16),
            jax.ShapeDtypeStruct((local, ep_count * CAP, 1), f32),
            jax.ShapeDtypeStruct((ep_count, local, rows), jnp.int32),
            jax.ShapeDtypeStruct((width, rows), bf16),
        ],
        scratch_shapes=[
            pltpu.VMEM((ep_count, tall, width), bf16),
            pltpu.VMEM((local * CAP, rows), bf16),
            pltpu.VMEM((2, local, CAP, width), bf16),
            pltpu.SemaphoreType.DMA((10,)),
            pltpu.SemaphoreType.DMA((10,)),
            pltpu.SemaphoreType.DMA((2,)),
            pltpu.SemaphoreType.DMA((3,)),
            pltpu.SemaphoreType.DMA((3,)),
        ],
        compiler_params=pltpu.CompilerParams(
            vmem_limit_bytes=VMEM_LIMIT, collective_id=0, has_side_effects=True
        ),
        cost_estimate=takes(62),
        name="gather_spread",
    )(own, slots, router_t, grad_quarter)


def front_kernel(
    x_ref,
    gain_ref,
    wq_ref,
    wk_ref,
    wv_ref,
    wo_ref,
    ffn_gain_ref,
    doc_ref,
    doc_column_ref,
    cos_ref,
    sin_ref,
    normed1_ref,
    q_ref,
    k_ref,
    v_ref,
    probs_ref,
    attended_ref,
    out_ref,
    residual_ref,
    normed2_ref,
    shared,
    beside,
    esend,
    erecv,
    asend,
    arecv,
    zsend,
    zrecv,
    send,
    recv,
    csend,
    crecv,
):
    chip, core, z, cx, cy, cd = places()
    other = 1 - core
    odd = z % 2
    c_peer = (chip, other, z)
    chips = (cx, cy, cd)
    z_peers = [(chip, core, (z + i) % 4) for i in (1, 2, 3)]
    pair = (chip, core, z + 1 - 2 * odd)
    rows, width = x_ref.shape
    quarter = wq_ref.shape[0]
    whole = HEAD_DIM * (quarter // HEAD_DIM)
    spare = quarter - whole
    greet([c_peer, *[(c, core, z) for c in chips], *z_peers])

    full_rows = pl.ds(pl.multiple_of(odd * spare, 16), whole)
    half_rows = pl.ds(pl.multiple_of((1 - odd) * whole, 16), spare)
    for i, ref in enumerate((wq_ref, wk_ref, wv_ref)):
        shared[i * spare : (i + 1) * spare] = ref[half_rows]
    trade = remote(shared, beside, esend, erecv, pair)
    trade.start()

    share, lanes = quarter // 4, width // 2
    my_lanes = pl.ds(pl.multiple_of(core * lanes, 128), lanes)

    def piece(c):
        return pl.ds(pl.multiple_of(c * share, 16), share)

    out_z = [
        remote(
            wo_ref.at[piece(chip), my_lanes],
            out_ref.at[z, piece(chip), my_lanes],
            zsend.at[i],
            zrecv.at[i],
            peer,
        )
        for i, peer in enumerate(z_peers)
    ]
    for i in (1, 0, 2):
        out_z[i].start()
    behind = [(z + 3 - i) % 4 for i in range(3)]

    def out_chip(i, j, c):
        at = out_ref.at[behind[i], piece(c), my_lanes]
        return remote(at, at, send.at[3 * i + j], recv.at[3 * i + j], (chips[j], core, z))

    def out_core(i, k):
        half = pl.ds(pl.multiple_of(k * lanes, 128), lanes)
        at = out_ref.at[behind[i], :, half]
        return remote(at, at, csend.at[i], crecv.at[i], c_peer)

    x = x_ref[...].astype(f32)
    rms1 = lax.rsqrt(jnp.sum(x * x, axis=-1, keepdims=True) * (1.0 / width) + EPS)
    normed1_ref[...] = (x * rms1 * gain_ref[...]).astype(bf16)
    out_ref[z] = wo_ref[...]

    cosine, sine = cos_ref[...], sin_ref[...]
    half_dim = HEAD_DIM // 2
    scale = 1.0 / math.sqrt(HEAD_DIM)
    row = lax.broadcasted_iota(jnp.int32, (rows, rows), 0)
    column = lax.broadcasted_iota(jnp.int32, (rows, rows), 1)
    allowed = (row >= column) & (doc_column_ref[...] == doc_ref[...])

    def turn(pre):
        a, b = pre[:half_dim], pre[half_dim:]
        return (
            jnp.concatenate([a * cosine - b * sine, b * cosine + a * sine], axis=0).astype(bf16)
        )

    def attend(h):
        scores = jnp.where(allowed, tn(q_ref[h], k_ref[h]) * scale, -1e30)
        raised = jnp.exp(scores - jnp.max(scores, axis=-1, keepdims=True))
        probs = raised * (1.0 / jnp.sum(raised, axis=-1, keepdims=True))
        probs_ref[h] = probs
        return nt(v_ref[h], probs.astype(bf16)).astype(bf16)

    def project(at):
        return [nt(ref[at], normed1_ref[...]) for ref in (wq_ref, wk_ref, wv_ref)]

    q, k, v = project(full_rows)
    heads = whole // HEAD_DIM
    for h in range(heads):
        at = slice(h * HEAD_DIM, (h + 1) * HEAD_DIM)
        q_ref[h], k_ref[h], v_ref[h] = turn(q[at]), turn(k[at]), v[at].astype(bf16)

    def attended_copy(number, start, size):
        at = attended_ref.at[pl.ds(pl.multiple_of(start, 16), size)]
        return lambda i: remote(
            at, at, asend.at[number, i], arecv.at[number, i], z_peers[i]
        )

    mine = z * quarter
    copies = []
    for h in range(heads):
        start = mine + odd * spare + h * HEAD_DIM
        attended_ref[pl.ds(pl.multiple_of(start, 16), HEAD_DIM)] = attend(h)
        copy = attended_copy(h, start, HEAD_DIM)
        copies += [copy(1), copy(0), copy(2)]
        for one in copies[-3:]:
            one.start()
        if h == 0:
            for i in range(3):
                out_z[i].wait_recv()
                for j in (2, 0, 1):
                    out_chip(i, j, chip).start()

    trade.wait_recv()
    for i, (ref, to) in enumerate(((wq_ref, q_ref), (wk_ref, k_ref), (wv_ref, v_ref))):
        normed1 = normed1_ref[...]
        here = nt(ref[half_rows], normed1)
        there = nt(beside[i * spare : (i + 1) * spare], normed1)
        first = jnp.where(odd == 1, there, here)
        second = jnp.where(odd == 1, here, there)
        both = jnp.concatenate([first, second], axis=0)
        to[heads] = both.astype(bf16) if to is v_ref else turn(both)
    last = attend(heads)
    last = jnp.where(odd == 1, last[spare:], last[:spare])
    start = mine + (1 - odd) * whole
    attended_ref[pl.ds(pl.multiple_of(start, 16), spare)] = last
    copy = attended_copy(heads, start, spare)
    copies += [copy(1), copy(0), copy(2)]
    for one in copies[-3:]:
        one.start()

    for i in range(3):
        for j in range(3):
            out_chip(i, j, chips[j]).wait_recv()
        out_core(i, core).start()
    for i in range(3):
        from_z = (z + 3 - i) % 4
        from_odd = from_z % 2
        for h in range(heads):
            attended_copy(h, from_z * quarter + from_odd * spare + h * HEAD_DIM, HEAD_DIM)(i).wait_recv()
        attended_copy(heads, from_z * quarter + (1 - from_odd) * whole, spare)(i).wait_recv()
        out_core(i, other).wait_recv()
    attended = attended_ref[...].T
    residual = x_ref[...].astype(f32) + nt(attended, out_ref[...].reshape(width, width))
    residual_ref[...] = residual
    rms2 = lax.rsqrt(jnp.sum(residual * residual, axis=-1, keepdims=True) * (1.0 / width) + EPS)
    normed2_ref[...] = (residual * rms2 * ffn_gain_ref[...]).astype(bf16)
    for one in (trade, *out_z, *copies):
        one.wait_send()
    for i in range(3):
        for j in range(3):
            out_chip(i, j, chip).wait_send()
        out_core(i, core).wait_send()


def front(x, gain, wq, wk, wv, wo, ffn_gain, doc, tables):
    rows, width = x.shape
    quarter = wq.shape[0]
    heads = -(-quarter // HEAD_DIM)
    spare = quarter % HEAD_DIM
    vmem = pl.BlockSpec(memory_space=pltpu.VMEM)
    dma = pltpu.SemaphoreType.DMA
    low = lambda *shape: jax.ShapeDtypeStruct(shape, bf16)
    return pl.pallas_call(
        front_kernel,
        in_specs=[vmem] * 11,
        out_specs=[vmem] * 9,
        out_shape=[
            low(rows, width),
            *[low(heads, HEAD_DIM, rows)] * 3,
            jax.ShapeDtypeStruct((heads, rows, rows), f32),
            low(width, rows),
            low(4, quarter, width),
            jax.ShapeDtypeStruct((rows, width), f32),
            low(rows, width),
        ],
        scratch_shapes=[
            pltpu.VMEM((3 * spare, width), bf16),
            pltpu.VMEM((3 * spare, width), bf16),
            dma,
            dma,
            dma((heads, 3)),
            dma((heads, 3)),
            dma((3,)),
            dma((3,)),
            dma((9,)),
            dma((9,)),
            dma((3,)),
            dma((3,)),
        ],
        compiler_params=pltpu.CompilerParams(
            vmem_limit_bytes=VMEM_LIMIT, collective_id=1, has_side_effects=True
        ),
        cost_estimate=takes(50),
        name="front",
    )(x, gain[None, :], wq, wk, wv, wo, ffn_gain[None, :], doc, doc.T, *tables)


def collect_sum_kernel(
    y_ref,
    slot_ref,
    gsw_ref,
    mine_ref,
    shared_gate_ref,
    shared_up_ref,
    shared_down_ref,
    forward_ref,
    out_ref,
    sum_ref,
    passed_ref,
    pick,
    ybuf,
    stage,
    given,
    sums,
    relay,
    land,
    zland,
    total,
    copied,
    core_send,
    core_recv,
    send,
    recv,
    zsend,
    zrecv,
    grads,
    *more,
):
    chip, core, z, cx, cy, cd = places()
    other = 1 - core
    x_peer, y_peer, c_peer = (cx, core, z), (cy, core, z), (chip, other, z)
    z_peers = [(chip, core, (z + i) % 4) for i in (1, 2, 3)]
    local, rows = slot_ref.shape[1:]
    tall = out_ref.shape[0]
    me = chip * 2 + core
    number = lax.broadcasted_iota(jnp.int32, (CAP, rows), 0)
    row = lax.broadcasted_iota(jnp.int32, (EXTRA, rows), 0)

    greet([x_peer, y_peer, c_peer, (cd, core, z), *z_peers])

    def sequence(t):
        p = t // 2
        x, y = (chip % 2 + 1 + p // 2) % 2, (chip // 2 + 1 + p % 2) % 2
        return (y * 2 + x) * 2 + (core + 1 + t % 2) % 2

    def in_copy(t):
        return pltpu.make_async_copy(y_ref.at[sequence(t)], ybuf.at[t % 2], copied.at[t % 2])

    def to_core(p):
        return remote(stage.at[p], given.at[p], core_send.at[p], core_recv.at[p], c_peer)

    units = 3
    unit = tall // units
    half, part = unit // 2, unit // 4

    def top(u):
        return pl.ds(u * unit, half)

    def low(u):
        return pl.ds(u * unit + half, half)

    def over(u, number, src, dst, peer):
        return remote(src, dst, send.at[u, number], recv.at[u, number], peer)

    far_top = [over(u, 0, sums.at[0, top(u)], relay.at[u, 0], x_peer) for u in range(units)]
    far_low = [over(u, 1, sums.at[0, low(u)], relay.at[u, 1], y_peer) for u in range(units)]
    x_top = [over(u, 2, sums.at[1, top(u)], land.at[0, top(u)], x_peer) for u in range(units)]
    x_low = [over(u, 3, sums.at[1, low(u)], land.at[0, low(u)], x_peer) for u in range(units)]
    y_low = [over(u, 4, sums.at[2, low(u)], land.at[1, low(u)], y_peer) for u in range(units)]
    y_top = [over(u, 5, sums.at[2, top(u)], land.at[1, top(u)], y_peer) for u in range(units)]

    in_copy(0).start()
    passed_ref[...] = forward_ref[...]
    start, share, give_back, end = weight_sum(grads, *more[:3], sum_ref, *more[3:])
    at = 0
    for ref in (shared_gate_ref, shared_up_ref, shared_down_ref):
        grads[at : at + ref.shape[0]] = ref[...]
        at += ref.shape[0]
    grads[at:] = jnp.zeros((grads.shape[0] - at, grads.shape[1]), bf16)
    start()

    def step(t, carry):
        @pl.when(t < 7)
        def _():
            in_copy(t + 1).start()

        p, s = t // 2, sequence(t)
        probs = jnp.zeros((EXTRA, rows), f32)
        for e in range(local):
            mask = slot_ref[s, e : e + 1, :] == number
            pick[e * CAP : (e + 1) * CAP, :] = mask.astype(f32).astype(bf16)
            column = gsw_ref[e, pl.ds(pl.multiple_of(s * CAP, 8), CAP), :]
            line = jnp.sum(jnp.where(mask, column, 0.0), axis=0, keepdims=True)
            probs = jnp.where(row == me * local + e, line, probs)
        in_copy(t).wait()
        back = tn(pick[...], ybuf[t % 2].reshape(local * CAP, -1))

        @pl.when(t % 2 == 0)
        def _():
            stage[p, :rows] = back.astype(bf16)
            stage[p, rows:] = jnp.zeros((tall - rows, back.shape[1]), bf16)
            stage[p, rows:, :rows] = probs.astype(bf16)
            to_core(p).start()

        @pl.when(t % 2 == 1)
        def _():
            to_core(p).wait_recv()
            sums[p, :rows] = (back + given[p, :rows].astype(f32)).astype(bf16)
            sums[p, rows:] = given[p, rows:]
            sums[p, rows:, :rows] = (probs + given[p, rows:, :rows].astype(f32)).astype(bf16)

        @pl.when(t == 1)
        def _():
            far_top[0].start()
            far_low[0].start()

        @pl.when(t == 3)
        def _():
            x_top[0].start()

        @pl.when(t == 5)
        def _():
            y_low[0].start()
            far_top[1].start()
            far_low[1].start()

        return carry

    lax.fori_loop(0, 8, step, 0)
    def relayed(u):
        far_low[u].wait_recv()
        at = slice(u * unit + half, (u + 1) * unit)
        sums[1, at] = (sums[1, at].astype(f32) + relay[u, 1].astype(f32)).astype(bf16)
        x_low[u].start()
        far_top[u].wait_recv()
        at = slice(u * unit, u * unit + half)
        sums[2, at] = (sums[2, at].astype(f32) + relay[u, 0].astype(f32)).astype(bf16)
        y_top[u].start()

    def block_of(u, q):
        return pl.ds(pl.multiple_of(u * unit + q * part, 16), part)

    def z_sems(u, number):
        return zsend.at[u, number], zrecv.at[u, number]

    scatter = [
        [
            remote(
                total.at[block_of(u, (z + i) % 4)],
                zland.at[u, i - 1],
                *z_sems(u, i - 1),
                z_peers[i - 1],
            )
            for i in (1, 2, 3)
        ]
        for u in range(units)
    ]

    def back_copy(u, q, i):
        at = out_ref.at[block_of(u, q)]
        return remote(at, at, *z_sems(u, 2 + i), z_peers[i - 1])

    def landed(u):
        for copy in (x_top[u], y_top[u], x_low[u], y_low[u]):
            copy.wait_recv()
        at = slice(u * unit, (u + 1) * unit)
        added = sums[3, at].astype(f32) + land[0, at].astype(f32) + land[1, at].astype(f32)
        ours = min(rows, (u + 1) * unit) - u * unit
        if ours == unit:
            total[at] = (added + mine_ref[at].astype(f32)).astype(bf16)
        else:
            here = slice(u * unit, u * unit + ours)
            total[here] = (added[:ours] + mine_ref[here].astype(f32)).astype(bf16)
            total[u * unit + ours : (u + 1) * unit] = added[ours:].astype(bf16)
        for i in (1, 0, 2):
            scatter[u][i].start()

    def summed(u):
        done = total[block_of(u, z)].astype(f32)
        for i in range(3):
            scatter[u][i].wait_recv()
            done = done + zland[u, i].astype(f32)
        out_ref[block_of(u, z)] = done.astype(bf16)
        for i in (2, 1, 3):
            back_copy(u, z, i).start()

    relayed(0)
    x_top[1].start()
    y_low[1].start()
    far_top[2].start()
    far_low[2].start()
    relayed(1)
    x_top[2].start()
    y_low[2].start()
    landed(0)
    relayed(2)
    share()
    landed(1)
    summed(0)
    landed(2)
    summed(1)
    give_back()
    summed(2)
    end()
    for u in range(units):
        for i in (1, 2, 3):
            back_copy(u, (z + 4 - i) % 4, i).wait_recv()
    for u in range(units):
        for copy in (far_top[u], far_low[u], x_top[u], x_low[u], y_low[u], y_top[u], *scatter[u]):
            copy.wait_send()
        for i in (1, 2, 3):
            back_copy(u, z, i).wait_send()
    for p in range(4):
        to_core(p).wait_send()


def collect_sum(y, slot, gsw, mine, forward, *shared):
    s, local, cap, width = y.shape
    rows = slot.shape[2]
    tall = rows + EXTRA
    dma = pltpu.SemaphoreType.DMA
    weights = 128 * (-(-sum(a.shape[0] for a in shared) // 128))
    vmem = pl.BlockSpec(memory_space=pltpu.VMEM)
    return pl.pallas_call(
        collect_sum_kernel,
        in_specs=[pl.BlockSpec(memory_space=pl.ANY)] + [vmem] * 7,
        out_specs=[vmem, vmem, vmem],
        out_shape=[
            jax.ShapeDtypeStruct((tall, width), bf16),
            jax.ShapeDtypeStruct((weights, width), bf16),
            jax.ShapeDtypeStruct(forward.shape, bf16),
        ],
        scratch_shapes=[
            pltpu.VMEM((local * cap, rows), bf16),
            pltpu.VMEM((2, local, cap, width), bf16),
            pltpu.VMEM((4, tall, width), bf16),
            pltpu.VMEM((4, tall, width), bf16),
            pltpu.VMEM((4, tall, width), bf16),
            pltpu.VMEM((3, 2, tall // 6, width), bf16),
            pltpu.VMEM((2, tall, width), bf16),
            pltpu.VMEM((3, 3, tall // 12, width), bf16),
            pltpu.VMEM((tall, width), bf16),
            dma((2,)),
            dma((4,)),
            dma((4,)),
            dma((3, 6)),
            dma((3, 6)),
            dma((3, 6)),
            dma((3, 6)),
            *weight_sum_scratch(weights, width),
        ],
        compiler_params=pltpu.CompilerParams(
            vmem_limit_bytes=VMEM_LIMIT, collective_id=2, has_side_effects=True
        ),
        cost_estimate=takes(131),
        name="collect_sum",
    )(y, slot, gsw, mine, *shared, forward)


def back_kernel(
    sums_ref,
    residual_ref,
    normed2_ref,
    grad_ref,
    router_ref,
    ffn_gain_ref,
    out_ref,
    q_ref,
    k_ref,
    v_ref,
    probs_ref,
    cos_ref,
    sin_ref,
    wq_ref,
    wk_ref,
    wv_ref,
    normed_ref,
    attended_ref,
    x_ref,
    gain_ref,
    tokens_ref,
    early_ref,
    late_ref,
    dq_ref,
    dk_ref,
    dv_ref,
    back_t,
    low_t,
    part,
    low_part,
    zland,
    mine,
    theirs,
    zsend,
    zrecv,
    lsend,
    lrecv,
    *more,
):
    chip, core, z, cx, cy, cd = places()
    odd = z % 2
    c_peer = (chip, 1 - core, z)
    z_peers = [(chip, core, (z + i) % 4) for i in (1, 2, 3)]
    quarter, width = wq_ref.shape
    rows = x_ref.shape[1]
    early, late = more[0], more[8]
    experts = router_ref.shape[0]
    whole = HEAD_DIM * (quarter // HEAD_DIM)
    spare = quarter - whole
    heads = whole // HEAD_DIM
    greet([c_peer, *[(c, core, z) for c in (cx, cy, cd)], *z_peers])

    logits = nt(router_ref[...], normed2_ref[...])
    raised = jnp.exp(logits - jnp.max(logits, axis=0, keepdims=True))
    gates = raised / jnp.sum(raised, axis=0, keepdims=True)
    grad_probs = sums_ref[rows:, :rows].astype(f32)
    grad_logits = gates * (grad_probs - jnp.sum(grad_probs * gates, axis=0, keepdims=True))
    grad_logits = grad_logits.astype(bf16)
    grad_router = nn(grad_logits, normed2_ref[...])
    grad_normed2 = sums_ref[:rows].astype(f32) + tn(grad_logits, router_ref[...])
    residual = residual_ref[...]
    rms2 = lax.rsqrt(jnp.sum(residual * residual, axis=-1, keepdims=True) * (1.0 / width) + EPS)
    grad_ffn = jnp.sum(grad_normed2 * residual * rms2, axis=0, keepdims=True)
    u = grad_normed2 * ffn_gain_ref[...]
    mean2 = jnp.sum(u * residual, axis=-1, keepdims=True) * (1.0 / width)
    added = rms2 * u - residual * (rms2 * rms2 * rms2 * mean2)
    back_t[...] = added.T + grad_ref[...].astype(f32)
    low_t[...] = back_t[...].astype(bf16)
    own = block(z, quarter)
    early[:quarter] = nt(low_t[own], attended_ref[...]).astype(bf16)
    early[quarter:] = grad_router.astype(bf16)
    start, share, give_back, end = weight_sum(early, *more[1:4], early_ref, *more[4:8])
    start()

    cosine, sine = cos_ref[...], sin_ref[...]
    half_dim = HEAD_DIM // 2
    scale = 1.0 / math.sqrt(HEAD_DIM)

    def turn_back(v):
        a, b = v[:half_dim] * scale, v[half_dim:] * scale
        turned = [a * cosine + b * sine, b * cosine - a * sine]
        return jnp.concatenate(turned, axis=0).astype(bf16)

    first_lane = z * quarter + odd * spare
    shared_lane = z * quarter + (1 - odd) * whole - odd * spare
    for h in range(heads + 1):
        lane = first_lane + h * HEAD_DIM if h < heads else shared_lane
        lane = pl.ds(pl.multiple_of(lane, HEAD_DIM), HEAD_DIM)
        grad_attended = tn(out_ref[:, lane], low_t[...]).astype(bf16)
        probs = probs_ref[h]
        grad_p = tn(grad_attended, v_ref[h])
        grad_v = nn(grad_attended, probs.astype(bf16)).astype(bf16)
        delta = jnp.sum(probs * grad_p, axis=-1, keepdims=True)
        grad_s = (probs * (grad_p - delta)).astype(bf16)
        grad_q = turn_back(nt(k_ref[h], grad_s))
        grad_k = turn_back(nn(q_ref[h], grad_s))
        for ref, value in ((dq_ref, grad_q), (dk_ref, grad_k), (dv_ref, grad_v)):
            if h < heads:
                at = pl.ds(pl.multiple_of(odd * spare + h * HEAD_DIM, 16), HEAD_DIM)
                ref[at] = value
            else:
                at = pl.ds(pl.multiple_of((1 - odd) * whole, 16), spare)
                ref[at] = jnp.where(odd == 1, value[spare:], value[:spare])
        if h == 0:
            share()

    x_all = x_ref[...].astype(f32)
    rms1 = lax.rsqrt(jnp.sum(x_all * x_all, axis=0, keepdims=True) * (1.0 / width) + EPS)
    part[...] = tn(wq_ref[...], dq_ref[...])
    part[...] += tn(wk_ref[...], dk_ref[...])
    part[...] += tn(wv_ref[...], dv_ref[...])
    low_part[...] = part[...].astype(bf16)
    to_z = [
        remote(
            low_part.at[block((z + i) % 4, quarter)],
            zland.at[i - 1],
            zsend.at[i - 1],
            zrecv.at[i - 1],
            z_peers[i - 1],
        )
        for i in (1, 2, 3)
    ]
    few_to_z = [
        remote(mine, theirs.at[i], lsend.at[i], lrecv.at[i], peer) for i, peer in enumerate(z_peers)
    ]
    along = part[...] * x_ref[...].astype(f32)
    mine[...] = jnp.zeros(mine.shape, f32)
    mine[0:1, :rows] = jnp.sum(along * gain_ref[...], axis=0, keepdims=True)
    mine[:, rows:] = nt(jnp.ones((8, rows), bf16), (along * rms1).astype(bf16))
    for copy in few_to_z:
        copy.start()
    for i in (1, 0, 2):
        to_z[i].start()

    give_back()
    normed = normed_ref[...]
    for i, ref in enumerate((dq_ref, dk_ref, dv_ref)):
        late[i * quarter : (i + 1) * quarter] = nn(ref[...], normed).astype(bf16)
    at = 3 * quarter
    for copy in few_to_z:
        copy.wait_recv()
    few = mine[...] + theirs[0] + theirs[1] + theirs[2]
    late[at:] = jnp.zeros((late.shape[0] - at, width), bf16)
    line = lax.broadcasted_iota(jnp.int32, (16, width), 0)
    gains = jnp.where(line == 0, few[0:1, rows:], jnp.where(line == 1, grad_ffn, 0.0))
    late[at : at + 16] = gains.astype(bf16)

    start, share, give_back, end_late = weight_sum(late, *more[9:12], late_ref, *more[12:16])
    start()
    share()

    total = part[own]
    for i in range(3):
        to_z[i].wait_recv()
        total = total + zland[i].astype(f32)
    x = x_ref[own].astype(f32)
    mean = few[0:1, :rows] * (1.0 / width)
    tokens_ref[...] = back_t[own] + rms1 * gain_ref[own] * total - x * (rms1 * rms1 * rms1 * mean)

    give_back()
    end()
    end_late()
    for copy in (*to_z, *few_to_z):
        copy.wait_send()


def back(*args):
    quarter, width = args[13].shape
    rows = args[1].shape[0]
    early, late = quarter + args[4].shape[0], 128 * (3 * quarter // 128 + 1)
    vmem = pl.BlockSpec(memory_space=pltpu.VMEM)
    dma = pltpu.SemaphoreType.DMA
    return pl.pallas_call(
        back_kernel,
        in_specs=[vmem] * len(args),
        out_specs=[vmem] * 3,
        out_shape=[
            jax.ShapeDtypeStruct((quarter, rows), f32),
            jax.ShapeDtypeStruct((early, width), bf16),
            jax.ShapeDtypeStruct((late, width), bf16),
        ],
        scratch_shapes=[
            *[pltpu.VMEM((quarter, rows), bf16)] * 3,
            pltpu.VMEM((width, rows), f32),
            pltpu.VMEM((width, rows), bf16),
            pltpu.VMEM((width, rows), f32),
            pltpu.VMEM((width, rows), bf16),
            pltpu.VMEM((3, quarter, rows), bf16),
            pltpu.VMEM((8, rows + width), f32),
            pltpu.VMEM((3, 8, rows + width), f32),
            dma((3,)),
            dma((3,)),
            dma((3,)),
            dma((3,)),
            *weight_sum_scratch(early, width),
            *weight_sum_scratch(late, width),
        ],
        compiler_params=pltpu.CompilerParams(
            vmem_limit_bytes=VMEM_LIMIT, collective_id=3, has_side_effects=True
        ),
        cost_estimate=takes(90),
        name="back",
    )(*args)


def widen_kernel(early_ref, late_ref, shared_ref, *out_refs):
    quarter = out_refs[0].shape[0]
    for i in range(3):
        out_refs[i][...] = late_ref[i * quarter : (i + 1) * quarter].astype(f32)
    out_refs[3][...] = early_ref[:quarter].astype(f32)
    out_refs[4][...] = early_ref[quarter:].astype(f32)
    out_refs[5][...] = late_ref[3 * quarter : 3 * quarter + 8].astype(f32)
    size = out_refs[6].shape[0]
    for i in range(3):
        out_refs[6 + i][...] = shared_ref[i * size : (i + 1) * size].astype(f32)


def widen(early, late, shared, quarter, hidden_units):
    width = early.shape[1]
    step = width // 5
    tall = [quarter] * 4 + [early.shape[0] - quarter, 8] + [hidden_units] * 3
    blocks = lambda lines: pl.BlockSpec((lines, step), lambda i: (0, i))
    return pl.pallas_call(
        widen_kernel,
        grid=(width // step,),
        in_specs=[blocks(a.shape[0]) for a in (early, late, shared)],
        out_specs=[blocks(lines) for lines in tall],
        out_shape=[jax.ShapeDtypeStruct((lines, width), f32) for lines in tall],
        compiler_params=pltpu.CompilerParams(vmem_limit_bytes=VMEM_LIMIT),
        cost_estimate=takes(8),
        name="widen",
    )(early, late, shared)


def plain_front(
    tokens, attn_gain, query_t, key_t, value_t, attn_out, ffn_gain, documents, tables
):
    rows, width = tokens.shape
    quarter = query_t.shape[0]
    hs, hs_count = lax.axis_index("hs"), lax.axis_size("hs")
    odd = (hs % 2) == 1
    spare = -quarter % HEAD_DIM
    heads = (quarter + spare) // HEAD_DIM

    def outer(w):
        return jnp.where(odd, w[:spare], w[quarter - spare :])

    sent = jnp.concatenate([outer(query_t), outer(key_t), outer(value_t)], axis=0)
    got = lax.ppermute(sent, "hs", [(i, i ^ 1) for i in range(hs_count)])

    def widened(w, extra):
        return jnp.where(
            odd, jnp.concatenate([extra, w], axis=0), jnp.concatenate([w, extra], axis=0)
        )

    x = tokens.astype(f32)
    rms1 = lax.rsqrt(jnp.mean(x * x, axis=-1, keepdims=True) + EPS)
    normed1 = (x * rms1 * attn_gain).astype(bf16)
    shape3 = (heads, HEAD_DIM, rows)
    q, k, v = [
        ein("cd,td->ct", widened(w, got[i * spare : (i + 1) * spare]), normed1).reshape(shape3)
        for i, w in enumerate((query_t, key_t, value_t))
    ]
    q, k, v = rope(q, *tables).astype(bf16), rope(k, *tables).astype(bf16), v.astype(bf16)
    positions = jnp.arange(rows, dtype=jnp.int32)
    doc = documents[0]
    allowed = (positions[:, None] >= positions[None, :]) & (doc[:, None] == doc[None, :])
    scale = 1.0 / math.sqrt(HEAD_DIM)
    scores = jnp.where(allowed[None], ein("hdq,hdk->hqk", q, k) * scale, -1e30)
    raised = jnp.exp(scores - jnp.max(scores, axis=-1, keepdims=True))
    probs = raised / jnp.sum(raised, axis=-1, keepdims=True)
    attended = ein("hdk,hqk->hdq", v, probs.astype(bf16)).astype(bf16).reshape(-1, rows)
    attended = jnp.where(odd, attended[spare:], attended[:quarter])
    attended_t = lax.all_gather(attended, "hs", axis=0, tiled=True)
    out_t = lax.all_gather(attn_out.T, "hs", axis=0, tiled=True)
    residual = x + ein("ct,oc->to", attended_t, out_t)
    rms2 = lax.rsqrt(jnp.mean(residual * residual, axis=-1, keepdims=True) + EPS)
    normed2 = (residual * rms2 * ffn_gain).astype(bf16)
    return normed1, q, k, v, probs, attended_t, out_t, residual, normed2


def over_ep(a):
    return lax.psum(a.astype(bf16), EP).astype(f32)


def plain_back(
    sums,
    residual,
    normed2,
    grad_t,
    router_t,
    ffn_gain,
    out_t,
    q,
    k,
    v,
    probs,
    tables,
    query_t,
    key_t,
    value_t,
    normed1,
    attended_t,
    tokens,
    attn_gain,
):
    rows, width = tokens.shape
    quarter = query_t.shape[0]
    hs = lax.axis_index("hs")
    odd = (hs % 2) == 1
    spare = -quarter % HEAD_DIM
    held = quarter + spare
    col0 = hs * quarter

    def own(v):
        v = v.astype(bf16).reshape(held, rows)
        return jnp.where(odd, v[spare:], v[:quarter])

    gates = jax.nn.softmax(nt(normed2, router_t), axis=-1)
    grad_probs = sums[rows:, :rows].T.astype(f32)
    grad_logits = (
        gates * (grad_probs - jnp.sum(grad_probs * gates, axis=-1, keepdims=True))
    ).astype(bf16)
    grad_router = tn(grad_logits, normed2)
    grad_normed2 = sums[:rows].astype(f32) + dot(grad_logits, router_t)
    rms2 = lax.rsqrt(jnp.mean(residual * residual, axis=-1, keepdims=True) + EPS)
    grad_ffn_gain = jnp.sum(grad_normed2 * residual * rms2, axis=0)
    u = grad_normed2 * ffn_gain
    grad_residual = (
        grad_t.T.astype(f32)
        + rms2 * u
        - residual * rms2**3 * jnp.mean(u * residual, axis=-1, keepdims=True)
    )
    back_t = grad_residual.T
    low_t = back_t.astype(bf16)
    out_held = lax.dynamic_slice_in_dim(out_t, jnp.where(odd, col0 - spare, col0), held, 1)
    grad_attended = tn(out_held, low_t).astype(bf16).reshape(-1, HEAD_DIM, rows)
    grad_p = ein("hdq,hdk->hqk", grad_attended, v)
    grad_v = own(ein("hdq,hqk->hdk", grad_attended, probs.astype(bf16)))
    grad_s = (probs * (grad_p - jnp.sum(probs * grad_p, axis=-1, keepdims=True))).astype(bf16)
    scale = 1.0 / math.sqrt(HEAD_DIM)
    grad_q = own(rope_back(ein("hdk,hqk->hdq", k, grad_s) * scale, *tables))
    grad_k = own(rope_back(ein("hdq,hqk->hdk", q, grad_s) * scale, *tables))
    own_rows = lambda a: lax.dynamic_slice_in_dim(a, col0, quarter, 0)
    heads_sums = [
        over_ep(dot(grad_q, normed1)),
        over_ep(dot(grad_k, normed1)),
        over_ep(dot(grad_v, normed1)),
        over_ep(nt(own_rows(low_t), attended_t)),
    ]
    part = tn(query_t, grad_q) + tn(key_t, grad_k) + tn(value_t, grad_v)
    grad_n1 = lax.psum_scatter(part.astype(bf16), "hs", scatter_dimension=0, tiled=True)
    grad_n1 = grad_n1.astype(f32)
    x = tokens.T.astype(f32)
    x_own = own_rows(x)
    rms_t = lax.rsqrt(jnp.mean(x * x, axis=0, keepdims=True) + EPS)
    w1 = grad_n1 * own_rows(attn_gain)[:, None]
    mean1 = lax.psum(jnp.sum(w1 * x_own, axis=0, keepdims=True), "hs") / width
    grad_tokens = own_rows(back_t) + rms_t * w1 - x_own * rms_t**3 * mean1
    gain_own = jnp.sum(grad_n1 * x_own * rms_t, axis=1)
    gain_part = lax.dynamic_update_slice_in_dim(jnp.zeros((width,), f32), gain_own, col0, 0)
    grad_attn_gain = lax.psum(gain_part, (*EP, "hs"))
    return (
        grad_tokens,
        heads_sums,
        over_ep(grad_router),
        grad_attn_gain,
        lax.psum(grad_ffn_gain, EP),
    )


def shards(
    tokens,
    attn_gain,
    attn_query,
    attn_key,
    attn_value,
    attn_out,
    ffn_gain,
    router,
    shared_gate,
    shared_up,
    shared_down,
    expert_gate,
    expert_up,
    expert_down,
    routes,
    documents,
    out_grad,
):
    rows, width = tokens.shape
    quarter = out_grad.shape[1]
    hs = lax.axis_index("hs")
    ep_count = lax.axis_size("xy") * lax.axis_size("core")
    ep = lax.axis_index("xy") * lax.axis_size("core") + lax.axis_index("core")
    local = expert_gate.shape[0]
    experts = router.shape[1]
    small = ep_count == 8 and lax.axis_size("hs") == 4

    query_t, key_t, value_t, router_t = attn_query.T, attn_key.T, attn_value.T, router.T
    positions = jnp.arange(rows, dtype=jnp.int32)
    below = (positions[:, None] > positions[None, :]).astype(bf16)
    chosen = jnp.any(
        routes[:, :, None] == jnp.arange(experts, dtype=jnp.int32)[None, None, :], axis=1
    )
    own_slots = jnp.where(chosen, dot(below, chosen.astype(bf16)), -1.0).T.astype(bf16)
    tables = rope_tables(rows)

    if small:
        ahead = front(
            tokens, attn_gain, query_t, key_t, value_t, attn_out.T, ffn_gain, documents, tables
        )
    else:
        ahead = plain_front(
            tokens, attn_gain, query_t, key_t, value_t, attn_out, ffn_gain, documents, tables
        )
    normed1, q, k, v, probs, attended_t, out_t, residual, normed2 = ahead
    out_t = out_t.reshape(width, width)

    first = ep * local
    rolled = jnp.roll(router_t, -first, axis=0)
    gate_t, up_t = expert_gate.swapaxes(1, 2), expert_up.swapaxes(1, 2)
    weights = gate_t, up_t, expert_down
    if small:
        ex_in, slot_weight, slot, grad_t = gather_spread(
            normed2, own_slots, rolled, out_grad.T, local, ep_count
        )
        ex_out, ex_gate, ex_up, near = experts_forward(ex_in, slot_weight, *weights, grad_t)
        out_part, far, given = collect_sending(ex_out, slot, grad_t, near)
        ex_grad = spread_grad(grad_t, near, far, given, slot)
    else:
        grad_all_t = lax.all_gather(out_grad.T, (*EP, "hs"), axis=0, tiled=True)
        grad_all_t = grad_all_t.reshape(ep_count, width, rows)
        grad_t = lax.dynamic_index_in_dim(grad_all_t, ep, 0, keepdims=False)
        slot = lax.dynamic_slice_in_dim(
            lax.all_gather(own_slots, EP, axis=0), first, local, 1
        ).astype(jnp.int32)
        normed_all = lax.all_gather(normed2, EP, axis=0, tiled=True)
        ex_in, slot_weight = spread(normed_all, slot, rolled)
        ex_out, ex_gate, ex_up = experts_forward(ex_in, slot_weight, *weights)
        out_part = collect(ex_out, slot)
        ex_grad = spread(grad_all_t, slot)
    out_part = out_part.reshape(ep_count * rows, width)
    ex_back, grad_gate_t, grad_up_t, grad_expert_down, grad_slot_weight = experts_backward(
        ex_in, ex_grad, ex_gate, ex_up, slot_weight, *weights
    )

    sh_gate = dot(normed2, shared_gate)
    sh_up = dot(normed2, shared_up)
    sh_sig = jax.nn.sigmoid(sh_gate)
    sh_act = sh_gate * sh_sig
    sh_hidden = (sh_act * sh_up).astype(bf16)
    shared_part = dot(sh_hidden, shared_down)
    grad_sh = ein("dt,fd->tf", grad_t, shared_down)
    grad_sh_gate = (grad_sh * sh_up * sh_sig * (1 + sh_gate * (1 - sh_sig))).astype(bf16)
    grad_sh_up = (grad_sh * sh_act).astype(bf16)
    shared_grads = [
        ein("tf,td->fd", grad_sh_gate, normed2).astype(bf16),
        ein("tf,td->fd", grad_sh_up, normed2).astype(bf16),
        ein("tf,dt->fd", sh_hidden, grad_t).astype(bf16),
    ]
    shared_back = ein("tf,df->td", grad_sh_gate, shared_gate) + ein(
        "tf,df->td", grad_sh_up, shared_up
    )

    if small:
        back_sums, shared_sums, shared_part = collect_sum(
            ex_back, slot, grad_slot_weight, shared_back.astype(bf16), shared_part.astype(bf16), *shared_grads
        )
        grad_tokens, early, late = back(
            back_sums,
            residual,
            normed2,
            grad_t,
            router_t,
            ffn_gain[None, :],
            out_t,
            q,
            k,
            v,
            probs,
            *tables,
            query_t,
            key_t,
            value_t,
            normed1,
            attended_t,
            tokens.T,
            attn_gain[:, None],
        )
        *heads_sums, grad_router, gains, sum_gate, sum_up, sum_down = widen(
            early, late, shared_sums, quarter, shared_down.shape[0]
        )
        shared_sums = sum_gate, sum_up, sum_down
        grad_attn_gain, grad_ffn_gain = gains[0], gains[1]
    else:
        back_part = collect(ex_back, slot, grad_slot_weight, first, experts).reshape(-1, width)
        back_rows = lax.psum_scatter(back_part, EP, scatter_dimension=0, tiled=True).astype(f32)
        back_rows = jnp.concatenate([back_rows[:rows] + shared_back, back_rows[rows:]], axis=0)
        back_sums = lax.psum(back_rows.astype(bf16), "hs")
        shared_sums = [over_ep(a) for a in shared_grads]
        grad_tokens, heads_sums, grad_router, grad_attn_gain, grad_ffn_gain = plain_back(
            back_sums,
            residual,
            normed2,
            grad_t,
            router_t,
            ffn_gain,
            out_t,
            q,
            k,
            v,
            probs,
            tables,
            query_t,
            key_t,
            value_t,
            normed1,
            attended_t,
            tokens,
            attn_gain,
        )

    rows_major = Layout(major_to_minor=(0, 1))
    out_part = with_layout_constraint(out_part, rows_major)
    out_rows = lax.psum_scatter(out_part, EP, scatter_dimension=0, tiled=True)
    out_rows = with_layout_constraint(out_rows, rows_major)
    out_rows = (out_rows.astype(f32) + shared_part.astype(f32)).astype(bf16)
    out_quarter = lax.psum_scatter(out_rows, "hs", scatter_dimension=1, tiled=True)
    residual_quarter = lax.dynamic_slice_in_dim(residual, hs * quarter, quarter, 1)
    output = (residual_quarter + out_quarter.astype(f32)).astype(bf16)

    return (
        output,
        grad_tokens.T,
        grad_attn_gain,
        *[a.T for a in heads_sums],
        grad_ffn_gain,
        grad_router.T,
        shared_sums[0].T,
        shared_sums[1].T,
        shared_sums[2],
        grad_gate_t.swapaxes(1, 2),
        grad_up_t.swapaxes(1, 2),
        grad_expert_down,
    )


def solution(mesh):
    ep_count, hs_count = mesh.devices.shape
    cut = Mesh(mesh.devices.reshape(ep_count // 2, 2, hs_count), ("xy", "core", "hs"))
    return jax.shard_map(
        shards,
        mesh=cut,
        in_specs=(
            P(EP, None),
            P(),
            P(None, "hs"),
            P(None, "hs"),
            P(None, "hs"),
            P(None, "hs"),
            P(),
            P(),
            P(None, "hs"),
            P(None, "hs"),
            P("hs", None),
            P(EP, None, "hs"),
            P(EP, None, "hs"),
            P(EP, "hs", None),
            P(EP, None),
            P(EP, None),
            P(EP, "hs"),
        ),
        out_specs=(
            P(EP, "hs"),
            P(EP, "hs"),
            P(),
            P(None, "hs"),
            P(None, "hs"),
            P(None, "hs"),
            P(None, "hs"),
            P(),
            P(),
            P(None, "hs"),
            P(None, "hs"),
            P("hs", None),
            P(EP, None, "hs"),
            P(EP, None, "hs"),
            P(EP, "hs", None),
        ),
        check_vma=False,
    )
```

```python
import functools
import math

import jax
import jax.numpy as jnp
import numpy as np
from jax import lax
from jax.experimental import pallas as pl
from jax.experimental.layout import Layout, with_layout_constraint
from jax.experimental.pallas import tpu as pltpu
from jax.sharding import Mesh
from jax.sharding import PartitionSpec as P

HEADS = 10
HEAD_DIM = 128
CAP = 112
EPS = 1e-06
EP = ("xy", "core")
bf16 = jnp.bfloat16
f32 = jnp.float32


def dot(a, b):
    return jnp.dot(a, b, preferred_element_type=f32)


def ein(spec, a, b):
    return jnp.einsum(spec, a, b, preferred_element_type=f32)


def rope_tables(rows):
    half = HEAD_DIM // 2
    frequency = 10000.0 ** (-np.arange(half) * 2.0 / HEAD_DIM)
    angles = frequency[:, None] * np.arange(rows)[None, :]
    return jnp.asarray(np.cos(angles), f32), jnp.asarray(np.sin(angles), f32)


def rope(v, cosine, sine):
    half = HEAD_DIM // 2
    a, b = v[:, :half], v[:, half:]
    return jnp.concatenate([a * cosine - b * sine, b * cosine + a * sine], axis=1)


def rope_back(v, cosine, sine):
    half = HEAD_DIM // 2
    a, b = v[:, :half], v[:, half:]
    return jnp.concatenate([a * cosine + b * sine, b * cosine - a * sine], axis=1)


VMEM_LIMIT = 60 * 1024 * 1024
PAD = 256


def nn(a, b):
    return lax.dot_general(a, b, (((1,), (0,)), ((), ())), preferred_element_type=f32)


def nt(a, b):
    return lax.dot_general(a, b, (((1,), (1,)), ((), ())), preferred_element_type=f32)


def tn(a, b):
    return lax.dot_general(a, b, (((0,), (0,)), ((), ())), preferred_element_type=f32)


def takes(microseconds):
    return pl.CostEstimate(flops=0, transcendentals=0, bytes_accessed=microseconds * 3_000_000)


def slot_masks(slot_ref, at):
    local, rows = slot_ref.shape[-2:]
    number = lax.broadcasted_iota(jnp.int32, (CAP, rows), 0)
    return [slot_ref[at, e : e + 1, :] == number for e in range(local)]


def spread_kernel(weighted, *refs):
    if weighted:
        rows_ref, slot_ref, router_ref, x_ref, sw_ref, pick = refs
    else:
        rows_ref, slot_ref, x_ref, pick = refs
    local = slot_ref.shape[1]
    rows = rows_ref[...] if weighted else rows_ref[0]
    masks = slot_masks(slot_ref, 0)
    if weighted:
        logits = nt(router_ref[...], rows)
        raised = jnp.exp(logits - jnp.max(logits, axis=0, keepdims=True))
        gates = raised / jnp.sum(raised, axis=0, keepdims=True)
    for e in range(local):
        pick[e * CAP : (e + 1) * CAP, :] = masks[e].astype(f32).astype(bf16)
        if weighted:
            sw_ref[e] = jnp.sum(
                jnp.where(masks[e], gates[e : e + 1, :], 0.0), axis=1, keepdims=True
            )
    product = nn if weighted else nt
    x_ref[...] = product(pick[...], rows).astype(bf16).reshape(x_ref.shape)


def spread(all_rows, slot, router_t=None):
    s, local, rows = slot.shape
    weighted = router_t is not None
    if weighted:
        width = all_rows.shape[1]
        block = pl.BlockSpec((rows, width), lambda i: (i, 0))
    else:
        width = all_rows.shape[1]
        block = pl.BlockSpec((1, width, rows), lambda i: (i, 0, 0))
    in_specs = [
        block,
        pl.BlockSpec((1, local, rows), lambda i: (i, 0, 0)),
    ]
    out_specs = [pl.BlockSpec((1, local, CAP, width), lambda i: (i, 0, 0, 0))]
    out_shape = [jax.ShapeDtypeStruct((s, local, CAP, width), bf16)]
    args = [all_rows, slot]
    if weighted:
        in_specs.append(pl.BlockSpec(router_t.shape, lambda i: (0, 0)))
        out_specs.append(pl.BlockSpec((local, CAP, 1), lambda i: (0, i, 0)))
        out_shape.append(jax.ShapeDtypeStruct((local, s * CAP, 1), f32))
        args.append(router_t)
    out = pl.pallas_call(
        functools.partial(spread_kernel, weighted),
        grid=(s,),
        in_specs=in_specs,
        out_specs=out_specs,
        out_shape=out_shape,
        scratch_shapes=[pltpu.VMEM((local * CAP, rows), bf16)],
        compiler_params=pltpu.CompilerParams(vmem_limit_bytes=VMEM_LIMIT),
        cost_estimate=takes(17),
        name="spread",
    )(*args)
    return out if weighted else out[0]


def padded(ref, out):
    ff = ref.shape[1]
    out[:ff, :] = ref[0]
    out[ff:, :] = jnp.zeros((out.shape[0] - ff, out.shape[1]), out.dtype)


def experts_forward_kernel(
    x_ref, sw_ref, wg_ref, wu_ref, wd_ref, y_ref, gate_ref, up_ref, wg, wu, wd
):
    padded(wg_ref, wg)
    padded(wu_ref, wu)
    padded(wd_ref, wd)
    rows, width = gate_ref.shape[1], x_ref.shape[3]
    x = x_ref[...].reshape(rows, width)
    gate = nt(x, wg[...])
    up = nt(x, wu[...])
    gate_ref[0] = gate
    up_ref[0] = up
    act = gate / (1.0 + jnp.exp(-gate))
    hidden = (act * up).astype(bf16).astype(f32)
    hidden_w = (hidden * sw_ref[0]).astype(bf16)
    y_ref[...] = nn(hidden_w, wd[...]).astype(bf16).reshape(y_ref.shape)


def experts_backward_kernel(
    groups,
    x_ref,
    gx_ref,
    gate_ref,
    up_ref,
    sw_ref,
    wg_ref,
    wu_ref,
    wd_ref,
    dx_ref,
    dg_ref,
    du_ref,
    dd_ref,
    gsw_ref,
    wg,
    wu,
    wd,
):
    padded(wg_ref, wg)
    padded(wu_ref, wu)
    padded(wd_ref, wd)
    rows, width = gate_ref.shape[1], x_ref.shape[3]
    ff = wg_ref.shape[1]
    x = x_ref[...].reshape(rows, width)
    gx = gx_ref[...].reshape(rows, width)
    gate, up, sw = gate_ref[0], up_ref[0], sw_ref[0]
    sig = 1.0 / (1.0 + jnp.exp(-gate))
    act = gate * sig
    hidden = (act * up).astype(bf16).astype(f32)
    gh = nt(gx, wd[...])
    gsw_ref[0] = jnp.sum(gh * hidden, axis=-1, keepdims=True)
    gh = gh * sw
    gg = (gh * up * sig * (1.0 + gate * (1.0 - sig))).astype(bf16)
    gu = (gh * act).astype(bf16)
    sums = (
        (dd_ref, tn((hidden * sw).astype(bf16), gx)[:ff]),
        (dg_ref, tn(gg, x)[:ff]),
        (du_ref, tn(gu, x)[:ff]),
    )
    if groups == 1:
        for ref, value in sums:
            ref[0] = value
    else:

        @pl.when(pl.program_id(1) == 0)
        def _():
            for ref, value in sums:
                ref[0] = value

        @pl.when(pl.program_id(1) > 0)
        def _():
            for ref, value in sums:
                ref[0] += value

    dx_ref[...] = (nn(gg, wg[...]) + nn(gu, wu[...])).astype(bf16).reshape(dx_ref.shape)


def sending(remote_too, collective_id):
    if not remote_too:
        return pltpu.CompilerParams(vmem_limit_bytes=VMEM_LIMIT)
    return pltpu.CompilerParams(
        vmem_limit_bytes=VMEM_LIMIT, collective_id=collective_id, has_side_effects=True
    )


def expert_specs(s, width):
    group = min(s, 8)
    slots = pl.BlockSpec((group, 1, CAP, width), lambda i, j: (j, i, 0, 0))
    lines = lambda columns: pl.BlockSpec((1, group * CAP, columns), lambda i, j: (i, j, 0))
    per = lambda *shape: pl.BlockSpec((1, *shape), lambda i, j: (i, 0, 0))
    return s // group, slots, lines, per


def experts_forward_sending_kernel(
    x_ref,
    sw_ref,
    wg_ref,
    wu_ref,
    wd_ref,
    grad_ref,
    y_ref,
    gate_ref,
    up_ref,
    near_ref,
    wg,
    wu,
    wd,
    send,
    recv,
):
    chip, core, z, cx, cy, cd = places()
    peers = [(cx, core, z), (cy, core, z)]
    copies = [
        remote(grad_ref, near_ref.at[i], send.at[i], recv.at[i], peer) for i, peer in enumerate(peers)
    ]

    @pl.when(pl.program_id(0) == 0)
    def _():
        greet(peers)
        for copy in copies:
            copy.start()

    experts_forward_kernel(
        x_ref, sw_ref, wg_ref, wu_ref, wd_ref, y_ref, gate_ref, up_ref, wg, wu, wd
    )

    @pl.when(pl.program_id(0) == pl.num_programs(0) - 1)
    def _():
        for copy in copies:
            copy.wait()


def experts_forward(x, sw, wg, wu, wd, grad=None):
    s, local, cap, width = x.shape
    ff = wg.shape[1]
    rows = s * cap
    groups, slots, lines, per = expert_specs(s, width)
    middle = jax.ShapeDtypeStruct((local, rows, PAD), f32)
    kernel = experts_forward_kernel
    in_specs = [slots, lines(1)] + [per(ff, width)] * 3
    out_specs = [slots, lines(PAD), lines(PAD)]
    out_shape = [jax.ShapeDtypeStruct(x.shape, bf16), middle, middle]
    scratch = [pltpu.VMEM((PAD, width), bf16)] * 3
    args = [x, sw, wg, wu, wd]
    if grad is not None:
        kernel = experts_forward_sending_kernel
        in_specs.append(pl.BlockSpec(memory_space=pl.ANY))
        out_specs.append(pl.BlockSpec(memory_space=pl.ANY))
        out_shape.append(jax.ShapeDtypeStruct((2, *grad.shape), bf16))
        scratch += [pltpu.SemaphoreType.DMA((2,))] * 2
        args.append(grad)
    return pl.pallas_call(
        kernel,
        grid=(local, groups),
        in_specs=in_specs,
        out_specs=out_specs,
        out_shape=out_shape,
        scratch_shapes=scratch,
        compiler_params=sending(grad is not None, 4),
        cost_estimate=takes(31),
        name="experts_forward",
    )(*args)


def experts_backward(x, gx, gate, up, sw, wg, wu, wd):
    s, local, cap, width = x.shape
    ff = wg.shape[1]
    rows = s * cap
    groups, slots, lines, per = expert_specs(s, width)
    return pl.pallas_call(
        functools.partial(experts_backward_kernel, groups),
        grid=(local, groups),
        in_specs=[slots, slots, lines(PAD), lines(PAD), lines(1)]
        + [per(ff, width)] * 3,
        out_specs=[slots] + [per(ff, width)] * 3 + [lines(1)],
        out_shape=[jax.ShapeDtypeStruct(x.shape, bf16)]
        + [jax.ShapeDtypeStruct((local, ff, width), f32)] * 3
        + [jax.ShapeDtypeStruct((local, rows, 1), f32)],
        scratch_shapes=[pltpu.VMEM((PAD, width), bf16)] * 3,
        compiler_params=pltpu.CompilerParams(vmem_limit_bytes=VMEM_LIMIT),
        cost_estimate=takes(47),
        name="experts_backward",
    )(x, gx, gate, up, sw, wg, wu, wd)


def collect_kernel(y_ref, slot_ref, out_ref, pick):
    local = slot_ref.shape[1]
    masks = slot_masks(slot_ref, 0)
    for e in range(local):
        pick[e * CAP : (e + 1) * CAP, :] = masks[e].astype(f32).astype(bf16)
    out_ref[0] = tn(pick[...], y_ref[...].reshape(pick.shape[0], -1)).astype(bf16)


def collect_sending_kernel(
    y_ref, slot_ref, grad_ref, near_ref, out_ref, far_ref, given_ref, pick, send, recv, csend, crecv
):
    chip, core, z, cx, cy, cd = places()
    x_peer, y_peer, c_peer = (cx, core, z), (cy, core, z), (chip, 1 - core, z)
    half = grad_ref.shape[0] // 2
    top, low = pl.ds(0, half), pl.ds(half, half)
    relays = [
        remote(near_ref.at[0, top], far_ref.at[top], send.at[0], recv.at[0], y_peer),
        remote(near_ref.at[1, low], far_ref.at[low], send.at[1], recv.at[1], x_peer),
    ]
    passes = [
        remote(ref, given_ref.at[i], csend.at[i], crecv.at[i], c_peer)
        for i, ref in enumerate((grad_ref, near_ref.at[0], near_ref.at[1], far_ref))
    ]

    @pl.when(pl.program_id(0) == 0)
    def _():
        greet([x_peer, y_peer, c_peer])
        for copy in (*relays, *passes[:3]):
            copy.start()

    collect_kernel(y_ref, slot_ref, out_ref, pick)

    @pl.when(pl.program_id(0) == pl.num_programs(0) - 1)
    def _():
        for copy in relays:
            copy.wait_recv()
        passes[3].start()
        for copy in passes:
            copy.wait()
        for copy in relays:
            copy.wait_send()


def collect_back_kernel(experts, y_ref, slot_ref, gsw_ref, first_ref, out_ref, pick):
    local, rows = slot_ref.shape[1:]
    first = first_ref[0]
    masks = slot_masks(slot_ref, 0)
    number = lax.broadcasted_iota(jnp.int32, (experts, rows), 0)
    probs = jnp.zeros((experts, rows), f32)
    for e in range(local):
        pick[e * CAP : (e + 1) * CAP, :] = masks[e].astype(f32).astype(bf16)
        line = jnp.sum(jnp.where(masks[e], gsw_ref[e], 0.0), axis=0, keepdims=True)
        probs = jnp.where(number == first + e, line, probs)
    out_ref[0, :rows] = tn(pick[...], y_ref[...].reshape(pick.shape[0], -1)).astype(bf16)
    out_ref[0, rows:] = jnp.zeros((experts, out_ref.shape[2]), bf16)
    out_ref[0, rows:, :rows] = probs.astype(bf16)


def collect_sending(y, slot, grad, near):
    s, local, cap, width = y.shape
    rows = slot.shape[2]
    dma = pltpu.SemaphoreType.DMA
    whole = pl.BlockSpec(memory_space=pl.ANY)
    return pl.pallas_call(
        collect_sending_kernel,
        grid=(s,),
        in_specs=[
            pl.BlockSpec((1, local, cap, width), lambda i: (i, 0, 0, 0)),
            pl.BlockSpec((1, local, rows), lambda i: (i, 0, 0)),
            whole,
            whole,
        ],
        out_specs=[pl.BlockSpec((1, rows, width), lambda i: (i, 0, 0)), whole, whole],
        out_shape=[
            jax.ShapeDtypeStruct((s, rows, width), bf16),
            jax.ShapeDtypeStruct(grad.shape, bf16),
            jax.ShapeDtypeStruct((4, *grad.shape), bf16),
        ],
        scratch_shapes=[
            pltpu.VMEM((local * cap, rows), bf16),
            dma((2,)),
            dma((2,)),
            dma((4,)),
            dma((4,)),
        ],
        compiler_params=sending(True, 5),
        cost_estimate=takes(20),
        name="collect_sending",
    )(y, slot, grad, near)


def spread_grad_kernel(grad_ref, near_ref, far_ref, given_ref, slot_ref, x_ref, pick, gbuf, xbuf, come, gone):
    chip, core = lax.axis_index("xy"), lax.axis_index("core")
    local, rows = slot_ref.shape[1:]
    here = [grad_ref, near_ref.at[0], near_ref.at[1], far_ref]
    sources = [(here[t // 2], given_ref.at[t // 2])[t % 2] for t in range(8)]

    def in_copy(t):
        return pltpu.make_async_copy(sources[t], gbuf.at[t % 2], come.at[t % 2])

    def out_copy(t, src):
        return pltpu.make_async_copy(xbuf.at[t % 2], x_ref.at[src], gone.at[t % 2])

    number = lax.broadcasted_iota(jnp.int32, (CAP, rows), 0)
    in_copy(0).start()
    for t in range(8):
        if t < 7:
            in_copy(t + 1).start()
        x, y = (chip % 2 + (t // 2) % 2) % 2, (chip // 2 + t // 4) % 2
        src = (y * 2 + x) * 2 + (core + t % 2) % 2
        slots = slot_ref[src]
        for e in range(local):
            mask = slots[e : e + 1, :] == number
            pick[e * CAP : (e + 1) * CAP, :] = mask.astype(f32).astype(bf16)
        in_copy(t).wait()
        if t >= 2:
            out_copy(t, src).wait()
        xbuf[t % 2] = nt(pick[...], gbuf[t % 2]).astype(bf16).reshape(xbuf.shape[1:])
        out_copy(t, src).start()
    out_copy(0, 0).wait()
    out_copy(1, 0).wait()


def spread_grad(grad, near, far, given, slot):
    s, local, rows = slot.shape
    width = grad.shape[0]
    whole = pl.BlockSpec(memory_space=pl.ANY)
    dma = pltpu.SemaphoreType.DMA
    return pl.pallas_call(
        spread_grad_kernel,
        in_specs=[whole] * 4 + [pl.BlockSpec(memory_space=pltpu.VMEM)],
        out_specs=whole,
        out_shape=jax.ShapeDtypeStruct((s, local, CAP, width), bf16),
        scratch_shapes=[
            pltpu.VMEM((local * CAP, rows), bf16),
            pltpu.VMEM((2, width, rows), bf16),
            pltpu.VMEM((2, local, CAP, width), bf16),
            dma((2,)),
            dma((2,)),
        ],
        compiler_params=sending(False, 0),
        cost_estimate=takes(16),
        name="spread_grad",
    )(grad, near, far, given, slot)


def collect(y, slot, gsw=None, first=None, experts=0):
    s, local, cap, width = y.shape
    rows = slot.shape[2]
    in_specs = [
        pl.BlockSpec((1, local, cap, width), lambda i: (i, 0, 0, 0)),
        pl.BlockSpec((1, local, rows), lambda i: (i, 0, 0)),
    ]
    args = [y, slot]
    kernel = collect_kernel
    tall = rows
    if gsw is not None:
        in_specs += [
            pl.BlockSpec((local, cap, 1), lambda i: (0, i, 0)),
            pl.BlockSpec(memory_space=pltpu.SMEM),
        ]
        args += [gsw, first.reshape(1)]
        kernel = functools.partial(collect_back_kernel, experts)
        tall = rows + experts
    return pl.pallas_call(
        kernel,
        grid=(s,),
        in_specs=in_specs,
        out_specs=pl.BlockSpec((1, tall, width), lambda i: (i, 0, 0)),
        out_shape=jax.ShapeDtypeStruct((s, tall, width), bf16),
        scratch_shapes=[pltpu.VMEM((local * cap, rows), bf16)],
        compiler_params=pltpu.CompilerParams(vmem_limit_bytes=VMEM_LIMIT),
        cost_estimate=takes(17),
        name="collect",
    )(*args)


MESH = pl.DeviceIdType.MESH
EXTRA = 64


def places():
    chip, core, z = lax.axis_index("xy"), lax.axis_index("core"), lax.axis_index("hs")
    x, y = chip % 2, chip // 2
    return chip, core, z, y * 2 + (1 - x), (1 - y) * 2 + x, (1 - y) * 2 + (1 - x)


def greet(peers):
    barrier = pltpu.get_barrier_semaphore()
    for peer in peers:
        pl.semaphore_signal(barrier, inc=1, device_id=peer, device_id_type=MESH)
    pl.semaphore_wait(barrier, len(peers))


def remote(src, dst, send, recv, peer):
    return pltpu.make_async_remote_copy(
        src_ref=src, dst_ref=dst, send_sem=send, recv_sem=recv, device_id=peer, device_id_type=MESH
    )


def block(q, size):
    return pl.ds(pl.multiple_of(q * size, 16), size)


def weight_sum(grads, given, half, land, out_ref, csend, crecv, send, recv):
    chip, core, z, cx, cy, cd = places()
    other = 1 - core
    c_peer = (chip, other, z)
    chips = (cx, cy, cd)
    count = grads.shape[0] // 2
    piece = count // 4

    to_core = remote(grads.at[block(other, count)], given, csend.at[0], crecv.at[0], c_peer)
    scatter = [
        remote(half.at[block(c, piece)], land.at[i], send.at[i], recv.at[i], (c, core, z))
        for i, c in enumerate(chips)
    ]

    def share():
        to_core.wait_recv()
        half[...] = (grads[block(core, count)].astype(f32) + given[...].astype(f32)).astype(bf16)
        for i in (2, 0, 1):
            scatter[i].start()

    def place(c, k):
        return pl.ds(pl.multiple_of(k * count + c * piece, 16), piece)

    def give(number, c, k, sems, peer):
        return remote(out_ref.at[place(c, k)], out_ref.at[place(c, k)], *sems(number), peer)

    def chip_sems(i):
        return send.at[3 + i], recv.at[3 + i]

    def core_sems(i):
        return csend.at[1 + i], crecv.at[1 + i]

    gather = [give(i, chip, core, chip_sems, (c, core, z)) for i, c in enumerate(chips)]
    over = [give(i, c, core, core_sems, c_peer) for i, c in enumerate((*chips, chip))]

    def give_back():
        done = half[block(chip, piece)].astype(f32)
        for i in range(3):
            scatter[i].wait_recv()
            done = done + land[i].astype(f32)
        out_ref[place(chip, core)] = done.astype(bf16)
        for i in (2, 0, 1):
            gather[i].start()
        over[3].start()

    def end():
        for i, c in enumerate(chips):
            give(i, c, core, chip_sems, (c, core, z)).wait_recv()
            over[i].start()
        for i, c in enumerate((*chips, chip)):
            give(i, c, other, core_sems, c_peer).wait_recv()
        for copy in (to_core, *scatter, *gather, *over):
            copy.wait_send()

    return to_core.start, share, give_back, end


def weight_sum_scratch(tall, width):
    dma = pltpu.SemaphoreType.DMA
    return [
        pltpu.VMEM((tall, width), bf16),
        pltpu.VMEM((tall // 2, width), bf16),
        pltpu.VMEM((tall // 2, width), bf16),
        pltpu.VMEM((3, tall // 8, width), bf16),
        dma((5,)),
        dma((5,)),
        dma((6,)),
        dma((6,)),
    ]


def gather_spread_kernel(
    own_ref,
    slots_ref,
    router_ref,
    grad_ref,
    x_ref,
    sw_ref,
    slot_ref,
    grad_all_ref,
    held,
    pick,
    xbuf,
    send,
    recv,
    copied,
    zsend,
    zrecv,
):
    chip, core, z, cx, cy, cd = places()
    other = 1 - core
    x_peer, y_peer, c_peer = (cx, core, z), (cy, core, z), (chip, other, z)
    tall = held.shape[1]
    half = tall // 2
    local, rows = slot_ref.shape[1:]
    me = chip * 2 + core
    top, low = pl.ds(0, half), pl.ds(half, half)

    def at(c, k):
        return c * 2 + k

    def move(number, src_slot, part, peer):
        return remote(
            held.at[src_slot, part], held.at[src_slot, part], send.at[number], recv.at[number], peer
        )

    whole = pl.ds(0, tall)
    z_peers = [(chip, core, (z + i) % 4) for i in (1, 2, 3)]
    greet([x_peer, y_peer, c_peer, *z_peers])
    quarter = grad_ref.shape[0]

    def grad_copy(i, q):
        return remote(
            grad_ref, grad_all_ref.at[block(q, quarter)], zsend.at[i], zrecv.at[i], z_peers[i]
        )

    held[me, :rows] = own_ref[...]
    held[me, rows:] = jnp.zeros((EXTRA, own_ref.shape[1]), bf16)
    held[me, rows:, :rows] = slots_ref[...]
    x_top, x_low = move(0, me, top, x_peer), move(1, me, low, x_peer)
    y_low, y_top = move(2, me, low, y_peer), move(3, me, top, y_peer)
    to_core = move(4, me, whole, c_peer)
    relay_top, relay_low = move(5, at(cx, core), top, y_peer), move(6, at(cy, core), low, x_peer)
    pass_x, pass_y = move(7, at(cx, core), whole, c_peer), move(8, at(cy, core), whole, c_peer)
    pass_d = move(9, at(cd, core), whole, c_peer)
    for copy in (x_top, y_low, x_low, y_top, to_core, *[grad_copy(i, z) for i in (1, 0, 2)]):
        copy.start()
    grad_all_ref[block(z, quarter)] = grad_ref[...]

    def arrived(number, slot, part):
        move(number, slot, part, c_peer).wait_recv()

    number = lax.broadcasted_iota(jnp.int32, (CAP, rows), 0)
    first = me * local
    line = lax.broadcasted_iota(jnp.int32, (local, EXTRA), 0)
    column = lax.broadcasted_iota(jnp.int32, (local, EXTRA), 1)
    chosen = (column == line + first).astype(f32).astype(bf16)

    def out_copy(t, src):
        return pltpu.make_async_copy(xbuf.at[t % 2], x_ref.at[src], copied.at[t % 2])

    def step(t, carry):
        @pl.when(t == 1)
        def _():
            arrived(4, at(chip, other), whole)

        @pl.when(t == 2)
        def _():
            arrived(0, at(cx, core), top)
            relay_top.start()
            arrived(2, at(cy, core), low)
            relay_low.start()
            arrived(1, at(cx, core), low)
            pass_x.start()

        @pl.when(t == 3)
        def _():
            arrived(3, at(cy, core), top)
            pass_y.start()
            arrived(7, at(cx, other), whole)

        @pl.when(t == 5)
        def _():
            arrived(8, at(cy, other), whole)

        @pl.when(t == 6)
        def _():
            arrived(5, at(cd, core), top)
            arrived(6, at(cd, core), low)
            pass_d.start()

        @pl.when(t == 7)
        def _():
            arrived(9, at(cd, other), whole)

        x, y = (chip % 2 + (t // 2) % 2) % 2, (chip // 2 + t // 4) % 2
        src = (y * 2 + x) * 2 + (core + t % 2) % 2
        slots = nn(chosen, held[src, rows:, :rows]).astype(jnp.int32)
        slot_ref[src] = slots
        logits = nt(router_ref[...], held[src, :rows])
        raised = jnp.exp(logits - jnp.max(logits, axis=0, keepdims=True))
        gates = raised / jnp.sum(raised, axis=0, keepdims=True)
        for e in range(local):
            mask = slots[e : e + 1, :] == number
            pick[e * CAP : (e + 1) * CAP, :] = mask.astype(f32).astype(bf16)
            sw_ref[e, pl.ds(pl.multiple_of(src * CAP, 8), CAP), :] = jnp.sum(
                jnp.where(mask, gates[e : e + 1, :], 0.0), axis=1, keepdims=True
            )

        @pl.when(t >= 2)
        def _():
            out_copy(t, src).wait()

        xbuf[t % 2] = nn(pick[...], held[src, :rows]).astype(bf16).reshape(xbuf.shape[1:])
        out_copy(t, src).start()
        return carry

    lax.fori_loop(0, 8, step, 0)
    out_copy(0, me).wait()
    out_copy(1, me).wait()
    for i in range(3):
        grad_copy(i, (z + 3 - i) % 4).wait_recv()
        grad_copy(i, z).wait_send()
    for copy in (x_top, x_low, y_low, y_top, to_core, relay_top, relay_low, pass_x, pass_y, pass_d):
        copy.wait_send()


def gather_spread(own, slots, router_t, grad_quarter, local, ep_count):
    rows, width = own.shape
    tall = rows + EXTRA
    vmem = pl.BlockSpec(memory_space=pltpu.VMEM)
    return pl.pallas_call(
        gather_spread_kernel,
        in_specs=[vmem] * 4,
        out_specs=[pl.BlockSpec(memory_space=pl.ANY), vmem, vmem, vmem],
        out_shape=[
            jax.ShapeDtypeStruct((ep_count, local, CAP, width), bf16),
            jax.ShapeDtypeStruct((local, ep_count * CAP, 1), f32),
            jax.ShapeDtypeStruct((ep_count, local, rows), jnp.int32),
            jax.ShapeDtypeStruct((width, rows), bf16),
        ],
        scratch_shapes=[
            pltpu.VMEM((ep_count, tall, width), bf16),
            pltpu.VMEM((local * CAP, rows), bf16),
            pltpu.VMEM((2, local, CAP, width), bf16),
            pltpu.SemaphoreType.DMA((10,)),
            pltpu.SemaphoreType.DMA((10,)),
            pltpu.SemaphoreType.DMA((2,)),
            pltpu.SemaphoreType.DMA((3,)),
            pltpu.SemaphoreType.DMA((3,)),
        ],
        compiler_params=pltpu.CompilerParams(
            vmem_limit_bytes=VMEM_LIMIT, collective_id=0, has_side_effects=True
        ),
        cost_estimate=takes(62),
        name="gather_spread",
    )(own, slots, router_t, grad_quarter)


def front_kernel(
    x_ref,
    gain_ref,
    wq_ref,
    wk_ref,
    wv_ref,
    wo_ref,
    doc_ref,
    cos_ref,
    sin_ref,
    normed1_ref,
    q_ref,
    k_ref,
    v_ref,
    probs_ref,
    attended_ref,
    out_ref,
    residual_ref,
    normed2_ref,
    shared,
    beside,
    esend,
    erecv,
    asend,
    arecv,
    zsend,
    zrecv,
    send,
    recv,
    csend,
    crecv,
):
    chip, core, z, cx, cy, cd = places()
    other = 1 - core
    odd = z % 2
    c_peer = (chip, other, z)
    chips = (cx, cy, cd)
    z_peers = [(chip, core, (z + i) % 4) for i in (1, 2, 3)]
    pair = (chip, core, z + 1 - 2 * odd)
    rows, width = x_ref.shape
    quarter = wq_ref.shape[0]
    whole = HEAD_DIM * (quarter // HEAD_DIM)
    spare = quarter - whole
    greet([c_peer, *[(c, core, z) for c in chips], *z_peers])

    full_rows = pl.ds(pl.multiple_of(odd * spare, 16), whole)
    half_rows = pl.ds(pl.multiple_of((1 - odd) * whole, 16), spare)
    for i, ref in enumerate((wq_ref, wk_ref, wv_ref)):
        shared[i * spare : (i + 1) * spare] = ref[half_rows]
    trade = remote(shared, beside, esend, erecv, pair)
    trade.start()

    share, lanes = quarter // 4, width // 2
    my_lanes = pl.ds(pl.multiple_of(core * lanes, 128), lanes)

    def piece(c):
        return pl.ds(pl.multiple_of(c * share, 16), share)

    out_z = [
        remote(
            wo_ref.at[piece(chip), my_lanes],
            out_ref.at[z, piece(chip), my_lanes],
            zsend.at[i],
            zrecv.at[i],
            peer,
        )
        for i, peer in enumerate(z_peers)
    ]
    for i in (1, 0, 2):
        out_z[i].start()
    behind = [(z + 3 - i) % 4 for i in range(3)]

    def out_chip(i, j, c):
        at = out_ref.at[behind[i], piece(c), my_lanes]
        return remote(at, at, send.at[3 * i + j], recv.at[3 * i + j], (chips[j], core, z))

    def out_core(i, k):
        half = pl.ds(pl.multiple_of(k * lanes, 128), lanes)
        at = out_ref.at[behind[i], :, half]
        return remote(at, at, csend.at[i], crecv.at[i], c_peer)

    x = x_ref[...].astype(f32)
    rms1 = lax.rsqrt(jnp.sum(x * x, axis=-1, keepdims=True) * (1.0 / width) + EPS)
    normed1_ref[...] = (x * rms1 * gain_ref[0:1]).astype(bf16)
    out_ref[z] = wo_ref[...]

    cosine, sine = cos_ref[...], sin_ref[...]
    half_dim = HEAD_DIM // 2
    scale = 1.0 / math.sqrt(HEAD_DIM)
    row = lax.broadcasted_iota(jnp.int32, (rows, rows), 0)
    column = lax.broadcasted_iota(jnp.int32, (rows, rows), 1)
    doc = jnp.broadcast_to(doc_ref[...].astype(f32), (rows, rows))
    allowed = (row >= column) & (doc == doc.T)

    def turn(pre):
        a, b = pre[:half_dim], pre[half_dim:]
        return (
            jnp.concatenate([a * cosine - b * sine, b * cosine + a * sine], axis=0).astype(bf16)
        )

    def attend(h):
        scores = jnp.where(allowed, tn(q_ref[h], k_ref[h]) * scale, -1e30)
        raised = jnp.exp(scores - jnp.max(scores, axis=-1, keepdims=True))
        probs = raised * (1.0 / jnp.sum(raised, axis=-1, keepdims=True))
        probs_ref[h] = probs
        return nt(v_ref[h], probs.astype(bf16)).astype(bf16)

    def project(at):
        return [nt(ref[at], normed1_ref[...]) for ref in (wq_ref, wk_ref, wv_ref)]

    q, k, v = project(full_rows)
    heads = whole // HEAD_DIM
    for h in range(heads):
        at = slice(h * HEAD_DIM, (h + 1) * HEAD_DIM)
        q_ref[h], k_ref[h], v_ref[h] = turn(q[at]), turn(k[at]), v[at].astype(bf16)

    def attended_copy(number, start, size):
        at = attended_ref.at[pl.ds(pl.multiple_of(start, 16), size)]
        return lambda i: remote(
            at, at, asend.at[number, i], arecv.at[number, i], z_peers[i]
        )

    mine = z * quarter
    copies = []
    for h in range(heads):
        start = mine + odd * spare + h * HEAD_DIM
        attended_ref[pl.ds(pl.multiple_of(start, 16), HEAD_DIM)] = attend(h)
        copy = attended_copy(h, start, HEAD_DIM)
        copies += [copy(1), copy(0), copy(2)]
        for one in copies[-3:]:
            one.start()
        if h == 0:
            for i in range(3):
                out_z[i].wait_recv()
                for j in (2, 0, 1):
                    out_chip(i, j, chip).start()

    trade.wait_recv()
    for i, (ref, to) in enumerate(((wq_ref, q_ref), (wk_ref, k_ref), (wv_ref, v_ref))):
        normed1 = normed1_ref[...]
        here = nt(ref[half_rows], normed1)
        there = nt(beside[i * spare : (i + 1) * spare], normed1)
        first = jnp.where(odd == 1, there, here)
        second = jnp.where(odd == 1, here, there)
        both = jnp.concatenate([first, second], axis=0)
        to[heads] = both.astype(bf16) if to is v_ref else turn(both)
    last = attend(heads)
    last = jnp.where(odd == 1, last[spare:], last[:spare])
    start = mine + (1 - odd) * whole
    attended_ref[pl.ds(pl.multiple_of(start, 16), spare)] = last
    copy = attended_copy(heads, start, spare)
    copies += [copy(1), copy(0), copy(2)]
    for one in copies[-3:]:
        one.start()

    for i in range(3):
        for j in range(3):
            out_chip(i, j, chips[j]).wait_recv()
        out_core(i, core).start()
    for i in range(3):
        from_z = (z + 3 - i) % 4
        from_odd = from_z % 2
        for h in range(heads):
            attended_copy(h, from_z * quarter + from_odd * spare + h * HEAD_DIM, HEAD_DIM)(i).wait_recv()
        attended_copy(heads, from_z * quarter + (1 - from_odd) * whole, spare)(i).wait_recv()
        out_core(i, other).wait_recv()
    attended = attended_ref[...].T
    residual = x_ref[...].astype(f32) + nt(attended, out_ref[...].reshape(width, width))
    residual_ref[...] = residual
    rms2 = lax.rsqrt(jnp.sum(residual * residual, axis=-1, keepdims=True) * (1.0 / width) + EPS)
    normed2_ref[...] = (residual * rms2 * gain_ref[1:2]).astype(bf16)
    for one in (trade, *out_z, *copies):
        one.wait_send()
    for i in range(3):
        for j in range(3):
            out_chip(i, j, chip).wait_send()
        out_core(i, core).wait_send()


def front(x, gains, wq, wk, wv, wo, doc, tables):
    rows, width = x.shape
    quarter = wq.shape[0]
    heads = -(-quarter // HEAD_DIM)
    spare = quarter % HEAD_DIM
    vmem = pl.BlockSpec(memory_space=pltpu.VMEM)
    dma = pltpu.SemaphoreType.DMA
    low = lambda *shape: jax.ShapeDtypeStruct(shape, bf16)
    return pl.pallas_call(
        front_kernel,
        in_specs=[vmem] * 9,
        out_specs=[vmem] * 9,
        out_shape=[
            low(rows, width),
            *[low(heads, HEAD_DIM, rows)] * 3,
            jax.ShapeDtypeStruct((heads, rows, rows), f32),
            low(width, rows),
            low(4, quarter, width),
            jax.ShapeDtypeStruct((rows, width), f32),
            low(rows, width),
        ],
        scratch_shapes=[
            pltpu.VMEM((3 * spare, width), bf16),
            pltpu.VMEM((3 * spare, width), bf16),
            dma,
            dma,
            dma((heads, 3)),
            dma((heads, 3)),
            dma((3,)),
            dma((3,)),
            dma((9,)),
            dma((9,)),
            dma((3,)),
            dma((3,)),
        ],
        compiler_params=pltpu.CompilerParams(
            vmem_limit_bytes=VMEM_LIMIT, collective_id=1, has_side_effects=True
        ),
        cost_estimate=takes(50),
        name="front",
    )(x, gains, wq, wk, wv, wo, doc, *tables)


def collect_sum_kernel(
    y_ref,
    slot_ref,
    gsw_ref,
    normed_ref,
    grad_ref,
    gate_ref,
    up_ref,
    down_ref,
    out_ref,
    sum_ref,
    forward_ref,
    mine,
    pick,
    ybuf,
    stage,
    given,
    sums,
    relay,
    land,
    zland,
    copied,
    core_send,
    core_recv,
    send,
    recv,
    zsend,
    zrecv,
    grads,
    *more,
):
    chip, core, z, cx, cy, cd = places()
    other = 1 - core
    x_peer, y_peer, c_peer = (cx, core, z), (cy, core, z), (chip, other, z)
    z_peers = [(chip, core, (z + i) % 4) for i in (1, 2, 3)]
    local, rows = slot_ref.shape[1:]
    tall = out_ref.shape[0]
    me = chip * 2 + core
    number = lax.broadcasted_iota(jnp.int32, (CAP, rows), 0)
    row = lax.broadcasted_iota(jnp.int32, (EXTRA, rows), 0)

    greet([x_peer, y_peer, c_peer, (cd, core, z), *z_peers])

    def sequence(t):
        p = t // 2
        x, y = (chip % 2 + 1 + p // 2) % 2, (chip // 2 + 1 + p % 2) % 2
        return (y * 2 + x) * 2 + (core + 1 + t % 2) % 2

    def in_copy(t):
        return pltpu.make_async_copy(y_ref.at[sequence(t)], ybuf.at[t % 2], copied.at[t % 2])

    def to_core(p):
        return remote(stage.at[p % 2], given.at[p], core_send.at[p], core_recv.at[p], c_peer)

    units = 3
    unit = tall // units
    half, part = unit // 2, unit // 4

    def top(u):
        return pl.ds(u * unit, half)

    def low(u):
        return pl.ds(u * unit + half, half)

    def over(u, number, src, dst, peer):
        return remote(src, dst, send.at[u, number], recv.at[u, number], peer)

    far_top = [over(u, 0, sums.at[0, top(u)], relay.at[u, 0], x_peer) for u in range(units)]
    far_low = [over(u, 1, sums.at[0, low(u)], relay.at[u, 1], y_peer) for u in range(units)]
    x_top = [over(u, 2, sums.at[1, top(u)], land.at[0, top(u)], x_peer) for u in range(units)]
    x_low = [over(u, 3, sums.at[1, low(u)], land.at[0, low(u)], x_peer) for u in range(units)]
    y_low = [over(u, 4, sums.at[2, low(u)], land.at[1, low(u)], y_peer) for u in range(units)]
    y_top = [over(u, 5, sums.at[2, top(u)], land.at[1, top(u)], y_peer) for u in range(units)]

    in_copy(0).start()
    start, share, give_back, end = weight_sum(grads, *more[:3], sum_ref, *more[3:])

    def shared_expert():
        normed, grad_t = normed_ref[...], grad_ref[...]
        size = gate_ref.shape[0]
        gate, up = nt(gate_ref[...], normed), nt(up_ref[...], normed)
        sig = 1.0 / (1.0 + jnp.exp(-gate))
        act = gate * sig
        hidden = (act * up).astype(bf16)
        forward_ref[...] = tn(hidden, down_ref[...]).astype(bf16)
        grad_hidden = nn(down_ref[...], grad_t)
        grad_gate = (grad_hidden * up * sig * (1.0 + gate * (1.0 - sig))).astype(bf16)
        grad_up = (grad_hidden * act).astype(bf16)
        grads[:size] = nn(grad_gate, normed).astype(bf16)
        grads[size : 2 * size] = nn(grad_up, normed).astype(bf16)
        grads[2 * size : 3 * size] = nt(hidden, grad_t).astype(bf16)
        grads[3 * size :] = jnp.zeros((grads.shape[0] - 3 * size, grads.shape[1]), bf16)
        start()
        mine[...] = (tn(grad_gate, gate_ref[...]) + tn(grad_up, up_ref[...])).astype(bf16)

    def step(t, carry):
        @pl.when(t < 7)
        def _():
            in_copy(t + 1).start()

        p, s = t // 2, sequence(t)
        probs = jnp.zeros((EXTRA, rows), f32)
        for e in range(local):
            mask = slot_ref[s, e : e + 1, :] == number
            pick[e * CAP : (e + 1) * CAP, :] = mask.astype(f32).astype(bf16)
            column = gsw_ref[e, pl.ds(pl.multiple_of(s * CAP, 8), CAP), :]
            line = jnp.sum(jnp.where(mask, column, 0.0), axis=0, keepdims=True)
            probs = jnp.where(row == me * local + e, line, probs)
        in_copy(t).wait()
        back = tn(pick[...], ybuf[t % 2].reshape(local * CAP, -1))

        @pl.when(t % 2 == 0)
        def _():
            @pl.when(p >= 2)
            def _():
                to_core(p - 2).wait_send()

            stage[p % 2, :rows] = back.astype(bf16)
            stage[p % 2, rows:] = jnp.zeros((tall - rows, back.shape[1]), bf16)
            stage[p % 2, rows:, :rows] = probs.astype(bf16)
            to_core(p).start()

        @pl.when(t % 2 == 1)
        def _():
            to_core(p).wait_recv()
            sums[p, :rows] = (back + given[p, :rows].astype(f32)).astype(bf16)
            sums[p, rows:] = given[p, rows:]
            sums[p, rows:, :rows] = (probs + given[p, rows:, :rows].astype(f32)).astype(bf16)

        @pl.when(t == 1)
        def _():
            far_top[0].start()
            far_low[0].start()

        @pl.when(t == 3)
        def _():
            x_top[0].start()

        @pl.when(t == 5)
        def _():
            y_low[0].start()
            far_top[1].start()
            far_low[1].start()

        return carry

    lax.fori_loop(0, 8, step, 0)
    def relayed(u):
        far_low[u].wait_recv()
        at = slice(u * unit + half, (u + 1) * unit)
        sums[1, at] = (sums[1, at].astype(f32) + relay[u, 1].astype(f32)).astype(bf16)
        x_low[u].start()
        far_top[u].wait_recv()
        at = slice(u * unit, u * unit + half)
        sums[2, at] = (sums[2, at].astype(f32) + relay[u, 0].astype(f32)).astype(bf16)
        y_top[u].start()

    def block_of(u, q):
        return pl.ds(pl.multiple_of(u * unit + q * part, 16), part)

    def z_sems(u, number):
        return zsend.at[u, number], zrecv.at[u, number]

    scatter = [
        [
            remote(
                sums.at[3, block_of(u, (z + i) % 4)],
                zland.at[u, i - 1],
                *z_sems(u, i - 1),
                z_peers[i - 1],
            )
            for i in (1, 2, 3)
        ]
        for u in range(units)
    ]

    def back_copy(u, q, i):
        at = out_ref.at[block_of(u, q)]
        return remote(at, at, *z_sems(u, 2 + i), z_peers[i - 1])

    def landed(u):
        for copy in (x_top[u], y_top[u], x_low[u], y_low[u]):
            copy.wait_recv()
        at = slice(u * unit, (u + 1) * unit)
        added = sums[3, at].astype(f32) + land[0, at].astype(f32) + land[1, at].astype(f32)
        ours = min(rows, (u + 1) * unit) - u * unit
        if ours == unit:
            sums[3, at] = (added + mine[at].astype(f32)).astype(bf16)
        else:
            here = slice(u * unit, u * unit + ours)
            sums[3, here] = (added[:ours] + mine[here].astype(f32)).astype(bf16)
            sums[3, u * unit + ours : (u + 1) * unit] = added[ours:].astype(bf16)
        for i in (1, 0, 2):
            scatter[u][i].start()

    def summed(u):
        done = sums[3, block_of(u, z)].astype(f32)
        for i in range(3):
            scatter[u][i].wait_recv()
            done = done + zland[u, i].astype(f32)
        out_ref[block_of(u, z)] = done.astype(bf16)
        for i in (2, 1, 3):
            back_copy(u, z, i).start()

    relayed(0)
    x_top[1].start()
    y_low[1].start()
    far_top[2].start()
    far_low[2].start()
    shared_expert()
    relayed(1)
    x_top[2].start()
    y_low[2].start()
    landed(0)
    relayed(2)
    share()
    landed(1)
    summed(0)
    landed(2)
    summed(1)
    give_back()
    summed(2)
    end()
    for u in range(units):
        for i in (1, 2, 3):
            back_copy(u, (z + 4 - i) % 4, i).wait_recv()
    for u in range(units):
        for copy in (far_top[u], far_low[u], x_top[u], x_low[u], y_low[u], y_top[u], *scatter[u]):
            copy.wait_send()
        for i in (1, 2, 3):
            back_copy(u, z, i).wait_send()
    for p in (2, 3):
        to_core(p).wait_send()


def collect_sum(y, slot, gsw, normed, grad_t, *shared):
    s, local, cap, width = y.shape
    rows = slot.shape[2]
    tall = rows + EXTRA
    dma = pltpu.SemaphoreType.DMA
    weights = 128 * (-(-sum(a.shape[0] for a in shared) // 128))
    vmem = pl.BlockSpec(memory_space=pltpu.VMEM)
    return pl.pallas_call(
        collect_sum_kernel,
        in_specs=[pl.BlockSpec(memory_space=pl.ANY)] + [vmem] * 7,
        out_specs=[vmem, vmem, vmem],
        out_shape=[
            jax.ShapeDtypeStruct((tall, width), bf16),
            jax.ShapeDtypeStruct((weights, width), bf16),
            jax.ShapeDtypeStruct((rows, width), bf16),
        ],
        scratch_shapes=[
            pltpu.VMEM((rows, width), bf16),
            pltpu.VMEM((local * cap, rows), bf16),
            pltpu.VMEM((2, local, cap, width), bf16),
            pltpu.VMEM((2, tall, width), bf16),
            pltpu.VMEM((4, tall, width), bf16),
            pltpu.VMEM((4, tall, width), bf16),
            pltpu.VMEM((3, 2, tall // 6, width), bf16),
            pltpu.VMEM((2, tall, width), bf16),
            pltpu.VMEM((3, 3, tall // 12, width), bf16),
            dma((2,)),
            dma((4,)),
            dma((4,)),
            dma((3, 6)),
            dma((3, 6)),
            dma((3, 6)),
            dma((3, 6)),
            *weight_sum_scratch(weights, width),
        ],
        compiler_params=pltpu.CompilerParams(
            vmem_limit_bytes=VMEM_LIMIT, collective_id=2, has_side_effects=True
        ),
        cost_estimate=takes(131),
        name="collect_sum",
    )(y, slot, gsw, normed, grad_t, *shared)


def back_kernel(
    sums_ref,
    residual_ref,
    normed2_ref,
    grad_ref,
    router_ref,
    ffn_gain_ref,
    out_ref,
    q_ref,
    k_ref,
    v_ref,
    probs_ref,
    cos_ref,
    sin_ref,
    wq_ref,
    wk_ref,
    wv_ref,
    normed_ref,
    attended_ref,
    x_ref,
    gain_ref,
    tokens_ref,
    early_ref,
    first_ref,
    second_ref,
    shared_ref,
    dq_ref,
    dk_ref,
    dv_ref,
    x_t,
    gain_column,
    back_t,
    low_t,
    part,
    low_part,
    zland,
    mine,
    theirs,
    zsend,
    zrecv,
    lsend,
    lrecv,
    *more,
):
    chip, core, z, cx, cy, cd = places()
    odd = z % 2
    c_peer = (chip, 1 - core, z)
    z_peers = [(chip, core, (z + i) % 4) for i in (1, 2, 3)]
    quarter, width = wq_ref.shape
    rows = x_ref.shape[0]
    groups = [
        weight_sum(*more[8 * i : 8 * i + 4], ref, *more[8 * i + 4 : 8 * i + 8])
        for i, ref in enumerate((early_ref, first_ref, second_ref, shared_ref))
    ]
    early, *by_head = [more[8 * i] for i in range(4)]
    START, SHARE, GIVE_BACK, END = range(4)
    experts = router_ref.shape[0]
    whole = HEAD_DIM * (quarter // HEAD_DIM)
    spare = quarter - whole
    heads = whole // HEAD_DIM
    greet([c_peer, *[(c, core, z) for c in (cx, cy, cd)], *z_peers])

    logits = nt(router_ref[...], normed2_ref[...])
    raised = jnp.exp(logits - jnp.max(logits, axis=0, keepdims=True))
    gates = raised / jnp.sum(raised, axis=0, keepdims=True)
    grad_probs = sums_ref[rows:, :rows].astype(f32)
    grad_logits = gates * (grad_probs - jnp.sum(grad_probs * gates, axis=0, keepdims=True))
    grad_logits = grad_logits.astype(bf16)
    grad_router = nn(grad_logits, normed2_ref[...])
    grad_normed2 = sums_ref[:rows].astype(f32) + tn(grad_logits, router_ref[...])
    residual = residual_ref[...]
    rms2 = lax.rsqrt(jnp.sum(residual * residual, axis=-1, keepdims=True) * (1.0 / width) + EPS)
    grad_ffn = jnp.sum(grad_normed2 * residual * rms2, axis=0, keepdims=True)
    u = grad_normed2 * ffn_gain_ref[1:2]
    mean2 = jnp.sum(u * residual, axis=-1, keepdims=True) * (1.0 / width)
    added = rms2 * u - residual * (rms2 * rms2 * rms2 * mean2)
    back_t[...] = added.T + grad_ref[...].astype(f32)
    low_t[...] = back_t[...].astype(bf16)
    own = block(z, quarter)
    early[:quarter] = nt(low_t[own], attended_ref[...]).astype(bf16)
    early[quarter:] = grad_router.astype(bf16)
    groups[0][START]()
    normed = normed_ref[...]

    cosine, sine = cos_ref[...], sin_ref[...]
    half_dim = HEAD_DIM // 2
    scale = 1.0 / math.sqrt(HEAD_DIM)

    def turn_back(v):
        a, b = v[:half_dim] * scale, v[half_dim:] * scale
        turned = [a * cosine + b * sine, b * cosine - a * sine]
        return jnp.concatenate(turned, axis=0).astype(bf16)

    first_lane = z * quarter + odd * spare
    shared_lane = z * quarter + (1 - odd) * whole - odd * spare
    for h in range(heads + 1):
        lane = first_lane + h * HEAD_DIM if h < heads else shared_lane
        lane = pl.ds(pl.multiple_of(lane, HEAD_DIM), HEAD_DIM)
        grad_attended = tn(out_ref[:, lane], low_t[...]).astype(bf16)
        probs = probs_ref[h]
        grad_p = tn(grad_attended, v_ref[h])
        grad_v = nn(grad_attended, probs.astype(bf16)).astype(bf16)
        delta = jnp.sum(probs * grad_p, axis=-1, keepdims=True)
        grad_s = (probs * (grad_p - delta)).astype(bf16)
        grad_q = turn_back(nt(k_ref[h], grad_s))
        grad_k = turn_back(nn(q_ref[h], grad_s))
        for i, (ref, value) in enumerate(((dq_ref, grad_q), (dk_ref, grad_k), (dv_ref, grad_v))):
            if h < heads:
                size = HEAD_DIM
                at = pl.ds(pl.multiple_of(odd * spare + h * HEAD_DIM, 16), size)
            else:
                size = spare
                at = pl.ds(pl.multiple_of((1 - odd) * whole, 16), size)
                value = jnp.where(odd == 1, value[spare:], value[:spare])
            ref[at] = value
            by_head[h][i * size : (i + 1) * size] = nn(value, normed).astype(bf16)
        if h < heads:
            groups[1 + h][START]()
            groups[h][SHARE]()

    x_t[...] = x_ref[...].T
    gain_column[...] = jnp.broadcast_to(gain_ref[0:1], (8, width)).T
    x_all = x_t[...].astype(f32)
    rms1 = lax.rsqrt(jnp.sum(x_all * x_all, axis=0, keepdims=True) * (1.0 / width) + EPS)
    part[...] = tn(wq_ref[...], dq_ref[...])
    part[...] += tn(wk_ref[...], dk_ref[...])
    part[...] += tn(wv_ref[...], dv_ref[...])
    low_part[...] = part[...].astype(bf16)
    to_z = [
        remote(
            low_part.at[block((z + i) % 4, quarter)],
            zland.at[i - 1],
            zsend.at[i - 1],
            zrecv.at[i - 1],
            z_peers[i - 1],
        )
        for i in (1, 2, 3)
    ]
    few_to_z = [
        remote(mine, theirs.at[i], lsend.at[i], lrecv.at[i], peer) for i, peer in enumerate(z_peers)
    ]
    along = part[...] * x_t[...].astype(f32)
    mine[...] = jnp.zeros(mine.shape, f32)
    mine[0:1, :rows] = jnp.sum(along * gain_column[:, 0:1], axis=0, keepdims=True)
    mine[:, rows:] = nt(jnp.ones((8, rows), bf16), (along * rms1).astype(bf16))
    for copy in few_to_z:
        copy.start()
    for i in (1, 0, 2):
        to_z[i].start()

    at = 3 * spare
    late = by_head[heads]
    for copy in few_to_z:
        copy.wait_recv()
    few = mine[...] + theirs[0] + theirs[1] + theirs[2]
    late[at:] = jnp.zeros((late.shape[0] - at, width), bf16)
    line = lax.broadcasted_iota(jnp.int32, (16, width), 0)
    gains = jnp.where(line == 0, few[0:1, rows:], jnp.where(line == 1, grad_ffn, 0.0))
    late[at : at + 16] = gains.astype(bf16)
    groups[3][START]()
    groups[2][SHARE]()
    groups[0][GIVE_BACK]()
    groups[3][SHARE]()
    groups[1][GIVE_BACK]()

    total = part[own]
    for i in range(3):
        to_z[i].wait_recv()
        total = total + zland[i].astype(f32)
    x = x_t[own].astype(f32)
    mean = few[0:1, :rows] * (1.0 / width)
    tokens_ref[...] = back_t[own] + rms1 * gain_column[own, 0:1] * total - x * (rms1 * rms1 * rms1 * mean)

    groups[2][GIVE_BACK]()
    groups[3][GIVE_BACK]()
    for group in groups:
        group[END]()
    for copy in (*to_z, *few_to_z):
        copy.wait_send()


def back(*args):
    quarter, width = args[13].shape
    rows = args[1].shape[0]
    spare = quarter % HEAD_DIM
    tall = [quarter + args[4].shape[0], 3 * HEAD_DIM, 3 * HEAD_DIM, 3 * spare + 64]
    vmem = pl.BlockSpec(memory_space=pltpu.VMEM)
    dma = pltpu.SemaphoreType.DMA
    return pl.pallas_call(
        back_kernel,
        in_specs=[vmem] * len(args),
        out_specs=[vmem] * 5,
        out_shape=[
            jax.ShapeDtypeStruct((quarter, rows), f32),
            *[jax.ShapeDtypeStruct((lines, width), bf16) for lines in tall],
        ],
        scratch_shapes=[
            *[pltpu.VMEM((quarter, rows), bf16)] * 3,
            pltpu.VMEM((width, rows), bf16),
            pltpu.VMEM((width, 8), f32),
            pltpu.VMEM((width, rows), f32),
            pltpu.VMEM((width, rows), bf16),
            pltpu.VMEM((width, rows), f32),
            pltpu.VMEM((width, rows), bf16),
            pltpu.VMEM((3, quarter, rows), bf16),
            pltpu.VMEM((8, rows + width), f32),
            pltpu.VMEM((3, 8, rows + width), f32),
            dma((3,)),
            dma((3,)),
            dma((3,)),
            dma((3,)),
            *[one for lines in tall for one in weight_sum_scratch(lines, width)],
        ],
        compiler_params=pltpu.CompilerParams(
            vmem_limit_bytes=VMEM_LIMIT, collective_id=3, has_side_effects=True
        ),
        cost_estimate=takes(90),
        name="back",
    )(*args)


def widen_kernel(early_ref, first_ref, second_ref, last_ref, shared_ref, *out_refs):
    quarter = out_refs[0].shape[0]
    odd = lax.axis_index("hs") % 2
    whole = HEAD_DIM * (quarter // HEAD_DIM)
    spare = quarter - whole
    for i in range(3):
        for h, ref in enumerate((first_ref, second_ref)):
            at = pl.ds(pl.multiple_of(odd * spare + h * HEAD_DIM, 8), HEAD_DIM)
            out_refs[i][at] = ref[i * HEAD_DIM : (i + 1) * HEAD_DIM].astype(f32)
        at = pl.ds(pl.multiple_of((1 - odd) * whole, 8), spare)
        out_refs[i][at] = last_ref[i * spare : (i + 1) * spare].astype(f32)
    out_refs[3][...] = early_ref[:quarter].astype(f32)
    out_refs[4][...] = early_ref[quarter:].astype(f32)
    out_refs[5][...] = last_ref[3 * spare : 3 * spare + 16].astype(f32)
    size = out_refs[6].shape[0]
    for i in range(3):
        out_refs[6 + i][...] = shared_ref[i * size : (i + 1) * size].astype(f32)


def widen(sums, quarter, hidden_units):
    width = sums[0].shape[1]
    step = width // 5
    tall = [quarter] * 4 + [sums[0].shape[0] - quarter, 16] + [hidden_units] * 3
    blocks = lambda lines: pl.BlockSpec((lines, step), lambda i: (0, i))
    return pl.pallas_call(
        widen_kernel,
        grid=(width // step,),
        in_specs=[blocks(a.shape[0]) for a in sums],
        out_specs=[blocks(lines) for lines in tall],
        out_shape=[jax.ShapeDtypeStruct((lines, width), f32) for lines in tall],
        compiler_params=pltpu.CompilerParams(vmem_limit_bytes=VMEM_LIMIT),
        cost_estimate=takes(8),
        name="widen",
    )(*sums)


def plain_front(
    tokens, attn_gain, query_t, key_t, value_t, attn_out, ffn_gain, documents, tables
):
    rows, width = tokens.shape
    quarter = query_t.shape[0]
    hs, hs_count = lax.axis_index("hs"), lax.axis_size("hs")
    odd = (hs % 2) == 1
    spare = -quarter % HEAD_DIM
    heads = (quarter + spare) // HEAD_DIM

    def outer(w):
        return jnp.where(odd, w[:spare], w[quarter - spare :])

    sent = jnp.concatenate([outer(query_t), outer(key_t), outer(value_t)], axis=0)
    got = lax.ppermute(sent, "hs", [(i, i ^ 1) for i in range(hs_count)])

    def widened(w, extra):
        return jnp.where(
            odd, jnp.concatenate([extra, w], axis=0), jnp.concatenate([w, extra], axis=0)
        )

    x = tokens.astype(f32)
    rms1 = lax.rsqrt(jnp.mean(x * x, axis=-1, keepdims=True) + EPS)
    normed1 = (x * rms1 * attn_gain).astype(bf16)
    shape3 = (heads, HEAD_DIM, rows)
    q, k, v = [
        ein("cd,td->ct", widened(w, got[i * spare : (i + 1) * spare]), normed1).reshape(shape3)
        for i, w in enumerate((query_t, key_t, value_t))
    ]
    q, k, v = rope(q, *tables).astype(bf16), rope(k, *tables).astype(bf16), v.astype(bf16)
    positions = jnp.arange(rows, dtype=jnp.int32)
    doc = documents[0]
    allowed = (positions[:, None] >= positions[None, :]) & (doc[:, None] == doc[None, :])
    scale = 1.0 / math.sqrt(HEAD_DIM)
    scores = jnp.where(allowed[None], ein("hdq,hdk->hqk", q, k) * scale, -1e30)
    raised = jnp.exp(scores - jnp.max(scores, axis=-1, keepdims=True))
    probs = raised / jnp.sum(raised, axis=-1, keepdims=True)
    attended = ein("hdk,hqk->hdq", v, probs.astype(bf16)).astype(bf16).reshape(-1, rows)
    attended = jnp.where(odd, attended[spare:], attended[:quarter])
    attended_t = lax.all_gather(attended, "hs", axis=0, tiled=True)
    out_t = lax.all_gather(attn_out.T, "hs", axis=0, tiled=True)
    residual = x + ein("ct,oc->to", attended_t, out_t)
    rms2 = lax.rsqrt(jnp.mean(residual * residual, axis=-1, keepdims=True) + EPS)
    normed2 = (residual * rms2 * ffn_gain).astype(bf16)
    return normed1, q, k, v, probs, attended_t, out_t, residual, normed2


def over_ep(a):
    return lax.psum(a.astype(bf16), EP).astype(f32)


def plain_back(
    sums,
    residual,
    normed2,
    grad_t,
    router_t,
    ffn_gain,
    out_t,
    q,
    k,
    v,
    probs,
    tables,
    query_t,
    key_t,
    value_t,
    normed1,
    attended_t,
    tokens,
    attn_gain,
):
    rows, width = tokens.shape
    quarter = query_t.shape[0]
    hs = lax.axis_index("hs")
    odd = (hs % 2) == 1
    spare = -quarter % HEAD_DIM
    held = quarter + spare
    col0 = hs * quarter

    def own(v):
        v = v.astype(bf16).reshape(held, rows)
        return jnp.where(odd, v[spare:], v[:quarter])

    gates = jax.nn.softmax(nt(normed2, router_t), axis=-1)
    grad_probs = sums[rows:, :rows].T.astype(f32)
    grad_logits = (
        gates * (grad_probs - jnp.sum(grad_probs * gates, axis=-1, keepdims=True))
    ).astype(bf16)
    grad_router = tn(grad_logits, normed2)
    grad_normed2 = sums[:rows].astype(f32) + dot(grad_logits, router_t)
    rms2 = lax.rsqrt(jnp.mean(residual * residual, axis=-1, keepdims=True) + EPS)
    grad_ffn_gain = jnp.sum(grad_normed2 * residual * rms2, axis=0)
    u = grad_normed2 * ffn_gain
    grad_residual = (
        grad_t.T.astype(f32)
        + rms2 * u
        - residual * rms2**3 * jnp.mean(u * residual, axis=-1, keepdims=True)
    )
    back_t = grad_residual.T
    low_t = back_t.astype(bf16)
    out_held = lax.dynamic_slice_in_dim(out_t, jnp.where(odd, col0 - spare, col0), held, 1)
    grad_attended = tn(out_held, low_t).astype(bf16).reshape(-1, HEAD_DIM, rows)
    grad_p = ein("hdq,hdk->hqk", grad_attended, v)
    grad_v = own(ein("hdq,hqk->hdk", grad_attended, probs.astype(bf16)))
    grad_s = (probs * (grad_p - jnp.sum(probs * grad_p, axis=-1, keepdims=True))).astype(bf16)
    scale = 1.0 / math.sqrt(HEAD_DIM)
    grad_q = own(rope_back(ein("hdk,hqk->hdq", k, grad_s) * scale, *tables))
    grad_k = own(rope_back(ein("hdq,hqk->hdk", q, grad_s) * scale, *tables))
    own_rows = lambda a: lax.dynamic_slice_in_dim(a, col0, quarter, 0)
    heads_sums = [
        over_ep(dot(grad_q, normed1)),
        over_ep(dot(grad_k, normed1)),
        over_ep(dot(grad_v, normed1)),
        over_ep(nt(own_rows(low_t), attended_t)),
    ]
    part = tn(query_t, grad_q) + tn(key_t, grad_k) + tn(value_t, grad_v)
    grad_n1 = lax.psum_scatter(part.astype(bf16), "hs", scatter_dimension=0, tiled=True)
    grad_n1 = grad_n1.astype(f32)
    x = tokens.T.astype(f32)
    x_own = own_rows(x)
    rms_t = lax.rsqrt(jnp.mean(x * x, axis=0, keepdims=True) + EPS)
    w1 = grad_n1 * own_rows(attn_gain)[:, None]
    mean1 = lax.psum(jnp.sum(w1 * x_own, axis=0, keepdims=True), "hs") / width
    grad_tokens = own_rows(back_t) + rms_t * w1 - x_own * rms_t**3 * mean1
    gain_own = jnp.sum(grad_n1 * x_own * rms_t, axis=1)
    gain_part = lax.dynamic_update_slice_in_dim(jnp.zeros((width,), f32), gain_own, col0, 0)
    grad_attn_gain = lax.psum(gain_part, (*EP, "hs"))
    return (
        grad_tokens,
        heads_sums,
        over_ep(grad_router),
        grad_attn_gain,
        lax.psum(grad_ffn_gain, EP),
    )


def shards(
    tokens,
    attn_gain,
    attn_query,
    attn_key,
    attn_value,
    attn_out,
    ffn_gain,
    router,
    shared_gate,
    shared_up,
    shared_down,
    expert_gate,
    expert_up,
    expert_down,
    routes,
    documents,
    out_grad,
):
    rows, width = tokens.shape
    quarter = out_grad.shape[1]
    hs = lax.axis_index("hs")
    ep_count = lax.axis_size("xy") * lax.axis_size("core")
    ep = lax.axis_index("xy") * lax.axis_size("core") + lax.axis_index("core")
    local = expert_gate.shape[0]
    experts = router.shape[1]
    small = ep_count == 8 and lax.axis_size("hs") == 4

    query_t, key_t, value_t, router_t = attn_query.T, attn_key.T, attn_value.T, router.T
    positions = jnp.arange(rows, dtype=jnp.int32)
    below = (positions[:, None] > positions[None, :]).astype(bf16)
    chosen = jnp.any(
        routes[:, :, None] == jnp.arange(experts, dtype=jnp.int32)[None, None, :], axis=1
    )
    own_slots = jnp.where(chosen, dot(below, chosen.astype(bf16)), -1.0).T.astype(bf16)
    tables = rope_tables(rows)

    if small:
        both_gains = jnp.stack([attn_gain, ffn_gain])
        ahead = front(
            tokens, both_gains, query_t, key_t, value_t, attn_out.T, documents, tables
        )
    else:
        ahead = plain_front(
            tokens, attn_gain, query_t, key_t, value_t, attn_out, ffn_gain, documents, tables
        )
    normed1, q, k, v, probs, attended_t, out_t, residual, normed2 = ahead
    out_t = out_t.reshape(width, width)

    first = ep * local
    rolled = jnp.roll(router_t, -first, axis=0)
    gate_t, up_t = expert_gate.swapaxes(1, 2), expert_up.swapaxes(1, 2)
    weights = gate_t, up_t, expert_down
    if small:
        ex_in, slot_weight, slot, grad_t = gather_spread(
            normed2, own_slots, rolled, out_grad.T, local, ep_count
        )
        ex_out, ex_gate, ex_up, near = experts_forward(ex_in, slot_weight, *weights, grad_t)
        out_part, far, given = collect_sending(ex_out, slot, grad_t, near)
        ex_grad = spread_grad(grad_t, near, far, given, slot)
    else:
        grad_all_t = lax.all_gather(out_grad.T, (*EP, "hs"), axis=0, tiled=True)
        grad_all_t = grad_all_t.reshape(ep_count, width, rows)
        grad_t = lax.dynamic_index_in_dim(grad_all_t, ep, 0, keepdims=False)
        slot = lax.dynamic_slice_in_dim(
            lax.all_gather(own_slots, EP, axis=0), first, local, 1
        ).astype(jnp.int32)
        normed_all = lax.all_gather(normed2, EP, axis=0, tiled=True)
        ex_in, slot_weight = spread(normed_all, slot, rolled)
        ex_out, ex_gate, ex_up = experts_forward(ex_in, slot_weight, *weights)
        out_part = collect(ex_out, slot)
        ex_grad = spread(grad_all_t, slot)
    out_part = out_part.reshape(ep_count * rows, width)
    ex_back, grad_gate_t, grad_up_t, grad_expert_down, grad_slot_weight = experts_backward(
        ex_in, ex_grad, ex_gate, ex_up, slot_weight, *weights
    )

    if small:
        back_sums, shared_sums, shared_part = collect_sum(
            ex_back, slot, grad_slot_weight, normed2, grad_t, shared_gate.T, shared_up.T, shared_down
        )
        grad_tokens, *sums = back(
            back_sums,
            residual,
            normed2,
            grad_t,
            router_t,
            both_gains,
            out_t,
            q,
            k,
            v,
            probs,
            *tables,
            query_t,
            key_t,
            value_t,
            normed1,
            attended_t,
            tokens,
            both_gains,
        )
        *heads_sums, grad_router, gains, sum_gate, sum_up, sum_down = widen(
            [*sums, shared_sums], quarter, shared_down.shape[0]
        )
        shared_sums = sum_gate, sum_up, sum_down
        grad_attn_gain, grad_ffn_gain = gains[0], gains[1]
    else:
        sh_gate = dot(normed2, shared_gate)
        sh_up = dot(normed2, shared_up)
        sh_sig = jax.nn.sigmoid(sh_gate)
        sh_act = sh_gate * sh_sig
        sh_hidden = (sh_act * sh_up).astype(bf16)
        shared_part = dot(sh_hidden, shared_down)
        grad_sh = ein("dt,fd->tf", grad_t, shared_down)
        grad_sh_gate = (grad_sh * sh_up * sh_sig * (1 + sh_gate * (1 - sh_sig))).astype(bf16)
        grad_sh_up = (grad_sh * sh_act).astype(bf16)
        shared_grads = [
            ein("tf,td->fd", grad_sh_gate, normed2).astype(bf16),
            ein("tf,td->fd", grad_sh_up, normed2).astype(bf16),
            ein("tf,dt->fd", sh_hidden, grad_t).astype(bf16),
        ]
        shared_back = ein("tf,df->td", grad_sh_gate, shared_gate) + ein(
            "tf,df->td", grad_sh_up, shared_up
        )
        back_part = collect(ex_back, slot, grad_slot_weight, first, experts).reshape(-1, width)
        back_rows = lax.psum_scatter(back_part, EP, scatter_dimension=0, tiled=True).astype(f32)
        back_rows = jnp.concatenate([back_rows[:rows] + shared_back, back_rows[rows:]], axis=0)
        back_sums = lax.psum(back_rows.astype(bf16), "hs")
        shared_sums = [over_ep(a) for a in shared_grads]
        grad_tokens, heads_sums, grad_router, grad_attn_gain, grad_ffn_gain = plain_back(
            back_sums,
            residual,
            normed2,
            grad_t,
            router_t,
            ffn_gain,
            out_t,
            q,
            k,
            v,
            probs,
            tables,
            query_t,
            key_t,
            value_t,
            normed1,
            attended_t,
            tokens,
            attn_gain,
        )

    rows_major = Layout(major_to_minor=(0, 1))
    out_part = with_layout_constraint(out_part, rows_major)
    out_rows = lax.psum_scatter(out_part, EP, scatter_dimension=0, tiled=True)
    out_rows = with_layout_constraint(out_rows, rows_major)
    out_rows = (out_rows.astype(f32) + shared_part.astype(f32)).astype(bf16)
    out_quarter = lax.psum_scatter(out_rows, "hs", scatter_dimension=1, tiled=True)
    residual_quarter = lax.dynamic_slice_in_dim(residual, hs * quarter, quarter, 1)
    output = (residual_quarter + out_quarter.astype(f32)).astype(bf16)

    return (
        output,
        grad_tokens.T,
        grad_attn_gain,
        *[a.T for a in heads_sums],
        grad_ffn_gain,
        grad_router.T,
        shared_sums[0].T,
        shared_sums[1].T,
        shared_sums[2],
        grad_gate_t.swapaxes(1, 2),
        grad_up_t.swapaxes(1, 2),
        grad_expert_down,
    )


def solution(mesh):
    ep_count, hs_count = mesh.devices.shape
    cut = Mesh(mesh.devices.reshape(ep_count // 2, 2, hs_count), ("xy", "core", "hs"))
    return jax.shard_map(
        shards,
        mesh=cut,
        in_specs=(
            P(EP, None),
            P(),
            P(None, "hs"),
            P(None, "hs"),
            P(None, "hs"),
            P(None, "hs"),
            P(),
            P(),
            P(None, "hs"),
            P(None, "hs"),
            P("hs", None),
            P(EP, None, "hs"),
            P(EP, None, "hs"),
            P(EP, "hs", None),
            P(EP, None),
            P(EP, None),
            P(EP, "hs"),
        ),
        out_specs=(
            P(EP, "hs"),
            P(EP, "hs"),
            P(),
            P(None, "hs"),
            P(None, "hs"),
            P(None, "hs"),
            P(None, "hs"),
            P(),
            P(),
            P(None, "hs"),
            P(None, "hs"),
            P("hs", None),
            P(EP, None, "hs"),
            P(EP, None, "hs"),
            P(EP, "hs", None),
        ),
        check_vma=False,
    )
```

```python
import functools
import math

import jax
import jax.numpy as jnp
import numpy as np
from jax import lax
from jax.experimental import pallas as pl
from jax.experimental.layout import Layout, with_layout_constraint
from jax.experimental.pallas import tpu as pltpu
from jax.sharding import Mesh
from jax.sharding import PartitionSpec as P

HEADS = 10
HEAD_DIM = 128
CAP = 112
EPS = 1e-06
EP = ("xy", "core")
bf16 = jnp.bfloat16
f32 = jnp.float32


def dot(a, b):
    return jnp.dot(a, b, preferred_element_type=f32)


def ein(spec, a, b):
    return jnp.einsum(spec, a, b, preferred_element_type=f32)


def rope_tables(rows):
    half = HEAD_DIM // 2
    frequency = 10000.0 ** (-np.arange(half) * 2.0 / HEAD_DIM)
    angles = frequency[:, None] * np.arange(rows)[None, :]
    return jnp.asarray(np.cos(angles), f32), jnp.asarray(np.sin(angles), f32)


def rope(v, cosine, sine):
    half = HEAD_DIM // 2
    a, b = v[:, :half], v[:, half:]
    return jnp.concatenate([a * cosine - b * sine, b * cosine + a * sine], axis=1)


def rope_back(v, cosine, sine):
    half = HEAD_DIM // 2
    a, b = v[:, :half], v[:, half:]
    return jnp.concatenate([a * cosine + b * sine, b * cosine - a * sine], axis=1)


VMEM_LIMIT = 60 * 1024 * 1024
PAD = 256


def nn(a, b):
    return lax.dot_general(a, b, (((1,), (0,)), ((), ())), preferred_element_type=f32)


def nt(a, b):
    return lax.dot_general(a, b, (((1,), (1,)), ((), ())), preferred_element_type=f32)


def tn(a, b):
    return lax.dot_general(a, b, (((0,), (0,)), ((), ())), preferred_element_type=f32)


def takes(microseconds):
    return pl.CostEstimate(flops=0, transcendentals=0, bytes_accessed=microseconds * 3_000_000)


def slot_masks(slot_ref, at):
    local, rows = slot_ref.shape[-2:]
    number = lax.broadcasted_iota(jnp.int32, (CAP, rows), 0)
    return [slot_ref[at, e : e + 1, :] == number for e in range(local)]


def spread_kernel(weighted, *refs):
    if weighted:
        rows_ref, slot_ref, router_ref, x_ref, sw_ref, pick = refs
    else:
        rows_ref, slot_ref, x_ref, pick = refs
    local = slot_ref.shape[1]
    rows = rows_ref[...] if weighted else rows_ref[0]
    masks = slot_masks(slot_ref, 0)
    if weighted:
        logits = nt(router_ref[...], rows)
        raised = jnp.exp(logits - jnp.max(logits, axis=0, keepdims=True))
        gates = raised / jnp.sum(raised, axis=0, keepdims=True)
    for e in range(local):
        pick[e * CAP : (e + 1) * CAP, :] = masks[e].astype(f32).astype(bf16)
        if weighted:
            sw_ref[e] = jnp.sum(
                jnp.where(masks[e], gates[e : e + 1, :], 0.0), axis=1, keepdims=True
            )
    product = nn if weighted else nt
    x_ref[...] = product(pick[...], rows).astype(bf16).reshape(x_ref.shape)


def spread(all_rows, slot, router_t=None):
    s, local, rows = slot.shape
    weighted = router_t is not None
    if weighted:
        width = all_rows.shape[1]
        block = pl.BlockSpec((rows, width), lambda i: (i, 0))
    else:
        width = all_rows.shape[1]
        block = pl.BlockSpec((1, width, rows), lambda i: (i, 0, 0))
    in_specs = [
        block,
        pl.BlockSpec((1, local, rows), lambda i: (i, 0, 0)),
    ]
    out_specs = [pl.BlockSpec((1, local, CAP, width), lambda i: (i, 0, 0, 0))]
    out_shape = [jax.ShapeDtypeStruct((s, local, CAP, width), bf16)]
    args = [all_rows, slot]
    if weighted:
        in_specs.append(pl.BlockSpec(router_t.shape, lambda i: (0, 0)))
        out_specs.append(pl.BlockSpec((local, CAP, 1), lambda i: (0, i, 0)))
        out_shape.append(jax.ShapeDtypeStruct((local, s * CAP, 1), f32))
        args.append(router_t)
    out = pl.pallas_call(
        functools.partial(spread_kernel, weighted),
        grid=(s,),
        in_specs=in_specs,
        out_specs=out_specs,
        out_shape=out_shape,
        scratch_shapes=[pltpu.VMEM((local * CAP, rows), bf16)],
        compiler_params=pltpu.CompilerParams(vmem_limit_bytes=VMEM_LIMIT),
        cost_estimate=takes(17),
        name="spread",
    )(*args)
    return out if weighted else out[0]


def padded(ref, out):
    ff = ref.shape[1]
    out[:ff, :] = ref[0]
    out[ff:, :] = jnp.zeros((out.shape[0] - ff, out.shape[1]), out.dtype)


def experts_forward_kernel(
    x_ref, sw_ref, wg_ref, wu_ref, wd_ref, y_ref, gate_ref, up_ref, wg, wu, wd
):
    padded(wg_ref, wg)
    padded(wu_ref, wu)
    padded(wd_ref, wd)
    rows, width = gate_ref.shape[1], x_ref.shape[3]
    x = x_ref[...].reshape(rows, width)
    gate = nt(x, wg[...])
    up = nt(x, wu[...])
    gate_ref[0] = gate
    up_ref[0] = up
    act = gate / (1.0 + jnp.exp(-gate))
    hidden = (act * up).astype(bf16).astype(f32)
    hidden_w = (hidden * sw_ref[0]).astype(bf16)
    y_ref[...] = nn(hidden_w, wd[...]).astype(bf16).reshape(y_ref.shape)


def experts_backward_kernel(
    groups,
    x_ref,
    gx_ref,
    gate_ref,
    up_ref,
    sw_ref,
    wg_ref,
    wu_ref,
    wd_ref,
    dx_ref,
    dg_ref,
    du_ref,
    dd_ref,
    gsw_ref,
    wg,
    wu,
    wd,
):
    padded(wg_ref, wg)
    padded(wu_ref, wu)
    padded(wd_ref, wd)
    rows, width = gate_ref.shape[1], x_ref.shape[3]
    ff = wg_ref.shape[1]
    x = x_ref[...].reshape(rows, width)
    gx = gx_ref[...].reshape(rows, width)
    gate, up, sw = gate_ref[0], up_ref[0], sw_ref[0]
    sig = 1.0 / (1.0 + jnp.exp(-gate))
    act = gate * sig
    hidden = (act * up).astype(bf16).astype(f32)
    gh = nt(gx, wd[...])
    gsw_ref[0] = jnp.sum(gh * hidden, axis=-1, keepdims=True)
    gh = gh * sw
    gg = (gh * up * sig * (1.0 + gate * (1.0 - sig))).astype(bf16)
    gu = (gh * act).astype(bf16)
    sums = (
        (dd_ref, tn((hidden * sw).astype(bf16), gx)[:ff]),
        (dg_ref, tn(gg, x)[:ff]),
        (du_ref, tn(gu, x)[:ff]),
    )
    if groups == 1:
        for ref, value in sums:
            ref[0] = value
    else:

        @pl.when(pl.program_id(1) == 0)
        def _():
            for ref, value in sums:
                ref[0] = value

        @pl.when(pl.program_id(1) > 0)
        def _():
            for ref, value in sums:
                ref[0] += value

    dx_ref[...] = (nn(gg, wg[...]) + nn(gu, wu[...])).astype(bf16).reshape(dx_ref.shape)


def sending(remote_too, collective_id):
    if not remote_too:
        return pltpu.CompilerParams(vmem_limit_bytes=VMEM_LIMIT)
    return pltpu.CompilerParams(
        vmem_limit_bytes=VMEM_LIMIT, collective_id=collective_id, has_side_effects=True
    )


def expert_specs(s, width):
    group = min(s, 8)
    slots = pl.BlockSpec((group, 1, CAP, width), lambda i, j: (j, i, 0, 0))
    lines = lambda columns: pl.BlockSpec((1, group * CAP, columns), lambda i, j: (i, j, 0))
    per = lambda *shape: pl.BlockSpec((1, *shape), lambda i, j: (i, 0, 0))
    return s // group, slots, lines, per


def experts_forward_sending_kernel(
    x_ref,
    sw_ref,
    wg_ref,
    wu_ref,
    wd_ref,
    grad_ref,
    y_ref,
    gate_ref,
    up_ref,
    near_ref,
    wg,
    wu,
    wd,
    send,
    recv,
):
    chip, core, z, cx, cy, cd = places()
    peers = [(cx, core, z), (cy, core, z)]
    copies = [
        remote(grad_ref, near_ref.at[i], send.at[i], recv.at[i], peer) for i, peer in enumerate(peers)
    ]

    @pl.when(pl.program_id(0) == 0)
    def _():
        greet(peers)
        for copy in copies:
            copy.start()

    experts_forward_kernel(
        x_ref, sw_ref, wg_ref, wu_ref, wd_ref, y_ref, gate_ref, up_ref, wg, wu, wd
    )

    @pl.when(pl.program_id(0) == pl.num_programs(0) - 1)
    def _():
        for copy in copies:
            copy.wait()


def experts_forward(x, sw, wg, wu, wd, grad=None):
    s, local, cap, width = x.shape
    ff = wg.shape[1]
    rows = s * cap
    groups, slots, lines, per = expert_specs(s, width)
    middle = jax.ShapeDtypeStruct((local, rows, PAD), f32)
    kernel = experts_forward_kernel
    in_specs = [slots, lines(1)] + [per(ff, width)] * 3
    out_specs = [slots, lines(PAD), lines(PAD)]
    out_shape = [jax.ShapeDtypeStruct(x.shape, bf16), middle, middle]
    scratch = [pltpu.VMEM((PAD, width), bf16)] * 3
    args = [x, sw, wg, wu, wd]
    if grad is not None:
        kernel = experts_forward_sending_kernel
        in_specs.append(pl.BlockSpec(memory_space=pl.ANY))
        out_specs.append(pl.BlockSpec(memory_space=pl.ANY))
        out_shape.append(jax.ShapeDtypeStruct((2, *grad.shape), bf16))
        scratch += [pltpu.SemaphoreType.DMA((2,))] * 2
        args.append(grad)
    return pl.pallas_call(
        kernel,
        grid=(local, groups),
        in_specs=in_specs,
        out_specs=out_specs,
        out_shape=out_shape,
        scratch_shapes=scratch,
        compiler_params=sending(grad is not None, 4),
        cost_estimate=takes(31),
        name="experts_forward",
    )(*args)


def experts_backward(x, gx, gate, up, sw, wg, wu, wd):
    s, local, cap, width = x.shape
    ff = wg.shape[1]
    rows = s * cap
    groups, slots, lines, per = expert_specs(s, width)
    return pl.pallas_call(
        functools.partial(experts_backward_kernel, groups),
        grid=(local, groups),
        in_specs=[slots, slots, lines(PAD), lines(PAD), lines(1)]
        + [per(ff, width)] * 3,
        out_specs=[slots] + [per(ff, width)] * 3 + [lines(1)],
        out_shape=[jax.ShapeDtypeStruct(x.shape, bf16)]
        + [jax.ShapeDtypeStruct((local, ff, width), f32)] * 3
        + [jax.ShapeDtypeStruct((local, rows, 1), f32)],
        scratch_shapes=[pltpu.VMEM((PAD, width), bf16)] * 3,
        compiler_params=pltpu.CompilerParams(vmem_limit_bytes=VMEM_LIMIT),
        cost_estimate=takes(47),
        name="experts_backward",
    )(x, gx, gate, up, sw, wg, wu, wd)


def collect_kernel(y_ref, slot_ref, out_ref, pick):
    local = slot_ref.shape[1]
    masks = slot_masks(slot_ref, 0)
    for e in range(local):
        pick[e * CAP : (e + 1) * CAP, :] = masks[e].astype(f32).astype(bf16)
    out_ref[0] = tn(pick[...], y_ref[...].reshape(pick.shape[0], -1)).astype(bf16)


def collect_sending_kernel(
    y_ref, slot_ref, grad_ref, near_ref, out_ref, far_ref, given_ref, pick, send, recv, csend, crecv
):
    chip, core, z, cx, cy, cd = places()
    x_peer, y_peer, c_peer = (cx, core, z), (cy, core, z), (chip, 1 - core, z)
    half = grad_ref.shape[0] // 2
    top, low = pl.ds(0, half), pl.ds(half, half)
    relays = [
        remote(near_ref.at[0, top], far_ref.at[top], send.at[0], recv.at[0], y_peer),
        remote(near_ref.at[1, low], far_ref.at[low], send.at[1], recv.at[1], x_peer),
    ]
    passes = [
        remote(ref, given_ref.at[i], csend.at[i], crecv.at[i], c_peer)
        for i, ref in enumerate((grad_ref, near_ref.at[0], near_ref.at[1], far_ref))
    ]

    @pl.when(pl.program_id(0) == 0)
    def _():
        greet([x_peer, y_peer, c_peer])
        for copy in (*relays, *passes[:3]):
            copy.start()

    collect_kernel(y_ref, slot_ref, out_ref, pick)

    @pl.when(pl.program_id(0) == pl.num_programs(0) - 1)
    def _():
        for copy in relays:
            copy.wait_recv()
        passes[3].start()
        for copy in passes:
            copy.wait()
        for copy in relays:
            copy.wait_send()


def collect_back_kernel(experts, y_ref, slot_ref, gsw_ref, first_ref, out_ref, pick):
    local, rows = slot_ref.shape[1:]
    first = first_ref[0]
    masks = slot_masks(slot_ref, 0)
    number = lax.broadcasted_iota(jnp.int32, (experts, rows), 0)
    probs = jnp.zeros((experts, rows), f32)
    for e in range(local):
        pick[e * CAP : (e + 1) * CAP, :] = masks[e].astype(f32).astype(bf16)
        line = jnp.sum(jnp.where(masks[e], gsw_ref[e], 0.0), axis=0, keepdims=True)
        probs = jnp.where(number == first + e, line, probs)
    out_ref[0, :rows] = tn(pick[...], y_ref[...].reshape(pick.shape[0], -1)).astype(bf16)
    out_ref[0, rows:] = jnp.zeros((experts, out_ref.shape[2]), bf16)
    out_ref[0, rows:, :rows] = probs.astype(bf16)


def collect_sending(y, slot, grad, near):
    s, local, cap, width = y.shape
    rows = slot.shape[2]
    dma = pltpu.SemaphoreType.DMA
    whole = pl.BlockSpec(memory_space=pl.ANY)
    return pl.pallas_call(
        collect_sending_kernel,
        grid=(s,),
        in_specs=[
            pl.BlockSpec((1, local, cap, width), lambda i: (i, 0, 0, 0)),
            pl.BlockSpec((1, local, rows), lambda i: (i, 0, 0)),
            whole,
            whole,
        ],
        out_specs=[pl.BlockSpec((1, rows, width), lambda i: (i, 0, 0)), whole, whole],
        out_shape=[
            jax.ShapeDtypeStruct((s, rows, width), bf16),
            jax.ShapeDtypeStruct(grad.shape, bf16),
            jax.ShapeDtypeStruct((4, *grad.shape), bf16),
        ],
        scratch_shapes=[
            pltpu.VMEM((local * cap, rows), bf16),
            dma((2,)),
            dma((2,)),
            dma((4,)),
            dma((4,)),
        ],
        compiler_params=sending(True, 5),
        cost_estimate=takes(20),
        name="collect_sending",
    )(y, slot, grad, near)


def spread_grad_kernel(grad_ref, near_ref, far_ref, given_ref, slot_ref, x_ref, pick, gbuf, xbuf, come, gone):
    chip, core = lax.axis_index("xy"), lax.axis_index("core")
    local, rows = slot_ref.shape[1:]
    here = [grad_ref, near_ref.at[0], near_ref.at[1], far_ref]
    sources = [(here[t // 2], given_ref.at[t // 2])[t % 2] for t in range(8)]

    def in_copy(t):
        return pltpu.make_async_copy(sources[t], gbuf.at[t % 2], come.at[t % 2])

    def out_copy(t, src):
        return pltpu.make_async_copy(xbuf.at[t % 2], x_ref.at[src], gone.at[t % 2])

    number = lax.broadcasted_iota(jnp.int32, (CAP, rows), 0)
    in_copy(0).start()
    for t in range(8):
        if t < 7:
            in_copy(t + 1).start()
        x, y = (chip % 2 + (t // 2) % 2) % 2, (chip // 2 + t // 4) % 2
        src = (y * 2 + x) * 2 + (core + t % 2) % 2
        slots = slot_ref[src]
        for e in range(local):
            mask = slots[e : e + 1, :] == number
            pick[e * CAP : (e + 1) * CAP, :] = mask.astype(f32).astype(bf16)
        in_copy(t).wait()
        if t >= 2:
            out_copy(t, src).wait()
        xbuf[t % 2] = nt(pick[...], gbuf[t % 2]).astype(bf16).reshape(xbuf.shape[1:])
        out_copy(t, src).start()
    out_copy(0, 0).wait()
    out_copy(1, 0).wait()


def spread_grad(grad, near, far, given, slot):
    s, local, rows = slot.shape
    width = grad.shape[0]
    whole = pl.BlockSpec(memory_space=pl.ANY)
    dma = pltpu.SemaphoreType.DMA
    return pl.pallas_call(
        spread_grad_kernel,
        in_specs=[whole] * 4 + [pl.BlockSpec(memory_space=pltpu.VMEM)],
        out_specs=whole,
        out_shape=jax.ShapeDtypeStruct((s, local, CAP, width), bf16),
        scratch_shapes=[
            pltpu.VMEM((local * CAP, rows), bf16),
            pltpu.VMEM((2, width, rows), bf16),
            pltpu.VMEM((2, local, CAP, width), bf16),
            dma((2,)),
            dma((2,)),
        ],
        compiler_params=sending(False, 0),
        cost_estimate=takes(16),
        name="spread_grad",
    )(grad, near, far, given, slot)


def collect(y, slot, gsw=None, first=None, experts=0):
    s, local, cap, width = y.shape
    rows = slot.shape[2]
    in_specs = [
        pl.BlockSpec((1, local, cap, width), lambda i: (i, 0, 0, 0)),
        pl.BlockSpec((1, local, rows), lambda i: (i, 0, 0)),
    ]
    args = [y, slot]
    kernel = collect_kernel
    tall = rows
    if gsw is not None:
        in_specs += [
            pl.BlockSpec((local, cap, 1), lambda i: (0, i, 0)),
            pl.BlockSpec(memory_space=pltpu.SMEM),
        ]
        args += [gsw, first.reshape(1)]
        kernel = functools.partial(collect_back_kernel, experts)
        tall = rows + experts
    return pl.pallas_call(
        kernel,
        grid=(s,),
        in_specs=in_specs,
        out_specs=pl.BlockSpec((1, tall, width), lambda i: (i, 0, 0)),
        out_shape=jax.ShapeDtypeStruct((s, tall, width), bf16),
        scratch_shapes=[pltpu.VMEM((local * cap, rows), bf16)],
        compiler_params=pltpu.CompilerParams(vmem_limit_bytes=VMEM_LIMIT),
        cost_estimate=takes(17),
        name="collect",
    )(*args)


MESH = pl.DeviceIdType.MESH
EXTRA = 64


def places():
    chip, core, z = lax.axis_index("xy"), lax.axis_index("core"), lax.axis_index("hs")
    x, y = chip % 2, chip // 2
    return chip, core, z, y * 2 + (1 - x), (1 - y) * 2 + x, (1 - y) * 2 + (1 - x)


def greet(peers):
    barrier = pltpu.get_barrier_semaphore()
    for peer in peers:
        pl.semaphore_signal(barrier, inc=1, device_id=peer, device_id_type=MESH)
    pl.semaphore_wait(barrier, len(peers))


def remote(src, dst, send, recv, peer):
    return pltpu.make_async_remote_copy(
        src_ref=src, dst_ref=dst, send_sem=send, recv_sem=recv, device_id=peer, device_id_type=MESH
    )


def block(q, size):
    return pl.ds(pl.multiple_of(q * size, 16), size)


def weight_sum(grads, given, half, land, out_ref, csend, crecv, send, recv):
    chip, core, z, cx, cy, cd = places()
    other = 1 - core
    c_peer = (chip, other, z)
    chips = (cx, cy, cd)
    count = grads.shape[0] // 2
    piece = count // 4

    to_core = remote(grads.at[block(other, count)], given, csend.at[0], crecv.at[0], c_peer)
    scatter = [
        remote(half.at[block(c, piece)], land.at[i], send.at[i], recv.at[i], (c, core, z))
        for i, c in enumerate(chips)
    ]

    def share():
        to_core.wait_recv()
        half[...] = (grads[block(core, count)].astype(f32) + given[...].astype(f32)).astype(bf16)
        for i in (2, 0, 1):
            scatter[i].start()

    def place(c, k):
        return pl.ds(pl.multiple_of(k * count + c * piece, 16), piece)

    def give(number, c, k, sems, peer):
        return remote(out_ref.at[place(c, k)], out_ref.at[place(c, k)], *sems(number), peer)

    def chip_sems(i):
        return send.at[3 + i], recv.at[3 + i]

    def core_sems(i):
        return csend.at[1 + i], crecv.at[1 + i]

    gather = [give(i, chip, core, chip_sems, (c, core, z)) for i, c in enumerate(chips)]
    over = [give(i, c, core, core_sems, c_peer) for i, c in enumerate((*chips, chip))]

    def give_back():
        done = half[block(chip, piece)].astype(f32)
        for i in range(3):
            scatter[i].wait_recv()
            done = done + land[i].astype(f32)
        out_ref[place(chip, core)] = done.astype(bf16)
        for i in (2, 0, 1):
            gather[i].start()
        over[3].start()

    def end():
        for i, c in enumerate(chips):
            give(i, c, core, chip_sems, (c, core, z)).wait_recv()
            over[i].start()
        for i, c in enumerate((*chips, chip)):
            give(i, c, other, core_sems, c_peer).wait_recv()
        for copy in (to_core, *scatter, *gather, *over):
            copy.wait_send()

    return to_core.start, share, give_back, end


def weight_sum_scratch(tall, width):
    dma = pltpu.SemaphoreType.DMA
    return [
        pltpu.VMEM((tall, width), bf16),
        pltpu.VMEM((tall // 2, width), bf16),
        pltpu.VMEM((tall // 2, width), bf16),
        pltpu.VMEM((3, tall // 8, width), bf16),
        dma((5,)),
        dma((5,)),
        dma((6,)),
        dma((6,)),
    ]


def gather_spread_kernel(
    own_ref,
    slots_ref,
    router_ref,
    grad_ref,
    x_ref,
    sw_ref,
    slot_ref,
    grad_all_ref,
    held,
    pick,
    xbuf,
    send,
    recv,
    copied,
    zsend,
    zrecv,
):
    chip, core, z, cx, cy, cd = places()
    other = 1 - core
    x_peer, y_peer, c_peer = (cx, core, z), (cy, core, z), (chip, other, z)
    tall = held.shape[1]
    half = tall // 2
    local, rows = slot_ref.shape[1:]
    me = chip * 2 + core
    top, low = pl.ds(0, half), pl.ds(half, half)

    def at(c, k):
        return c * 2 + k

    def move(number, src_slot, part, peer):
        return remote(
            held.at[src_slot, part], held.at[src_slot, part], send.at[number], recv.at[number], peer
        )

    whole = pl.ds(0, tall)
    z_peers = [(chip, core, (z + i) % 4) for i in (1, 2, 3)]
    greet([x_peer, y_peer, c_peer, *z_peers])
    quarter = grad_ref.shape[0]

    def grad_copy(i, q):
        return remote(
            grad_ref, grad_all_ref.at[block(q, quarter)], zsend.at[i], zrecv.at[i], z_peers[i]
        )

    held[me, :rows] = own_ref[...]
    packed = tall - rows
    held[me, rows:, 2 * rows :] = jnp.zeros((packed, own_ref.shape[1] - 2 * rows), bf16)
    held[me, rows:, :rows] = slots_ref[:packed]
    held[me, rows:, rows : 2 * rows] = slots_ref[packed:]
    x_top, x_low = move(0, me, top, x_peer), move(1, me, low, x_peer)
    y_low, y_top = move(2, me, low, y_peer), move(3, me, top, y_peer)
    to_core = move(4, me, whole, c_peer)
    relay_top, relay_low = move(5, at(cx, core), top, y_peer), move(6, at(cy, core), low, x_peer)
    pass_x, pass_y = move(7, at(cx, core), whole, c_peer), move(8, at(cy, core), whole, c_peer)
    pass_d = move(9, at(cd, core), whole, c_peer)
    for copy in (x_top, y_low, x_low, y_top, to_core, *[grad_copy(i, z) for i in (1, 0, 2)]):
        copy.start()
    grad_all_ref[block(z, quarter)] = grad_ref[...]

    def arrived(number, slot, part):
        move(number, slot, part, c_peer).wait_recv()

    number = lax.broadcasted_iota(jnp.int32, (CAP, rows), 0)
    first = me * local
    line = lax.broadcasted_iota(jnp.int32, (local, EXTRA), 0)
    column = lax.broadcasted_iota(jnp.int32, (local, EXTRA), 1)
    chosen = (column == line + first).astype(f32).astype(bf16)

    def out_copy(t, src):
        return pltpu.make_async_copy(xbuf.at[t % 2], x_ref.at[src], copied.at[t % 2])

    def step(t, carry):
        @pl.when(t == 1)
        def _():
            arrived(4, at(chip, other), whole)

        @pl.when(t == 2)
        def _():
            arrived(0, at(cx, core), top)
            relay_top.start()
            arrived(2, at(cy, core), low)
            relay_low.start()
            arrived(1, at(cx, core), low)
            pass_x.start()

        @pl.when(t == 3)
        def _():
            arrived(3, at(cy, core), top)
            pass_y.start()
            arrived(7, at(cx, other), whole)

        @pl.when(t == 5)
        def _():
            arrived(8, at(cy, other), whole)

        @pl.when(t == 6)
        def _():
            arrived(5, at(cd, core), top)
            arrived(6, at(cd, core), low)
            pass_d.start()

        @pl.when(t == 7)
        def _():
            arrived(9, at(cd, other), whole)

        x, y = (chip % 2 + (t // 2) % 2) % 2, (chip // 2 + t // 4) % 2
        src = (y * 2 + x) * 2 + (core + t % 2) % 2
        slots = nn(chosen[:, :packed], held[src, rows:, :rows])
        slots += nn(chosen[:, packed:], held[src, rows:, rows : 2 * rows])
        slots = slots.astype(jnp.int32)
        slot_ref[src] = slots
        logits = nt(router_ref[...], held[src, :rows])
        raised = jnp.exp(logits - jnp.max(logits, axis=0, keepdims=True))
        gates = raised / jnp.sum(raised, axis=0, keepdims=True)
        for e in range(local):
            mask = slots[e : e + 1, :] == number
            pick[e * CAP : (e + 1) * CAP, :] = mask.astype(f32).astype(bf16)
            sw_ref[e, pl.ds(pl.multiple_of(src * CAP, 8), CAP), :] = jnp.sum(
                jnp.where(mask, gates[e : e + 1, :], 0.0), axis=1, keepdims=True
            )

        @pl.when(t >= 2)
        def _():
            out_copy(t, src).wait()

        xbuf[t % 2] = nn(pick[...], held[src, :rows]).astype(bf16).reshape(xbuf.shape[1:])
        out_copy(t, src).start()
        return carry

    lax.fori_loop(0, 8, step, 0)
    out_copy(0, me).wait()
    out_copy(1, me).wait()
    for i in range(3):
        grad_copy(i, (z + 3 - i) % 4).wait_recv()
        grad_copy(i, z).wait_send()
    for copy in (x_top, x_low, y_low, y_top, to_core, relay_top, relay_low, pass_x, pass_y, pass_d):
        copy.wait_send()


def gather_spread(own, slots, router_t, grad_quarter, local, ep_count):
    rows, width = own.shape
    tall = rows + EXTRA // 2
    vmem = pl.BlockSpec(memory_space=pltpu.VMEM)
    return pl.pallas_call(
        gather_spread_kernel,
        in_specs=[vmem] * 4,
        out_specs=[pl.BlockSpec(memory_space=pl.ANY), vmem, vmem, vmem],
        out_shape=[
            jax.ShapeDtypeStruct((ep_count, local, CAP, width), bf16),
            jax.ShapeDtypeStruct((local, ep_count * CAP, 1), f32),
            jax.ShapeDtypeStruct((ep_count, local, rows), jnp.int32),
            jax.ShapeDtypeStruct((width, rows), bf16),
        ],
        scratch_shapes=[
            pltpu.VMEM((ep_count, tall, width), bf16),
            pltpu.VMEM((local * CAP, rows), bf16),
            pltpu.VMEM((2, local, CAP, width), bf16),
            pltpu.SemaphoreType.DMA((10,)),
            pltpu.SemaphoreType.DMA((10,)),
            pltpu.SemaphoreType.DMA((2,)),
            pltpu.SemaphoreType.DMA((3,)),
            pltpu.SemaphoreType.DMA((3,)),
        ],
        compiler_params=pltpu.CompilerParams(
            vmem_limit_bytes=VMEM_LIMIT, collective_id=0, has_side_effects=True
        ),
        cost_estimate=takes(62),
        name="gather_spread",
    )(own, slots, router_t, grad_quarter)


def front_kernel(
    x_ref,
    gain_ref,
    wq_ref,
    wk_ref,
    wv_ref,
    wo_ref,
    doc_ref,
    cos_ref,
    sin_ref,
    normed1_out,
    q_out,
    k_out,
    v_out,
    probs_out,
    attended_out,
    out_out,
    residual_ref,
    normed2_ref,
    normed1_ref,
    q_ref,
    k_ref,
    v_ref,
    probs_ref,
    attended_ref,
    out_ref,
    gone,
    shared,
    beside,
    esend,
    erecv,
    asend,
    arecv,
    zsend,
    zrecv,
    send,
    recv,
    csend,
    crecv,
):
    chip, core, z, cx, cy, cd = places()
    other = 1 - core
    odd = z % 2
    c_peer = (chip, other, z)
    chips = (cx, cy, cd)
    z_peers = [(chip, core, (z + i) % 4) for i in (1, 2, 3)]
    pair = (chip, core, z + 1 - 2 * odd)
    rows, width = x_ref.shape
    quarter = wq_ref.shape[0]
    whole = HEAD_DIM * (quarter // HEAD_DIM)
    spare = quarter - whole
    greet([c_peer, *[(c, core, z) for c in chips], *z_peers])

    full_rows = pl.ds(pl.multiple_of(odd * spare, 16), whole)
    half_rows = pl.ds(pl.multiple_of((1 - odd) * whole, 16), spare)
    for i, ref in enumerate((wq_ref, wk_ref, wv_ref)):
        shared[i * spare : (i + 1) * spare] = ref[half_rows]
    trade = remote(shared, beside, esend, erecv, pair)
    trade.start()

    share, lanes = quarter // 4, width // 2
    my_lanes = pl.ds(pl.multiple_of(core * lanes, 128), lanes)

    def piece(c):
        return pl.ds(pl.multiple_of(c * share, 16), share)

    out_z = [
        remote(
            wo_ref.at[piece(chip), my_lanes],
            out_ref.at[z, piece(chip), my_lanes],
            zsend.at[i],
            zrecv.at[i],
            peer,
        )
        for i, peer in enumerate(z_peers)
    ]
    for i in (1, 0, 2):
        out_z[i].start()
    behind = [(z + 3 - i) % 4 for i in range(3)]

    def out_chip(i, j, c):
        at = out_ref.at[behind[i], piece(c), my_lanes]
        return remote(at, at, send.at[3 * i + j], recv.at[3 * i + j], (chips[j], core, z))

    def out_core(i, k):
        half = pl.ds(pl.multiple_of(k * lanes, 128), lanes)
        at = out_ref.at[behind[i], :, half]
        return remote(at, at, csend.at[i], crecv.at[i], c_peer)

    x = x_ref[...].astype(f32)
    rms1 = lax.rsqrt(jnp.sum(x * x, axis=-1, keepdims=True) * (1.0 / width) + EPS)
    normed1_ref[...] = (x * rms1 * gain_ref[0:1]).astype(bf16)
    out_ref[z] = wo_ref[...]

    cosine, sine = cos_ref[...], sin_ref[...]
    half_dim = HEAD_DIM // 2
    scale = 1.0 / math.sqrt(HEAD_DIM)
    row = lax.broadcasted_iota(jnp.int32, (rows, rows), 0)
    column = lax.broadcasted_iota(jnp.int32, (rows, rows), 1)
    doc = jnp.broadcast_to(doc_ref[...].astype(f32), (rows, rows))
    allowed = (row >= column) & (doc == doc.T)

    kept = (normed1_ref, q_ref, k_ref, v_ref, probs_ref, attended_ref, out_ref)
    outs = (normed1_out, q_out, k_out, v_out, probs_out, attended_out, out_out)
    writes = [pltpu.make_async_copy(a, b, gone.at[i]) for i, (a, b) in enumerate(zip(kept, outs))]
    writes[0].start()

    def turn(pre):
        a, b = pre[:half_dim], pre[half_dim:]
        return (
            jnp.concatenate([a * cosine - b * sine, b * cosine + a * sine], axis=0).astype(bf16)
        )

    def attend(h):
        scores = jnp.where(allowed, tn(q_ref[h], k_ref[h]) * scale, -1e30)
        raised = jnp.exp(scores - jnp.max(scores, axis=-1, keepdims=True))
        probs = raised * (1.0 / jnp.sum(raised, axis=-1, keepdims=True))
        probs_ref[h] = probs
        return nt(v_ref[h], probs.astype(bf16)).astype(bf16)

    def project(at):
        return [nt(ref[at], normed1_ref[...]) for ref in (wq_ref, wk_ref, wv_ref)]

    q, k, v = project(full_rows)
    heads = whole // HEAD_DIM
    for h in range(heads):
        at = slice(h * HEAD_DIM, (h + 1) * HEAD_DIM)
        q_ref[h], k_ref[h], v_ref[h] = turn(q[at]), turn(k[at]), v[at].astype(bf16)

    def attended_copy(number, start, size):
        at = attended_ref.at[pl.ds(pl.multiple_of(start, 16), size)]
        return lambda i: remote(
            at, at, asend.at[number, i], arecv.at[number, i], z_peers[i]
        )

    mine = z * quarter
    copies = []
    for h in range(heads):
        start = mine + odd * spare + h * HEAD_DIM
        attended_ref[pl.ds(pl.multiple_of(start, 16), HEAD_DIM)] = attend(h)
        copy = attended_copy(h, start, HEAD_DIM)
        copies += [copy(1), copy(0), copy(2)]
        for one in copies[-3:]:
            one.start()
        if h == 0:
            for i in range(3):
                out_z[i].wait_recv()
                for j in (2, 0, 1):
                    out_chip(i, j, chip).start()

    trade.wait_recv()
    for i, (ref, to) in enumerate(((wq_ref, q_ref), (wk_ref, k_ref), (wv_ref, v_ref))):
        normed1 = normed1_ref[...]
        here = nt(ref[half_rows], normed1)
        there = nt(beside[i * spare : (i + 1) * spare], normed1)
        first = jnp.where(odd == 1, there, here)
        second = jnp.where(odd == 1, here, there)
        both = jnp.concatenate([first, second], axis=0)
        to[heads] = both.astype(bf16) if to is v_ref else turn(both)
    last = attend(heads)
    for i in (1, 2, 3, 4):
        writes[i].start()
    last = jnp.where(odd == 1, last[spare:], last[:spare])
    start = mine + (1 - odd) * whole
    attended_ref[pl.ds(pl.multiple_of(start, 16), spare)] = last
    copy = attended_copy(heads, start, spare)
    copies += [copy(1), copy(0), copy(2)]
    for one in copies[-3:]:
        one.start()

    for i in range(3):
        for j in range(3):
            out_chip(i, j, chips[j]).wait_recv()
        out_core(i, core).start()
    for i in range(3):
        from_z = (z + 3 - i) % 4
        from_odd = from_z % 2
        for h in range(heads):
            attended_copy(h, from_z * quarter + from_odd * spare + h * HEAD_DIM, HEAD_DIM)(i).wait_recv()
        attended_copy(heads, from_z * quarter + (1 - from_odd) * whole, spare)(i).wait_recv()
        out_core(i, other).wait_recv()
    writes[5].start()
    writes[6].start()
    attended = attended_ref[...].T
    residual = x_ref[...].astype(f32) + nt(attended, out_ref[...].reshape(width, width))
    residual_ref[...] = residual
    rms2 = lax.rsqrt(jnp.sum(residual * residual, axis=-1, keepdims=True) * (1.0 / width) + EPS)
    normed2_ref[...] = (residual * rms2 * gain_ref[1:2]).astype(bf16)
    for write in writes:
        write.wait()
    for one in (trade, *out_z, *copies):
        one.wait_send()
    for i in range(3):
        for j in range(3):
            out_chip(i, j, chip).wait_send()
        out_core(i, core).wait_send()


def front(x, gains, wq, wk, wv, wo, doc, tables):
    rows, width = x.shape
    quarter = wq.shape[0]
    heads = -(-quarter // HEAD_DIM)
    spare = quarter % HEAD_DIM
    vmem = pl.BlockSpec(memory_space=pltpu.VMEM)
    dma = pltpu.SemaphoreType.DMA
    low = lambda *shape: jax.ShapeDtypeStruct(shape, bf16)
    early = [
        low(rows, width),
        *[low(heads, HEAD_DIM, rows)] * 3,
        jax.ShapeDtypeStruct((heads, rows, rows), f32),
        low(width, rows),
        low(4, quarter, width),
    ]
    return pl.pallas_call(
        front_kernel,
        in_specs=[vmem] * 9,
        out_specs=[pl.BlockSpec(memory_space=pl.ANY)] * len(early) + [vmem] * 2,
        out_shape=[*early, jax.ShapeDtypeStruct((rows, width), f32), low(rows, width)],
        scratch_shapes=[
            *[pltpu.VMEM(a.shape, a.dtype) for a in early],
            dma((len(early),)),
            pltpu.VMEM((3 * spare, width), bf16),
            pltpu.VMEM((3 * spare, width), bf16),
            dma,
            dma,
            dma((heads, 3)),
            dma((heads, 3)),
            dma((3,)),
            dma((3,)),
            dma((9,)),
            dma((9,)),
            dma((3,)),
            dma((3,)),
        ],
        compiler_params=pltpu.CompilerParams(
            vmem_limit_bytes=VMEM_LIMIT, collective_id=1, has_side_effects=True
        ),
        cost_estimate=takes(50),
        name="front",
    )(x, gains, wq, wk, wv, wo, doc, *tables)


def collect_sum_kernel(
    y_ref,
    slot_ref,
    gsw_ref,
    normed_ref,
    grad_ref,
    gate_ref,
    up_ref,
    down_ref,
    out_ref,
    sum_ref,
    forward_ref,
    mine,
    pick,
    ybuf,
    stage,
    given,
    sums,
    relay,
    land,
    zland,
    copied,
    core_send,
    core_recv,
    send,
    recv,
    zsend,
    zrecv,
    grads,
    *more,
):
    chip, core, z, cx, cy, cd = places()
    other = 1 - core
    x_peer, y_peer, c_peer = (cx, core, z), (cy, core, z), (chip, other, z)
    z_peers = [(chip, core, (z + i) % 4) for i in (1, 2, 3)]
    local, rows = slot_ref.shape[1:]
    tall = out_ref.shape[0]
    me = chip * 2 + core
    number = lax.broadcasted_iota(jnp.int32, (CAP, rows), 0)
    row = lax.broadcasted_iota(jnp.int32, (EXTRA, rows), 0)

    greet([x_peer, y_peer, c_peer, (cd, core, z), *z_peers])

    def sequence(t):
        p = t // 2
        x, y = (chip % 2 + 1 + p // 2) % 2, (chip // 2 + 1 + p % 2) % 2
        return (y * 2 + x) * 2 + (core + 1 + t % 2) % 2

    def in_copy(t):
        return pltpu.make_async_copy(y_ref.at[sequence(t)], ybuf.at[t % 2], copied.at[t % 2])

    def to_core(p):
        return remote(stage.at[p % 2], given.at[p], core_send.at[p], core_recv.at[p], c_peer)

    units = 3
    unit = tall // units
    half, part = unit // 2, unit // 4

    def top(u):
        return pl.ds(u * unit, half)

    def low(u):
        return pl.ds(u * unit + half, half)

    def over(u, number, src, dst, peer):
        return remote(src, dst, send.at[u, number], recv.at[u, number], peer)

    far_top = [over(u, 0, sums.at[0, top(u)], relay.at[u, 0], x_peer) for u in range(units)]
    far_low = [over(u, 1, sums.at[0, low(u)], relay.at[u, 1], y_peer) for u in range(units)]
    x_top = [over(u, 2, sums.at[1, top(u)], land.at[0, top(u)], x_peer) for u in range(units)]
    x_low = [over(u, 3, sums.at[1, low(u)], land.at[0, low(u)], x_peer) for u in range(units)]
    y_low = [over(u, 4, sums.at[2, low(u)], land.at[1, low(u)], y_peer) for u in range(units)]
    y_top = [over(u, 5, sums.at[2, top(u)], land.at[1, top(u)], y_peer) for u in range(units)]

    in_copy(0).start()
    start, share, give_back, end = weight_sum(grads, *more[:3], sum_ref, *more[3:])

    def shared_expert():
        normed, grad_t = normed_ref[...], grad_ref[...]
        size = gate_ref.shape[0]
        gate, up = nt(gate_ref[...], normed), nt(up_ref[...], normed)
        sig = 1.0 / (1.0 + jnp.exp(-gate))
        act = gate * sig
        hidden = (act * up).astype(bf16)
        forward_ref[...] = tn(hidden, down_ref[...]).astype(bf16)
        grad_hidden = nn(down_ref[...], grad_t)
        grad_gate = (grad_hidden * up * sig * (1.0 + gate * (1.0 - sig))).astype(bf16)
        grad_up = (grad_hidden * act).astype(bf16)
        grads[:size] = nn(grad_gate, normed).astype(bf16)
        grads[size : 2 * size] = nn(grad_up, normed).astype(bf16)
        grads[2 * size : 3 * size] = nt(hidden, grad_t).astype(bf16)
        grads[3 * size :] = jnp.zeros((grads.shape[0] - 3 * size, grads.shape[1]), bf16)
        start()
        mine[...] = (tn(grad_gate, gate_ref[...]) + tn(grad_up, up_ref[...])).astype(bf16)

    def step(t, carry):
        @pl.when(t < 7)
        def _():
            in_copy(t + 1).start()

        p, s = t // 2, sequence(t)
        probs = jnp.zeros((EXTRA, rows), f32)
        for e in range(local):
            mask = slot_ref[s, e : e + 1, :] == number
            pick[e * CAP : (e + 1) * CAP, :] = mask.astype(f32).astype(bf16)
            column = gsw_ref[e, pl.ds(pl.multiple_of(s * CAP, 8), CAP), :]
            line = jnp.sum(jnp.where(mask, column, 0.0), axis=0, keepdims=True)
            probs = jnp.where(row == me * local + e, line, probs)
        in_copy(t).wait()
        back = tn(pick[...], ybuf[t % 2].reshape(local * CAP, -1))

        @pl.when(t % 2 == 0)
        def _():
            @pl.when(p >= 2)
            def _():
                to_core(p - 2).wait_send()

            stage[p % 2, :rows] = back.astype(bf16)
            stage[p % 2, rows:] = jnp.zeros((tall - rows, back.shape[1]), bf16)
            stage[p % 2, rows:, :rows] = probs.astype(bf16)
            to_core(p).start()

        @pl.when(t % 2 == 1)
        def _():
            to_core(p).wait_recv()
            sums[p, :rows] = (back + given[p, :rows].astype(f32)).astype(bf16)
            sums[p, rows:] = given[p, rows:]
            sums[p, rows:, :rows] = (probs + given[p, rows:, :rows].astype(f32)).astype(bf16)

        @pl.when(t == 1)
        def _():
            far_top[0].start()
            far_low[0].start()

        @pl.when(t == 3)
        def _():
            x_top[0].start()

        @pl.when(t == 5)
        def _():
            y_low[0].start()
            far_top[1].start()
            far_low[1].start()

        return carry

    lax.fori_loop(0, 8, step, 0)
    def relayed(u):
        far_low[u].wait_recv()
        at = slice(u * unit + half, (u + 1) * unit)
        sums[1, at] = (sums[1, at].astype(f32) + relay[u, 1].astype(f32)).astype(bf16)
        x_low[u].start()
        far_top[u].wait_recv()
        at = slice(u * unit, u * unit + half)
        sums[2, at] = (sums[2, at].astype(f32) + relay[u, 0].astype(f32)).astype(bf16)
        y_top[u].start()

    def block_of(u, q):
        return pl.ds(pl.multiple_of(u * unit + q * part, 16), part)

    def z_sems(u, number):
        return zsend.at[u, number], zrecv.at[u, number]

    scatter = [
        [
            remote(
                sums.at[3, block_of(u, (z + i) % 4)],
                zland.at[u, i - 1],
                *z_sems(u, i - 1),
                z_peers[i - 1],
            )
            for i in (1, 2, 3)
        ]
        for u in range(units)
    ]

    def back_copy(u, q, i):
        at = out_ref.at[block_of(u, q)]
        return remote(at, at, *z_sems(u, 2 + i), z_peers[i - 1])

    def landed(u):
        for copy in (x_top[u], y_top[u], x_low[u], y_low[u]):
            copy.wait_recv()
        at = slice(u * unit, (u + 1) * unit)
        added = sums[3, at].astype(f32) + land[0, at].astype(f32) + land[1, at].astype(f32)
        ours = min(rows, (u + 1) * unit) - u * unit
        if ours == unit:
            sums[3, at] = (added + mine[at].astype(f32)).astype(bf16)
        else:
            here = slice(u * unit, u * unit + ours)
            sums[3, here] = (added[:ours] + mine[here].astype(f32)).astype(bf16)
            sums[3, u * unit + ours : (u + 1) * unit] = added[ours:].astype(bf16)
        for i in (1, 0, 2):
            scatter[u][i].start()

    def summed(u):
        done = sums[3, block_of(u, z)].astype(f32)
        for i in range(3):
            scatter[u][i].wait_recv()
            done = done + zland[u, i].astype(f32)
        out_ref[block_of(u, z)] = done.astype(bf16)
        for i in (2, 1, 3):
            back_copy(u, z, i).start()

    relayed(0)
    x_top[1].start()
    y_low[1].start()
    far_top[2].start()
    far_low[2].start()
    shared_expert()
    relayed(1)
    x_top[2].start()
    y_low[2].start()
    landed(0)
    relayed(2)
    share()
    landed(1)
    summed(0)
    landed(2)
    summed(1)
    give_back()
    summed(2)
    end()
    for u in range(units):
        for i in (1, 2, 3):
            back_copy(u, (z + 4 - i) % 4, i).wait_recv()
    for u in range(units):
        for copy in (far_top[u], far_low[u], x_top[u], x_low[u], y_low[u], y_top[u], *scatter[u]):
            copy.wait_send()
        for i in (1, 2, 3):
            back_copy(u, z, i).wait_send()
    for p in (2, 3):
        to_core(p).wait_send()


def collect_sum(y, slot, gsw, normed, grad_t, *shared):
    s, local, cap, width = y.shape
    rows = slot.shape[2]
    tall = rows + EXTRA
    dma = pltpu.SemaphoreType.DMA
    weights = 128 * (-(-sum(a.shape[0] for a in shared) // 128))
    vmem = pl.BlockSpec(memory_space=pltpu.VMEM)
    return pl.pallas_call(
        collect_sum_kernel,
        in_specs=[pl.BlockSpec(memory_space=pl.ANY)] + [vmem] * 7,
        out_specs=[vmem, vmem, vmem],
        out_shape=[
            jax.ShapeDtypeStruct((tall, width), bf16),
            jax.ShapeDtypeStruct((weights, width), bf16),
            jax.ShapeDtypeStruct((rows, width), bf16),
        ],
        scratch_shapes=[
            pltpu.VMEM((rows, width), bf16),
            pltpu.VMEM((local * cap, rows), bf16),
            pltpu.VMEM((2, local, cap, width), bf16),
            pltpu.VMEM((2, tall, width), bf16),
            pltpu.VMEM((4, tall, width), bf16),
            pltpu.VMEM((4, tall, width), bf16),
            pltpu.VMEM((3, 2, tall // 6, width), bf16),
            pltpu.VMEM((2, tall, width), bf16),
            pltpu.VMEM((3, 3, tall // 12, width), bf16),
            dma((2,)),
            dma((4,)),
            dma((4,)),
            dma((3, 6)),
            dma((3, 6)),
            dma((3, 6)),
            dma((3, 6)),
            *weight_sum_scratch(weights, width),
        ],
        compiler_params=pltpu.CompilerParams(
            vmem_limit_bytes=VMEM_LIMIT, collective_id=2, has_side_effects=True
        ),
        cost_estimate=takes(131),
        name="collect_sum",
    )(y, slot, gsw, normed, grad_t, *shared)


def back_kernel(
    sums_ref,
    residual_ref,
    normed2_ref,
    grad_ref,
    router_ref,
    gain_ref,
    cos_ref,
    sin_ref,
    *refs,
):
    late, outs, rest = refs[:11], refs[11:16], refs[16:]
    held, sems, rest = rest[:11], rest[11], rest[12:]
    loads = [pltpu.make_async_copy(a, b, sems.at[i]) for i, (a, b) in enumerate(zip(late, held))]
    for load in loads:
        load.start()
    back_steps(
        loads,
        sums_ref,
        residual_ref,
        normed2_ref,
        grad_ref,
        router_ref,
        gain_ref,
        cos_ref,
        sin_ref,
        *held,
        *outs,
        *rest,
    )


def back_steps(
    loads,
    sums_ref,
    residual_ref,
    normed2_ref,
    grad_ref,
    router_ref,
    gain_ref,
    cos_ref,
    sin_ref,
    out_ref,
    q_ref,
    k_ref,
    v_ref,
    probs_ref,
    wq_ref,
    wk_ref,
    wv_ref,
    attended_ref,
    x_ref,
    normed_ref,
    tokens_ref,
    early_ref,
    first_ref,
    second_ref,
    shared_ref,
    dq_ref,
    dk_ref,
    dv_ref,
    x_t,
    gain_column,
    back_t,
    low_t,
    part,
    low_part,
    zland,
    mine,
    theirs,
    zsend,
    zrecv,
    lsend,
    lrecv,
    *more,
):
    chip, core, z, cx, cy, cd = places()
    odd = z % 2
    c_peer = (chip, 1 - core, z)
    z_peers = [(chip, core, (z + i) % 4) for i in (1, 2, 3)]
    quarter, width = wq_ref.shape
    rows = x_ref.shape[0]
    groups = [
        weight_sum(*more[8 * i : 8 * i + 4], ref, *more[8 * i + 4 : 8 * i + 8])
        for i, ref in enumerate((early_ref, first_ref, second_ref, shared_ref))
    ]
    early, *by_head = [more[8 * i] for i in range(4)]
    START, SHARE, GIVE_BACK, END = range(4)
    experts = router_ref.shape[0]
    whole = HEAD_DIM * (quarter // HEAD_DIM)
    spare = quarter - whole
    heads = whole // HEAD_DIM
    greet([c_peer, *[(c, core, z) for c in (cx, cy, cd)], *z_peers])

    logits = nt(router_ref[...], normed2_ref[...])
    raised = jnp.exp(logits - jnp.max(logits, axis=0, keepdims=True))
    gates = raised / jnp.sum(raised, axis=0, keepdims=True)
    grad_probs = sums_ref[rows:, :rows].astype(f32)
    grad_logits = gates * (grad_probs - jnp.sum(grad_probs * gates, axis=0, keepdims=True))
    grad_logits = grad_logits.astype(bf16)
    grad_router = nn(grad_logits, normed2_ref[...])
    grad_normed2 = sums_ref[:rows].astype(f32) + tn(grad_logits, router_ref[...])
    residual = residual_ref[...]
    rms2 = lax.rsqrt(jnp.sum(residual * residual, axis=-1, keepdims=True) * (1.0 / width) + EPS)
    grad_ffn = jnp.sum(grad_normed2 * residual * rms2, axis=0, keepdims=True)
    u = grad_normed2 * gain_ref[1:2]
    mean2 = jnp.sum(u * residual, axis=-1, keepdims=True) * (1.0 / width)
    added = rms2 * u - residual * (rms2 * rms2 * rms2 * mean2)
    back_t[...] = added.T + grad_ref[...].astype(f32)
    low_t[...] = back_t[...].astype(bf16)
    own = block(z, quarter)

    cosine, sine = cos_ref[...], sin_ref[...]
    half_dim = HEAD_DIM // 2
    scale = 1.0 / math.sqrt(HEAD_DIM)

    def turn_back(v):
        a, b = v[:half_dim] * scale, v[half_dim:] * scale
        turned = [a * cosine + b * sine, b * cosine - a * sine]
        return jnp.concatenate(turned, axis=0).astype(bf16)

    for i in range(5):
        loads[i].wait()
    first_lane = z * quarter + odd * spare
    shared_lane = z * quarter + (1 - odd) * whole - odd * spare
    for h in range(heads + 1):
        lane = first_lane + h * HEAD_DIM if h < heads else shared_lane
        lane = pl.ds(pl.multiple_of(lane, HEAD_DIM), HEAD_DIM)
        grad_attended = tn(out_ref[:, lane], low_t[...]).astype(bf16)
        probs = probs_ref[h]
        grad_p = tn(grad_attended, v_ref[h])
        grad_v = nn(grad_attended, probs.astype(bf16)).astype(bf16)
        delta = jnp.sum(probs * grad_p, axis=-1, keepdims=True)
        grad_s = (probs * (grad_p - delta)).astype(bf16)
        grad_q = turn_back(nt(k_ref[h], grad_s))
        grad_k = turn_back(nn(q_ref[h], grad_s))
        for ref, value in ((dq_ref, grad_q), (dk_ref, grad_k), (dv_ref, grad_v)):
            if h < heads:
                at = pl.ds(pl.multiple_of(odd * spare + h * HEAD_DIM, 16), HEAD_DIM)
                ref[at] = value
            else:
                at = pl.ds(pl.multiple_of((1 - odd) * whole, 16), spare)
                ref[at] = jnp.where(odd == 1, value[spare:], value[:spare])

    for i in (5, 6, 7):
        loads[i].wait()
    part[...] = tn(wq_ref[...], dq_ref[...])
    part[...] += tn(wk_ref[...], dk_ref[...])
    part[...] += tn(wv_ref[...], dv_ref[...])
    low_part[...] = part[...].astype(bf16)
    to_z = [
        remote(
            low_part.at[block((z + i) % 4, quarter)],
            zland.at[i - 1],
            zsend.at[i - 1],
            zrecv.at[i - 1],
            z_peers[i - 1],
        )
        for i in (1, 2, 3)
    ]
    few_to_z = [
        remote(mine, theirs.at[i], lsend.at[i], lrecv.at[i], peer) for i, peer in enumerate(z_peers)
    ]
    for i in (1, 0, 2):
        to_z[i].start()
    loads[8].wait()
    loads[9].wait()
    loads[10].wait()
    early[:quarter] = nt(low_t[own], attended_ref[...]).astype(bf16)
    early[quarter:] = grad_router.astype(bf16)
    groups[0][START]()
    x_t[...] = x_ref[...].T
    gain_column[...] = jnp.broadcast_to(gain_ref[0:1], (8, width)).T
    x_all = x_t[...].astype(f32)
    rms1 = lax.rsqrt(jnp.sum(x_all * x_all, axis=0, keepdims=True) * (1.0 / width) + EPS)
    along = part[...] * x_all
    mine[...] = jnp.zeros(mine.shape, f32)
    mine[0:1, :rows] = jnp.sum(along * gain_column[:, 0:1], axis=0, keepdims=True)
    mine[:, rows:] = nt(jnp.ones((8, rows), bf16), (along * rms1).astype(bf16))
    for copy in few_to_z:
        copy.start()

    normed = normed_ref[...]
    for h in range(heads + 1):
        if h < heads:
            size, at = HEAD_DIM, odd * spare + h * HEAD_DIM
        else:
            size, at = spare, (1 - odd) * whole
        at = pl.ds(pl.multiple_of(at, 16), size)
        for i, ref in enumerate((dq_ref, dk_ref, dv_ref)):
            by_head[h][i * size : (i + 1) * size] = nn(ref[at], normed).astype(bf16)
        if h < heads:
            groups[1 + h][START]()
            groups[h][SHARE]()
    at = 3 * spare
    late = by_head[heads]
    for copy in few_to_z:
        copy.wait_recv()
    few = mine[...] + theirs[0] + theirs[1] + theirs[2]
    late[at:] = jnp.zeros((late.shape[0] - at, width), bf16)
    line = lax.broadcasted_iota(jnp.int32, (16, width), 0)
    gains = jnp.where(line == 0, few[0:1, rows:], jnp.where(line == 1, grad_ffn, 0.0))
    late[at : at + 16] = gains.astype(bf16)
    groups[3][START]()
    groups[2][SHARE]()
    groups[0][GIVE_BACK]()
    groups[3][SHARE]()
    groups[1][GIVE_BACK]()

    total = part[own]
    for i in range(3):
        to_z[i].wait_recv()
        total = total + zland[i].astype(f32)
    x = x_t[own].astype(f32)
    mean = few[0:1, :rows] * (1.0 / width)
    tokens_ref[...] = back_t[own] + rms1 * gain_column[own, 0:1] * total - x * (rms1 * rms1 * rms1 * mean)

    groups[2][GIVE_BACK]()
    groups[3][GIVE_BACK]()
    for group in groups:
        group[END]()
    for copy in (*to_z, *few_to_z):
        copy.wait_send()


def back(now, late):
    quarter, width = late[5].shape
    rows = now[1].shape[0]
    spare = quarter % HEAD_DIM
    tall = [quarter + now[4].shape[0], 3 * HEAD_DIM, 3 * HEAD_DIM, 3 * spare + 64]
    vmem = pl.BlockSpec(memory_space=pltpu.VMEM)
    dma = pltpu.SemaphoreType.DMA
    return pl.pallas_call(
        back_kernel,
        in_specs=[vmem] * len(now) + [pl.BlockSpec(memory_space=pl.ANY)] * len(late),
        out_specs=[vmem] * 5,
        out_shape=[
            jax.ShapeDtypeStruct((quarter, rows), f32),
            *[jax.ShapeDtypeStruct((lines, width), bf16) for lines in tall],
        ],
        scratch_shapes=[
            *[pltpu.VMEM(a.shape, a.dtype) for a in late],
            dma((len(late),)),
            *[pltpu.VMEM((quarter, rows), bf16)] * 3,
            pltpu.VMEM((width, rows), bf16),
            pltpu.VMEM((width, 8), f32),
            pltpu.VMEM((width, rows), f32),
            pltpu.VMEM((width, rows), bf16),
            pltpu.VMEM((width, rows), f32),
            pltpu.VMEM((width, rows), bf16),
            pltpu.VMEM((3, quarter, rows), bf16),
            pltpu.VMEM((8, rows + width), f32),
            pltpu.VMEM((3, 8, rows + width), f32),
            dma((3,)),
            dma((3,)),
            dma((3,)),
            dma((3,)),
            *[one for lines in tall for one in weight_sum_scratch(lines, width)],
        ],
        compiler_params=pltpu.CompilerParams(
            vmem_limit_bytes=VMEM_LIMIT, collective_id=3, has_side_effects=True
        ),
        cost_estimate=takes(90),
        name="back",
    )(*now, *late)


def widen_kernel(early_ref, first_ref, second_ref, last_ref, shared_ref, *out_refs):
    quarter = out_refs[0].shape[0]
    odd = lax.axis_index("hs") % 2
    whole = HEAD_DIM * (quarter // HEAD_DIM)
    spare = quarter - whole
    for i in range(3):
        for h, ref in enumerate((first_ref, second_ref)):
            at = pl.ds(pl.multiple_of(odd * spare + h * HEAD_DIM, 8), HEAD_DIM)
            out_refs[i][at] = ref[i * HEAD_DIM : (i + 1) * HEAD_DIM].astype(f32)
        at = pl.ds(pl.multiple_of((1 - odd) * whole, 8), spare)
        out_refs[i][at] = last_ref[i * spare : (i + 1) * spare].astype(f32)
    out_refs[3][...] = early_ref[:quarter].astype(f32)
    out_refs[4][...] = early_ref[quarter:].astype(f32)
    out_refs[5][...] = last_ref[3 * spare : 3 * spare + 16].astype(f32)
    size = out_refs[6].shape[0]
    for i in range(3):
        out_refs[6 + i][...] = shared_ref[i * size : (i + 1) * size].astype(f32)


def widen(sums, quarter, hidden_units):
    width = sums[0].shape[1]
    step = width // 5
    tall = [quarter] * 4 + [sums[0].shape[0] - quarter, 16] + [hidden_units] * 3
    blocks = lambda lines: pl.BlockSpec((lines, step), lambda i: (0, i))
    return pl.pallas_call(
        widen_kernel,
        grid=(width // step,),
        in_specs=[blocks(a.shape[0]) for a in sums],
        out_specs=[blocks(lines) for lines in tall],
        out_shape=[jax.ShapeDtypeStruct((lines, width), f32) for lines in tall],
        compiler_params=pltpu.CompilerParams(vmem_limit_bytes=VMEM_LIMIT),
        cost_estimate=takes(8),
        name="widen",
    )(*sums)


def plain_front(
    tokens, attn_gain, query_t, key_t, value_t, attn_out, ffn_gain, documents, tables
):
    rows, width = tokens.shape
    quarter = query_t.shape[0]
    hs, hs_count = lax.axis_index("hs"), lax.axis_size("hs")
    odd = (hs % 2) == 1
    spare = -quarter % HEAD_DIM
    heads = (quarter + spare) // HEAD_DIM

    def outer(w):
        return jnp.where(odd, w[:spare], w[quarter - spare :])

    sent = jnp.concatenate([outer(query_t), outer(key_t), outer(value_t)], axis=0)
    got = lax.ppermute(sent, "hs", [(i, i ^ 1) for i in range(hs_count)])

    def widened(w, extra):
        return jnp.where(
            odd, jnp.concatenate([extra, w], axis=0), jnp.concatenate([w, extra], axis=0)
        )

    x = tokens.astype(f32)
    rms1 = lax.rsqrt(jnp.mean(x * x, axis=-1, keepdims=True) + EPS)
    normed1 = (x * rms1 * attn_gain).astype(bf16)
    shape3 = (heads, HEAD_DIM, rows)
    q, k, v = [
        ein("cd,td->ct", widened(w, got[i * spare : (i + 1) * spare]), normed1).reshape(shape3)
        for i, w in enumerate((query_t, key_t, value_t))
    ]
    q, k, v = rope(q, *tables).astype(bf16), rope(k, *tables).astype(bf16), v.astype(bf16)
    positions = jnp.arange(rows, dtype=jnp.int32)
    doc = documents[0]
    allowed = (positions[:, None] >= positions[None, :]) & (doc[:, None] == doc[None, :])
    scale = 1.0 / math.sqrt(HEAD_DIM)
    scores = jnp.where(allowed[None], ein("hdq,hdk->hqk", q, k) * scale, -1e30)
    raised = jnp.exp(scores - jnp.max(scores, axis=-1, keepdims=True))
    probs = raised / jnp.sum(raised, axis=-1, keepdims=True)
    attended = ein("hdk,hqk->hdq", v, probs.astype(bf16)).astype(bf16).reshape(-1, rows)
    attended = jnp.where(odd, attended[spare:], attended[:quarter])
    attended_t = lax.all_gather(attended, "hs", axis=0, tiled=True)
    out_t = lax.all_gather(attn_out.T, "hs", axis=0, tiled=True)
    residual = x + ein("ct,oc->to", attended_t, out_t)
    rms2 = lax.rsqrt(jnp.mean(residual * residual, axis=-1, keepdims=True) + EPS)
    normed2 = (residual * rms2 * ffn_gain).astype(bf16)
    return normed1, q, k, v, probs, attended_t, out_t, residual, normed2


def over_ep(a):
    return lax.psum(a.astype(bf16), EP).astype(f32)


def plain_back(
    sums,
    residual,
    normed2,
    grad_t,
    router_t,
    ffn_gain,
    out_t,
    q,
    k,
    v,
    probs,
    tables,
    query_t,
    key_t,
    value_t,
    normed1,
    attended_t,
    tokens,
    attn_gain,
):
    rows, width = tokens.shape
    quarter = query_t.shape[0]
    hs = lax.axis_index("hs")
    odd = (hs % 2) == 1
    spare = -quarter % HEAD_DIM
    held = quarter + spare
    col0 = hs * quarter

    def own(v):
        v = v.astype(bf16).reshape(held, rows)
        return jnp.where(odd, v[spare:], v[:quarter])

    gates = jax.nn.softmax(nt(normed2, router_t), axis=-1)
    grad_probs = sums[rows:, :rows].T.astype(f32)
    grad_logits = (
        gates * (grad_probs - jnp.sum(grad_probs * gates, axis=-1, keepdims=True))
    ).astype(bf16)
    grad_router = tn(grad_logits, normed2)
    grad_normed2 = sums[:rows].astype(f32) + dot(grad_logits, router_t)
    rms2 = lax.rsqrt(jnp.mean(residual * residual, axis=-1, keepdims=True) + EPS)
    grad_ffn_gain = jnp.sum(grad_normed2 * residual * rms2, axis=0)
    u = grad_normed2 * ffn_gain
    grad_residual = (
        grad_t.T.astype(f32)
        + rms2 * u
        - residual * rms2**3 * jnp.mean(u * residual, axis=-1, keepdims=True)
    )
    back_t = grad_residual.T
    low_t = back_t.astype(bf16)
    out_held = lax.dynamic_slice_in_dim(out_t, jnp.where(odd, col0 - spare, col0), held, 1)
    grad_attended = tn(out_held, low_t).astype(bf16).reshape(-1, HEAD_DIM, rows)
    grad_p = ein("hdq,hdk->hqk", grad_attended, v)
    grad_v = own(ein("hdq,hqk->hdk", grad_attended, probs.astype(bf16)))
    grad_s = (probs * (grad_p - jnp.sum(probs * grad_p, axis=-1, keepdims=True))).astype(bf16)
    scale = 1.0 / math.sqrt(HEAD_DIM)
    grad_q = own(rope_back(ein("hdk,hqk->hdq", k, grad_s) * scale, *tables))
    grad_k = own(rope_back(ein("hdq,hqk->hdk", q, grad_s) * scale, *tables))
    own_rows = lambda a: lax.dynamic_slice_in_dim(a, col0, quarter, 0)
    heads_sums = [
        over_ep(dot(grad_q, normed1)),
        over_ep(dot(grad_k, normed1)),
        over_ep(dot(grad_v, normed1)),
        over_ep(nt(own_rows(low_t), attended_t)),
    ]
    part = tn(query_t, grad_q) + tn(key_t, grad_k) + tn(value_t, grad_v)
    grad_n1 = lax.psum_scatter(part.astype(bf16), "hs", scatter_dimension=0, tiled=True)
    grad_n1 = grad_n1.astype(f32)
    x = tokens.T.astype(f32)
    x_own = own_rows(x)
    rms_t = lax.rsqrt(jnp.mean(x * x, axis=0, keepdims=True) + EPS)
    w1 = grad_n1 * own_rows(attn_gain)[:, None]
    mean1 = lax.psum(jnp.sum(w1 * x_own, axis=0, keepdims=True), "hs") / width
    grad_tokens = own_rows(back_t) + rms_t * w1 - x_own * rms_t**3 * mean1
    gain_own = jnp.sum(grad_n1 * x_own * rms_t, axis=1)
    gain_part = lax.dynamic_update_slice_in_dim(jnp.zeros((width,), f32), gain_own, col0, 0)
    grad_attn_gain = lax.psum(gain_part, (*EP, "hs"))
    return (
        grad_tokens,
        heads_sums,
        over_ep(grad_router),
        grad_attn_gain,
        lax.psum(grad_ffn_gain, EP),
    )


def shards(
    tokens,
    attn_gain,
    attn_query,
    attn_key,
    attn_value,
    attn_out,
    ffn_gain,
    router,
    shared_gate,
    shared_up,
    shared_down,
    expert_gate,
    expert_up,
    expert_down,
    routes,
    documents,
    out_grad,
):
    rows, width = tokens.shape
    quarter = out_grad.shape[1]
    hs = lax.axis_index("hs")
    ep_count = lax.axis_size("xy") * lax.axis_size("core")
    ep = lax.axis_index("xy") * lax.axis_size("core") + lax.axis_index("core")
    local = expert_gate.shape[0]
    experts = router.shape[1]
    small = ep_count == 8 and lax.axis_size("hs") == 4

    query_t, key_t, value_t, router_t = attn_query.T, attn_key.T, attn_value.T, router.T
    positions = jnp.arange(rows, dtype=jnp.int32)
    below = (positions[:, None] > positions[None, :]).astype(bf16)
    chosen = jnp.any(
        routes[:, :, None] == jnp.arange(experts, dtype=jnp.int32)[None, None, :], axis=1
    )
    own_slots = jnp.where(chosen, dot(below, chosen.astype(bf16)), -1.0).T.astype(bf16)
    tables = rope_tables(rows)

    if small:
        both_gains = jnp.stack([attn_gain, ffn_gain])
        ahead = front(
            tokens, both_gains, query_t, key_t, value_t, attn_out.T, documents, tables
        )
    else:
        ahead = plain_front(
            tokens, attn_gain, query_t, key_t, value_t, attn_out, ffn_gain, documents, tables
        )
    normed1, q, k, v, probs, attended_t, out_t, residual, normed2 = ahead
    out_t = out_t.reshape(width, width)

    first = ep * local
    rolled = jnp.roll(router_t, -first, axis=0)
    gate_t, up_t = expert_gate.swapaxes(1, 2), expert_up.swapaxes(1, 2)
    weights = gate_t, up_t, expert_down
    if small:
        ex_in, slot_weight, slot, grad_t = gather_spread(
            normed2, own_slots, rolled, out_grad.T, local, ep_count
        )
        ex_out, ex_gate, ex_up, near = experts_forward(ex_in, slot_weight, *weights, grad_t)
        out_part, far, given = collect_sending(ex_out, slot, grad_t, near)
        ex_grad = spread_grad(grad_t, near, far, given, slot)
    else:
        grad_all_t = lax.all_gather(out_grad.T, (*EP, "hs"), axis=0, tiled=True)
        grad_all_t = grad_all_t.reshape(ep_count, width, rows)
        grad_t = lax.dynamic_index_in_dim(grad_all_t, ep, 0, keepdims=False)
        slot = lax.dynamic_slice_in_dim(
            lax.all_gather(own_slots, EP, axis=0), first, local, 1
        ).astype(jnp.int32)
        normed_all = lax.all_gather(normed2, EP, axis=0, tiled=True)
        ex_in, slot_weight = spread(normed_all, slot, rolled)
        ex_out, ex_gate, ex_up = experts_forward(ex_in, slot_weight, *weights)
        out_part = collect(ex_out, slot)
        ex_grad = spread(grad_all_t, slot)
    out_part = out_part.reshape(ep_count * rows, width)
    ex_back, grad_gate_t, grad_up_t, grad_expert_down, grad_slot_weight = experts_backward(
        ex_in, ex_grad, ex_gate, ex_up, slot_weight, *weights
    )

    if small:
        back_sums, shared_sums, shared_part = collect_sum(
            ex_back, slot, grad_slot_weight, normed2, grad_t, shared_gate.T, shared_up.T, shared_down
        )
        grad_tokens, *sums = back(
            (back_sums, residual, normed2, grad_t, router_t, both_gains, *tables),
            (out_t, q, k, v, probs, query_t, key_t, value_t, attended_t, tokens, normed1),
        )
        *heads_sums, grad_router, gains, sum_gate, sum_up, sum_down = widen(
            [*sums, shared_sums], quarter, shared_down.shape[0]
        )
        shared_sums = sum_gate, sum_up, sum_down
        grad_attn_gain, grad_ffn_gain = gains[0], gains[1]
    else:
        sh_gate = dot(normed2, shared_gate)
        sh_up = dot(normed2, shared_up)
        sh_sig = jax.nn.sigmoid(sh_gate)
        sh_act = sh_gate * sh_sig
        sh_hidden = (sh_act * sh_up).astype(bf16)
        shared_part = dot(sh_hidden, shared_down)
        grad_sh = ein("dt,fd->tf", grad_t, shared_down)
        grad_sh_gate = (grad_sh * sh_up * sh_sig * (1 + sh_gate * (1 - sh_sig))).astype(bf16)
        grad_sh_up = (grad_sh * sh_act).astype(bf16)
        shared_grads = [
            ein("tf,td->fd", grad_sh_gate, normed2).astype(bf16),
            ein("tf,td->fd", grad_sh_up, normed2).astype(bf16),
            ein("tf,dt->fd", sh_hidden, grad_t).astype(bf16),
        ]
        shared_back = ein("tf,df->td", grad_sh_gate, shared_gate) + ein(
            "tf,df->td", grad_sh_up, shared_up
        )
        back_part = collect(ex_back, slot, grad_slot_weight, first, experts).reshape(-1, width)
        back_rows = lax.psum_scatter(back_part, EP, scatter_dimension=0, tiled=True).astype(f32)
        back_rows = jnp.concatenate([back_rows[:rows] + shared_back, back_rows[rows:]], axis=0)
        back_sums = lax.psum(back_rows.astype(bf16), "hs")
        shared_sums = [over_ep(a) for a in shared_grads]
        grad_tokens, heads_sums, grad_router, grad_attn_gain, grad_ffn_gain = plain_back(
            back_sums,
            residual,
            normed2,
            grad_t,
            router_t,
            ffn_gain,
            out_t,
            q,
            k,
            v,
            probs,
            tables,
            query_t,
            key_t,
            value_t,
            normed1,
            attended_t,
            tokens,
            attn_gain,
        )

    rows_major = Layout(major_to_minor=(0, 1))
    out_part = with_layout_constraint(out_part, rows_major)
    out_rows = lax.psum_scatter(out_part, EP, scatter_dimension=0, tiled=True)
    out_rows = with_layout_constraint(out_rows, rows_major)
    out_rows = (out_rows.astype(f32) + shared_part.astype(f32)).astype(bf16)
    out_quarter = lax.psum_scatter(out_rows, "hs", scatter_dimension=1, tiled=True)
    residual_quarter = lax.dynamic_slice_in_dim(residual, hs * quarter, quarter, 1)
    output = (residual_quarter + out_quarter.astype(f32)).astype(bf16)

    return (
        output,
        grad_tokens.T,
        grad_attn_gain,
        *[a.T for a in heads_sums],
        grad_ffn_gain,
        grad_router.T,
        shared_sums[0].T,
        shared_sums[1].T,
        shared_sums[2],
        grad_gate_t.swapaxes(1, 2),
        grad_up_t.swapaxes(1, 2),
        grad_expert_down,
    )


def solution(mesh):
    ep_count, hs_count = mesh.devices.shape
    cut = Mesh(mesh.devices.reshape(ep_count // 2, 2, hs_count), ("xy", "core", "hs"))
    return jax.shard_map(
        shards,
        mesh=cut,
        in_specs=(
            P(EP, None),
            P(),
            P(None, "hs"),
            P(None, "hs"),
            P(None, "hs"),
            P(None, "hs"),
            P(),
            P(),
            P(None, "hs"),
            P(None, "hs"),
            P("hs", None),
            P(EP, None, "hs"),
            P(EP, None, "hs"),
            P(EP, "hs", None),
            P(EP, None),
            P(EP, None),
            P(EP, "hs"),
        ),
        out_specs=(
            P(EP, "hs"),
            P(EP, "hs"),
            P(),
            P(None, "hs"),
            P(None, "hs"),
            P(None, "hs"),
            P(None, "hs"),
            P(),
            P(),
            P(None, "hs"),
            P(None, "hs"),
            P("hs", None),
            P(EP, None, "hs"),
            P(EP, None, "hs"),
            P(EP, "hs", None),
        ),
        check_vma=False,
    )
```

```python
import functools
import math

import jax
import jax.numpy as jnp
import numpy as np
from jax import lax
from jax.experimental import pallas as pl
from jax.experimental.layout import Layout, with_layout_constraint
from jax.experimental.pallas import tpu as pltpu
from jax.sharding import Mesh
from jax.sharding import PartitionSpec as P

HEADS = 10
HEAD_DIM = 128
CAP = 112
EPS = 1e-06
EP = ("xy", "core")
bf16 = jnp.bfloat16
f32 = jnp.float32


def dot(a, b):
    return jnp.dot(a, b, preferred_element_type=f32)


def ein(spec, a, b):
    return jnp.einsum(spec, a, b, preferred_element_type=f32)


def rope_tables(rows):
    half = HEAD_DIM // 2
    frequency = 10000.0 ** (-np.arange(half) * 2.0 / HEAD_DIM)
    angles = frequency[:, None] * np.arange(rows)[None, :]
    return jnp.asarray(np.cos(angles), f32), jnp.asarray(np.sin(angles), f32)


def rope(v, cosine, sine):
    half = HEAD_DIM // 2
    a, b = v[:, :half], v[:, half:]
    return jnp.concatenate([a * cosine - b * sine, b * cosine + a * sine], axis=1)


def rope_back(v, cosine, sine):
    half = HEAD_DIM // 2
    a, b = v[:, :half], v[:, half:]
    return jnp.concatenate([a * cosine + b * sine, b * cosine - a * sine], axis=1)


VMEM_LIMIT = 60 * 1024 * 1024
PAD = 256


def nn(a, b):
    return lax.dot_general(a, b, (((1,), (0,)), ((), ())), preferred_element_type=f32)


def nt(a, b):
    return lax.dot_general(a, b, (((1,), (1,)), ((), ())), preferred_element_type=f32)


def tn(a, b):
    return lax.dot_general(a, b, (((0,), (0,)), ((), ())), preferred_element_type=f32)


def takes(microseconds):
    return pl.CostEstimate(flops=0, transcendentals=0, bytes_accessed=microseconds * 3_000_000)


def slot_masks(slot_ref, at):
    local, rows = slot_ref.shape[-2:]
    number = lax.broadcasted_iota(jnp.int32, (CAP, rows), 0)
    return [slot_ref[at, e : e + 1, :] == number for e in range(local)]


def spread_kernel(weighted, *refs):
    if weighted:
        rows_ref, slot_ref, router_ref, x_ref, sw_ref, pick = refs
    else:
        rows_ref, slot_ref, x_ref, pick = refs
    local = slot_ref.shape[1]
    rows = rows_ref[...] if weighted else rows_ref[0]
    masks = slot_masks(slot_ref, 0)
    if weighted:
        logits = nt(router_ref[...], rows)
        raised = jnp.exp(logits - jnp.max(logits, axis=0, keepdims=True))
        gates = raised / jnp.sum(raised, axis=0, keepdims=True)
    for e in range(local):
        pick[e * CAP : (e + 1) * CAP, :] = masks[e].astype(f32).astype(bf16)
        if weighted:
            sw_ref[e] = jnp.sum(
                jnp.where(masks[e], gates[e : e + 1, :], 0.0), axis=1, keepdims=True
            )
    product = nn if weighted else nt
    x_ref[...] = product(pick[...], rows).astype(bf16).reshape(x_ref.shape)


def spread(all_rows, slot, router_t=None):
    s, local, rows = slot.shape
    weighted = router_t is not None
    if weighted:
        width = all_rows.shape[1]
        block = pl.BlockSpec((rows, width), lambda i: (i, 0))
    else:
        width = all_rows.shape[1]
        block = pl.BlockSpec((1, width, rows), lambda i: (i, 0, 0))
    in_specs = [
        block,
        pl.BlockSpec((1, local, rows), lambda i: (i, 0, 0)),
    ]
    out_specs = [pl.BlockSpec((1, local, CAP, width), lambda i: (i, 0, 0, 0))]
    out_shape = [jax.ShapeDtypeStruct((s, local, CAP, width), bf16)]
    args = [all_rows, slot]
    if weighted:
        in_specs.append(pl.BlockSpec(router_t.shape, lambda i: (0, 0)))
        out_specs.append(pl.BlockSpec((local, CAP, 1), lambda i: (0, i, 0)))
        out_shape.append(jax.ShapeDtypeStruct((local, s * CAP, 1), f32))
        args.append(router_t)
    out = pl.pallas_call(
        functools.partial(spread_kernel, weighted),
        grid=(s,),
        in_specs=in_specs,
        out_specs=out_specs,
        out_shape=out_shape,
        scratch_shapes=[pltpu.VMEM((local * CAP, rows), bf16)],
        compiler_params=pltpu.CompilerParams(vmem_limit_bytes=VMEM_LIMIT),
        cost_estimate=takes(17),
        name="spread",
    )(*args)
    return out if weighted else out[0]


def padded(ref, out):
    ff = ref.shape[1]
    out[:ff, :] = ref[0]
    out[ff:, :] = jnp.zeros((out.shape[0] - ff, out.shape[1]), out.dtype)


def experts_forward_kernel(
    x_ref, sw_ref, wg_ref, wu_ref, wd_ref, y_ref, gate_ref, up_ref, wg, wu, wd
):
    padded(wg_ref, wg)
    padded(wu_ref, wu)
    padded(wd_ref, wd)
    rows, width = gate_ref.shape[1], x_ref.shape[3]
    x = x_ref[...].reshape(rows, width)
    gate = nt(x, wg[...])
    up = nt(x, wu[...])
    gate_ref[0] = gate
    up_ref[0] = up
    act = gate / (1.0 + jnp.exp(-gate))
    hidden = (act * up).astype(bf16).astype(f32)
    hidden_w = (hidden * sw_ref[0]).astype(bf16)
    y_ref[...] = nn(hidden_w, wd[...]).astype(bf16).reshape(y_ref.shape)


def experts_backward_kernel(
    groups,
    x_ref,
    gx_ref,
    gate_ref,
    up_ref,
    sw_ref,
    wg_ref,
    wu_ref,
    wd_ref,
    dx_ref,
    dg_ref,
    du_ref,
    dd_ref,
    gsw_ref,
    wg,
    wu,
    wd,
):
    padded(wg_ref, wg)
    padded(wu_ref, wu)
    padded(wd_ref, wd)
    rows, width = gate_ref.shape[1], x_ref.shape[3]
    ff = wg_ref.shape[1]
    x = x_ref[...].reshape(rows, width)
    gx = gx_ref[...].reshape(rows, width)
    gate, up, sw = gate_ref[0], up_ref[0], sw_ref[0]
    sig = 1.0 / (1.0 + jnp.exp(-gate))
    act = gate * sig
    hidden = (act * up).astype(bf16).astype(f32)
    gh = nt(gx, wd[...])
    gsw_ref[0] = jnp.sum(gh * hidden, axis=-1, keepdims=True)
    gh = gh * sw
    gg = (gh * up * sig * (1.0 + gate * (1.0 - sig))).astype(bf16)
    gu = (gh * act).astype(bf16)
    sums = (
        (dd_ref, tn((hidden * sw).astype(bf16), gx)[:ff]),
        (dg_ref, tn(gg, x)[:ff]),
        (du_ref, tn(gu, x)[:ff]),
    )
    if groups == 1:
        for ref, value in sums:
            ref[0] = value
    else:

        @pl.when(pl.program_id(1) == 0)
        def _():
            for ref, value in sums:
                ref[0] = value

        @pl.when(pl.program_id(1) > 0)
        def _():
            for ref, value in sums:
                ref[0] += value

    dx_ref[...] = (nn(gg, wg[...]) + nn(gu, wu[...])).astype(bf16).reshape(dx_ref.shape)


def sending(remote_too, collective_id):
    if not remote_too:
        return pltpu.CompilerParams(vmem_limit_bytes=VMEM_LIMIT)
    return pltpu.CompilerParams(
        vmem_limit_bytes=VMEM_LIMIT, collective_id=collective_id, has_side_effects=True
    )


def expert_specs(s, width):
    group = min(s, 8)
    slots = pl.BlockSpec((group, 1, CAP, width), lambda i, j: (j, i, 0, 0))
    lines = lambda columns: pl.BlockSpec((1, group * CAP, columns), lambda i, j: (i, j, 0))
    per = lambda *shape: pl.BlockSpec((1, *shape), lambda i, j: (i, 0, 0))
    return s // group, slots, lines, per


def experts_forward_sending_kernel(
    x_ref,
    sw_ref,
    wg_ref,
    wu_ref,
    wd_ref,
    grad_ref,
    y_ref,
    gate_ref,
    up_ref,
    near_ref,
    wg,
    wu,
    wd,
    send,
    recv,
):
    chip, core, z, cx, cy, cd = places()
    peers = [(cx, core, z), (cy, core, z)]
    copies = [
        remote(grad_ref, near_ref.at[i], send.at[i], recv.at[i], peer) for i, peer in enumerate(peers)
    ]

    @pl.when(pl.program_id(0) == 0)
    def _():
        greet(peers)
        for copy in copies:
            copy.start()

    experts_forward_kernel(
        x_ref, sw_ref, wg_ref, wu_ref, wd_ref, y_ref, gate_ref, up_ref, wg, wu, wd
    )

    @pl.when(pl.program_id(0) == pl.num_programs(0) - 1)
    def _():
        for copy in copies:
            copy.wait()


def experts_forward(x, sw, wg, wu, wd, grad=None):
    s, local, cap, width = x.shape
    ff = wg.shape[1]
    rows = s * cap
    groups, slots, lines, per = expert_specs(s, width)
    middle = jax.ShapeDtypeStruct((local, rows, PAD), f32)
    kernel = experts_forward_kernel
    in_specs = [slots, lines(1)] + [per(ff, width)] * 3
    out_specs = [slots, lines(PAD), lines(PAD)]
    out_shape = [jax.ShapeDtypeStruct(x.shape, bf16), middle, middle]
    scratch = [pltpu.VMEM((PAD, width), bf16)] * 3
    args = [x, sw, wg, wu, wd]
    if grad is not None:
        kernel = experts_forward_sending_kernel
        in_specs.append(pl.BlockSpec(memory_space=pl.ANY))
        out_specs.append(pl.BlockSpec(memory_space=pl.ANY))
        out_shape.append(jax.ShapeDtypeStruct((2, *grad.shape), bf16))
        scratch += [pltpu.SemaphoreType.DMA((2,))] * 2
        args.append(grad)
    return pl.pallas_call(
        kernel,
        grid=(local, groups),
        in_specs=in_specs,
        out_specs=out_specs,
        out_shape=out_shape,
        scratch_shapes=scratch,
        compiler_params=sending(grad is not None, 4),
        cost_estimate=takes(31),
        name="experts_forward",
    )(*args)


def experts_backward(x, gx, gate, up, sw, wg, wu, wd):
    s, local, cap, width = x.shape
    ff = wg.shape[1]
    rows = s * cap
    groups, slots, lines, per = expert_specs(s, width)
    return pl.pallas_call(
        functools.partial(experts_backward_kernel, groups),
        grid=(local, groups),
        in_specs=[slots, slots, lines(PAD), lines(PAD), lines(1)]
        + [per(ff, width)] * 3,
        out_specs=[slots] + [per(ff, width)] * 3 + [lines(1)],
        out_shape=[jax.ShapeDtypeStruct(x.shape, bf16)]
        + [jax.ShapeDtypeStruct((local, ff, width), f32)] * 3
        + [jax.ShapeDtypeStruct((local, rows, 1), f32)],
        scratch_shapes=[pltpu.VMEM((PAD, width), bf16)] * 3,
        compiler_params=pltpu.CompilerParams(vmem_limit_bytes=VMEM_LIMIT),
        cost_estimate=takes(47),
        name="experts_backward",
    )(x, gx, gate, up, sw, wg, wu, wd)


def collect_kernel(y_ref, slot_ref, out_ref, pick):
    local = slot_ref.shape[1]
    masks = slot_masks(slot_ref, 0)
    for e in range(local):
        pick[e * CAP : (e + 1) * CAP, :] = masks[e].astype(f32).astype(bf16)
    out_ref[0] = tn(pick[...], y_ref[...].reshape(pick.shape[0], -1)).astype(bf16)


def collect_sending_kernel(
    y_ref, slot_ref, grad_ref, near_ref, out_ref, far_ref, given_ref, pick, send, recv, csend, crecv
):
    chip, core, z, cx, cy, cd = places()
    x_peer, y_peer, c_peer = (cx, core, z), (cy, core, z), (chip, 1 - core, z)
    half = grad_ref.shape[0] // 2
    top, low = pl.ds(0, half), pl.ds(half, half)
    relays = [
        remote(near_ref.at[0, top], far_ref.at[top], send.at[0], recv.at[0], y_peer),
        remote(near_ref.at[1, low], far_ref.at[low], send.at[1], recv.at[1], x_peer),
    ]
    passes = [
        remote(ref, given_ref.at[i], csend.at[i], crecv.at[i], c_peer)
        for i, ref in enumerate((grad_ref, near_ref.at[0], near_ref.at[1], far_ref))
    ]

    @pl.when(pl.program_id(0) == 0)
    def _():
        greet([x_peer, y_peer, c_peer])
        for copy in (*relays, *passes[:3]):
            copy.start()

    collect_kernel(y_ref, slot_ref, out_ref, pick)

    @pl.when(pl.program_id(0) == pl.num_programs(0) - 1)
    def _():
        for copy in relays:
            copy.wait_recv()
        passes[3].start()
        for copy in passes:
            copy.wait()
        for copy in relays:
            copy.wait_send()


def collect_back_kernel(experts, y_ref, slot_ref, gsw_ref, first_ref, out_ref, pick):
    local, rows = slot_ref.shape[1:]
    first = first_ref[0]
    masks = slot_masks(slot_ref, 0)
    number = lax.broadcasted_iota(jnp.int32, (experts, rows), 0)
    probs = jnp.zeros((experts, rows), f32)
    for e in range(local):
        pick[e * CAP : (e + 1) * CAP, :] = masks[e].astype(f32).astype(bf16)
        line = jnp.sum(jnp.where(masks[e], gsw_ref[e], 0.0), axis=0, keepdims=True)
        probs = jnp.where(number == first + e, line, probs)
    out_ref[0, :rows] = tn(pick[...], y_ref[...].reshape(pick.shape[0], -1)).astype(bf16)
    out_ref[0, rows:] = jnp.zeros((experts, out_ref.shape[2]), bf16)
    out_ref[0, rows:, :rows] = probs.astype(bf16)


def collect_sending(y, slot, grad, near):
    s, local, cap, width = y.shape
    rows = slot.shape[2]
    dma = pltpu.SemaphoreType.DMA
    whole = pl.BlockSpec(memory_space=pl.ANY)
    return pl.pallas_call(
        collect_sending_kernel,
        grid=(s,),
        in_specs=[
            pl.BlockSpec((1, local, cap, width), lambda i: (i, 0, 0, 0)),
            pl.BlockSpec((1, local, rows), lambda i: (i, 0, 0)),
            whole,
            whole,
        ],
        out_specs=[pl.BlockSpec((1, rows, width), lambda i: (i, 0, 0)), whole, whole],
        out_shape=[
            jax.ShapeDtypeStruct((s, rows, width), bf16),
            jax.ShapeDtypeStruct(grad.shape, bf16),
            jax.ShapeDtypeStruct((4, *grad.shape), bf16),
        ],
        scratch_shapes=[
            pltpu.VMEM((local * cap, rows), bf16),
            dma((2,)),
            dma((2,)),
            dma((4,)),
            dma((4,)),
        ],
        compiler_params=sending(True, 5),
        cost_estimate=takes(20),
        name="collect_sending",
    )(y, slot, grad, near)


def spread_grad_kernel(grad_ref, near_ref, far_ref, given_ref, slot_ref, x_ref, pick, gbuf, xbuf, come, gone):
    chip, core = lax.axis_index("xy"), lax.axis_index("core")
    local, rows = slot_ref.shape[1:]
    here = [grad_ref, near_ref.at[0], near_ref.at[1], far_ref]
    sources = [(here[t // 2], given_ref.at[t // 2])[t % 2] for t in range(8)]

    def in_copy(t):
        return pltpu.make_async_copy(sources[t], gbuf.at[t % 2], come.at[t % 2])

    def out_copy(t, src):
        return pltpu.make_async_copy(xbuf.at[t % 2], x_ref.at[src], gone.at[t % 2])

    number = lax.broadcasted_iota(jnp.int32, (CAP, rows), 0)
    in_copy(0).start()
    for t in range(8):
        if t < 7:
            in_copy(t + 1).start()
        x, y = (chip % 2 + (t // 2) % 2) % 2, (chip // 2 + t // 4) % 2
        src = (y * 2 + x) * 2 + (core + t % 2) % 2
        slots = slot_ref[src]
        for e in range(local):
            mask = slots[e : e + 1, :] == number
            pick[e * CAP : (e + 1) * CAP, :] = mask.astype(f32).astype(bf16)
        in_copy(t).wait()
        if t >= 2:
            out_copy(t, src).wait()
        xbuf[t % 2] = nt(pick[...], gbuf[t % 2]).astype(bf16).reshape(xbuf.shape[1:])
        out_copy(t, src).start()
    out_copy(0, 0).wait()
    out_copy(1, 0).wait()


def spread_grad(grad, near, far, given, slot):
    s, local, rows = slot.shape
    width = grad.shape[0]
    whole = pl.BlockSpec(memory_space=pl.ANY)
    dma = pltpu.SemaphoreType.DMA
    return pl.pallas_call(
        spread_grad_kernel,
        in_specs=[whole] * 4 + [pl.BlockSpec(memory_space=pltpu.VMEM)],
        out_specs=whole,
        out_shape=jax.ShapeDtypeStruct((s, local, CAP, width), bf16),
        scratch_shapes=[
            pltpu.VMEM((local * CAP, rows), bf16),
            pltpu.VMEM((2, width, rows), bf16),
            pltpu.VMEM((2, local, CAP, width), bf16),
            dma((2,)),
            dma((2,)),
        ],
        compiler_params=sending(False, 0),
        cost_estimate=takes(16),
        name="spread_grad",
    )(grad, near, far, given, slot)


def collect(y, slot, gsw=None, first=None, experts=0):
    s, local, cap, width = y.shape
    rows = slot.shape[2]
    in_specs = [
        pl.BlockSpec((1, local, cap, width), lambda i: (i, 0, 0, 0)),
        pl.BlockSpec((1, local, rows), lambda i: (i, 0, 0)),
    ]
    args = [y, slot]
    kernel = collect_kernel
    tall = rows
    if gsw is not None:
        in_specs += [
            pl.BlockSpec((local, cap, 1), lambda i: (0, i, 0)),
            pl.BlockSpec(memory_space=pltpu.SMEM),
        ]
        args += [gsw, first.reshape(1)]
        kernel = functools.partial(collect_back_kernel, experts)
        tall = rows + experts
    return pl.pallas_call(
        kernel,
        grid=(s,),
        in_specs=in_specs,
        out_specs=pl.BlockSpec((1, tall, width), lambda i: (i, 0, 0)),
        out_shape=jax.ShapeDtypeStruct((s, tall, width), bf16),
        scratch_shapes=[pltpu.VMEM((local * cap, rows), bf16)],
        compiler_params=pltpu.CompilerParams(vmem_limit_bytes=VMEM_LIMIT),
        cost_estimate=takes(17),
        name="collect",
    )(*args)


MESH = pl.DeviceIdType.MESH
EXTRA = 64
SUM_STARTS = (0, 192, 384)


def places():
    chip, core, z = lax.axis_index("xy"), lax.axis_index("core"), lax.axis_index("hs")
    x, y = chip % 2, chip // 2
    return chip, core, z, y * 2 + (1 - x), (1 - y) * 2 + x, (1 - y) * 2 + (1 - x)


def greet(peers):
    barrier = pltpu.get_barrier_semaphore()
    for peer in peers:
        pl.semaphore_signal(barrier, inc=1, device_id=peer, device_id_type=MESH)
    pl.semaphore_wait(barrier, len(peers))


def remote(src, dst, send, recv, peer):
    return pltpu.make_async_remote_copy(
        src_ref=src, dst_ref=dst, send_sem=send, recv_sem=recv, device_id=peer, device_id_type=MESH
    )


def block(q, size):
    return pl.ds(pl.multiple_of(q * size, 16), size)


def weight_gather(out_ref, csend, crecv, send, recv):
    chip, core, z, cx, cy, cd = places()
    other = 1 - core
    c_peer = (chip, other, z)
    chips = (cx, cy, cd)
    count = out_ref.shape[0] // 2
    piece = count // 4

    def place(c, k):
        return pl.ds(pl.multiple_of(k * count + c * piece, 16), piece)

    def give(number, c, k, sems, peer):
        return remote(out_ref.at[place(c, k)], out_ref.at[place(c, k)], *sems(number), peer)

    def chip_sems(i):
        return send.at[3 + i], recv.at[3 + i]

    def core_sems(i):
        return csend.at[1 + i], crecv.at[1 + i]

    gather = [give(i, chip, core, chip_sems, (c, core, z)) for i, c in enumerate(chips)]
    over = [give(i, c, core, core_sems, c_peer) for i, c in enumerate((*chips, chip))]

    def put(done):
        out_ref[place(chip, core)] = done.astype(bf16)
        for i in (2, 0, 1):
            gather[i].start()
        over[3].start()

    def end():
        for i, c in enumerate(chips):
            give(i, c, core, chip_sems, (c, core, z)).wait_recv()
            over[i].start()
        for i, c in enumerate((*chips, chip)):
            give(i, c, other, core_sems, c_peer).wait_recv()
        for copy in (*gather, *over):
            copy.wait_send()

    return put, end


def weight_sum(grads, given, half, land, out_ref, csend, crecv, send, recv):
    chip, core, z, cx, cy, cd = places()
    other = 1 - core
    c_peer = (chip, other, z)
    chips = (cx, cy, cd)
    count = grads.shape[0] // 2
    piece = count // 4

    to_core = remote(grads.at[block(other, count)], given, csend.at[0], crecv.at[0], c_peer)
    scatter = [
        remote(half.at[block(c, piece)], land.at[i], send.at[i], recv.at[i], (c, core, z))
        for i, c in enumerate(chips)
    ]
    if out_ref is not None:
        put, gathered = weight_gather(out_ref, csend, crecv, send, recv)

    def share():
        to_core.wait_recv()
        half[...] = (grads[block(core, count)].astype(f32) + given[...].astype(f32)).astype(bf16)
        for i in (2, 0, 1):
            scatter[i].start()

    def total():
        done = half[block(chip, piece)].astype(f32)
        for i in range(3):
            scatter[i].wait_recv()
            done = done + land[i].astype(f32)
        return done

    def give_back():
        put(total())

    def end():
        if out_ref is not None:
            gathered()
        for copy in (to_core, *scatter):
            copy.wait_send()

    return to_core.start, share, give_back, end, total


def weight_sum_scratch(tall, width):
    dma = pltpu.SemaphoreType.DMA
    return [
        pltpu.VMEM((tall, width), bf16),
        pltpu.VMEM((tall // 2, width), bf16),
        pltpu.VMEM((tall // 2, width), bf16),
        pltpu.VMEM((3, tall // 8, width), bf16),
        dma((5,)),
        dma((5,)),
        dma((6,)),
        dma((6,)),
    ]


def gather_spread_kernel(
    own_ref,
    slots_ref,
    router_ref,
    grad_ref,
    x_ref,
    sw_ref,
    slot_ref,
    grad_all_ref,
    held,
    pick,
    xbuf,
    send,
    recv,
    copied,
    zsend,
    zrecv,
):
    chip, core, z, cx, cy, cd = places()
    other = 1 - core
    x_peer, y_peer, c_peer = (cx, core, z), (cy, core, z), (chip, other, z)
    tall = held.shape[1]
    half = tall // 2
    local, rows = slot_ref.shape[1:]
    me = chip * 2 + core
    top, low = pl.ds(0, half), pl.ds(half, half)

    def at(c, k):
        return c * 2 + k

    def move(number, src_slot, part, peer):
        return remote(
            held.at[src_slot, part], held.at[src_slot, part], send.at[number], recv.at[number], peer
        )

    whole = pl.ds(0, tall)
    z_peers = [(chip, core, (z + i) % 4) for i in (1, 2, 3)]
    greet([x_peer, y_peer, c_peer, *z_peers])
    quarter = grad_ref.shape[0]

    def grad_copy(i, q):
        return remote(
            grad_ref, grad_all_ref.at[block(q, quarter)], zsend.at[i], zrecv.at[i], z_peers[i]
        )

    held[me, :rows] = own_ref[...]
    packed = tall - rows
    held[me, rows:, 2 * rows :] = jnp.zeros((packed, own_ref.shape[1] - 2 * rows), bf16)
    held[me, rows:, :rows] = slots_ref[:packed]
    held[me, rows:, rows : 2 * rows] = slots_ref[packed:]
    x_top, x_low = move(0, me, top, x_peer), move(1, me, low, x_peer)
    y_low, y_top = move(2, me, low, y_peer), move(3, me, top, y_peer)
    to_core = move(4, me, whole, c_peer)
    relay_top, relay_low = move(5, at(cx, core), top, y_peer), move(6, at(cy, core), low, x_peer)
    pass_x, pass_y = move(7, at(cx, core), whole, c_peer), move(8, at(cy, core), whole, c_peer)
    pass_d = move(9, at(cd, core), whole, c_peer)
    for copy in (x_top, y_low, x_low, y_top, to_core, *[grad_copy(i, z) for i in (1, 0, 2)]):
        copy.start()
    grad_all_ref[block(z, quarter)] = grad_ref[...]

    def arrived(number, slot, part):
        move(number, slot, part, c_peer).wait_recv()

    number = lax.broadcasted_iota(jnp.int32, (CAP, rows), 0)
    first = me * local
    line = lax.broadcasted_iota(jnp.int32, (local, EXTRA), 0)
    column = lax.broadcasted_iota(jnp.int32, (local, EXTRA), 1)
    chosen = (column == line + first).astype(f32).astype(bf16)

    def out_copy(t, src):
        return pltpu.make_async_copy(xbuf.at[t % 2], x_ref.at[src], copied.at[t % 2])

    def step(t, carry):
        @pl.when(t == 1)
        def _():
            arrived(4, at(chip, other), whole)

        @pl.when(t == 2)
        def _():
            arrived(0, at(cx, core), top)
            relay_top.start()
            arrived(2, at(cy, core), low)
            relay_low.start()
            arrived(1, at(cx, core), low)
            pass_x.start()

        @pl.when(t == 3)
        def _():
            arrived(3, at(cy, core), top)
            pass_y.start()
            arrived(7, at(cx, other), whole)

        @pl.when(t == 5)
        def _():
            arrived(8, at(cy, other), whole)

        @pl.when(t == 6)
        def _():
            arrived(5, at(cd, core), top)
            arrived(6, at(cd, core), low)
            pass_d.start()

        @pl.when(t == 7)
        def _():
            arrived(9, at(cd, other), whole)

        x, y = (chip % 2 + (t // 2) % 2) % 2, (chip // 2 + t // 4) % 2
        src = (y * 2 + x) * 2 + (core + t % 2) % 2
        slots = nn(chosen[:, :packed], held[src, rows:, :rows])
        slots += nn(chosen[:, packed:], held[src, rows:, rows : 2 * rows])
        slots = slots.astype(jnp.int32)
        slot_ref[src] = slots
        logits = nt(router_ref[...], held[src, :rows])
        raised = jnp.exp(logits - jnp.max(logits, axis=0, keepdims=True))
        gates = raised / jnp.sum(raised, axis=0, keepdims=True)
        for e in range(local):
            mask = slots[e : e + 1, :] == number
            pick[e * CAP : (e + 1) * CAP, :] = mask.astype(f32).astype(bf16)
            sw_ref[e, pl.ds(pl.multiple_of(src * CAP, 8), CAP), :] = jnp.sum(
                jnp.where(mask, gates[e : e + 1, :], 0.0), axis=1, keepdims=True
            )

        @pl.when(t >= 2)
        def _():
            out_copy(t, src).wait()

        xbuf[t % 2] = nn(pick[...], held[src, :rows]).astype(bf16).reshape(xbuf.shape[1:])
        out_copy(t, src).start()
        return carry

    lax.fori_loop(0, 8, step, 0)
    out_copy(0, me).wait()
    out_copy(1, me).wait()
    for i in range(3):
        grad_copy(i, (z + 3 - i) % 4).wait_recv()
        grad_copy(i, z).wait_send()
    for copy in (x_top, x_low, y_low, y_top, to_core, relay_top, relay_low, pass_x, pass_y, pass_d):
        copy.wait_send()


def gather_spread(own, slots, router_t, grad_quarter, local, ep_count):
    rows, width = own.shape
    tall = rows + EXTRA // 2
    vmem = pl.BlockSpec(memory_space=pltpu.VMEM)
    return pl.pallas_call(
        gather_spread_kernel,
        in_specs=[vmem] * 4,
        out_specs=[pl.BlockSpec(memory_space=pl.ANY), vmem, vmem, vmem],
        out_shape=[
            jax.ShapeDtypeStruct((ep_count, local, CAP, width), bf16),
            jax.ShapeDtypeStruct((local, ep_count * CAP, 1), f32),
            jax.ShapeDtypeStruct((ep_count, local, rows), jnp.int32),
            jax.ShapeDtypeStruct((width, rows), bf16),
        ],
        scratch_shapes=[
            pltpu.VMEM((ep_count, tall, width), bf16),
            pltpu.VMEM((local * CAP, rows), bf16),
            pltpu.VMEM((2, local, CAP, width), bf16),
            pltpu.SemaphoreType.DMA((10,)),
            pltpu.SemaphoreType.DMA((10,)),
            pltpu.SemaphoreType.DMA((2,)),
            pltpu.SemaphoreType.DMA((3,)),
            pltpu.SemaphoreType.DMA((3,)),
        ],
        compiler_params=pltpu.CompilerParams(
            vmem_limit_bytes=VMEM_LIMIT, collective_id=0, has_side_effects=True
        ),
        cost_estimate=takes(62),
        name="gather_spread",
    )(own, slots, router_t, grad_quarter)


def front_kernel(
    x_ref,
    gain_ref,
    wq_ref,
    wk_ref,
    wv_ref,
    wo_ref,
    doc_ref,
    cos_ref,
    sin_ref,
    normed1_out,
    q_out,
    k_out,
    v_out,
    probs_out,
    attended_out,
    out_out,
    residual_ref,
    normed2_ref,
    normed1_ref,
    q_ref,
    k_ref,
    v_ref,
    probs_ref,
    attended_ref,
    out_ref,
    gone,
    shared,
    beside,
    esend,
    erecv,
    asend,
    arecv,
    zsend,
    zrecv,
    send,
    recv,
    csend,
    crecv,
):
    chip, core, z, cx, cy, cd = places()
    other = 1 - core
    odd = z % 2
    c_peer = (chip, other, z)
    chips = (cx, cy, cd)
    z_peers = [(chip, core, (z + i) % 4) for i in (1, 2, 3)]
    pair = (chip, core, z + 1 - 2 * odd)
    rows, width = x_ref.shape
    quarter = wq_ref.shape[0]
    whole = HEAD_DIM * (quarter // HEAD_DIM)
    spare = quarter - whole
    greet([c_peer, *[(c, core, z) for c in chips], *z_peers])

    full_rows = pl.ds(pl.multiple_of(odd * spare, 16), whole)
    half_rows = pl.ds(pl.multiple_of((1 - odd) * whole, 16), spare)
    for i, ref in enumerate((wq_ref, wk_ref, wv_ref)):
        shared[i * spare : (i + 1) * spare] = ref[half_rows]
    trade = remote(shared, beside, esend, erecv, pair)
    trade.start()

    share, lanes = quarter // 4, width // 2
    my_lanes = pl.ds(pl.multiple_of(core * lanes, 128), lanes)

    def piece(c):
        return pl.ds(pl.multiple_of(c * share, 16), share)

    out_z = [
        remote(
            wo_ref.at[piece(chip), my_lanes],
            out_ref.at[z, piece(chip), my_lanes],
            zsend.at[i],
            zrecv.at[i],
            peer,
        )
        for i, peer in enumerate(z_peers)
    ]
    for i in (1, 0, 2):
        out_z[i].start()
    behind = [(z + 3 - i) % 4 for i in range(3)]

    def out_chip(i, j, c):
        at = out_ref.at[behind[i], piece(c), my_lanes]
        return remote(at, at, send.at[3 * i + j], recv.at[3 * i + j], (chips[j], core, z))

    def out_core(i, k):
        half = pl.ds(pl.multiple_of(k * lanes, 128), lanes)
        at = out_ref.at[behind[i], :, half]
        return remote(at, at, csend.at[i], crecv.at[i], c_peer)

    x = x_ref[...].astype(f32)
    rms1 = lax.rsqrt(jnp.sum(x * x, axis=-1, keepdims=True) * (1.0 / width) + EPS)
    normed1_ref[...] = (x * rms1 * gain_ref[0:1]).astype(bf16)
    out_ref[z] = wo_ref[...]

    cosine, sine = cos_ref[...], sin_ref[...]
    half_dim = HEAD_DIM // 2
    scale = 1.0 / math.sqrt(HEAD_DIM)
    row = lax.broadcasted_iota(jnp.int32, (rows, rows), 0)
    column = lax.broadcasted_iota(jnp.int32, (rows, rows), 1)
    doc = jnp.broadcast_to(doc_ref[...].astype(f32), (rows, rows))
    allowed = (row >= column) & (doc == doc.T)

    kept = (normed1_ref, q_ref, k_ref, v_ref, probs_ref, attended_ref, out_ref)
    outs = (normed1_out, q_out, k_out, v_out, probs_out, attended_out, out_out)
    writes = [pltpu.make_async_copy(a, b, gone.at[i]) for i, (a, b) in enumerate(zip(kept, outs))]
    writes[0].start()

    def turn(pre):
        a, b = pre[:half_dim], pre[half_dim:]
        return (
            jnp.concatenate([a * cosine - b * sine, b * cosine + a * sine], axis=0).astype(bf16)
        )

    def attend(h):
        scores = jnp.where(allowed, tn(q_ref[h], k_ref[h]) * scale, -1e30)
        raised = jnp.exp(scores - jnp.max(scores, axis=-1, keepdims=True))
        probs = raised * (1.0 / jnp.sum(raised, axis=-1, keepdims=True))
        probs_ref[h] = probs
        return nt(v_ref[h], probs.astype(bf16)).astype(bf16)

    def project(at):
        return [nt(ref[at], normed1_ref[...]) for ref in (wq_ref, wk_ref, wv_ref)]

    q, k, v = project(full_rows)
    heads = whole // HEAD_DIM
    for h in range(heads):
        at = slice(h * HEAD_DIM, (h + 1) * HEAD_DIM)
        q_ref[h], k_ref[h], v_ref[h] = turn(q[at]), turn(k[at]), v[at].astype(bf16)

    def attended_copy(number, start, size):
        at = attended_ref.at[pl.ds(pl.multiple_of(start, 16), size)]
        return lambda i: remote(
            at, at, asend.at[number, i], arecv.at[number, i], z_peers[i]
        )

    mine = z * quarter
    copies = []
    for h in range(heads):
        start = mine + odd * spare + h * HEAD_DIM
        attended_ref[pl.ds(pl.multiple_of(start, 16), HEAD_DIM)] = attend(h)
        copy = attended_copy(h, start, HEAD_DIM)
        copies += [copy(1), copy(0), copy(2)]
        for one in copies[-3:]:
            one.start()
        if h == 0:
            for i in range(3):
                out_z[i].wait_recv()
                for j in (2, 0, 1):
                    out_chip(i, j, chip).start()

    trade.wait_recv()
    for i, (ref, to) in enumerate(((wq_ref, q_ref), (wk_ref, k_ref), (wv_ref, v_ref))):
        normed1 = normed1_ref[...]
        here = nt(ref[half_rows], normed1)
        there = nt(beside[i * spare : (i + 1) * spare], normed1)
        first = jnp.where(odd == 1, there, here)
        second = jnp.where(odd == 1, here, there)
        both = jnp.concatenate([first, second], axis=0)
        to[heads] = both.astype(bf16) if to is v_ref else turn(both)
    last = attend(heads)
    for i in (1, 2, 3, 4):
        writes[i].start()
    last = jnp.where(odd == 1, last[spare:], last[:spare])
    start = mine + (1 - odd) * whole
    attended_ref[pl.ds(pl.multiple_of(start, 16), spare)] = last
    copy = attended_copy(heads, start, spare)
    copies += [copy(1), copy(0), copy(2)]
    for one in copies[-3:]:
        one.start()

    for i in range(3):
        for j in range(3):
            out_chip(i, j, chips[j]).wait_recv()
        out_core(i, core).start()
    for i in range(3):
        from_z = (z + 3 - i) % 4
        from_odd = from_z % 2
        for h in range(heads):
            attended_copy(h, from_z * quarter + from_odd * spare + h * HEAD_DIM, HEAD_DIM)(i).wait_recv()
        attended_copy(heads, from_z * quarter + (1 - from_odd) * whole, spare)(i).wait_recv()
        out_core(i, other).wait_recv()
    writes[5].start()
    writes[6].start()
    attended = attended_ref[...].T
    residual = x_ref[...].astype(f32) + nt(attended, out_ref[...].reshape(width, width))
    residual_ref[...] = residual
    rms2 = lax.rsqrt(jnp.sum(residual * residual, axis=-1, keepdims=True) * (1.0 / width) + EPS)
    normed2_ref[...] = (residual * rms2 * gain_ref[1:2]).astype(bf16)
    for write in writes:
        write.wait()
    for one in (trade, *out_z, *copies):
        one.wait_send()
    for i in range(3):
        for j in range(3):
            out_chip(i, j, chip).wait_send()
        out_core(i, core).wait_send()


def front(x, gains, wq, wk, wv, wo, doc, tables):
    rows, width = x.shape
    quarter = wq.shape[0]
    heads = -(-quarter // HEAD_DIM)
    spare = quarter % HEAD_DIM
    vmem = pl.BlockSpec(memory_space=pltpu.VMEM)
    dma = pltpu.SemaphoreType.DMA
    low = lambda *shape: jax.ShapeDtypeStruct(shape, bf16)
    early = [
        low(rows, width),
        *[low(heads, HEAD_DIM, rows)] * 3,
        jax.ShapeDtypeStruct((heads, rows, rows), f32),
        low(width, rows),
        low(4, quarter, width),
    ]
    return pl.pallas_call(
        front_kernel,
        in_specs=[vmem] * 9,
        out_specs=[pl.BlockSpec(memory_space=pl.ANY)] * len(early) + [vmem] * 2,
        out_shape=[*early, jax.ShapeDtypeStruct((rows, width), f32), low(rows, width)],
        scratch_shapes=[
            *[pltpu.VMEM(a.shape, a.dtype) for a in early],
            dma((len(early),)),
            pltpu.VMEM((3 * spare, width), bf16),
            pltpu.VMEM((3 * spare, width), bf16),
            dma,
            dma,
            dma((heads, 3)),
            dma((heads, 3)),
            dma((3,)),
            dma((3,)),
            dma((9,)),
            dma((9,)),
            dma((3,)),
            dma((3,)),
        ],
        compiler_params=pltpu.CompilerParams(
            vmem_limit_bytes=VMEM_LIMIT, collective_id=1, has_side_effects=True
        ),
        cost_estimate=takes(50),
        name="front",
    )(x, gains, wq, wk, wv, wo, doc, *tables)


def collect_sum_kernel(
    y_ref,
    slot_ref,
    gsw_ref,
    normed_ref,
    grad_ref,
    gate_ref,
    up_ref,
    down_ref,
    out_ref,
    sum_ref,
    forward_ref,
    mine,
    pick,
    ybuf,
    stage,
    given,
    sums,
    relay,
    land,
    zland,
    copied,
    core_send,
    core_recv,
    send,
    recv,
    zsend,
    zrecv,
    grads,
    *more,
):
    chip, core, z, cx, cy, cd = places()
    other = 1 - core
    x_peer, y_peer, c_peer = (cx, core, z), (cy, core, z), (chip, other, z)
    z_peers = [(chip, core, (z + i) % 4) for i in (1, 2, 3)]
    local, rows = slot_ref.shape[1:]
    tall = out_ref.shape[0]
    me = chip * 2 + core
    number = lax.broadcasted_iota(jnp.int32, (CAP, rows), 0)
    row = lax.broadcasted_iota(jnp.int32, (EXTRA, rows), 0)

    greet([x_peer, y_peer, c_peer, (cd, core, z), *z_peers])

    def sequence(t):
        p = t // 2
        x, y = (chip % 2 + 1 + p // 2) % 2, (chip // 2 + 1 + p % 2) % 2
        return (y * 2 + x) * 2 + (core + 1 + t % 2) % 2

    def in_copy(t):
        return pltpu.make_async_copy(y_ref.at[sequence(t)], ybuf.at[t % 2], copied.at[t % 2])

    def to_core(p):
        return remote(stage.at[p % 2], given.at[p], core_send.at[p], core_recv.at[p], c_peer)

    starts = (*SUM_STARTS, tall)
    units = len(starts) - 1
    sizes = [starts[u + 1] - starts[u] for u in range(units)]

    def top(u):
        return pl.ds(starts[u], sizes[u] // 2)

    def low(u):
        return pl.ds(starts[u] + sizes[u] // 2, sizes[u] // 2)

    def first(u, of):
        return pl.ds(0, sizes[u] // of)

    def over(u, number, src, dst, peer):
        return remote(src, dst, send.at[u, number], recv.at[u, number], peer)

    far_top = [over(u, 0, sums.at[0, top(u)], relay.at[u, 0, first(u, 2)], x_peer) for u in range(units)]
    far_low = [over(u, 1, sums.at[0, low(u)], relay.at[u, 1, first(u, 2)], y_peer) for u in range(units)]
    x_top = [over(u, 2, sums.at[1, top(u)], land.at[0, top(u)], x_peer) for u in range(units)]
    x_low = [over(u, 3, sums.at[1, low(u)], land.at[0, low(u)], x_peer) for u in range(units)]
    y_low = [over(u, 4, sums.at[2, low(u)], land.at[1, low(u)], y_peer) for u in range(units)]
    y_top = [over(u, 5, sums.at[2, top(u)], land.at[1, top(u)], y_peer) for u in range(units)]

    in_copy(0).start()
    start, share, _, end, total = weight_sum(grads, *more[:3], None, *more[3:])

    def shared_expert():
        normed, grad_t = normed_ref[...], grad_ref[...]
        size = gate_ref.shape[0]
        gate, up = nt(gate_ref[...], normed), nt(up_ref[...], normed)
        sig = 1.0 / (1.0 + jnp.exp(-gate))
        act = gate * sig
        hidden = (act * up).astype(bf16)
        forward_ref[...] = tn(hidden, down_ref[...]).astype(bf16)
        grad_hidden = nn(down_ref[...], grad_t)
        grad_gate = (grad_hidden * up * sig * (1.0 + gate * (1.0 - sig))).astype(bf16)
        grad_up = (grad_hidden * act).astype(bf16)
        grads[:size] = nn(grad_gate, normed).astype(bf16)
        grads[size : 2 * size] = nn(grad_up, normed).astype(bf16)
        grads[2 * size : 3 * size] = nt(hidden, grad_t).astype(bf16)
        grads[3 * size :] = jnp.zeros((grads.shape[0] - 3 * size, grads.shape[1]), bf16)
        start()
        mine[...] = (tn(grad_gate, gate_ref[...]) + tn(grad_up, up_ref[...])).astype(bf16)

    def step(t, carry):
        @pl.when(t < 7)
        def _():
            in_copy(t + 1).start()

        p, s = t // 2, sequence(t)
        probs = jnp.zeros((EXTRA, rows), f32)
        for e in range(local):
            mask = slot_ref[s, e : e + 1, :] == number
            pick[e * CAP : (e + 1) * CAP, :] = mask.astype(f32).astype(bf16)
            column = gsw_ref[e, pl.ds(pl.multiple_of(s * CAP, 8), CAP), :]
            line = jnp.sum(jnp.where(mask, column, 0.0), axis=0, keepdims=True)
            probs = jnp.where(row == me * local + e, line, probs)
        in_copy(t).wait()
        back = tn(pick[...], ybuf[t % 2].reshape(local * CAP, -1))

        @pl.when(t % 2 == 0)
        def _():
            @pl.when(p >= 2)
            def _():
                to_core(p - 2).wait_send()

            stage[p % 2, :rows] = back.astype(bf16)
            stage[p % 2, rows:] = jnp.zeros((tall - rows, back.shape[1]), bf16)
            stage[p % 2, rows:, :rows] = probs.astype(bf16)
            to_core(p).start()

        @pl.when(t % 2 == 1)
        def _():
            to_core(p).wait_recv()
            sums[p, :rows] = (back + given[p, :rows].astype(f32)).astype(bf16)
            sums[p, rows:] = given[p, rows:]
            sums[p, rows:, :rows] = (probs + given[p, rows:, :rows].astype(f32)).astype(bf16)

        @pl.when(t == 1)
        def _():
            far_top[0].start()
            far_low[0].start()

        @pl.when(t == 3)
        def _():
            x_top[0].start()

        @pl.when(t == 5)
        def _():
            y_low[0].start()
            far_top[1].start()
            far_low[1].start()

        return carry

    lax.fori_loop(0, 8, step, 0)
    def relayed(u):
        far_low[u].wait_recv()
        at = low(u)
        sums[1, at] = (sums[1, at].astype(f32) + relay[u, 1, first(u, 2)].astype(f32)).astype(bf16)
        x_low[u].start()
        far_top[u].wait_recv()
        at = top(u)
        sums[2, at] = (sums[2, at].astype(f32) + relay[u, 0, first(u, 2)].astype(f32)).astype(bf16)
        y_top[u].start()

    def block_of(u, q):
        part = sizes[u] // 4
        return pl.ds(pl.multiple_of(starts[u] + q * part, 16), part)

    def z_sems(u, number):
        return zsend.at[u, number], zrecv.at[u, number]

    scatter = [
        [
            remote(
                sums.at[3, block_of(u, (z + i) % 4)],
                zland.at[u, i - 1, first(u, 4)],
                *z_sems(u, i - 1),
                z_peers[i - 1],
            )
            for i in (1, 2, 3)
        ]
        for u in range(units)
    ]

    def back_copy(u, q, i):
        at = out_ref.at[block_of(u, q)]
        return remote(at, at, *z_sems(u, 2 + i), z_peers[i - 1])

    def landed(u):
        for copy in (x_top[u], y_top[u], x_low[u], y_low[u]):
            copy.wait_recv()
        at = slice(starts[u], starts[u + 1])
        added = sums[3, at].astype(f32) + land[0, at].astype(f32) + land[1, at].astype(f32)
        ours = min(rows, starts[u + 1]) - starts[u]
        if ours == sizes[u]:
            sums[3, at] = (added + mine[at].astype(f32)).astype(bf16)
        else:
            here = slice(starts[u], starts[u] + ours)
            sums[3, here] = (added[:ours] + mine[here].astype(f32)).astype(bf16)
            sums[3, starts[u] + ours : starts[u + 1]] = added[ours:].astype(bf16)
        for i in (1, 0, 2):
            scatter[u][i].start()

    def summed(u):
        done = sums[3, block_of(u, z)].astype(f32)
        for i in range(3):
            scatter[u][i].wait_recv()
            done = done + zland[u, i, first(u, 4)].astype(f32)
        out_ref[block_of(u, z)] = done.astype(bf16)
        for i in (2, 1, 3):
            back_copy(u, z, i).start()

    relayed(0)
    for u in range(1, units):
        x_top[u].start()
        y_low[u].start()
        if u < units - 1:
            far_top[u + 1].start()
            far_low[u + 1].start()
        if u == 1:
            shared_expert()
        relayed(u)
        if u == units - 1:
            share()
        landed(u - 1)
        if u >= 2:
            summed(u - 2)
    landed(units - 1)
    summed(units - 2)
    sum_ref[...] = total().astype(bf16)
    end()
    summed(units - 1)
    for u in range(units):
        for i in (1, 2, 3):
            back_copy(u, (z + 4 - i) % 4, i).wait_recv()
    for u in range(units):
        for copy in (far_top[u], far_low[u], x_top[u], x_low[u], y_low[u], y_top[u], *scatter[u]):
            copy.wait_send()
        for i in (1, 2, 3):
            back_copy(u, z, i).wait_send()
    for p in (2, 3):
        to_core(p).wait_send()


def collect_sum(y, slot, gsw, normed, grad_t, *shared):
    s, local, cap, width = y.shape
    rows = slot.shape[2]
    tall = rows + EXTRA
    dma = pltpu.SemaphoreType.DMA
    units = len(SUM_STARTS)
    most = max(b - a for a, b in zip(SUM_STARTS, (*SUM_STARTS[1:], tall)))
    weights = 128 * (-(-sum(a.shape[0] for a in shared) // 128))
    vmem = pl.BlockSpec(memory_space=pltpu.VMEM)
    return pl.pallas_call(
        collect_sum_kernel,
        in_specs=[pl.BlockSpec(memory_space=pl.ANY)] + [vmem] * 7,
        out_specs=[vmem, vmem, vmem],
        out_shape=[
            jax.ShapeDtypeStruct((tall, width), bf16),
            jax.ShapeDtypeStruct((weights // 8, width), bf16),
            jax.ShapeDtypeStruct((rows, width), bf16),
        ],
        scratch_shapes=[
            pltpu.VMEM((rows, width), bf16),
            pltpu.VMEM((local * cap, rows), bf16),
            pltpu.VMEM((2, local, cap, width), bf16),
            pltpu.VMEM((2, tall, width), bf16),
            pltpu.VMEM((4, tall, width), bf16),
            pltpu.VMEM((4, tall, width), bf16),
            pltpu.VMEM((units, 2, most // 2, width), bf16),
            pltpu.VMEM((2, tall, width), bf16),
            pltpu.VMEM((units, 3, most // 4, width), bf16),
            dma((2,)),
            dma((4,)),
            dma((4,)),
            dma((units, 6)),
            dma((units, 6)),
            dma((units, 6)),
            dma((units, 6)),
            *weight_sum_scratch(weights, width),
        ],
        compiler_params=pltpu.CompilerParams(
            vmem_limit_bytes=VMEM_LIMIT, collective_id=2, has_side_effects=True
        ),
        cost_estimate=takes(131),
        name="collect_sum",
    )(y, slot, gsw, normed, grad_t, *shared)


def back_kernel(
    sums_ref,
    residual_ref,
    normed2_ref,
    grad_ref,
    router_ref,
    gain_ref,
    cos_ref,
    sin_ref,
    piece_ref,
    *refs,
):
    late, outs, rest = refs[:11], refs[11:17], refs[17:]
    held, sems, rest = rest[:11], rest[11], rest[12:]
    loads = [pltpu.make_async_copy(a, b, sems.at[i]) for i, (a, b) in enumerate(zip(late, held))]
    for load in loads:
        load.start()
    back_steps(
        loads,
        sums_ref,
        residual_ref,
        normed2_ref,
        grad_ref,
        router_ref,
        gain_ref,
        cos_ref,
        sin_ref,
        piece_ref,
        *held,
        *outs,
        *rest,
    )


def back_steps(
    loads,
    sums_ref,
    residual_ref,
    normed2_ref,
    grad_ref,
    router_ref,
    gain_ref,
    cos_ref,
    sin_ref,
    piece_ref,
    out_ref,
    q_ref,
    k_ref,
    v_ref,
    probs_ref,
    wq_ref,
    wk_ref,
    wv_ref,
    attended_ref,
    x_ref,
    normed_ref,
    tokens_ref,
    early_ref,
    first_ref,
    second_ref,
    shared_ref,
    shared_sum_ref,
    dq_ref,
    dk_ref,
    dv_ref,
    x_t,
    gain_column,
    back_t,
    low_t,
    part,
    low_part,
    zland,
    mine,
    theirs,
    zsend,
    zrecv,
    lsend,
    lrecv,
    *more,
):
    chip, core, z, cx, cy, cd = places()
    odd = z % 2
    c_peer = (chip, 1 - core, z)
    z_peers = [(chip, core, (z + i) % 4) for i in (1, 2, 3)]
    quarter, width = wq_ref.shape
    rows = x_ref.shape[0]
    groups = [
        weight_sum(*more[8 * i : 8 * i + 4], ref, *more[8 * i + 4 : 8 * i + 8])
        for i, ref in enumerate((early_ref, first_ref, second_ref, shared_ref))
    ]
    early, *by_head = [more[8 * i] for i in range(4)]
    START, SHARE, GIVE_BACK, END = range(4)
    experts = router_ref.shape[0]
    whole = HEAD_DIM * (quarter // HEAD_DIM)
    spare = quarter - whole
    heads = whole // HEAD_DIM
    greet([c_peer, *[(c, core, z) for c in (cx, cy, cd)], *z_peers])
    put, gathered = weight_gather(shared_sum_ref, *more[32:])
    put(piece_ref[...])

    logits = nt(router_ref[...], normed2_ref[...])
    raised = jnp.exp(logits - jnp.max(logits, axis=0, keepdims=True))
    gates = raised / jnp.sum(raised, axis=0, keepdims=True)
    grad_probs = sums_ref[rows:, :rows].astype(f32)
    grad_logits = gates * (grad_probs - jnp.sum(grad_probs * gates, axis=0, keepdims=True))
    grad_logits = grad_logits.astype(bf16)
    grad_router = nn(grad_logits, normed2_ref[...])
    grad_normed2 = sums_ref[:rows].astype(f32) + tn(grad_logits, router_ref[...])
    residual = residual_ref[...]
    rms2 = lax.rsqrt(jnp.sum(residual * residual, axis=-1, keepdims=True) * (1.0 / width) + EPS)
    grad_ffn = jnp.sum(grad_normed2 * residual * rms2, axis=0, keepdims=True)
    u = grad_normed2 * gain_ref[1:2]
    mean2 = jnp.sum(u * residual, axis=-1, keepdims=True) * (1.0 / width)
    added = rms2 * u - residual * (rms2 * rms2 * rms2 * mean2)
    back_t[...] = added.T + grad_ref[...].astype(f32)
    low_t[...] = back_t[...].astype(bf16)
    own = block(z, quarter)

    cosine, sine = cos_ref[...], sin_ref[...]
    half_dim = HEAD_DIM // 2
    scale = 1.0 / math.sqrt(HEAD_DIM)

    def turn_back(v):
        a, b = v[:half_dim] * scale, v[half_dim:] * scale
        turned = [a * cosine + b * sine, b * cosine - a * sine]
        return jnp.concatenate(turned, axis=0).astype(bf16)

    for i in range(5):
        loads[i].wait()
    first_lane = z * quarter + odd * spare
    shared_lane = z * quarter + (1 - odd) * whole - odd * spare
    for h in range(heads + 1):
        lane = first_lane + h * HEAD_DIM if h < heads else shared_lane
        lane = pl.ds(pl.multiple_of(lane, HEAD_DIM), HEAD_DIM)
        grad_attended = tn(out_ref[:, lane], low_t[...]).astype(bf16)
        probs = probs_ref[h]
        grad_p = tn(grad_attended, v_ref[h])
        grad_v = nn(grad_attended, probs.astype(bf16)).astype(bf16)
        delta = jnp.sum(probs * grad_p, axis=-1, keepdims=True)
        grad_s = (probs * (grad_p - delta)).astype(bf16)
        grad_q = turn_back(nt(k_ref[h], grad_s))
        grad_k = turn_back(nn(q_ref[h], grad_s))
        for ref, value in ((dq_ref, grad_q), (dk_ref, grad_k), (dv_ref, grad_v)):
            if h < heads:
                at = pl.ds(pl.multiple_of(odd * spare + h * HEAD_DIM, 16), HEAD_DIM)
                ref[at] = value
            else:
                at = pl.ds(pl.multiple_of((1 - odd) * whole, 16), spare)
                ref[at] = jnp.where(odd == 1, value[spare:], value[:spare])

    for i in (5, 6, 7):
        loads[i].wait()
    part[...] = tn(wq_ref[...], dq_ref[...])
    part[...] += tn(wk_ref[...], dk_ref[...])
    part[...] += tn(wv_ref[...], dv_ref[...])
    low_part[...] = part[...].astype(bf16)
    to_z = [
        remote(
            low_part.at[block((z + i) % 4, quarter)],
            zland.at[i - 1],
            zsend.at[i - 1],
            zrecv.at[i - 1],
            z_peers[i - 1],
        )
        for i in (1, 2, 3)
    ]
    few_to_z = [
        remote(mine, theirs.at[i], lsend.at[i], lrecv.at[i], peer) for i, peer in enumerate(z_peers)
    ]
    loads[9].wait()
    x_t[...] = x_ref[...].T
    gain_column[...] = jnp.broadcast_to(gain_ref[0:1], (8, width)).T
    x_all = x_t[...].astype(f32)
    rms1 = lax.rsqrt(jnp.sum(x_all * x_all, axis=0, keepdims=True) * (1.0 / width) + EPS)
    along = part[...] * x_all
    mine[...] = jnp.zeros(mine.shape, f32)
    mine[0:1, :rows] = jnp.sum(along * gain_column[:, 0:1], axis=0, keepdims=True)
    mine[:, rows:] = nt(jnp.ones((8, rows), bf16), (along * rms1).astype(bf16))
    for copy in few_to_z:
        copy.start()
    for i in (1, 0, 2):
        to_z[i].start()

    loads[8].wait()
    loads[10].wait()
    early[:quarter] = nt(low_t[own], attended_ref[...]).astype(bf16)
    early[quarter:] = grad_router.astype(bf16)
    groups[0][START]()
    normed = normed_ref[...]
    for h in range(heads + 1):
        if h < heads:
            size, at = HEAD_DIM, odd * spare + h * HEAD_DIM
        else:
            size, at = spare, (1 - odd) * whole
        at = pl.ds(pl.multiple_of(at, 16), size)
        for i, ref in enumerate((dq_ref, dk_ref, dv_ref)):
            by_head[h][i * size : (i + 1) * size] = nn(ref[at], normed).astype(bf16)
        if h < heads:
            groups[1 + h][START]()
            groups[h][SHARE]()
    at = 3 * spare
    late = by_head[heads]
    for copy in few_to_z:
        copy.wait_recv()
    few = mine[...] + theirs[0] + theirs[1] + theirs[2]
    late[at:] = jnp.zeros((late.shape[0] - at, width), bf16)
    line = lax.broadcasted_iota(jnp.int32, (16, width), 0)
    gains = jnp.where(line == 0, few[0:1, rows:], jnp.where(line == 1, grad_ffn, 0.0))
    late[at : at + 16] = gains.astype(bf16)
    groups[3][START]()
    groups[2][SHARE]()
    groups[0][GIVE_BACK]()
    groups[3][SHARE]()
    groups[1][GIVE_BACK]()

    total = part[own]
    for i in range(3):
        to_z[i].wait_recv()
        total = total + zland[i].astype(f32)
    x = x_t[own].astype(f32)
    mean = few[0:1, :rows] * (1.0 / width)
    tokens_ref[...] = back_t[own] + rms1 * gain_column[own, 0:1] * total - x * (rms1 * rms1 * rms1 * mean)

    groups[2][GIVE_BACK]()
    groups[3][GIVE_BACK]()
    gathered()
    for group in groups:
        group[END]()
    for copy in (*to_z, *few_to_z):
        copy.wait_send()


def back(now, late):
    quarter, width = late[5].shape
    rows = now[1].shape[0]
    spare = quarter % HEAD_DIM
    tall = [quarter + now[4].shape[0], 3 * HEAD_DIM, 3 * HEAD_DIM, 3 * spare + 64]
    shared = 8 * now[8].shape[0]
    vmem = pl.BlockSpec(memory_space=pltpu.VMEM)
    dma = pltpu.SemaphoreType.DMA
    return pl.pallas_call(
        back_kernel,
        in_specs=[vmem] * len(now) + [pl.BlockSpec(memory_space=pl.ANY)] * len(late),
        out_specs=[vmem] * 6,
        out_shape=[
            jax.ShapeDtypeStruct((quarter, rows), f32),
            *[jax.ShapeDtypeStruct((lines, width), bf16) for lines in (*tall, shared)],
        ],
        scratch_shapes=[
            *[pltpu.VMEM(a.shape, a.dtype) for a in late],
            dma((len(late),)),
            *[pltpu.VMEM((quarter, rows), bf16)] * 3,
            pltpu.VMEM((width, rows), bf16),
            pltpu.VMEM((width, 8), f32),
            pltpu.VMEM((width, rows), f32),
            pltpu.VMEM((width, rows), bf16),
            pltpu.VMEM((width, rows), f32),
            pltpu.VMEM((width, rows), bf16),
            pltpu.VMEM((3, quarter, rows), bf16),
            pltpu.VMEM((8, rows + width), f32),
            pltpu.VMEM((3, 8, rows + width), f32),
            dma((3,)),
            dma((3,)),
            dma((3,)),
            dma((3,)),
            *[one for lines in tall for one in weight_sum_scratch(lines, width)],
            dma((5,)),
            dma((5,)),
            dma((6,)),
            dma((6,)),
        ],
        compiler_params=pltpu.CompilerParams(
            vmem_limit_bytes=VMEM_LIMIT, collective_id=3, has_side_effects=True
        ),
        cost_estimate=takes(90),
        name="back",
    )(*now, *late)


def widen_kernel(early_ref, first_ref, second_ref, last_ref, shared_ref, *out_refs):
    quarter = out_refs[0].shape[0]
    odd = lax.axis_index("hs") % 2
    whole = HEAD_DIM * (quarter // HEAD_DIM)
    spare = quarter - whole
    for i in range(3):
        for h, ref in enumerate((first_ref, second_ref)):
            at = pl.ds(pl.multiple_of(odd * spare + h * HEAD_DIM, 8), HEAD_DIM)
            out_refs[i][at] = ref[i * HEAD_DIM : (i + 1) * HEAD_DIM].astype(f32)
        at = pl.ds(pl.multiple_of((1 - odd) * whole, 8), spare)
        out_refs[i][at] = last_ref[i * spare : (i + 1) * spare].astype(f32)
    out_refs[3][...] = early_ref[:quarter].astype(f32)
    out_refs[4][...] = early_ref[quarter:].astype(f32)
    out_refs[5][...] = last_ref[3 * spare : 3 * spare + 16].astype(f32)
    size = out_refs[6].shape[0]
    for i in range(3):
        out_refs[6 + i][...] = shared_ref[i * size : (i + 1) * size].astype(f32)


def widen(sums, quarter, hidden_units):
    width = sums[0].shape[1]
    step = width // 5
    tall = [quarter] * 4 + [sums[0].shape[0] - quarter, 16] + [hidden_units] * 3
    blocks = lambda lines: pl.BlockSpec((lines, step), lambda i: (0, i))
    return pl.pallas_call(
        widen_kernel,
        grid=(width // step,),
        in_specs=[blocks(a.shape[0]) for a in sums],
        out_specs=[blocks(lines) for lines in tall],
        out_shape=[jax.ShapeDtypeStruct((lines, width), f32) for lines in tall],
        compiler_params=pltpu.CompilerParams(vmem_limit_bytes=VMEM_LIMIT),
        cost_estimate=takes(8),
        name="widen",
    )(*sums)


def plain_front(
    tokens, attn_gain, query_t, key_t, value_t, attn_out, ffn_gain, documents, tables
):
    rows, width = tokens.shape
    quarter = query_t.shape[0]
    hs, hs_count = lax.axis_index("hs"), lax.axis_size("hs")
    odd = (hs % 2) == 1
    spare = -quarter % HEAD_DIM
    heads = (quarter + spare) // HEAD_DIM

    def outer(w):
        return jnp.where(odd, w[:spare], w[quarter - spare :])

    sent = jnp.concatenate([outer(query_t), outer(key_t), outer(value_t)], axis=0)
    got = lax.ppermute(sent, "hs", [(i, i ^ 1) for i in range(hs_count)])

    def widened(w, extra):
        return jnp.where(
            odd, jnp.concatenate([extra, w], axis=0), jnp.concatenate([w, extra], axis=0)
        )

    x = tokens.astype(f32)
    rms1 = lax.rsqrt(jnp.mean(x * x, axis=-1, keepdims=True) + EPS)
    normed1 = (x * rms1 * attn_gain).astype(bf16)
    shape3 = (heads, HEAD_DIM, rows)
    q, k, v = [
        ein("cd,td->ct", widened(w, got[i * spare : (i + 1) * spare]), normed1).reshape(shape3)
        for i, w in enumerate((query_t, key_t, value_t))
    ]
    q, k, v = rope(q, *tables).astype(bf16), rope(k, *tables).astype(bf16), v.astype(bf16)
    positions = jnp.arange(rows, dtype=jnp.int32)
    doc = documents[0]
    allowed = (positions[:, None] >= positions[None, :]) & (doc[:, None] == doc[None, :])
    scale = 1.0 / math.sqrt(HEAD_DIM)
    scores = jnp.where(allowed[None], ein("hdq,hdk->hqk", q, k) * scale, -1e30)
    raised = jnp.exp(scores - jnp.max(scores, axis=-1, keepdims=True))
    probs = raised / jnp.sum(raised, axis=-1, keepdims=True)
    attended = ein("hdk,hqk->hdq", v, probs.astype(bf16)).astype(bf16).reshape(-1, rows)
    attended = jnp.where(odd, attended[spare:], attended[:quarter])
    attended_t = lax.all_gather(attended, "hs", axis=0, tiled=True)
    out_t = lax.all_gather(attn_out.T, "hs", axis=0, tiled=True)
    residual = x + ein("ct,oc->to", attended_t, out_t)
    rms2 = lax.rsqrt(jnp.mean(residual * residual, axis=-1, keepdims=True) + EPS)
    normed2 = (residual * rms2 * ffn_gain).astype(bf16)
    return normed1, q, k, v, probs, attended_t, out_t, residual, normed2


def over_ep(a):
    return lax.psum(a.astype(bf16), EP).astype(f32)


def plain_back(
    sums,
    residual,
    normed2,
    grad_t,
    router_t,
    ffn_gain,
    out_t,
    q,
    k,
    v,
    probs,
    tables,
    query_t,
    key_t,
    value_t,
    normed1,
    attended_t,
    tokens,
    attn_gain,
):
    rows, width = tokens.shape
    quarter = query_t.shape[0]
    hs = lax.axis_index("hs")
    odd = (hs % 2) == 1
    spare = -quarter % HEAD_DIM
    held = quarter + spare
    col0 = hs * quarter

    def own(v):
        v = v.astype(bf16).reshape(held, rows)
        return jnp.where(odd, v[spare:], v[:quarter])

    gates = jax.nn.softmax(nt(normed2, router_t), axis=-1)
    grad_probs = sums[rows:, :rows].T.astype(f32)
    grad_logits = (
        gates * (grad_probs - jnp.sum(grad_probs * gates, axis=-1, keepdims=True))
    ).astype(bf16)
    grad_router = tn(grad_logits, normed2)
    grad_normed2 = sums[:rows].astype(f32) + dot(grad_logits, router_t)
    rms2 = lax.rsqrt(jnp.mean(residual * residual, axis=-1, keepdims=True) + EPS)
    grad_ffn_gain = jnp.sum(grad_normed2 * residual * rms2, axis=0)
    u = grad_normed2 * ffn_gain
    grad_residual = (
        grad_t.T.astype(f32)
        + rms2 * u
        - residual * rms2**3 * jnp.mean(u * residual, axis=-1, keepdims=True)
    )
    back_t = grad_residual.T
    low_t = back_t.astype(bf16)
    out_held = lax.dynamic_slice_in_dim(out_t, jnp.where(odd, col0 - spare, col0), held, 1)
    grad_attended = tn(out_held, low_t).astype(bf16).reshape(-1, HEAD_DIM, rows)
    grad_p = ein("hdq,hdk->hqk", grad_attended, v)
    grad_v = own(ein("hdq,hqk->hdk", grad_attended, probs.astype(bf16)))
    grad_s = (probs * (grad_p - jnp.sum(probs * grad_p, axis=-1, keepdims=True))).astype(bf16)
    scale = 1.0 / math.sqrt(HEAD_DIM)
    grad_q = own(rope_back(ein("hdk,hqk->hdq", k, grad_s) * scale, *tables))
    grad_k = own(rope_back(ein("hdq,hqk->hdk", q, grad_s) * scale, *tables))
    own_rows = lambda a: lax.dynamic_slice_in_dim(a, col0, quarter, 0)
    heads_sums = [
        over_ep(dot(grad_q, normed1)),
        over_ep(dot(grad_k, normed1)),
        over_ep(dot(grad_v, normed1)),
        over_ep(nt(own_rows(low_t), attended_t)),
    ]
    part = tn(query_t, grad_q) + tn(key_t, grad_k) + tn(value_t, grad_v)
    grad_n1 = lax.psum_scatter(part.astype(bf16), "hs", scatter_dimension=0, tiled=True)
    grad_n1 = grad_n1.astype(f32)
    x = tokens.T.astype(f32)
    x_own = own_rows(x)
    rms_t = lax.rsqrt(jnp.mean(x * x, axis=0, keepdims=True) + EPS)
    w1 = grad_n1 * own_rows(attn_gain)[:, None]
    mean1 = lax.psum(jnp.sum(w1 * x_own, axis=0, keepdims=True), "hs") / width
    grad_tokens = own_rows(back_t) + rms_t * w1 - x_own * rms_t**3 * mean1
    gain_own = jnp.sum(grad_n1 * x_own * rms_t, axis=1)
    gain_part = lax.dynamic_update_slice_in_dim(jnp.zeros((width,), f32), gain_own, col0, 0)
    grad_attn_gain = lax.psum(gain_part, (*EP, "hs"))
    return (
        grad_tokens,
        heads_sums,
        over_ep(grad_router),
        grad_attn_gain,
        lax.psum(grad_ffn_gain, EP),
    )


def shards(
    tokens,
    attn_gain,
    attn_query,
    attn_key,
    attn_value,
    attn_out,
    ffn_gain,
    router,
    shared_gate,
    shared_up,
    shared_down,
    expert_gate,
    expert_up,
    expert_down,
    routes,
    documents,
    out_grad,
):
    rows, width = tokens.shape
    quarter = out_grad.shape[1]
    hs = lax.axis_index("hs")
    ep_count = lax.axis_size("xy") * lax.axis_size("core")
    ep = lax.axis_index("xy") * lax.axis_size("core") + lax.axis_index("core")
    local = expert_gate.shape[0]
    experts = router.shape[1]
    small = ep_count == 8 and lax.axis_size("hs") == 4

    query_t, key_t, value_t, router_t = attn_query.T, attn_key.T, attn_value.T, router.T
    positions = jnp.arange(rows, dtype=jnp.int32)
    below = (positions[:, None] > positions[None, :]).astype(bf16)
    chosen = jnp.any(
        routes[:, :, None] == jnp.arange(experts, dtype=jnp.int32)[None, None, :], axis=1
    )
    own_slots = jnp.where(chosen, dot(below, chosen.astype(bf16)), -1.0).T.astype(bf16)
    tables = rope_tables(rows)

    if small:
        both_gains = jnp.stack([attn_gain, ffn_gain])
        ahead = front(
            tokens, both_gains, query_t, key_t, value_t, attn_out.T, documents, tables
        )
    else:
        ahead = plain_front(
            tokens, attn_gain, query_t, key_t, value_t, attn_out, ffn_gain, documents, tables
        )
    normed1, q, k, v, probs, attended_t, out_t, residual, normed2 = ahead
    out_t = out_t.reshape(width, width)

    first = ep * local
    rolled = jnp.roll(router_t, -first, axis=0)
    gate_t, up_t = expert_gate.swapaxes(1, 2), expert_up.swapaxes(1, 2)
    weights = gate_t, up_t, expert_down
    if small:
        ex_in, slot_weight, slot, grad_t = gather_spread(
            normed2, own_slots, rolled, out_grad.T, local, ep_count
        )
        ex_out, ex_gate, ex_up, near = experts_forward(ex_in, slot_weight, *weights, grad_t)
        out_part, far, given = collect_sending(ex_out, slot, grad_t, near)
        ex_grad = spread_grad(grad_t, near, far, given, slot)
    else:
        grad_all_t = lax.all_gather(out_grad.T, (*EP, "hs"), axis=0, tiled=True)
        grad_all_t = grad_all_t.reshape(ep_count, width, rows)
        grad_t = lax.dynamic_index_in_dim(grad_all_t, ep, 0, keepdims=False)
        slot = lax.dynamic_slice_in_dim(
            lax.all_gather(own_slots, EP, axis=0), first, local, 1
        ).astype(jnp.int32)
        normed_all = lax.all_gather(normed2, EP, axis=0, tiled=True)
        ex_in, slot_weight = spread(normed_all, slot, rolled)
        ex_out, ex_gate, ex_up = experts_forward(ex_in, slot_weight, *weights)
        out_part = collect(ex_out, slot)
        ex_grad = spread(grad_all_t, slot)
    out_part = out_part.reshape(ep_count * rows, width)
    ex_back, grad_gate_t, grad_up_t, grad_expert_down, grad_slot_weight = experts_backward(
        ex_in, ex_grad, ex_gate, ex_up, slot_weight, *weights
    )

    if small:
        back_sums, shared_piece, shared_part = collect_sum(
            ex_back, slot, grad_slot_weight, normed2, grad_t, shared_gate.T, shared_up.T, shared_down
        )
        grad_tokens, *sums = back(
            (back_sums, residual, normed2, grad_t, router_t, both_gains, *tables, shared_piece),
            (out_t, q, k, v, probs, query_t, key_t, value_t, attended_t, tokens, normed1),
        )
        *heads_sums, grad_router, gains, sum_gate, sum_up, sum_down = widen(
            sums, quarter, shared_down.shape[0]
        )
        shared_sums = sum_gate, sum_up, sum_down
        grad_attn_gain, grad_ffn_gain = gains[0], gains[1]
    else:
        sh_gate = dot(normed2, shared_gate)
        sh_up = dot(normed2, shared_up)
        sh_sig = jax.nn.sigmoid(sh_gate)
        sh_act = sh_gate * sh_sig
        sh_hidden = (sh_act * sh_up).astype(bf16)
        shared_part = dot(sh_hidden, shared_down)
        grad_sh = ein("dt,fd->tf", grad_t, shared_down)
        grad_sh_gate = (grad_sh * sh_up * sh_sig * (1 + sh_gate * (1 - sh_sig))).astype(bf16)
        grad_sh_up = (grad_sh * sh_act).astype(bf16)
        shared_grads = [
            ein("tf,td->fd", grad_sh_gate, normed2).astype(bf16),
            ein("tf,td->fd", grad_sh_up, normed2).astype(bf16),
            ein("tf,dt->fd", sh_hidden, grad_t).astype(bf16),
        ]
        shared_back = ein("tf,df->td", grad_sh_gate, shared_gate) + ein(
            "tf,df->td", grad_sh_up, shared_up
        )
        back_part = collect(ex_back, slot, grad_slot_weight, first, experts).reshape(-1, width)
        back_rows = lax.psum_scatter(back_part, EP, scatter_dimension=0, tiled=True).astype(f32)
        back_rows = jnp.concatenate([back_rows[:rows] + shared_back, back_rows[rows:]], axis=0)
        back_sums = lax.psum(back_rows.astype(bf16), "hs")
        shared_sums = [over_ep(a) for a in shared_grads]
        grad_tokens, heads_sums, grad_router, grad_attn_gain, grad_ffn_gain = plain_back(
            back_sums,
            residual,
            normed2,
            grad_t,
            router_t,
            ffn_gain,
            out_t,
            q,
            k,
            v,
            probs,
            tables,
            query_t,
            key_t,
            value_t,
            normed1,
            attended_t,
            tokens,
            attn_gain,
        )

    rows_major = Layout(major_to_minor=(0, 1))
    out_part = with_layout_constraint(out_part, rows_major)
    out_rows = lax.psum_scatter(out_part, EP, scatter_dimension=0, tiled=True)
    out_rows = with_layout_constraint(out_rows, rows_major)
    out_rows = (out_rows.astype(f32) + shared_part.astype(f32)).astype(bf16)
    out_quarter = lax.psum_scatter(out_rows, "hs", scatter_dimension=1, tiled=True)
    residual_quarter = lax.dynamic_slice_in_dim(residual, hs * quarter, quarter, 1)
    output = (residual_quarter + out_quarter.astype(f32)).astype(bf16)

    return (
        output,
        grad_tokens.T,
        grad_attn_gain,
        *[a.T for a in heads_sums],
        grad_ffn_gain,
        grad_router.T,
        shared_sums[0].T,
        shared_sums[1].T,
        shared_sums[2],
        grad_gate_t.swapaxes(1, 2),
        grad_up_t.swapaxes(1, 2),
        grad_expert_down,
    )


def solution(mesh):
    ep_count, hs_count = mesh.devices.shape
    cut = Mesh(mesh.devices.reshape(ep_count // 2, 2, hs_count), ("xy", "core", "hs"))
    return jax.shard_map(
        shards,
        mesh=cut,
        in_specs=(
            P(EP, None),
            P(),
            P(None, "hs"),
            P(None, "hs"),
            P(None, "hs"),
            P(None, "hs"),
            P(),
            P(),
            P(None, "hs"),
            P(None, "hs"),
            P("hs", None),
            P(EP, None, "hs"),
            P(EP, None, "hs"),
            P(EP, "hs", None),
            P(EP, None),
            P(EP, None),
            P(EP, "hs"),
        ),
        out_specs=(
            P(EP, "hs"),
            P(EP, "hs"),
            P(),
            P(None, "hs"),
            P(None, "hs"),
            P(None, "hs"),
            P(None, "hs"),
            P(),
            P(),
            P(None, "hs"),
            P(None, "hs"),
            P("hs", None),
            P(EP, None, "hs"),
            P(EP, None, "hs"),
            P(EP, "hs", None),
        ),
        check_vma=False,
    )
```

```python
import functools
import math

import jax
import jax.numpy as jnp
import numpy as np
from jax import lax
from jax.experimental import pallas as pl
from jax.experimental.layout import Layout, with_layout_constraint
from jax.experimental.pallas import tpu as pltpu
from jax.sharding import Mesh
from jax.sharding import PartitionSpec as P

HEADS = 10
HEAD_DIM = 128
CAP = 112
EPS = 1e-06
EP = ("xy", "core")
bf16 = jnp.bfloat16
f32 = jnp.float32


def dot(a, b):
    return jnp.dot(a, b, preferred_element_type=f32)


def ein(spec, a, b):
    return jnp.einsum(spec, a, b, preferred_element_type=f32)


def rope_tables(rows):
    half = HEAD_DIM // 2
    frequency = 10000.0 ** (-np.arange(half) * 2.0 / HEAD_DIM)
    angles = frequency[:, None] * np.arange(rows)[None, :]
    return jnp.asarray(np.cos(angles), f32), jnp.asarray(np.sin(angles), f32)


def rope(v, cosine, sine):
    half = HEAD_DIM // 2
    a, b = v[:, :half], v[:, half:]
    return jnp.concatenate([a * cosine - b * sine, b * cosine + a * sine], axis=1)


def rope_back(v, cosine, sine):
    half = HEAD_DIM // 2
    a, b = v[:, :half], v[:, half:]
    return jnp.concatenate([a * cosine + b * sine, b * cosine - a * sine], axis=1)


VMEM_LIMIT = 60 * 1024 * 1024
PAD = 256


def nn(a, b):
    return lax.dot_general(a, b, (((1,), (0,)), ((), ())), preferred_element_type=f32)


def nt(a, b):
    return lax.dot_general(a, b, (((1,), (1,)), ((), ())), preferred_element_type=f32)


def tn(a, b):
    return lax.dot_general(a, b, (((0,), (0,)), ((), ())), preferred_element_type=f32)


def takes(microseconds):
    return pl.CostEstimate(flops=0, transcendentals=0, bytes_accessed=microseconds * 3_000_000)


def slot_masks(slot_ref, at):
    local, rows = slot_ref.shape[-2:]
    number = lax.broadcasted_iota(jnp.int32, (CAP, rows), 0)
    return [slot_ref[at, e : e + 1, :] == number for e in range(local)]


def spread_kernel(weighted, *refs):
    if weighted:
        rows_ref, slot_ref, router_ref, x_ref, sw_ref, pick = refs
    else:
        rows_ref, slot_ref, x_ref, pick = refs
    local = slot_ref.shape[1]
    rows = rows_ref[...] if weighted else rows_ref[0]
    masks = slot_masks(slot_ref, 0)
    if weighted:
        logits = nt(router_ref[...], rows)
        raised = jnp.exp(logits - jnp.max(logits, axis=0, keepdims=True))
        gates = raised / jnp.sum(raised, axis=0, keepdims=True)
    for e in range(local):
        pick[e * CAP : (e + 1) * CAP, :] = masks[e].astype(f32).astype(bf16)
        if weighted:
            sw_ref[e] = jnp.sum(
                jnp.where(masks[e], gates[e : e + 1, :], 0.0), axis=1, keepdims=True
            )
    product = nn if weighted else nt
    x_ref[...] = product(pick[...], rows).astype(bf16).reshape(x_ref.shape)


def spread(all_rows, slot, router_t=None):
    s, local, rows = slot.shape
    weighted = router_t is not None
    if weighted:
        width = all_rows.shape[1]
        block = pl.BlockSpec((rows, width), lambda i: (i, 0))
    else:
        width = all_rows.shape[1]
        block = pl.BlockSpec((1, width, rows), lambda i: (i, 0, 0))
    in_specs = [
        block,
        pl.BlockSpec((1, local, rows), lambda i: (i, 0, 0)),
    ]
    out_specs = [pl.BlockSpec((1, local, CAP, width), lambda i: (i, 0, 0, 0))]
    out_shape = [jax.ShapeDtypeStruct((s, local, CAP, width), bf16)]
    args = [all_rows, slot]
    if weighted:
        in_specs.append(pl.BlockSpec(router_t.shape, lambda i: (0, 0)))
        out_specs.append(pl.BlockSpec((local, CAP, 1), lambda i: (0, i, 0)))
        out_shape.append(jax.ShapeDtypeStruct((local, s * CAP, 1), f32))
        args.append(router_t)
    out = pl.pallas_call(
        functools.partial(spread_kernel, weighted),
        grid=(s,),
        in_specs=in_specs,
        out_specs=out_specs,
        out_shape=out_shape,
        scratch_shapes=[pltpu.VMEM((local * CAP, rows), bf16)],
        compiler_params=pltpu.CompilerParams(vmem_limit_bytes=VMEM_LIMIT),
        cost_estimate=takes(17),
        name="spread",
    )(*args)
    return out if weighted else out[0]


def padded(ref, out):
    ff = ref.shape[1]
    out[:ff, :] = ref[0]
    out[ff:, :] = jnp.zeros((out.shape[0] - ff, out.shape[1]), out.dtype)


def experts_forward_kernel(
    x_ref, sw_ref, wg_ref, wu_ref, wd_ref, y_ref, gate_ref, up_ref, wg, wu, wd
):
    padded(wg_ref, wg)
    padded(wu_ref, wu)
    padded(wd_ref, wd)
    rows, width = gate_ref.shape[1], x_ref.shape[3]
    x = x_ref[...].reshape(rows, width)
    gate = nt(x, wg[...])
    up = nt(x, wu[...])
    gate_ref[0] = gate
    up_ref[0] = up
    act = gate / (1.0 + jnp.exp(-gate))
    hidden = (act * up).astype(bf16).astype(f32)
    hidden_w = (hidden * sw_ref[0]).astype(bf16)
    y_ref[...] = nn(hidden_w, wd[...]).astype(bf16).reshape(y_ref.shape)


def experts_backward_kernel(
    groups,
    x_ref,
    gx_ref,
    gate_ref,
    up_ref,
    sw_ref,
    wg_ref,
    wu_ref,
    wd_ref,
    dx_ref,
    dg_ref,
    du_ref,
    dd_ref,
    gsw_ref,
    wg,
    wu,
    wd,
):
    padded(wg_ref, wg)
    padded(wu_ref, wu)
    padded(wd_ref, wd)
    rows, width = gate_ref.shape[1], x_ref.shape[3]
    ff = wg_ref.shape[1]
    x = x_ref[...].reshape(rows, width)
    gx = gx_ref[...].reshape(rows, width)
    gate, up, sw = gate_ref[0], up_ref[0], sw_ref[0]
    sig = 1.0 / (1.0 + jnp.exp(-gate))
    act = gate * sig
    hidden = (act * up).astype(bf16).astype(f32)
    gh = nt(gx, wd[...])
    gsw_ref[0] = jnp.sum(gh * hidden, axis=-1, keepdims=True)
    gh = gh * sw
    gg = (gh * up * sig * (1.0 + gate * (1.0 - sig))).astype(bf16)
    gu = (gh * act).astype(bf16)
    sums = (
        (dd_ref, tn((hidden * sw).astype(bf16), gx)[:ff]),
        (dg_ref, tn(gg, x)[:ff]),
        (du_ref, tn(gu, x)[:ff]),
    )
    if groups == 1:
        for ref, value in sums:
            ref[0] = value
    else:

        @pl.when(pl.program_id(1) == 0)
        def _():
            for ref, value in sums:
                ref[0] = value

        @pl.when(pl.program_id(1) > 0)
        def _():
            for ref, value in sums:
                ref[0] += value

    dx_ref[...] = (nn(gg, wg[...]) + nn(gu, wu[...])).astype(bf16).reshape(dx_ref.shape)


def sending(remote_too, collective_id):
    if not remote_too:
        return pltpu.CompilerParams(vmem_limit_bytes=VMEM_LIMIT)
    return pltpu.CompilerParams(
        vmem_limit_bytes=VMEM_LIMIT, collective_id=collective_id, has_side_effects=True
    )


def expert_specs(s, width):
    group = min(s, 8)
    slots = pl.BlockSpec((group, 1, CAP, width), lambda i, j: (j, i, 0, 0))
    lines = lambda columns: pl.BlockSpec((1, group * CAP, columns), lambda i, j: (i, j, 0))
    per = lambda *shape: pl.BlockSpec((1, *shape), lambda i, j: (i, 0, 0))
    return s // group, slots, lines, per


def experts_forward_sending_kernel(
    x_ref,
    sw_ref,
    wg_ref,
    wu_ref,
    wd_ref,
    grad_ref,
    y_ref,
    gate_ref,
    up_ref,
    near_ref,
    wg,
    wu,
    wd,
    send,
    recv,
):
    chip, core, z, cx, cy, cd = places()
    peers = [(cx, core, z), (cy, core, z)]
    copies = [
        remote(grad_ref, near_ref.at[i], send.at[i], recv.at[i], peer) for i, peer in enumerate(peers)
    ]

    @pl.when(pl.program_id(0) == 0)
    def _():
        greet(peers)
        for copy in copies:
            copy.start()

    experts_forward_kernel(
        x_ref, sw_ref, wg_ref, wu_ref, wd_ref, y_ref, gate_ref, up_ref, wg, wu, wd
    )

    @pl.when(pl.program_id(0) == pl.num_programs(0) - 1)
    def _():
        for copy in copies:
            copy.wait()


def experts_forward(x, sw, wg, wu, wd, grad=None):
    s, local, cap, width = x.shape
    ff = wg.shape[1]
    rows = s * cap
    groups, slots, lines, per = expert_specs(s, width)
    middle = jax.ShapeDtypeStruct((local, rows, PAD), f32)
    kernel = experts_forward_kernel
    in_specs = [slots, lines(1)] + [per(ff, width)] * 3
    out_specs = [slots, lines(PAD), lines(PAD)]
    out_shape = [jax.ShapeDtypeStruct(x.shape, bf16), middle, middle]
    scratch = [pltpu.VMEM((PAD, width), bf16)] * 3
    args = [x, sw, wg, wu, wd]
    if grad is not None:
        kernel = experts_forward_sending_kernel
        in_specs.append(pl.BlockSpec(memory_space=pl.ANY))
        out_specs.append(pl.BlockSpec(memory_space=pl.ANY))
        out_shape.append(jax.ShapeDtypeStruct((2, *grad.shape), bf16))
        scratch += [pltpu.SemaphoreType.DMA((2,))] * 2
        args.append(grad)
    return pl.pallas_call(
        kernel,
        grid=(local, groups),
        in_specs=in_specs,
        out_specs=out_specs,
        out_shape=out_shape,
        scratch_shapes=scratch,
        compiler_params=sending(grad is not None, 4),
        cost_estimate=takes(31),
        name="experts_forward",
    )(*args)


def experts_backward(x, gx, gate, up, sw, wg, wu, wd):
    s, local, cap, width = x.shape
    ff = wg.shape[1]
    rows = s * cap
    groups, slots, lines, per = expert_specs(s, width)
    return pl.pallas_call(
        functools.partial(experts_backward_kernel, groups),
        grid=(local, groups),
        in_specs=[slots, slots, lines(PAD), lines(PAD), lines(1)]
        + [per(ff, width)] * 3,
        out_specs=[slots] + [per(ff, width)] * 3 + [lines(1)],
        out_shape=[jax.ShapeDtypeStruct(x.shape, bf16)]
        + [jax.ShapeDtypeStruct((local, ff, width), f32)] * 3
        + [jax.ShapeDtypeStruct((local, rows, 1), f32)],
        scratch_shapes=[pltpu.VMEM((PAD, width), bf16)] * 3,
        compiler_params=pltpu.CompilerParams(vmem_limit_bytes=VMEM_LIMIT),
        cost_estimate=takes(47),
        name="experts_backward",
    )(x, gx, gate, up, sw, wg, wu, wd)


def collect_kernel(y_ref, slot_ref, out_ref, pick):
    local = slot_ref.shape[1]
    masks = slot_masks(slot_ref, 0)
    for e in range(local):
        pick[e * CAP : (e + 1) * CAP, :] = masks[e].astype(f32).astype(bf16)
    out_ref[0] = tn(pick[...], y_ref[...].reshape(pick.shape[0], -1)).astype(bf16)


def collect_sending_kernel(
    y_ref, slot_ref, grad_ref, near_ref, out_ref, far_ref, given_ref, pick, send, recv, csend, crecv
):
    chip, core, z, cx, cy, cd = places()
    x_peer, y_peer, c_peer = (cx, core, z), (cy, core, z), (chip, 1 - core, z)
    half = grad_ref.shape[0] // 2
    top, low = pl.ds(0, half), pl.ds(half, half)
    relays = [
        remote(near_ref.at[0, top], far_ref.at[top], send.at[0], recv.at[0], y_peer),
        remote(near_ref.at[1, low], far_ref.at[low], send.at[1], recv.at[1], x_peer),
    ]
    passes = [
        remote(ref, given_ref.at[i], csend.at[i], crecv.at[i], c_peer)
        for i, ref in enumerate((grad_ref, near_ref.at[0], near_ref.at[1], far_ref))
    ]

    @pl.when(pl.program_id(0) == 0)
    def _():
        greet([x_peer, y_peer, c_peer])
        for copy in (*relays, *passes[:3]):
            copy.start()

    collect_kernel(y_ref, slot_ref, out_ref, pick)

    @pl.when(pl.program_id(0) == pl.num_programs(0) - 1)
    def _():
        for copy in relays:
            copy.wait_recv()
        passes[3].start()
        for copy in passes:
            copy.wait()
        for copy in relays:
            copy.wait_send()


def collect_back_kernel(experts, y_ref, slot_ref, gsw_ref, first_ref, out_ref, pick):
    local, rows = slot_ref.shape[1:]
    first = first_ref[0]
    masks = slot_masks(slot_ref, 0)
    number = lax.broadcasted_iota(jnp.int32, (experts, rows), 0)
    probs = jnp.zeros((experts, rows), f32)
    for e in range(local):
        pick[e * CAP : (e + 1) * CAP, :] = masks[e].astype(f32).astype(bf16)
        line = jnp.sum(jnp.where(masks[e], gsw_ref[e], 0.0), axis=0, keepdims=True)
        probs = jnp.where(number == first + e, line, probs)
    out_ref[0, :rows] = tn(pick[...], y_ref[...].reshape(pick.shape[0], -1)).astype(bf16)
    out_ref[0, rows:] = jnp.zeros((experts, out_ref.shape[2]), bf16)
    out_ref[0, rows:, :rows] = probs.astype(bf16)


def collect_sending(y, slot, grad, near):
    s, local, cap, width = y.shape
    rows = slot.shape[2]
    dma = pltpu.SemaphoreType.DMA
    whole = pl.BlockSpec(memory_space=pl.ANY)
    return pl.pallas_call(
        collect_sending_kernel,
        grid=(s,),
        in_specs=[
            pl.BlockSpec((1, local, cap, width), lambda i: (i, 0, 0, 0)),
            pl.BlockSpec((1, local, rows), lambda i: (i, 0, 0)),
            whole,
            whole,
        ],
        out_specs=[pl.BlockSpec((1, rows, width), lambda i: (i, 0, 0)), whole, whole],
        out_shape=[
            jax.ShapeDtypeStruct((s, rows, width), bf16),
            jax.ShapeDtypeStruct(grad.shape, bf16),
            jax.ShapeDtypeStruct((4, *grad.shape), bf16),
        ],
        scratch_shapes=[
            pltpu.VMEM((local * cap, rows), bf16),
            dma((2,)),
            dma((2,)),
            dma((4,)),
            dma((4,)),
        ],
        compiler_params=sending(True, 5),
        cost_estimate=takes(20),
        name="collect_sending",
    )(y, slot, grad, near)


def spread_grad_kernel(grad_ref, near_ref, far_ref, given_ref, slot_ref, x_ref, pick, gbuf, xbuf, come, gone):
    chip, core = lax.axis_index("xy"), lax.axis_index("core")
    local, rows = slot_ref.shape[1:]
    here = [grad_ref, near_ref.at[0], near_ref.at[1], far_ref]
    sources = [(here[t // 2], given_ref.at[t // 2])[t % 2] for t in range(8)]

    def in_copy(t):
        return pltpu.make_async_copy(sources[t], gbuf.at[t % 2], come.at[t % 2])

    def out_copy(t, src):
        return pltpu.make_async_copy(xbuf.at[t % 2], x_ref.at[src], gone.at[t % 2])

    number = lax.broadcasted_iota(jnp.int32, (CAP, rows), 0)
    in_copy(0).start()
    for t in range(8):
        if t < 7:
            in_copy(t + 1).start()
        x, y = (chip % 2 + (t // 2) % 2) % 2, (chip // 2 + t // 4) % 2
        src = (y * 2 + x) * 2 + (core + t % 2) % 2
        slots = slot_ref[src]
        for e in range(local):
            mask = slots[e : e + 1, :] == number
            pick[e * CAP : (e + 1) * CAP, :] = mask.astype(f32).astype(bf16)
        in_copy(t).wait()
        if t >= 2:
            out_copy(t, src).wait()
        xbuf[t % 2] = nt(pick[...], gbuf[t % 2]).astype(bf16).reshape(xbuf.shape[1:])
        out_copy(t, src).start()
    out_copy(0, 0).wait()
    out_copy(1, 0).wait()


def spread_grad(grad, near, far, given, slot):
    s, local, rows = slot.shape
    width = grad.shape[0]
    whole = pl.BlockSpec(memory_space=pl.ANY)
    dma = pltpu.SemaphoreType.DMA
    return pl.pallas_call(
        spread_grad_kernel,
        in_specs=[whole] * 4 + [pl.BlockSpec(memory_space=pltpu.VMEM)],
        out_specs=whole,
        out_shape=jax.ShapeDtypeStruct((s, local, CAP, width), bf16),
        scratch_shapes=[
            pltpu.VMEM((local * CAP, rows), bf16),
            pltpu.VMEM((2, width, rows), bf16),
            pltpu.VMEM((2, local, CAP, width), bf16),
            dma((2,)),
            dma((2,)),
        ],
        compiler_params=sending(False, 0),
        cost_estimate=takes(16),
        name="spread_grad",
    )(grad, near, far, given, slot)


def collect(y, slot, gsw=None, first=None, experts=0):
    s, local, cap, width = y.shape
    rows = slot.shape[2]
    in_specs = [
        pl.BlockSpec((1, local, cap, width), lambda i: (i, 0, 0, 0)),
        pl.BlockSpec((1, local, rows), lambda i: (i, 0, 0)),
    ]
    args = [y, slot]
    kernel = collect_kernel
    tall = rows
    if gsw is not None:
        in_specs += [
            pl.BlockSpec((local, cap, 1), lambda i: (0, i, 0)),
            pl.BlockSpec(memory_space=pltpu.SMEM),
        ]
        args += [gsw, first.reshape(1)]
        kernel = functools.partial(collect_back_kernel, experts)
        tall = rows + experts
    return pl.pallas_call(
        kernel,
        grid=(s,),
        in_specs=in_specs,
        out_specs=pl.BlockSpec((1, tall, width), lambda i: (i, 0, 0)),
        out_shape=jax.ShapeDtypeStruct((s, tall, width), bf16),
        scratch_shapes=[pltpu.VMEM((local * cap, rows), bf16)],
        compiler_params=pltpu.CompilerParams(vmem_limit_bytes=VMEM_LIMIT),
        cost_estimate=takes(17),
        name="collect",
    )(*args)


MESH = pl.DeviceIdType.MESH
EXTRA = 64
SUM_STARTS = (0, 192, 320, 448)


def places():
    chip, core, z = lax.axis_index("xy"), lax.axis_index("core"), lax.axis_index("hs")
    x, y = chip % 2, chip // 2
    return chip, core, z, y * 2 + (1 - x), (1 - y) * 2 + x, (1 - y) * 2 + (1 - x)


def greet(peers):
    barrier = pltpu.get_barrier_semaphore()
    for peer in peers:
        pl.semaphore_signal(barrier, inc=1, device_id=peer, device_id_type=MESH)
    pl.semaphore_wait(barrier, len(peers))


def remote(src, dst, send, recv, peer):
    return pltpu.make_async_remote_copy(
        src_ref=src, dst_ref=dst, send_sem=send, recv_sem=recv, device_id=peer, device_id_type=MESH
    )


def block(q, size):
    return pl.ds(pl.multiple_of(q * size, 16), size)


def weight_gather(out_ref, csend, crecv, send, recv):
    chip, core, z, cx, cy, cd = places()
    other = 1 - core
    c_peer = (chip, other, z)
    chips = (cx, cy, cd)
    count = out_ref.shape[0] // 2
    piece = count // 4

    def place(c, k):
        return pl.ds(pl.multiple_of(k * count + c * piece, 16), piece)

    def give(number, c, k, sems, peer):
        return remote(out_ref.at[place(c, k)], out_ref.at[place(c, k)], *sems(number), peer)

    def chip_sems(i):
        return send.at[3 + i], recv.at[3 + i]

    def core_sems(i):
        return csend.at[1 + i], crecv.at[1 + i]

    gather = [give(i, chip, core, chip_sems, (c, core, z)) for i, c in enumerate(chips)]
    over = [give(i, c, core, core_sems, c_peer) for i, c in enumerate((*chips, chip))]

    def put(done):
        out_ref[place(chip, core)] = done.astype(bf16)
        for i in (2, 0, 1):
            gather[i].start()
        over[3].start()

    def end():
        for i, c in enumerate(chips):
            give(i, c, core, chip_sems, (c, core, z)).wait_recv()
            over[i].start()
        for i, c in enumerate((*chips, chip)):
            give(i, c, other, core_sems, c_peer).wait_recv()
        for copy in (*gather, *over):
            copy.wait_send()

    return put, end


def weight_sum(grads, given, half, land, out_ref, csend, crecv, send, recv):
    chip, core, z, cx, cy, cd = places()
    other = 1 - core
    c_peer = (chip, other, z)
    chips = (cx, cy, cd)
    count = grads.shape[0] // 2
    piece = count // 4

    to_core = remote(grads.at[block(other, count)], given, csend.at[0], crecv.at[0], c_peer)
    scatter = [
        remote(half.at[block(c, piece)], land.at[i], send.at[i], recv.at[i], (c, core, z))
        for i, c in enumerate(chips)
    ]
    if out_ref is not None:
        put, gathered = weight_gather(out_ref, csend, crecv, send, recv)

    def share():
        to_core.wait_recv()
        half[...] = (grads[block(core, count)].astype(f32) + given[...].astype(f32)).astype(bf16)
        for i in (2, 0, 1):
            scatter[i].start()

    def total():
        done = half[block(chip, piece)].astype(f32)
        for i in range(3):
            scatter[i].wait_recv()
            done = done + land[i].astype(f32)
        return done

    def give_back():
        put(total())

    def end():
        if out_ref is not None:
            gathered()
        for copy in (to_core, *scatter):
            copy.wait_send()

    return to_core.start, share, give_back, end, total


def weight_sum_scratch(tall, width):
    dma = pltpu.SemaphoreType.DMA
    return [
        pltpu.VMEM((tall, width), bf16),
        pltpu.VMEM((tall // 2, width), bf16),
        pltpu.VMEM((tall // 2, width), bf16),
        pltpu.VMEM((3, tall // 8, width), bf16),
        dma((5,)),
        dma((5,)),
        dma((6,)),
        dma((6,)),
    ]


def gather_spread_kernel(
    own_ref,
    slots_ref,
    router_ref,
    grad_ref,
    x_ref,
    sw_ref,
    slot_ref,
    grad_all_ref,
    held,
    pick,
    xbuf,
    send,
    recv,
    copied,
    zsend,
    zrecv,
):
    chip, core, z, cx, cy, cd = places()
    other = 1 - core
    x_peer, y_peer, c_peer = (cx, core, z), (cy, core, z), (chip, other, z)
    tall = held.shape[1]
    half = tall // 2
    local, rows = slot_ref.shape[1:]
    me = chip * 2 + core
    top, low = pl.ds(0, half), pl.ds(half, half)

    def at(c, k):
        return c * 2 + k

    def move(number, src_slot, part, peer):
        return remote(
            held.at[src_slot, part], held.at[src_slot, part], send.at[number], recv.at[number], peer
        )

    whole = pl.ds(0, tall)
    z_peers = [(chip, core, (z + i) % 4) for i in (1, 2, 3)]
    greet([x_peer, y_peer, c_peer, *z_peers])
    quarter = grad_ref.shape[0]

    def grad_copy(i, q):
        return remote(
            grad_ref, grad_all_ref.at[block(q, quarter)], zsend.at[i], zrecv.at[i], z_peers[i]
        )

    held[me, :rows] = own_ref[...]
    packed = tall - rows
    held[me, rows:, 2 * rows :] = jnp.zeros((packed, own_ref.shape[1] - 2 * rows), bf16)
    held[me, rows:, :rows] = slots_ref[:packed]
    held[me, rows:, rows : 2 * rows] = slots_ref[packed:]
    x_top, x_low = move(0, me, top, x_peer), move(1, me, low, x_peer)
    y_low, y_top = move(2, me, low, y_peer), move(3, me, top, y_peer)
    to_core = move(4, me, whole, c_peer)
    relay_top, relay_low = move(5, at(cx, core), top, y_peer), move(6, at(cy, core), low, x_peer)
    pass_x, pass_y = move(7, at(cx, core), whole, c_peer), move(8, at(cy, core), whole, c_peer)
    pass_d = move(9, at(cd, core), whole, c_peer)
    for copy in (x_top, y_low, x_low, y_top, to_core, *[grad_copy(i, z) for i in (1, 0, 2)]):
        copy.start()
    grad_all_ref[block(z, quarter)] = grad_ref[...]

    def arrived(number, slot, part):
        move(number, slot, part, c_peer).wait_recv()

    number = lax.broadcasted_iota(jnp.int32, (CAP, rows), 0)
    first = me * local
    line = lax.broadcasted_iota(jnp.int32, (local, EXTRA), 0)
    column = lax.broadcasted_iota(jnp.int32, (local, EXTRA), 1)
    chosen = (column == line + first).astype(f32).astype(bf16)

    def out_copy(t, src):
        return pltpu.make_async_copy(xbuf.at[t % 2], x_ref.at[src], copied.at[t % 2])

    def step(t, carry):
        @pl.when(t == 1)
        def _():
            arrived(4, at(chip, other), whole)

        @pl.when(t == 2)
        def _():
            arrived(0, at(cx, core), top)
            relay_top.start()
            arrived(2, at(cy, core), low)
            relay_low.start()
            arrived(1, at(cx, core), low)
            pass_x.start()

        @pl.when(t == 3)
        def _():
            arrived(3, at(cy, core), top)
            pass_y.start()
            arrived(7, at(cx, other), whole)

        @pl.when(t == 5)
        def _():
            arrived(8, at(cy, other), whole)

        @pl.when(t == 6)
        def _():
            arrived(5, at(cd, core), top)
            arrived(6, at(cd, core), low)
            pass_d.start()

        @pl.when(t == 7)
        def _():
            arrived(9, at(cd, other), whole)

        x, y = (chip % 2 + (t // 2) % 2) % 2, (chip // 2 + t // 4) % 2
        src = (y * 2 + x) * 2 + (core + t % 2) % 2
        slots = nn(chosen[:, :packed], held[src, rows:, :rows])
        slots += nn(chosen[:, packed:], held[src, rows:, rows : 2 * rows])
        slots = slots.astype(jnp.int32)
        slot_ref[src] = slots
        logits = nt(router_ref[...], held[src, :rows])
        raised = jnp.exp(logits - jnp.max(logits, axis=0, keepdims=True))
        gates = raised / jnp.sum(raised, axis=0, keepdims=True)
        for e in range(local):
            mask = slots[e : e + 1, :] == number
            pick[e * CAP : (e + 1) * CAP, :] = mask.astype(f32).astype(bf16)
            sw_ref[e, pl.ds(pl.multiple_of(src * CAP, 8), CAP), :] = jnp.sum(
                jnp.where(mask, gates[e : e + 1, :], 0.0), axis=1, keepdims=True
            )

        @pl.when(t >= 2)
        def _():
            out_copy(t, src).wait()

        xbuf[t % 2] = nn(pick[...], held[src, :rows]).astype(bf16).reshape(xbuf.shape[1:])
        out_copy(t, src).start()
        return carry

    lax.fori_loop(0, 8, step, 0)
    out_copy(0, me).wait()
    out_copy(1, me).wait()
    for i in range(3):
        grad_copy(i, (z + 3 - i) % 4).wait_recv()
        grad_copy(i, z).wait_send()
    for copy in (x_top, x_low, y_low, y_top, to_core, relay_top, relay_low, pass_x, pass_y, pass_d):
        copy.wait_send()


def gather_spread(own, slots, router_t, grad_quarter, local, ep_count):
    rows, width = own.shape
    tall = rows + EXTRA // 2
    vmem = pl.BlockSpec(memory_space=pltpu.VMEM)
    return pl.pallas_call(
        gather_spread_kernel,
        in_specs=[vmem] * 4,
        out_specs=[pl.BlockSpec(memory_space=pl.ANY), vmem, vmem, vmem],
        out_shape=[
            jax.ShapeDtypeStruct((ep_count, local, CAP, width), bf16),
            jax.ShapeDtypeStruct((local, ep_count * CAP, 1), f32),
            jax.ShapeDtypeStruct((ep_count, local, rows), jnp.int32),
            jax.ShapeDtypeStruct((width, rows), bf16),
        ],
        scratch_shapes=[
            pltpu.VMEM((ep_count, tall, width), bf16),
            pltpu.VMEM((local * CAP, rows), bf16),
            pltpu.VMEM((2, local, CAP, width), bf16),
            pltpu.SemaphoreType.DMA((10,)),
            pltpu.SemaphoreType.DMA((10,)),
            pltpu.SemaphoreType.DMA((2,)),
            pltpu.SemaphoreType.DMA((3,)),
            pltpu.SemaphoreType.DMA((3,)),
        ],
        compiler_params=pltpu.CompilerParams(
            vmem_limit_bytes=VMEM_LIMIT, collective_id=0, has_side_effects=True
        ),
        cost_estimate=takes(62),
        name="gather_spread",
    )(own, slots, router_t, grad_quarter)


def front_kernel(
    x_ref,
    gain_ref,
    wq_ref,
    wk_ref,
    wv_ref,
    wo_ref,
    doc_ref,
    cos_ref,
    sin_ref,
    normed1_out,
    q_out,
    k_out,
    v_out,
    probs_out,
    attended_out,
    out_out,
    residual_ref,
    normed2_ref,
    normed1_ref,
    q_ref,
    k_ref,
    v_ref,
    probs_ref,
    attended_ref,
    out_ref,
    gone,
    shared,
    beside,
    esend,
    erecv,
    asend,
    arecv,
    zsend,
    zrecv,
    send,
    recv,
    csend,
    crecv,
):
    chip, core, z, cx, cy, cd = places()
    other = 1 - core
    odd = z % 2
    c_peer = (chip, other, z)
    chips = (cx, cy, cd)
    z_peers = [(chip, core, (z + i) % 4) for i in (1, 2, 3)]
    pair = (chip, core, z + 1 - 2 * odd)
    rows, width = x_ref.shape
    quarter = wq_ref.shape[0]
    whole = HEAD_DIM * (quarter // HEAD_DIM)
    spare = quarter - whole
    greet([c_peer, *[(c, core, z) for c in chips], *z_peers])

    full_rows = pl.ds(pl.multiple_of(odd * spare, 16), whole)
    half_rows = pl.ds(pl.multiple_of((1 - odd) * whole, 16), spare)
    for i, ref in enumerate((wq_ref, wk_ref, wv_ref)):
        shared[i * spare : (i + 1) * spare] = ref[half_rows]
    trade = remote(shared, beside, esend, erecv, pair)
    trade.start()

    share, lanes = quarter // 4, width // 2
    my_lanes = pl.ds(pl.multiple_of(core * lanes, 128), lanes)

    def piece(c):
        return pl.ds(pl.multiple_of(c * share, 16), share)

    out_z = [
        remote(
            wo_ref.at[piece(chip), my_lanes],
            out_ref.at[z, piece(chip), my_lanes],
            zsend.at[i],
            zrecv.at[i],
            peer,
        )
        for i, peer in enumerate(z_peers)
    ]
    for i in (1, 0, 2):
        out_z[i].start()
    behind = [(z + 3 - i) % 4 for i in range(3)]

    def out_chip(i, j, c):
        at = out_ref.at[behind[i], piece(c), my_lanes]
        return remote(at, at, send.at[3 * i + j], recv.at[3 * i + j], (chips[j], core, z))

    def out_core(i, k):
        half = pl.ds(pl.multiple_of(k * lanes, 128), lanes)
        at = out_ref.at[behind[i], :, half]
        return remote(at, at, csend.at[i], crecv.at[i], c_peer)

    x = x_ref[...].astype(f32)
    rms1 = lax.rsqrt(jnp.sum(x * x, axis=-1, keepdims=True) * (1.0 / width) + EPS)
    normed1_ref[...] = (x * rms1 * gain_ref[0:1]).astype(bf16)
    out_ref[z] = wo_ref[...]

    cosine, sine = cos_ref[...], sin_ref[...]
    half_dim = HEAD_DIM // 2
    scale = 1.0 / math.sqrt(HEAD_DIM)
    row = lax.broadcasted_iota(jnp.int32, (rows, rows), 0)
    column = lax.broadcasted_iota(jnp.int32, (rows, rows), 1)
    doc = jnp.broadcast_to(doc_ref[...].astype(f32), (rows, rows))
    allowed = (row >= column) & (doc == doc.T)

    kept = (normed1_ref, q_ref, k_ref, v_ref, probs_ref, attended_ref, out_ref)
    outs = (normed1_out, q_out, k_out, v_out, probs_out, attended_out, out_out)
    writes = [pltpu.make_async_copy(a, b, gone.at[i]) for i, (a, b) in enumerate(zip(kept, outs))]
    writes[0].start()

    def turn(pre):
        a, b = pre[:half_dim], pre[half_dim:]
        return (
            jnp.concatenate([a * cosine - b * sine, b * cosine + a * sine], axis=0).astype(bf16)
        )

    def attend(h):
        scores = jnp.where(allowed, tn(q_ref[h], k_ref[h]) * scale, -1e30)
        raised = jnp.exp(scores - jnp.max(scores, axis=-1, keepdims=True))
        probs = raised * (1.0 / jnp.sum(raised, axis=-1, keepdims=True))
        probs_ref[h] = probs
        return nt(v_ref[h], probs.astype(bf16)).astype(bf16)

    def project(at):
        return [nt(ref[at], normed1_ref[...]) for ref in (wq_ref, wk_ref, wv_ref)]

    q, k, v = project(full_rows)
    heads = whole // HEAD_DIM
    for h in range(heads):
        at = slice(h * HEAD_DIM, (h + 1) * HEAD_DIM)
        q_ref[h], k_ref[h], v_ref[h] = turn(q[at]), turn(k[at]), v[at].astype(bf16)

    def attended_copy(number, start, size):
        at = attended_ref.at[pl.ds(pl.multiple_of(start, 16), size)]
        return lambda i: remote(
            at, at, asend.at[number, i], arecv.at[number, i], z_peers[i]
        )

    mine = z * quarter
    copies = []
    for h in range(heads):
        start = mine + odd * spare + h * HEAD_DIM
        attended_ref[pl.ds(pl.multiple_of(start, 16), HEAD_DIM)] = attend(h)
        copy = attended_copy(h, start, HEAD_DIM)
        copies += [copy(1), copy(0), copy(2)]
        for one in copies[-3:]:
            one.start()
        if h == 0:
            for i in range(3):
                out_z[i].wait_recv()
                for j in (2, 0, 1):
                    out_chip(i, j, chip).start()

    trade.wait_recv()
    for i, (ref, to) in enumerate(((wq_ref, q_ref), (wk_ref, k_ref), (wv_ref, v_ref))):
        normed1 = normed1_ref[...]
        here = nt(ref[half_rows], normed1)
        there = nt(beside[i * spare : (i + 1) * spare], normed1)
        first = jnp.where(odd == 1, there, here)
        second = jnp.where(odd == 1, here, there)
        both = jnp.concatenate([first, second], axis=0)
        to[heads] = both.astype(bf16) if to is v_ref else turn(both)
    last = attend(heads)
    for i in (1, 2, 3, 4):
        writes[i].start()
    last = jnp.where(odd == 1, last[spare:], last[:spare])
    start = mine + (1 - odd) * whole
    attended_ref[pl.ds(pl.multiple_of(start, 16), spare)] = last
    copy = attended_copy(heads, start, spare)
    copies += [copy(1), copy(0), copy(2)]
    for one in copies[-3:]:
        one.start()

    for i in range(3):
        for j in range(3):
            out_chip(i, j, chips[j]).wait_recv()
        out_core(i, core).start()
    for i in range(3):
        from_z = (z + 3 - i) % 4
        from_odd = from_z % 2
        for h in range(heads):
            attended_copy(h, from_z * quarter + from_odd * spare + h * HEAD_DIM, HEAD_DIM)(i).wait_recv()
        attended_copy(heads, from_z * quarter + (1 - from_odd) * whole, spare)(i).wait_recv()
        out_core(i, other).wait_recv()
    writes[5].start()
    writes[6].start()
    attended = attended_ref[...].T
    residual = x_ref[...].astype(f32) + nt(attended, out_ref[...].reshape(width, width))
    residual_ref[...] = residual
    rms2 = lax.rsqrt(jnp.sum(residual * residual, axis=-1, keepdims=True) * (1.0 / width) + EPS)
    normed2_ref[...] = (residual * rms2 * gain_ref[1:2]).astype(bf16)
    for write in writes:
        write.wait()
    for one in (trade, *out_z, *copies):
        one.wait_send()
    for i in range(3):
        for j in range(3):
            out_chip(i, j, chip).wait_send()
        out_core(i, core).wait_send()


def front(x, gains, wq, wk, wv, wo, doc, tables):
    rows, width = x.shape
    quarter = wq.shape[0]
    heads = -(-quarter // HEAD_DIM)
    spare = quarter % HEAD_DIM
    vmem = pl.BlockSpec(memory_space=pltpu.VMEM)
    dma = pltpu.SemaphoreType.DMA
    low = lambda *shape: jax.ShapeDtypeStruct(shape, bf16)
    early = [
        low(rows, width),
        *[low(heads, HEAD_DIM, rows)] * 3,
        jax.ShapeDtypeStruct((heads, rows, rows), f32),
        low(width, rows),
        low(4, quarter, width),
    ]
    return pl.pallas_call(
        front_kernel,
        in_specs=[vmem] * 9,
        out_specs=[pl.BlockSpec(memory_space=pl.ANY)] * len(early) + [vmem] * 2,
        out_shape=[*early, jax.ShapeDtypeStruct((rows, width), f32), low(rows, width)],
        scratch_shapes=[
            *[pltpu.VMEM(a.shape, a.dtype) for a in early],
            dma((len(early),)),
            pltpu.VMEM((3 * spare, width), bf16),
            pltpu.VMEM((3 * spare, width), bf16),
            dma,
            dma,
            dma((heads, 3)),
            dma((heads, 3)),
            dma((3,)),
            dma((3,)),
            dma((9,)),
            dma((9,)),
            dma((3,)),
            dma((3,)),
        ],
        compiler_params=pltpu.CompilerParams(
            vmem_limit_bytes=VMEM_LIMIT, collective_id=1, has_side_effects=True
        ),
        cost_estimate=takes(50),
        name="front",
    )(x, gains, wq, wk, wv, wo, doc, *tables)


def collect_sum_kernel(
    y_ref,
    slot_ref,
    gsw_ref,
    normed_ref,
    grad_ref,
    gate_ref,
    up_ref,
    down_ref,
    out_ref,
    sum_ref,
    forward_ref,
    mine,
    pick,
    ybuf,
    stage,
    given,
    sums,
    relay,
    land,
    zland,
    copied,
    core_send,
    core_recv,
    send,
    recv,
    zsend,
    zrecv,
    grads,
    *more,
):
    chip, core, z, cx, cy, cd = places()
    other = 1 - core
    x_peer, y_peer, c_peer = (cx, core, z), (cy, core, z), (chip, other, z)
    z_peers = [(chip, core, (z + i) % 4) for i in (1, 2, 3)]
    local, rows = slot_ref.shape[1:]
    tall = out_ref.shape[0]
    me = chip * 2 + core
    number = lax.broadcasted_iota(jnp.int32, (CAP, rows), 0)
    row = lax.broadcasted_iota(jnp.int32, (EXTRA, rows), 0)

    greet([x_peer, y_peer, c_peer, (cd, core, z), *z_peers])

    def turn(t):
        theirs = (t % 2) * (1 - t // 7) + (7 - t) // 7
        return theirs * ((t + 1) // 2) + (1 - theirs) * (t // 2 - 1 + t // 7), theirs

    def sequence(t):
        p, theirs = turn(t)
        x, y = (chip % 2 + 1 + p // 2) % 2, (chip // 2 + 1 + p % 2) % 2
        return (y * 2 + x) * 2 + (core + theirs) % 2

    def in_copy(t):
        return pltpu.make_async_copy(y_ref.at[sequence(t)], ybuf.at[t % 2], copied.at[t % 2])

    def to_core(p):
        return remote(stage.at[p % 2], given.at[p], core_send.at[p], core_recv.at[p], c_peer)

    starts = (*SUM_STARTS, tall)
    units = len(starts) - 1
    sizes = [starts[u + 1] - starts[u] for u in range(units)]

    def top(u):
        return pl.ds(starts[u], sizes[u] // 2)

    def low(u):
        return pl.ds(starts[u] + sizes[u] // 2, sizes[u] // 2)

    def first(u, of):
        return pl.ds(0, sizes[u] // of)

    def over(u, number, src, dst, peer):
        return remote(src, dst, send.at[u, number], recv.at[u, number], peer)

    far_top = [over(u, 0, sums.at[0, top(u)], relay.at[u, 0, first(u, 2)], x_peer) for u in range(units)]
    far_low = [over(u, 1, sums.at[0, low(u)], relay.at[u, 1, first(u, 2)], y_peer) for u in range(units)]
    x_top = [over(u, 2, sums.at[1, top(u)], land.at[0, top(u)], x_peer) for u in range(units)]
    x_low = [over(u, 3, sums.at[1, low(u)], land.at[0, low(u)], x_peer) for u in range(units)]
    y_low = [over(u, 4, sums.at[2, low(u)], land.at[1, low(u)], y_peer) for u in range(units)]
    y_top = [over(u, 5, sums.at[2, top(u)], land.at[1, top(u)], y_peer) for u in range(units)]

    in_copy(0).start()
    start, share, _, end, total = weight_sum(grads, *more[:3], None, *more[3:])

    def shared_expert():
        normed, grad_t = normed_ref[...], grad_ref[...]
        size = gate_ref.shape[0]
        gate, up = nt(gate_ref[...], normed), nt(up_ref[...], normed)
        sig = 1.0 / (1.0 + jnp.exp(-gate))
        act = gate * sig
        hidden = (act * up).astype(bf16)
        forward_ref[...] = tn(hidden, down_ref[...]).astype(bf16)
        grad_hidden = nn(down_ref[...], grad_t)
        grad_gate = (grad_hidden * up * sig * (1.0 + gate * (1.0 - sig))).astype(bf16)
        grad_up = (grad_hidden * act).astype(bf16)
        grads[:size] = nn(grad_gate, normed).astype(bf16)
        grads[size : 2 * size] = nn(grad_up, normed).astype(bf16)
        grads[2 * size : 3 * size] = nt(hidden, grad_t).astype(bf16)
        grads[3 * size :] = jnp.zeros((grads.shape[0] - 3 * size, grads.shape[1]), bf16)
        start()
        mine[...] = (tn(grad_gate, gate_ref[...]) + tn(grad_up, up_ref[...])).astype(bf16)

    def step(t, carry):
        @pl.when(t < 7)
        def _():
            in_copy(t + 1).start()

        (p, theirs), s = turn(t), sequence(t)
        probs = jnp.zeros((EXTRA, rows), f32)
        for e in range(local):
            mask = slot_ref[s, e : e + 1, :] == number
            pick[e * CAP : (e + 1) * CAP, :] = mask.astype(f32).astype(bf16)
            column = gsw_ref[e, pl.ds(pl.multiple_of(s * CAP, 8), CAP), :]
            line = jnp.sum(jnp.where(mask, column, 0.0), axis=0, keepdims=True)
            probs = jnp.where(row == me * local + e, line, probs)
        in_copy(t).wait()
        back = tn(pick[...], ybuf[t % 2].reshape(local * CAP, -1))

        @pl.when(theirs == 1)
        def _():
            @pl.when(p >= 2)
            def _():
                to_core(p - 2).wait_send()

            stage[p % 2, :rows] = back.astype(bf16)
            stage[p % 2, rows:] = jnp.zeros((tall - rows, back.shape[1]), bf16)
            stage[p % 2, rows:, :rows] = probs.astype(bf16)
            to_core(p).start()

        @pl.when(theirs == 0)
        def _():
            to_core(p).wait_recv()
            sums[p, :rows] = (back + given[p, :rows].astype(f32)).astype(bf16)
            sums[p, rows:] = given[p, rows:]
            sums[p, rows:, :rows] = (probs + given[p, rows:, :rows].astype(f32)).astype(bf16)

        @pl.when(t == 2)
        def _():
            far_top[0].start()
            far_low[0].start()

        @pl.when(t == 4)
        def _():
            x_top[0].start()

        @pl.when(t == 6)
        def _():
            y_low[0].start()
            far_top[1].start()
            far_low[1].start()

        return carry

    lax.fori_loop(0, 8, step, 0)
    def relayed(u):
        far_low[u].wait_recv()
        at = low(u)
        sums[1, at] = (sums[1, at].astype(f32) + relay[u, 1, first(u, 2)].astype(f32)).astype(bf16)
        x_low[u].start()
        far_top[u].wait_recv()
        at = top(u)
        sums[2, at] = (sums[2, at].astype(f32) + relay[u, 0, first(u, 2)].astype(f32)).astype(bf16)
        y_top[u].start()

    def block_of(u, q):
        part = sizes[u] // 4
        return pl.ds(pl.multiple_of(starts[u] + q * part, 16), part)

    def z_sems(u, number):
        return zsend.at[u, number], zrecv.at[u, number]

    scatter = [
        [
            remote(
                sums.at[3, block_of(u, (z + i) % 4)],
                zland.at[u, i - 1, first(u, 4)],
                *z_sems(u, i - 1),
                z_peers[i - 1],
            )
            for i in (1, 2, 3)
        ]
        for u in range(units)
    ]

    def back_copy(u, q, i):
        at = out_ref.at[block_of(u, q)]
        return remote(at, at, *z_sems(u, 2 + i), z_peers[i - 1])

    def landed(u):
        for copy in (x_top[u], y_top[u], x_low[u], y_low[u]):
            copy.wait_recv()
        at = slice(starts[u], starts[u + 1])
        added = sums[3, at].astype(f32) + land[0, at].astype(f32) + land[1, at].astype(f32)
        ours = min(rows, starts[u + 1]) - starts[u]
        if ours == sizes[u]:
            sums[3, at] = (added + mine[at].astype(f32)).astype(bf16)
        else:
            here = slice(starts[u], starts[u] + ours)
            sums[3, here] = (added[:ours] + mine[here].astype(f32)).astype(bf16)
            sums[3, starts[u] + ours : starts[u + 1]] = added[ours:].astype(bf16)
        for i in (1, 0, 2):
            scatter[u][i].start()

    def summed(u):
        done = sums[3, block_of(u, z)].astype(f32)
        for i in range(3):
            scatter[u][i].wait_recv()
            done = done + zland[u, i, first(u, 4)].astype(f32)
        out_ref[block_of(u, z)] = done.astype(bf16)
        for i in (2, 1, 3):
            back_copy(u, z, i).start()

    for u in range(units):
        relayed(u)
        if u < units - 1:
            x_top[u + 1].start()
            y_low[u + 1].start()
        if u < units - 2:
            far_top[u + 2].start()
            far_low[u + 2].start()
        if u == 0:
            shared_expert()
        if u == units - 1:
            share()
        if u < units - 1:
            landed(u)
        if 1 <= u < units - 1:
            summed(u - 1)
    landed(units - 1)
    summed(units - 2)
    sum_ref[...] = total().astype(bf16)
    end()
    summed(units - 1)
    for u in range(units):
        for i in (1, 2, 3):
            back_copy(u, (z + 4 - i) % 4, i).wait_recv()
    for u in range(units):
        for copy in (far_top[u], far_low[u], x_top[u], x_low[u], y_low[u], y_top[u], *scatter[u]):
            copy.wait_send()
        for i in (1, 2, 3):
            back_copy(u, z, i).wait_send()
    for p in (2, 3):
        to_core(p).wait_send()


def collect_sum(y, slot, gsw, normed, grad_t, *shared):
    s, local, cap, width = y.shape
    rows = slot.shape[2]
    tall = rows + EXTRA
    dma = pltpu.SemaphoreType.DMA
    units = len(SUM_STARTS)
    most = max(b - a for a, b in zip(SUM_STARTS, (*SUM_STARTS[1:], tall)))
    weights = 128 * (-(-sum(a.shape[0] for a in shared) // 128))
    vmem = pl.BlockSpec(memory_space=pltpu.VMEM)
    return pl.pallas_call(
        collect_sum_kernel,
        in_specs=[pl.BlockSpec(memory_space=pl.ANY)] + [vmem] * 7,
        out_specs=[vmem, vmem, vmem],
        out_shape=[
            jax.ShapeDtypeStruct((tall, width), bf16),
            jax.ShapeDtypeStruct((weights // 8, width), bf16),
            jax.ShapeDtypeStruct((rows, width), bf16),
        ],
        scratch_shapes=[
            pltpu.VMEM((rows, width), bf16),
            pltpu.VMEM((local * cap, rows), bf16),
            pltpu.VMEM((2, local, cap, width), bf16),
            pltpu.VMEM((2, tall, width), bf16),
            pltpu.VMEM((4, tall, width), bf16),
            pltpu.VMEM((4, tall, width), bf16),
            pltpu.VMEM((units, 2, most // 2, width), bf16),
            pltpu.VMEM((2, tall, width), bf16),
            pltpu.VMEM((units, 3, most // 4, width), bf16),
            dma((2,)),
            dma((4,)),
            dma((4,)),
            dma((units, 6)),
            dma((units, 6)),
            dma((units, 6)),
            dma((units, 6)),
            *weight_sum_scratch(weights, width),
        ],
        compiler_params=pltpu.CompilerParams(
            vmem_limit_bytes=VMEM_LIMIT, collective_id=2, has_side_effects=True
        ),
        cost_estimate=takes(131),
        name="collect_sum",
    )(y, slot, gsw, normed, grad_t, *shared)


def back_kernel(
    sums_ref,
    residual_ref,
    normed2_ref,
    grad_ref,
    router_ref,
    gain_ref,
    cos_ref,
    sin_ref,
    piece_ref,
    *refs,
):
    late, outs, rest = refs[:11], refs[11:17], refs[17:]
    held, sems, rest = rest[:11], rest[11], rest[12:]
    loads = [pltpu.make_async_copy(a, b, sems.at[i]) for i, (a, b) in enumerate(zip(late, held))]
    for load in loads:
        load.start()
    back_steps(
        loads,
        sums_ref,
        residual_ref,
        normed2_ref,
        grad_ref,
        router_ref,
        gain_ref,
        cos_ref,
        sin_ref,
        piece_ref,
        *held,
        *outs,
        *rest,
    )


def back_steps(
    loads,
    sums_ref,
    residual_ref,
    normed2_ref,
    grad_ref,
    router_ref,
    gain_ref,
    cos_ref,
    sin_ref,
    piece_ref,
    out_ref,
    q_ref,
    k_ref,
    v_ref,
    probs_ref,
    wq_ref,
    wk_ref,
    wv_ref,
    attended_ref,
    x_ref,
    normed_ref,
    tokens_ref,
    early_ref,
    first_ref,
    second_ref,
    shared_ref,
    shared_sum_ref,
    dq_ref,
    dk_ref,
    dv_ref,
    x_t,
    gain_column,
    back_t,
    low_t,
    part,
    low_part,
    zland,
    mine,
    theirs,
    zsend,
    zrecv,
    lsend,
    lrecv,
    *more,
):
    chip, core, z, cx, cy, cd = places()
    odd = z % 2
    c_peer = (chip, 1 - core, z)
    z_peers = [(chip, core, (z + i) % 4) for i in (1, 2, 3)]
    quarter, width = wq_ref.shape
    rows = x_ref.shape[0]
    groups = [
        weight_sum(*more[8 * i : 8 * i + 4], ref, *more[8 * i + 4 : 8 * i + 8])
        for i, ref in enumerate((early_ref, first_ref, second_ref, shared_ref))
    ]
    early, *by_head = [more[8 * i] for i in range(4)]
    START, SHARE, GIVE_BACK, END = range(4)
    experts = router_ref.shape[0]
    whole = HEAD_DIM * (quarter // HEAD_DIM)
    spare = quarter - whole
    heads = whole // HEAD_DIM
    greet([c_peer, *[(c, core, z) for c in (cx, cy, cd)], *z_peers])
    put, gathered = weight_gather(shared_sum_ref, *more[32:])
    put(piece_ref[...])

    logits = nt(router_ref[...], normed2_ref[...])
    raised = jnp.exp(logits - jnp.max(logits, axis=0, keepdims=True))
    gates = raised / jnp.sum(raised, axis=0, keepdims=True)
    grad_probs = sums_ref[rows:, :rows].astype(f32)
    grad_logits = gates * (grad_probs - jnp.sum(grad_probs * gates, axis=0, keepdims=True))
    grad_logits = grad_logits.astype(bf16)
    grad_router = nn(grad_logits, normed2_ref[...])
    grad_normed2 = sums_ref[:rows].astype(f32) + tn(grad_logits, router_ref[...])
    residual = residual_ref[...]
    rms2 = lax.rsqrt(jnp.sum(residual * residual, axis=-1, keepdims=True) * (1.0 / width) + EPS)
    grad_ffn = jnp.sum(grad_normed2 * residual * rms2, axis=0, keepdims=True)
    u = grad_normed2 * gain_ref[1:2]
    mean2 = jnp.sum(u * residual, axis=-1, keepdims=True) * (1.0 / width)
    added = rms2 * u - residual * (rms2 * rms2 * rms2 * mean2)
    back_t[...] = added.T + grad_ref[...].astype(f32)
    low_t[...] = back_t[...].astype(bf16)
    own = block(z, quarter)

    cosine, sine = cos_ref[...], sin_ref[...]
    half_dim = HEAD_DIM // 2
    scale = 1.0 / math.sqrt(HEAD_DIM)

    def turn_back(v):
        a, b = v[:half_dim] * scale, v[half_dim:] * scale
        turned = [a * cosine + b * sine, b * cosine - a * sine]
        return jnp.concatenate(turned, axis=0).astype(bf16)

    for i in range(5):
        loads[i].wait()
    first_lane = z * quarter + odd * spare
    shared_lane = z * quarter + (1 - odd) * whole - odd * spare
    for h in range(heads + 1):
        lane = first_lane + h * HEAD_DIM if h < heads else shared_lane
        lane = pl.ds(pl.multiple_of(lane, HEAD_DIM), HEAD_DIM)
        grad_attended = tn(out_ref[:, lane], low_t[...]).astype(bf16)
        probs = probs_ref[h]
        grad_p = tn(grad_attended, v_ref[h])
        grad_v = nn(grad_attended, probs.astype(bf16)).astype(bf16)
        delta = jnp.sum(probs * grad_p, axis=-1, keepdims=True)
        grad_s = (probs * (grad_p - delta)).astype(bf16)
        grad_q = turn_back(nt(k_ref[h], grad_s))
        grad_k = turn_back(nn(q_ref[h], grad_s))
        for ref, value in ((dq_ref, grad_q), (dk_ref, grad_k), (dv_ref, grad_v)):
            if h < heads:
                at = pl.ds(pl.multiple_of(odd * spare + h * HEAD_DIM, 16), HEAD_DIM)
                ref[at] = value
            else:
                at = pl.ds(pl.multiple_of((1 - odd) * whole, 16), spare)
                ref[at] = jnp.where(odd == 1, value[spare:], value[:spare])

    for i in (5, 6, 7):
        loads[i].wait()
    part[...] = tn(wq_ref[...], dq_ref[...])
    part[...] += tn(wk_ref[...], dk_ref[...])
    part[...] += tn(wv_ref[...], dv_ref[...])
    low_part[...] = part[...].astype(bf16)
    to_z = [
        remote(
            low_part.at[block((z + i) % 4, quarter)],
            zland.at[i - 1],
            zsend.at[i - 1],
            zrecv.at[i - 1],
            z_peers[i - 1],
        )
        for i in (1, 2, 3)
    ]
    few_to_z = [
        remote(mine, theirs.at[i], lsend.at[i], lrecv.at[i], peer) for i, peer in enumerate(z_peers)
    ]
    loads[9].wait()
    x_t[...] = x_ref[...].T
    gain_column[...] = jnp.broadcast_to(gain_ref[0:1], (8, width)).T
    x_all = x_t[...].astype(f32)
    rms1 = lax.rsqrt(jnp.sum(x_all * x_all, axis=0, keepdims=True) * (1.0 / width) + EPS)
    along = part[...] * x_all
    mine[...] = jnp.zeros(mine.shape, f32)
    mine[0:1, :rows] = jnp.sum(along * gain_column[:, 0:1], axis=0, keepdims=True)
    mine[:, rows:] = nt(jnp.ones((8, rows), bf16), (along * rms1).astype(bf16))
    for copy in few_to_z:
        copy.start()
    for i in (1, 0, 2):
        to_z[i].start()

    loads[8].wait()
    loads[10].wait()
    early[:quarter] = nt(low_t[own], attended_ref[...]).astype(bf16)
    early[quarter:] = grad_router.astype(bf16)
    groups[0][START]()
    normed = normed_ref[...]
    for h in range(heads + 1):
        if h < heads:
            size, at = HEAD_DIM, odd * spare + h * HEAD_DIM
        else:
            size, at = spare, (1 - odd) * whole
        at = pl.ds(pl.multiple_of(at, 16), size)
        for i, ref in enumerate((dq_ref, dk_ref, dv_ref)):
            by_head[h][i * size : (i + 1) * size] = nn(ref[at], normed).astype(bf16)
        if h < heads:
            groups[1 + h][START]()
            groups[h][SHARE]()
    at = 3 * spare
    late = by_head[heads]
    for copy in few_to_z:
        copy.wait_recv()
    few = mine[...] + theirs[0] + theirs[1] + theirs[2]
    late[at:] = jnp.zeros((late.shape[0] - at, width), bf16)
    line = lax.broadcasted_iota(jnp.int32, (16, width), 0)
    gains = jnp.where(line == 0, few[0:1, rows:], jnp.where(line == 1, grad_ffn, 0.0))
    late[at : at + 16] = gains.astype(bf16)
    groups[3][START]()
    groups[2][SHARE]()
    groups[0][GIVE_BACK]()
    groups[3][SHARE]()
    groups[1][GIVE_BACK]()

    total = part[own]
    for i in range(3):
        to_z[i].wait_recv()
        total = total + zland[i].astype(f32)
    x = x_t[own].astype(f32)
    mean = few[0:1, :rows] * (1.0 / width)
    tokens_ref[...] = back_t[own] + rms1 * gain_column[own, 0:1] * total - x * (rms1 * rms1 * rms1 * mean)

    groups[2][GIVE_BACK]()
    groups[3][GIVE_BACK]()
    gathered()
    for group in groups:
        group[END]()
    for copy in (*to_z, *few_to_z):
        copy.wait_send()


def back(now, late):
    quarter, width = late[5].shape
    rows = now[1].shape[0]
    spare = quarter % HEAD_DIM
    tall = [quarter + now[4].shape[0], 3 * HEAD_DIM, 3 * HEAD_DIM, 3 * spare + 64]
    shared = 8 * now[8].shape[0]
    vmem = pl.BlockSpec(memory_space=pltpu.VMEM)
    dma = pltpu.SemaphoreType.DMA
    return pl.pallas_call(
        back_kernel,
        in_specs=[vmem] * len(now) + [pl.BlockSpec(memory_space=pl.ANY)] * len(late),
        out_specs=[vmem] * 6,
        out_shape=[
            jax.ShapeDtypeStruct((quarter, rows), f32),
            *[jax.ShapeDtypeStruct((lines, width), bf16) for lines in (*tall, shared)],
        ],
        scratch_shapes=[
            *[pltpu.VMEM(a.shape, a.dtype) for a in late],
            dma((len(late),)),
            *[pltpu.VMEM((quarter, rows), bf16)] * 3,
            pltpu.VMEM((width, rows), bf16),
            pltpu.VMEM((width, 8), f32),
            pltpu.VMEM((width, rows), f32),
            pltpu.VMEM((width, rows), bf16),
            pltpu.VMEM((width, rows), f32),
            pltpu.VMEM((width, rows), bf16),
            pltpu.VMEM((3, quarter, rows), bf16),
            pltpu.VMEM((8, rows + width), f32),
            pltpu.VMEM((3, 8, rows + width), f32),
            dma((3,)),
            dma((3,)),
            dma((3,)),
            dma((3,)),
            *[one for lines in tall for one in weight_sum_scratch(lines, width)],
            dma((5,)),
            dma((5,)),
            dma((6,)),
            dma((6,)),
        ],
        compiler_params=pltpu.CompilerParams(
            vmem_limit_bytes=VMEM_LIMIT, collective_id=3, has_side_effects=True
        ),
        cost_estimate=takes(90),
        name="back",
    )(*now, *late)


def widen_kernel(early_ref, first_ref, second_ref, last_ref, shared_ref, *out_refs):
    quarter = out_refs[0].shape[0]
    odd = lax.axis_index("hs") % 2
    whole = HEAD_DIM * (quarter // HEAD_DIM)
    spare = quarter - whole
    for i in range(3):
        for h, ref in enumerate((first_ref, second_ref)):
            at = pl.ds(pl.multiple_of(odd * spare + h * HEAD_DIM, 8), HEAD_DIM)
            out_refs[i][at] = ref[i * HEAD_DIM : (i + 1) * HEAD_DIM].astype(f32)
        at = pl.ds(pl.multiple_of((1 - odd) * whole, 8), spare)
        out_refs[i][at] = last_ref[i * spare : (i + 1) * spare].astype(f32)
    out_refs[3][...] = early_ref[:quarter].astype(f32)
    out_refs[4][...] = early_ref[quarter:].astype(f32)
    out_refs[5][...] = last_ref[3 * spare : 3 * spare + 16].astype(f32)
    size = out_refs[6].shape[0]
    for i in range(3):
        out_refs[6 + i][...] = shared_ref[i * size : (i + 1) * size].astype(f32)


def widen(sums, quarter, hidden_units):
    width = sums[0].shape[1]
    step = width // 5
    tall = [quarter] * 4 + [sums[0].shape[0] - quarter, 16] + [hidden_units] * 3
    blocks = lambda lines: pl.BlockSpec((lines, step), lambda i: (0, i))
    return pl.pallas_call(
        widen_kernel,
        grid=(width // step,),
        in_specs=[blocks(a.shape[0]) for a in sums],
        out_specs=[blocks(lines) for lines in tall],
        out_shape=[jax.ShapeDtypeStruct((lines, width), f32) for lines in tall],
        compiler_params=pltpu.CompilerParams(vmem_limit_bytes=VMEM_LIMIT),
        cost_estimate=takes(8),
        name="widen",
    )(*sums)


def plain_front(
    tokens, attn_gain, query_t, key_t, value_t, attn_out, ffn_gain, documents, tables
):
    rows, width = tokens.shape
    quarter = query_t.shape[0]
    hs, hs_count = lax.axis_index("hs"), lax.axis_size("hs")
    odd = (hs % 2) == 1
    spare = -quarter % HEAD_DIM
    heads = (quarter + spare) // HEAD_DIM

    def outer(w):
        return jnp.where(odd, w[:spare], w[quarter - spare :])

    sent = jnp.concatenate([outer(query_t), outer(key_t), outer(value_t)], axis=0)
    got = lax.ppermute(sent, "hs", [(i, i ^ 1) for i in range(hs_count)])

    def widened(w, extra):
        return jnp.where(
            odd, jnp.concatenate([extra, w], axis=0), jnp.concatenate([w, extra], axis=0)
        )

    x = tokens.astype(f32)
    rms1 = lax.rsqrt(jnp.mean(x * x, axis=-1, keepdims=True) + EPS)
    normed1 = (x * rms1 * attn_gain).astype(bf16)
    shape3 = (heads, HEAD_DIM, rows)
    q, k, v = [
        ein("cd,td->ct", widened(w, got[i * spare : (i + 1) * spare]), normed1).reshape(shape3)
        for i, w in enumerate((query_t, key_t, value_t))
    ]
    q, k, v = rope(q, *tables).astype(bf16), rope(k, *tables).astype(bf16), v.astype(bf16)
    positions = jnp.arange(rows, dtype=jnp.int32)
    doc = documents[0]
    allowed = (positions[:, None] >= positions[None, :]) & (doc[:, None] == doc[None, :])
    scale = 1.0 / math.sqrt(HEAD_DIM)
    scores = jnp.where(allowed[None], ein("hdq,hdk->hqk", q, k) * scale, -1e30)
    raised = jnp.exp(scores - jnp.max(scores, axis=-1, keepdims=True))
    probs = raised / jnp.sum(raised, axis=-1, keepdims=True)
    attended = ein("hdk,hqk->hdq", v, probs.astype(bf16)).astype(bf16).reshape(-1, rows)
    attended = jnp.where(odd, attended[spare:], attended[:quarter])
    attended_t = lax.all_gather(attended, "hs", axis=0, tiled=True)
    out_t = lax.all_gather(attn_out.T, "hs", axis=0, tiled=True)
    residual = x + ein("ct,oc->to", attended_t, out_t)
    rms2 = lax.rsqrt(jnp.mean(residual * residual, axis=-1, keepdims=True) + EPS)
    normed2 = (residual * rms2 * ffn_gain).astype(bf16)
    return normed1, q, k, v, probs, attended_t, out_t, residual, normed2


def over_ep(a):
    return lax.psum(a.astype(bf16), EP).astype(f32)


def plain_back(
    sums,
    residual,
    normed2,
    grad_t,
    router_t,
    ffn_gain,
    out_t,
    q,
    k,
    v,
    probs,
    tables,
    query_t,
    key_t,
    value_t,
    normed1,
    attended_t,
    tokens,
    attn_gain,
):
    rows, width = tokens.shape
    quarter = query_t.shape[0]
    hs = lax.axis_index("hs")
    odd = (hs % 2) == 1
    spare = -quarter % HEAD_DIM
    held = quarter + spare
    col0 = hs * quarter

    def own(v):
        v = v.astype(bf16).reshape(held, rows)
        return jnp.where(odd, v[spare:], v[:quarter])

    gates = jax.nn.softmax(nt(normed2, router_t), axis=-1)
    grad_probs = sums[rows:, :rows].T.astype(f32)
    grad_logits = (
        gates * (grad_probs - jnp.sum(grad_probs * gates, axis=-1, keepdims=True))
    ).astype(bf16)
    grad_router = tn(grad_logits, normed2)
    grad_normed2 = sums[:rows].astype(f32) + dot(grad_logits, router_t)
    rms2 = lax.rsqrt(jnp.mean(residual * residual, axis=-1, keepdims=True) + EPS)
    grad_ffn_gain = jnp.sum(grad_normed2 * residual * rms2, axis=0)
    u = grad_normed2 * ffn_gain
    grad_residual = (
        grad_t.T.astype(f32)
        + rms2 * u
        - residual * rms2**3 * jnp.mean(u * residual, axis=-1, keepdims=True)
    )
    back_t = grad_residual.T
    low_t = back_t.astype(bf16)
    out_held = lax.dynamic_slice_in_dim(out_t, jnp.where(odd, col0 - spare, col0), held, 1)
    grad_attended = tn(out_held, low_t).astype(bf16).reshape(-1, HEAD_DIM, rows)
    grad_p = ein("hdq,hdk->hqk", grad_attended, v)
    grad_v = own(ein("hdq,hqk->hdk", grad_attended, probs.astype(bf16)))
    grad_s = (probs * (grad_p - jnp.sum(probs * grad_p, axis=-1, keepdims=True))).astype(bf16)
    scale = 1.0 / math.sqrt(HEAD_DIM)
    grad_q = own(rope_back(ein("hdk,hqk->hdq", k, grad_s) * scale, *tables))
    grad_k = own(rope_back(ein("hdq,hqk->hdk", q, grad_s) * scale, *tables))
    own_rows = lambda a: lax.dynamic_slice_in_dim(a, col0, quarter, 0)
    heads_sums = [
        over_ep(dot(grad_q, normed1)),
        over_ep(dot(grad_k, normed1)),
        over_ep(dot(grad_v, normed1)),
        over_ep(nt(own_rows(low_t), attended_t)),
    ]
    part = tn(query_t, grad_q) + tn(key_t, grad_k) + tn(value_t, grad_v)
    grad_n1 = lax.psum_scatter(part.astype(bf16), "hs", scatter_dimension=0, tiled=True)
    grad_n1 = grad_n1.astype(f32)
    x = tokens.T.astype(f32)
    x_own = own_rows(x)
    rms_t = lax.rsqrt(jnp.mean(x * x, axis=0, keepdims=True) + EPS)
    w1 = grad_n1 * own_rows(attn_gain)[:, None]
    mean1 = lax.psum(jnp.sum(w1 * x_own, axis=0, keepdims=True), "hs") / width
    grad_tokens = own_rows(back_t) + rms_t * w1 - x_own * rms_t**3 * mean1
    gain_own = jnp.sum(grad_n1 * x_own * rms_t, axis=1)
    gain_part = lax.dynamic_update_slice_in_dim(jnp.zeros((width,), f32), gain_own, col0, 0)
    grad_attn_gain = lax.psum(gain_part, (*EP, "hs"))
    return (
        grad_tokens,
        heads_sums,
        over_ep(grad_router),
        grad_attn_gain,
        lax.psum(grad_ffn_gain, EP),
    )


def shards(
    tokens,
    attn_gain,
    attn_query,
    attn_key,
    attn_value,
    attn_out,
    ffn_gain,
    router,
    shared_gate,
    shared_up,
    shared_down,
    expert_gate,
    expert_up,
    expert_down,
    routes,
    documents,
    out_grad,
):
    rows, width = tokens.shape
    quarter = out_grad.shape[1]
    hs = lax.axis_index("hs")
    ep_count = lax.axis_size("xy") * lax.axis_size("core")
    ep = lax.axis_index("xy") * lax.axis_size("core") + lax.axis_index("core")
    local = expert_gate.shape[0]
    experts = router.shape[1]
    small = ep_count == 8 and lax.axis_size("hs") == 4

    query_t, key_t, value_t, router_t = attn_query.T, attn_key.T, attn_value.T, router.T
    positions = jnp.arange(rows, dtype=jnp.int32)
    below = (positions[:, None] > positions[None, :]).astype(bf16)
    chosen = jnp.any(
        routes[:, :, None] == jnp.arange(experts, dtype=jnp.int32)[None, None, :], axis=1
    )
    own_slots = jnp.where(chosen, dot(below, chosen.astype(bf16)), -1.0).T.astype(bf16)
    tables = rope_tables(rows)

    if small:
        both_gains = jnp.stack([attn_gain, ffn_gain])
        ahead = front(
            tokens, both_gains, query_t, key_t, value_t, attn_out.T, documents, tables
        )
    else:
        ahead = plain_front(
            tokens, attn_gain, query_t, key_t, value_t, attn_out, ffn_gain, documents, tables
        )
    normed1, q, k, v, probs, attended_t, out_t, residual, normed2 = ahead
    out_t = out_t.reshape(width, width)

    first = ep * local
    rolled = jnp.roll(router_t, -first, axis=0)
    gate_t, up_t = expert_gate.swapaxes(1, 2), expert_up.swapaxes(1, 2)
    weights = gate_t, up_t, expert_down
    if small:
        ex_in, slot_weight, slot, grad_t = gather_spread(
            normed2, own_slots, rolled, out_grad.T, local, ep_count
        )
        ex_out, ex_gate, ex_up, near = experts_forward(ex_in, slot_weight, *weights, grad_t)
        out_part, far, given = collect_sending(ex_out, slot, grad_t, near)
        ex_grad = spread_grad(grad_t, near, far, given, slot)
    else:
        grad_all_t = lax.all_gather(out_grad.T, (*EP, "hs"), axis=0, tiled=True)
        grad_all_t = grad_all_t.reshape(ep_count, width, rows)
        grad_t = lax.dynamic_index_in_dim(grad_all_t, ep, 0, keepdims=False)
        slot = lax.dynamic_slice_in_dim(
            lax.all_gather(own_slots, EP, axis=0), first, local, 1
        ).astype(jnp.int32)
        normed_all = lax.all_gather(normed2, EP, axis=0, tiled=True)
        ex_in, slot_weight = spread(normed_all, slot, rolled)
        ex_out, ex_gate, ex_up = experts_forward(ex_in, slot_weight, *weights)
        out_part = collect(ex_out, slot)
        ex_grad = spread(grad_all_t, slot)
    out_part = out_part.reshape(ep_count * rows, width)
    ex_back, grad_gate_t, grad_up_t, grad_expert_down, grad_slot_weight = experts_backward(
        ex_in, ex_grad, ex_gate, ex_up, slot_weight, *weights
    )

    if small:
        back_sums, shared_piece, shared_part = collect_sum(
            ex_back, slot, grad_slot_weight, normed2, grad_t, shared_gate.T, shared_up.T, shared_down
        )
        grad_tokens, *sums = back(
            (back_sums, residual, normed2, grad_t, router_t, both_gains, *tables, shared_piece),
            (out_t, q, k, v, probs, query_t, key_t, value_t, attended_t, tokens, normed1),
        )
        *heads_sums, grad_router, gains, sum_gate, sum_up, sum_down = widen(
            sums, quarter, shared_down.shape[0]
        )
        shared_sums = sum_gate, sum_up, sum_down
        grad_attn_gain, grad_ffn_gain = gains[0], gains[1]
    else:
        sh_gate = dot(normed2, shared_gate)
        sh_up = dot(normed2, shared_up)
        sh_sig = jax.nn.sigmoid(sh_gate)
        sh_act = sh_gate * sh_sig
        sh_hidden = (sh_act * sh_up).astype(bf16)
        shared_part = dot(sh_hidden, shared_down)
        grad_sh = ein("dt,fd->tf", grad_t, shared_down)
        grad_sh_gate = (grad_sh * sh_up * sh_sig * (1 + sh_gate * (1 - sh_sig))).astype(bf16)
        grad_sh_up = (grad_sh * sh_act).astype(bf16)
        shared_grads = [
            ein("tf,td->fd", grad_sh_gate, normed2).astype(bf16),
            ein("tf,td->fd", grad_sh_up, normed2).astype(bf16),
            ein("tf,dt->fd", sh_hidden, grad_t).astype(bf16),
        ]
        shared_back = ein("tf,df->td", grad_sh_gate, shared_gate) + ein(
            "tf,df->td", grad_sh_up, shared_up
        )
        back_part = collect(ex_back, slot, grad_slot_weight, first, experts).reshape(-1, width)
        back_rows = lax.psum_scatter(back_part, EP, scatter_dimension=0, tiled=True).astype(f32)
        back_rows = jnp.concatenate([back_rows[:rows] + shared_back, back_rows[rows:]], axis=0)
        back_sums = lax.psum(back_rows.astype(bf16), "hs")
        shared_sums = [over_ep(a) for a in shared_grads]
        grad_tokens, heads_sums, grad_router, grad_attn_gain, grad_ffn_gain = plain_back(
            back_sums,
            residual,
            normed2,
            grad_t,
            router_t,
            ffn_gain,
            out_t,
            q,
            k,
            v,
            probs,
            tables,
            query_t,
            key_t,
            value_t,
            normed1,
            attended_t,
            tokens,
            attn_gain,
        )

    rows_major = Layout(major_to_minor=(0, 1))
    out_part = with_layout_constraint(out_part, rows_major)
    out_rows = lax.psum_scatter(out_part, EP, scatter_dimension=0, tiled=True)
    out_rows = with_layout_constraint(out_rows, rows_major)
    out_rows = (out_rows.astype(f32) + shared_part.astype(f32)).astype(bf16)
    out_quarter = lax.psum_scatter(out_rows, "hs", scatter_dimension=1, tiled=True)
    residual_quarter = lax.dynamic_slice_in_dim(residual, hs * quarter, quarter, 1)
    output = (residual_quarter + out_quarter.astype(f32)).astype(bf16)

    return (
        output,
        grad_tokens.T,
        grad_attn_gain,
        *[a.T for a in heads_sums],
        grad_ffn_gain,
        grad_router.T,
        shared_sums[0].T,
        shared_sums[1].T,
        shared_sums[2],
        grad_gate_t.swapaxes(1, 2),
        grad_up_t.swapaxes(1, 2),
        grad_expert_down,
    )


def solution(mesh):
    ep_count, hs_count = mesh.devices.shape
    cut = Mesh(mesh.devices.reshape(ep_count // 2, 2, hs_count), ("xy", "core", "hs"))
    return jax.shard_map(
        shards,
        mesh=cut,
        in_specs=(
            P(EP, None),
            P(),
            P(None, "hs"),
            P(None, "hs"),
            P(None, "hs"),
            P(None, "hs"),
            P(),
            P(),
            P(None, "hs"),
            P(None, "hs"),
            P("hs", None),
            P(EP, None, "hs"),
            P(EP, None, "hs"),
            P(EP, "hs", None),
            P(EP, None),
            P(EP, None),
            P(EP, "hs"),
        ),
        out_specs=(
            P(EP, "hs"),
            P(EP, "hs"),
            P(),
            P(None, "hs"),
            P(None, "hs"),
            P(None, "hs"),
            P(None, "hs"),
            P(),
            P(),
            P(None, "hs"),
            P(None, "hs"),
            P("hs", None),
            P(EP, None, "hs"),
            P(EP, None, "hs"),
            P(EP, "hs", None),
        ),
        check_vma=False,
    )
```

```python
import functools
import math

import jax
import jax.numpy as jnp
import numpy as np
from jax import lax
from jax.experimental import pallas as pl
from jax.experimental.layout import Layout, with_layout_constraint
from jax.experimental.pallas import tpu as pltpu
from jax.sharding import Mesh
from jax.sharding import PartitionSpec as P

HEADS = 10
HEAD_DIM = 128
CAP = 112
EPS = 1e-06
EP = ("xy", "core")
bf16 = jnp.bfloat16
f32 = jnp.float32


def dot(a, b):
    return jnp.dot(a, b, preferred_element_type=f32)


def ein(spec, a, b):
    return jnp.einsum(spec, a, b, preferred_element_type=f32)


def rope_tables(rows):
    half = HEAD_DIM // 2
    frequency = 10000.0 ** (-np.arange(half) * 2.0 / HEAD_DIM)
    angles = frequency[:, None] * np.arange(rows)[None, :]
    return jnp.asarray(np.cos(angles), f32), jnp.asarray(np.sin(angles), f32)


def rope(v, cosine, sine):
    half = HEAD_DIM // 2
    a, b = v[:, :half], v[:, half:]
    return jnp.concatenate([a * cosine - b * sine, b * cosine + a * sine], axis=1)


def rope_back(v, cosine, sine):
    half = HEAD_DIM // 2
    a, b = v[:, :half], v[:, half:]
    return jnp.concatenate([a * cosine + b * sine, b * cosine - a * sine], axis=1)


VMEM_LIMIT = 60 * 1024 * 1024
PAD = 256


def nn(a, b):
    return lax.dot_general(a, b, (((1,), (0,)), ((), ())), preferred_element_type=f32)


def nt(a, b):
    return lax.dot_general(a, b, (((1,), (1,)), ((), ())), preferred_element_type=f32)


def tn(a, b):
    return lax.dot_general(a, b, (((0,), (0,)), ((), ())), preferred_element_type=f32)


def takes(microseconds):
    return pl.CostEstimate(flops=0, transcendentals=0, bytes_accessed=microseconds * 3_000_000)


def slot_masks(slot_ref, at):
    local, rows = slot_ref.shape[-2:]
    number = lax.broadcasted_iota(jnp.int32, (CAP, rows), 0)
    return [slot_ref[at, e : e + 1, :] == number for e in range(local)]


def spread_kernel(weighted, *refs):
    if weighted:
        rows_ref, slot_ref, router_ref, x_ref, sw_ref, pick = refs
    else:
        rows_ref, slot_ref, x_ref, pick = refs
    local = slot_ref.shape[1]
    rows = rows_ref[...] if weighted else rows_ref[0]
    masks = slot_masks(slot_ref, 0)
    if weighted:
        logits = nt(router_ref[...], rows)
        raised = jnp.exp(logits - jnp.max(logits, axis=0, keepdims=True))
        gates = raised / jnp.sum(raised, axis=0, keepdims=True)
    for e in range(local):
        pick[e * CAP : (e + 1) * CAP, :] = masks[e].astype(f32).astype(bf16)
        if weighted:
            sw_ref[e] = jnp.sum(
                jnp.where(masks[e], gates[e : e + 1, :], 0.0), axis=1, keepdims=True
            )
    product = nn if weighted else nt
    x_ref[...] = product(pick[...], rows).astype(bf16).reshape(x_ref.shape)


def spread(all_rows, slot, router_t=None):
    s, local, rows = slot.shape
    weighted = router_t is not None
    if weighted:
        width = all_rows.shape[1]
        block = pl.BlockSpec((rows, width), lambda i: (i, 0))
    else:
        width = all_rows.shape[1]
        block = pl.BlockSpec((1, width, rows), lambda i: (i, 0, 0))
    in_specs = [
        block,
        pl.BlockSpec((1, local, rows), lambda i: (i, 0, 0)),
    ]
    out_specs = [pl.BlockSpec((1, local, CAP, width), lambda i: (i, 0, 0, 0))]
    out_shape = [jax.ShapeDtypeStruct((s, local, CAP, width), bf16)]
    args = [all_rows, slot]
    if weighted:
        in_specs.append(pl.BlockSpec(router_t.shape, lambda i: (0, 0)))
        out_specs.append(pl.BlockSpec((local, CAP, 1), lambda i: (0, i, 0)))
        out_shape.append(jax.ShapeDtypeStruct((local, s * CAP, 1), f32))
        args.append(router_t)
    out = pl.pallas_call(
        functools.partial(spread_kernel, weighted),
        grid=(s,),
        in_specs=in_specs,
        out_specs=out_specs,
        out_shape=out_shape,
        scratch_shapes=[pltpu.VMEM((local * CAP, rows), bf16)],
        compiler_params=pltpu.CompilerParams(vmem_limit_bytes=VMEM_LIMIT),
        cost_estimate=takes(17),
        name="spread",
    )(*args)
    return out if weighted else out[0]


def padded(ref, out):
    ff = ref.shape[1]
    out[:ff, :] = ref[0]
    out[ff:, :] = jnp.zeros((out.shape[0] - ff, out.shape[1]), out.dtype)


def experts_forward_kernel(
    x_ref, sw_ref, wg_ref, wu_ref, wd_ref, y_ref, gate_ref, up_ref, wg, wu, wd
):
    padded(wg_ref, wg)
    padded(wu_ref, wu)
    padded(wd_ref, wd)
    rows, width = gate_ref.shape[1], x_ref.shape[3]
    x = x_ref[...].reshape(rows, width)
    gate = nt(x, wg[...])
    up = nt(x, wu[...])
    gate_ref[0] = gate
    up_ref[0] = up
    act = gate / (1.0 + jnp.exp(-gate))
    hidden = (act * up).astype(bf16).astype(f32)
    hidden_w = (hidden * sw_ref[0]).astype(bf16)
    y_ref[...] = nn(hidden_w, wd[...]).astype(bf16).reshape(y_ref.shape)


def experts_backward_kernel(
    groups,
    x_ref,
    gx_ref,
    gate_ref,
    up_ref,
    sw_ref,
    wg_ref,
    wu_ref,
    wd_ref,
    dx_ref,
    dg_ref,
    du_ref,
    dd_ref,
    gsw_ref,
    wg,
    wu,
    wd,
):
    padded(wg_ref, wg)
    padded(wu_ref, wu)
    padded(wd_ref, wd)
    rows, width = gate_ref.shape[1], x_ref.shape[3]
    ff = wg_ref.shape[1]
    x = x_ref[...].reshape(rows, width)
    gx = gx_ref[...].reshape(rows, width)
    gate, up, sw = gate_ref[0], up_ref[0], sw_ref[0]
    sig = 1.0 / (1.0 + jnp.exp(-gate))
    act = gate * sig
    hidden = (act * up).astype(bf16).astype(f32)
    gh = nt(gx, wd[...])
    gsw_ref[0] = jnp.sum(gh * hidden, axis=-1, keepdims=True)
    gh = gh * sw
    gg = (gh * up * sig * (1.0 + gate * (1.0 - sig))).astype(bf16)
    gu = (gh * act).astype(bf16)
    sums = (
        (dd_ref, tn((hidden * sw).astype(bf16), gx)[:ff]),
        (dg_ref, tn(gg, x)[:ff]),
        (du_ref, tn(gu, x)[:ff]),
    )
    if groups == 1:
        for ref, value in sums:
            ref[0] = value
    else:

        @pl.when(pl.program_id(1) == 0)
        def _():
            for ref, value in sums:
                ref[0] = value

        @pl.when(pl.program_id(1) > 0)
        def _():
            for ref, value in sums:
                ref[0] += value

    dx_ref[...] = (nn(gg, wg[...]) + nn(gu, wu[...])).astype(bf16).reshape(dx_ref.shape)


def sending(remote_too, collective_id):
    if not remote_too:
        return pltpu.CompilerParams(vmem_limit_bytes=VMEM_LIMIT)
    return pltpu.CompilerParams(
        vmem_limit_bytes=VMEM_LIMIT, collective_id=collective_id, has_side_effects=True
    )


def expert_specs(s, width):
    group = min(s, 8)
    slots = pl.BlockSpec((group, 1, CAP, width), lambda i, j: (j, i, 0, 0))
    lines = lambda columns: pl.BlockSpec((1, group * CAP, columns), lambda i, j: (i, j, 0))
    per = lambda *shape: pl.BlockSpec((1, *shape), lambda i, j: (i, 0, 0))
    return s // group, slots, lines, per


def experts_forward_sending_kernel(
    x_ref,
    sw_ref,
    wg_ref,
    wu_ref,
    wd_ref,
    grad_ref,
    y_ref,
    gate_ref,
    up_ref,
    near_ref,
    wg,
    wu,
    wd,
    send,
    recv,
):
    chip, core, z, cx, cy, cd = places()
    peers = [(cx, core, z), (cy, core, z)]
    copies = [
        remote(grad_ref, near_ref.at[i], send.at[i], recv.at[i], peer) for i, peer in enumerate(peers)
    ]

    @pl.when(pl.program_id(0) == 0)
    def _():
        greet(peers)
        for copy in copies:
            copy.start()

    experts_forward_kernel(
        x_ref, sw_ref, wg_ref, wu_ref, wd_ref, y_ref, gate_ref, up_ref, wg, wu, wd
    )

    @pl.when(pl.program_id(0) == pl.num_programs(0) - 1)
    def _():
        for copy in copies:
            copy.wait()


def experts_forward(x, sw, wg, wu, wd, grad=None):
    s, local, cap, width = x.shape
    ff = wg.shape[1]
    rows = s * cap
    groups, slots, lines, per = expert_specs(s, width)
    middle = jax.ShapeDtypeStruct((local, rows, PAD), f32)
    kernel = experts_forward_kernel
    in_specs = [slots, lines(1)] + [per(ff, width)] * 3
    out_specs = [slots, lines(PAD), lines(PAD)]
    out_shape = [jax.ShapeDtypeStruct(x.shape, bf16), middle, middle]
    scratch = [pltpu.VMEM((PAD, width), bf16)] * 3
    args = [x, sw, wg, wu, wd]
    if grad is not None:
        kernel = experts_forward_sending_kernel
        in_specs.append(pl.BlockSpec(memory_space=pl.ANY))
        out_specs.append(pl.BlockSpec(memory_space=pl.ANY))
        out_shape.append(jax.ShapeDtypeStruct((2, *grad.shape), bf16))
        scratch += [pltpu.SemaphoreType.DMA((2,))] * 2
        args.append(grad)
    return pl.pallas_call(
        kernel,
        grid=(local, groups),
        in_specs=in_specs,
        out_specs=out_specs,
        out_shape=out_shape,
        scratch_shapes=scratch,
        compiler_params=sending(grad is not None, 4),
        cost_estimate=takes(31),
        name="experts_forward",
    )(*args)


def experts_backward(x, gx, gate, up, sw, wg, wu, wd):
    s, local, cap, width = x.shape
    ff = wg.shape[1]
    rows = s * cap
    groups, slots, lines, per = expert_specs(s, width)
    return pl.pallas_call(
        functools.partial(experts_backward_kernel, groups),
        grid=(local, groups),
        in_specs=[slots, slots, lines(PAD), lines(PAD), lines(1)]
        + [per(ff, width)] * 3,
        out_specs=[slots] + [per(ff, width)] * 3 + [lines(1)],
        out_shape=[jax.ShapeDtypeStruct(x.shape, bf16)]
        + [jax.ShapeDtypeStruct((local, ff, width), f32)] * 3
        + [jax.ShapeDtypeStruct((local, rows, 1), f32)],
        scratch_shapes=[pltpu.VMEM((PAD, width), bf16)] * 3,
        compiler_params=pltpu.CompilerParams(vmem_limit_bytes=VMEM_LIMIT),
        cost_estimate=takes(47),
        name="experts_backward",
    )(x, gx, gate, up, sw, wg, wu, wd)


def collect_kernel(y_ref, slot_ref, out_ref, pick):
    local = slot_ref.shape[1]
    masks = slot_masks(slot_ref, 0)
    for e in range(local):
        pick[e * CAP : (e + 1) * CAP, :] = masks[e].astype(f32).astype(bf16)
    out_ref[0] = tn(pick[...], y_ref[...].reshape(pick.shape[0], -1)).astype(bf16)


def collect_sending_kernel(
    y_ref, slot_ref, grad_ref, near_ref, out_ref, far_ref, given_ref, pick, send, recv, csend, crecv
):
    chip, core, z, cx, cy, cd = places()
    x_peer, y_peer, c_peer = (cx, core, z), (cy, core, z), (chip, 1 - core, z)
    half = grad_ref.shape[0] // 2
    top, low = pl.ds(0, half), pl.ds(half, half)
    relays = [
        remote(near_ref.at[0, top], far_ref.at[top], send.at[0], recv.at[0], y_peer),
        remote(near_ref.at[1, low], far_ref.at[low], send.at[1], recv.at[1], x_peer),
    ]
    passes = [
        remote(ref, given_ref.at[i], csend.at[i], crecv.at[i], c_peer)
        for i, ref in enumerate((grad_ref, near_ref.at[0], near_ref.at[1], far_ref))
    ]

    @pl.when(pl.program_id(0) == 0)
    def _():
        greet([x_peer, y_peer, c_peer])
        for copy in (*relays, *passes[:3]):
            copy.start()

    collect_kernel(y_ref, slot_ref, out_ref, pick)

    @pl.when(pl.program_id(0) == pl.num_programs(0) - 1)
    def _():
        for copy in relays:
            copy.wait_recv()
        passes[3].start()
        for copy in passes:
            copy.wait()
        for copy in relays:
            copy.wait_send()


def collect_back_kernel(experts, y_ref, slot_ref, gsw_ref, first_ref, out_ref, pick):
    local, rows = slot_ref.shape[1:]
    first = first_ref[0]
    masks = slot_masks(slot_ref, 0)
    number = lax.broadcasted_iota(jnp.int32, (experts, rows), 0)
    probs = jnp.zeros((experts, rows), f32)
    for e in range(local):
        pick[e * CAP : (e + 1) * CAP, :] = masks[e].astype(f32).astype(bf16)
        line = jnp.sum(jnp.where(masks[e], gsw_ref[e], 0.0), axis=0, keepdims=True)
        probs = jnp.where(number == first + e, line, probs)
    out_ref[0, :rows] = tn(pick[...], y_ref[...].reshape(pick.shape[0], -1)).astype(bf16)
    out_ref[0, rows:] = jnp.zeros((experts, out_ref.shape[2]), bf16)
    out_ref[0, rows:, :rows] = probs.astype(bf16)


def collect_sending(y, slot, grad, near):
    s, local, cap, width = y.shape
    rows = slot.shape[2]
    dma = pltpu.SemaphoreType.DMA
    whole = pl.BlockSpec(memory_space=pl.ANY)
    return pl.pallas_call(
        collect_sending_kernel,
        grid=(s,),
        in_specs=[
            pl.BlockSpec((1, local, cap, width), lambda i: (i, 0, 0, 0)),
            pl.BlockSpec((1, local, rows), lambda i: (i, 0, 0)),
            whole,
            whole,
        ],
        out_specs=[pl.BlockSpec((1, rows, width), lambda i: (i, 0, 0)), whole, whole],
        out_shape=[
            jax.ShapeDtypeStruct((s, rows, width), bf16),
            jax.ShapeDtypeStruct(grad.shape, bf16),
            jax.ShapeDtypeStruct((4, *grad.shape), bf16),
        ],
        scratch_shapes=[
            pltpu.VMEM((local * cap, rows), bf16),
            dma((2,)),
            dma((2,)),
            dma((4,)),
            dma((4,)),
        ],
        compiler_params=sending(True, 5),
        cost_estimate=takes(20),
        name="collect_sending",
    )(y, slot, grad, near)


def spread_grad_kernel(grad_ref, near_ref, far_ref, given_ref, slot_ref, x_ref, pick, gbuf, xbuf, come, gone):
    chip, core = lax.axis_index("xy"), lax.axis_index("core")
    local, rows = slot_ref.shape[1:]
    here = [grad_ref, near_ref.at[0], near_ref.at[1], far_ref]
    sources = [(here[t // 2], given_ref.at[t // 2])[t % 2] for t in range(8)]

    def in_copy(t):
        return pltpu.make_async_copy(sources[t], gbuf.at[t % 2], come.at[t % 2])

    def out_copy(t, src):
        return pltpu.make_async_copy(xbuf.at[t % 2], x_ref.at[src], gone.at[t % 2])

    number = lax.broadcasted_iota(jnp.int32, (CAP, rows), 0)
    in_copy(0).start()
    for t in range(8):
        if t < 7:
            in_copy(t + 1).start()
        x, y = (chip % 2 + (t // 2) % 2) % 2, (chip // 2 + t // 4) % 2
        src = (y * 2 + x) * 2 + (core + t % 2) % 2
        slots = slot_ref[src]
        for e in range(local):
            mask = slots[e : e + 1, :] == number
            pick[e * CAP : (e + 1) * CAP, :] = mask.astype(f32).astype(bf16)
        in_copy(t).wait()
        if t >= 2:
            out_copy(t, src).wait()
        xbuf[t % 2] = nt(pick[...], gbuf[t % 2]).astype(bf16).reshape(xbuf.shape[1:])
        out_copy(t, src).start()
    out_copy(0, 0).wait()
    out_copy(1, 0).wait()


def spread_grad(grad, near, far, given, slot):
    s, local, rows = slot.shape
    width = grad.shape[0]
    whole = pl.BlockSpec(memory_space=pl.ANY)
    dma = pltpu.SemaphoreType.DMA
    return pl.pallas_call(
        spread_grad_kernel,
        in_specs=[whole] * 4 + [pl.BlockSpec(memory_space=pltpu.VMEM)],
        out_specs=whole,
        out_shape=jax.ShapeDtypeStruct((s, local, CAP, width), bf16),
        scratch_shapes=[
            pltpu.VMEM((local * CAP, rows), bf16),
            pltpu.VMEM((2, width, rows), bf16),
            pltpu.VMEM((2, local, CAP, width), bf16),
            dma((2,)),
            dma((2,)),
        ],
        compiler_params=sending(False, 0),
        cost_estimate=takes(16),
        name="spread_grad",
    )(grad, near, far, given, slot)


def collect(y, slot, gsw=None, first=None, experts=0):
    s, local, cap, width = y.shape
    rows = slot.shape[2]
    in_specs = [
        pl.BlockSpec((1, local, cap, width), lambda i: (i, 0, 0, 0)),
        pl.BlockSpec((1, local, rows), lambda i: (i, 0, 0)),
    ]
    args = [y, slot]
    kernel = collect_kernel
    tall = rows
    if gsw is not None:
        in_specs += [
            pl.BlockSpec((local, cap, 1), lambda i: (0, i, 0)),
            pl.BlockSpec(memory_space=pltpu.SMEM),
        ]
        args += [gsw, first.reshape(1)]
        kernel = functools.partial(collect_back_kernel, experts)
        tall = rows + experts
    return pl.pallas_call(
        kernel,
        grid=(s,),
        in_specs=in_specs,
        out_specs=pl.BlockSpec((1, tall, width), lambda i: (i, 0, 0)),
        out_shape=jax.ShapeDtypeStruct((s, tall, width), bf16),
        scratch_shapes=[pltpu.VMEM((local * cap, rows), bf16)],
        compiler_params=pltpu.CompilerParams(vmem_limit_bytes=VMEM_LIMIT),
        cost_estimate=takes(17),
        name="collect",
    )(*args)


MESH = pl.DeviceIdType.MESH
EXTRA = 64
SUM_STARTS = (0, 192, 320, 448)


def places():
    chip, core, z = lax.axis_index("xy"), lax.axis_index("core"), lax.axis_index("hs")
    x, y = chip % 2, chip // 2
    return chip, core, z, y * 2 + (1 - x), (1 - y) * 2 + x, (1 - y) * 2 + (1 - x)


def greet(peers):
    barrier = pltpu.get_barrier_semaphore()
    for peer in peers:
        pl.semaphore_signal(barrier, inc=1, device_id=peer, device_id_type=MESH)
    pl.semaphore_wait(barrier, len(peers))


def remote(src, dst, send, recv, peer):
    return pltpu.make_async_remote_copy(
        src_ref=src, dst_ref=dst, send_sem=send, recv_sem=recv, device_id=peer, device_id_type=MESH
    )


def block(q, size):
    return pl.ds(pl.multiple_of(q * size, 16), size)


def weight_gather(out_ref, csend, crecv, send, recv):
    chip, core, z, cx, cy, cd = places()
    other = 1 - core
    c_peer = (chip, other, z)
    chips = (cx, cy, cd)
    count = out_ref.shape[0] // 2
    piece = count // 4

    def place(c, k):
        return pl.ds(pl.multiple_of(k * count + c * piece, 16), piece)

    def give(number, c, k, sems, peer):
        return remote(out_ref.at[place(c, k)], out_ref.at[place(c, k)], *sems(number), peer)

    def chip_sems(i):
        return send.at[3 + i], recv.at[3 + i]

    def core_sems(i):
        return csend.at[1 + i], crecv.at[1 + i]

    gather = [give(i, chip, core, chip_sems, (c, core, z)) for i, c in enumerate(chips)]
    over = [give(i, c, core, core_sems, c_peer) for i, c in enumerate((*chips, chip))]

    def put(done):
        out_ref[place(chip, core)] = done.astype(bf16)
        for i in (2, 0, 1):
            gather[i].start()
        over[3].start()

    def end():
        for i, c in enumerate(chips):
            give(i, c, core, chip_sems, (c, core, z)).wait_recv()
            over[i].start()
        for i, c in enumerate((*chips, chip)):
            give(i, c, other, core_sems, c_peer).wait_recv()
        for copy in (*gather, *over):
            copy.wait_send()

    return put, end


def weight_sum(grads, given, half, land, out_ref, csend, crecv, send, recv):
    chip, core, z, cx, cy, cd = places()
    other = 1 - core
    c_peer = (chip, other, z)
    chips = (cx, cy, cd)
    count = grads.shape[0] // 2
    piece = count // 4

    to_core = remote(grads.at[block(other, count)], given, csend.at[0], crecv.at[0], c_peer)
    scatter = [
        remote(half.at[block(c, piece)], land.at[i], send.at[i], recv.at[i], (c, core, z))
        for i, c in enumerate(chips)
    ]
    if out_ref is not None:
        put, gathered = weight_gather(out_ref, csend, crecv, send, recv)

    def share():
        to_core.wait_recv()
        half[...] = (grads[block(core, count)].astype(f32) + given[...].astype(f32)).astype(bf16)
        for i in (2, 0, 1):
            scatter[i].start()

    def total():
        done = half[block(chip, piece)].astype(f32)
        for i in range(3):
            scatter[i].wait_recv()
            done = done + land[i].astype(f32)
        return done

    def give_back():
        put(total())

    def end():
        if out_ref is not None:
            gathered()
        for copy in (to_core, *scatter):
            copy.wait_send()

    return to_core.start, share, give_back, end, total


def weight_sum_scratch(tall, width):
    dma = pltpu.SemaphoreType.DMA
    return [
        pltpu.VMEM((tall, width), bf16),
        pltpu.VMEM((tall // 2, width), bf16),
        pltpu.VMEM((tall // 2, width), bf16),
        pltpu.VMEM((3, tall // 8, width), bf16),
        dma((5,)),
        dma((5,)),
        dma((6,)),
        dma((6,)),
    ]


def gather_spread_kernel(
    own_ref,
    slots_ref,
    router_ref,
    grad_ref,
    x_ref,
    sw_ref,
    slot_ref,
    grad_all_ref,
    held,
    pick,
    xbuf,
    send,
    recv,
    copied,
    zsend,
    zrecv,
):
    chip, core, z, cx, cy, cd = places()
    other = 1 - core
    x_peer, y_peer, c_peer = (cx, core, z), (cy, core, z), (chip, other, z)
    tall = held.shape[1]
    half = tall // 2
    local, rows = slot_ref.shape[1:]
    me = chip * 2 + core
    top, low = pl.ds(0, half), pl.ds(half, half)

    def at(c, k):
        return c * 2 + k

    def move(number, src_slot, part, peer):
        return remote(
            held.at[src_slot, part], held.at[src_slot, part], send.at[number], recv.at[number], peer
        )

    whole = pl.ds(0, tall)
    z_peers = [(chip, core, (z + i) % 4) for i in (1, 2, 3)]
    greet([x_peer, y_peer, c_peer, *z_peers])
    quarter = grad_ref.shape[0]

    def grad_copy(i, q):
        return remote(
            grad_ref, grad_all_ref.at[block(q, quarter)], zsend.at[i], zrecv.at[i], z_peers[i]
        )

    held[me, :rows] = own_ref[...]
    packed = tall - rows
    held[me, rows:, 2 * rows :] = jnp.zeros((packed, own_ref.shape[1] - 2 * rows), bf16)
    held[me, rows:, :rows] = slots_ref[:packed]
    held[me, rows:, rows : 2 * rows] = slots_ref[packed:]
    x_top, x_low = move(0, me, top, x_peer), move(1, me, low, x_peer)
    y_low, y_top = move(2, me, low, y_peer), move(3, me, top, y_peer)
    to_core = move(4, me, whole, c_peer)
    relay_top, relay_low = move(5, at(cx, core), top, y_peer), move(6, at(cy, core), low, x_peer)
    pass_x, pass_y = move(7, at(cx, core), whole, c_peer), move(8, at(cy, core), whole, c_peer)
    pass_d = move(9, at(cd, core), whole, c_peer)
    for copy in (x_top, y_low, x_low, y_top, to_core, *[grad_copy(i, z) for i in (1, 0, 2)]):
        copy.start()
    grad_all_ref[block(z, quarter)] = grad_ref[...]

    def arrived(number, slot, part):
        move(number, slot, part, c_peer).wait_recv()

    number = lax.broadcasted_iota(jnp.int32, (CAP, rows), 0)
    first = me * local
    line = lax.broadcasted_iota(jnp.int32, (local, EXTRA), 0)
    column = lax.broadcasted_iota(jnp.int32, (local, EXTRA), 1)
    chosen = (column == line + first).astype(f32).astype(bf16)

    def out_copy(t, src):
        return pltpu.make_async_copy(xbuf.at[t % 2], x_ref.at[src], copied.at[t % 2])

    def step(t, carry):
        @pl.when(t == 1)
        def _():
            arrived(4, at(chip, other), whole)

        @pl.when(t == 2)
        def _():
            arrived(0, at(cx, core), top)
            relay_top.start()
            arrived(2, at(cy, core), low)
            relay_low.start()
            arrived(1, at(cx, core), low)
            pass_x.start()

        @pl.when(t == 3)
        def _():
            arrived(3, at(cy, core), top)
            pass_y.start()
            arrived(7, at(cx, other), whole)

        @pl.when(t == 5)
        def _():
            arrived(8, at(cy, other), whole)

        @pl.when(t == 6)
        def _():
            arrived(5, at(cd, core), top)
            arrived(6, at(cd, core), low)
            pass_d.start()

        @pl.when(t == 7)
        def _():
            arrived(9, at(cd, other), whole)

        x, y = (chip % 2 + (t // 2) % 2) % 2, (chip // 2 + t // 4) % 2
        src = (y * 2 + x) * 2 + (core + t % 2) % 2
        slots = nn(chosen[:, :packed], held[src, rows:, :rows])
        slots += nn(chosen[:, packed:], held[src, rows:, rows : 2 * rows])
        slots = slots.astype(jnp.int32)
        slot_ref[src] = slots
        logits = nt(router_ref[...], held[src, :rows])
        raised = jnp.exp(logits - jnp.max(logits, axis=0, keepdims=True))
        gates = raised / jnp.sum(raised, axis=0, keepdims=True)
        for e in range(local):
            mask = slots[e : e + 1, :] == number
            pick[e * CAP : (e + 1) * CAP, :] = mask.astype(f32).astype(bf16)
            sw_ref[e, pl.ds(pl.multiple_of(src * CAP, 8), CAP), :] = jnp.sum(
                jnp.where(mask, gates[e : e + 1, :], 0.0), axis=1, keepdims=True
            )

        @pl.when(t >= 2)
        def _():
            out_copy(t, src).wait()

        xbuf[t % 2] = nn(pick[...], held[src, :rows]).astype(bf16).reshape(xbuf.shape[1:])
        out_copy(t, src).start()
        return carry

    lax.fori_loop(0, 8, step, 0)
    out_copy(0, me).wait()
    out_copy(1, me).wait()
    for i in range(3):
        grad_copy(i, (z + 3 - i) % 4).wait_recv()
        grad_copy(i, z).wait_send()
    for copy in (x_top, x_low, y_low, y_top, to_core, relay_top, relay_low, pass_x, pass_y, pass_d):
        copy.wait_send()


def gather_spread(own, slots, router_t, grad_quarter, local, ep_count):
    rows, width = own.shape
    tall = rows + EXTRA // 2
    vmem = pl.BlockSpec(memory_space=pltpu.VMEM)
    return pl.pallas_call(
        gather_spread_kernel,
        in_specs=[vmem] * 4,
        out_specs=[pl.BlockSpec(memory_space=pl.ANY), vmem, vmem, vmem],
        out_shape=[
            jax.ShapeDtypeStruct((ep_count, local, CAP, width), bf16),
            jax.ShapeDtypeStruct((local, ep_count * CAP, 1), f32),
            jax.ShapeDtypeStruct((ep_count, local, rows), jnp.int32),
            jax.ShapeDtypeStruct((width, rows), bf16),
        ],
        scratch_shapes=[
            pltpu.VMEM((ep_count, tall, width), bf16),
            pltpu.VMEM((local * CAP, rows), bf16),
            pltpu.VMEM((2, local, CAP, width), bf16),
            pltpu.SemaphoreType.DMA((10,)),
            pltpu.SemaphoreType.DMA((10,)),
            pltpu.SemaphoreType.DMA((2,)),
            pltpu.SemaphoreType.DMA((3,)),
            pltpu.SemaphoreType.DMA((3,)),
        ],
        compiler_params=pltpu.CompilerParams(
            vmem_limit_bytes=VMEM_LIMIT, collective_id=0, has_side_effects=True
        ),
        cost_estimate=takes(62),
        name="gather_spread",
    )(own, slots, router_t, grad_quarter)


def front_kernel(
    x_ref,
    gain_ref,
    wq_ref,
    wk_ref,
    wv_ref,
    wo_ref,
    doc_ref,
    cos_ref,
    sin_ref,
    normed1_out,
    q_out,
    k_out,
    v_out,
    probs_out,
    attended_out,
    out_out,
    residual_ref,
    normed2_ref,
    normed1_ref,
    q_ref,
    k_ref,
    v_ref,
    probs_ref,
    attended_ref,
    out_ref,
    gone,
    shared,
    beside,
    esend,
    erecv,
    asend,
    arecv,
    zsend,
    zrecv,
    send,
    recv,
    csend,
    crecv,
):
    chip, core, z, cx, cy, cd = places()
    other = 1 - core
    odd = z % 2
    c_peer = (chip, other, z)
    chips = (cx, cy, cd)
    z_peers = [(chip, core, (z + i) % 4) for i in (1, 2, 3)]
    pair = (chip, core, z + 1 - 2 * odd)
    rows, width = x_ref.shape
    quarter = wq_ref.shape[0]
    whole = HEAD_DIM * (quarter // HEAD_DIM)
    spare = quarter - whole
    greet([c_peer, *[(c, core, z) for c in chips], *z_peers])

    full_rows = pl.ds(pl.multiple_of(odd * spare, 16), whole)
    half_rows = pl.ds(pl.multiple_of((1 - odd) * whole, 16), spare)
    for i, ref in enumerate((wq_ref, wk_ref, wv_ref)):
        shared[i * spare : (i + 1) * spare] = ref[half_rows]
    trade = remote(shared, beside, esend, erecv, pair)
    trade.start()

    share, lanes = quarter // 4, width // 2
    my_lanes = pl.ds(pl.multiple_of(core * lanes, 128), lanes)

    def piece(c):
        return pl.ds(pl.multiple_of(c * share, 16), share)

    out_z = [
        remote(
            wo_ref.at[piece(chip), my_lanes],
            out_ref.at[z, piece(chip), my_lanes],
            zsend.at[i],
            zrecv.at[i],
            peer,
        )
        for i, peer in enumerate(z_peers)
    ]
    for i in (1, 0, 2):
        out_z[i].start()
    behind = [(z + 3 - i) % 4 for i in range(3)]

    def out_chip(i, j, c):
        at = out_ref.at[behind[i], piece(c), my_lanes]
        return remote(at, at, send.at[3 * i + j], recv.at[3 * i + j], (chips[j], core, z))

    def out_core(i, k):
        half = pl.ds(pl.multiple_of(k * lanes, 128), lanes)
        at = out_ref.at[behind[i], :, half]
        return remote(at, at, csend.at[i], crecv.at[i], c_peer)

    x = x_ref[...].astype(f32)
    rms1 = lax.rsqrt(jnp.sum(x * x, axis=-1, keepdims=True) * (1.0 / width) + EPS)
    normed1_ref[...] = (x * rms1 * gain_ref[0:1]).astype(bf16)
    out_ref[z] = wo_ref[...]

    cosine, sine = cos_ref[...], sin_ref[...]
    half_dim = HEAD_DIM // 2
    scale = 1.0 / math.sqrt(HEAD_DIM)
    row = lax.broadcasted_iota(jnp.int32, (rows, rows), 0)
    column = lax.broadcasted_iota(jnp.int32, (rows, rows), 1)
    doc = jnp.broadcast_to(doc_ref[...].astype(f32), (rows, rows))
    allowed = (row >= column) & (doc == doc.T)

    kept = (normed1_ref, q_ref, k_ref, v_ref, probs_ref, attended_ref, out_ref)
    outs = (normed1_out, q_out, k_out, v_out, probs_out, attended_out, out_out)
    writes = [pltpu.make_async_copy(a, b, gone.at[i]) for i, (a, b) in enumerate(zip(kept, outs))]
    writes[0].start()

    def turn(pre):
        a, b = pre[:half_dim], pre[half_dim:]
        return (
            jnp.concatenate([a * cosine - b * sine, b * cosine + a * sine], axis=0).astype(bf16)
        )

    def attend(h):
        scores = jnp.where(allowed, tn(q_ref[h], k_ref[h]) * scale, -1e30)
        raised = jnp.exp(scores - jnp.max(scores, axis=-1, keepdims=True))
        probs = raised * (1.0 / jnp.sum(raised, axis=-1, keepdims=True))
        probs_ref[h] = probs
        return nt(v_ref[h], probs.astype(bf16)).astype(bf16)

    def project(at):
        return [nt(ref[at], normed1_ref[...]) for ref in (wq_ref, wk_ref, wv_ref)]

    q, k, v = project(full_rows)
    heads = whole // HEAD_DIM
    for h in range(heads):
        at = slice(h * HEAD_DIM, (h + 1) * HEAD_DIM)
        q_ref[h], k_ref[h], v_ref[h] = turn(q[at]), turn(k[at]), v[at].astype(bf16)

    def attended_copy(number, start, size):
        at = attended_ref.at[pl.ds(pl.multiple_of(start, 16), size)]
        return lambda i: remote(
            at, at, asend.at[number, i], arecv.at[number, i], z_peers[i]
        )

    mine = z * quarter
    copies = []
    for h in range(heads):
        start = mine + odd * spare + h * HEAD_DIM
        attended_ref[pl.ds(pl.multiple_of(start, 16), HEAD_DIM)] = attend(h)
        copy = attended_copy(h, start, HEAD_DIM)
        copies += [copy(1), copy(0), copy(2)]
        for one in copies[-3:]:
            one.start()
        if h == 0:
            for i in range(3):
                out_z[i].wait_recv()
                for j in (2, 0, 1):
                    out_chip(i, j, chip).start()

    trade.wait_recv()
    for i, (ref, to) in enumerate(((wq_ref, q_ref), (wk_ref, k_ref), (wv_ref, v_ref))):
        normed1 = normed1_ref[...]
        here = nt(ref[half_rows], normed1)
        there = nt(beside[i * spare : (i + 1) * spare], normed1)
        first = jnp.where(odd == 1, there, here)
        second = jnp.where(odd == 1, here, there)
        both = jnp.concatenate([first, second], axis=0)
        to[heads] = both.astype(bf16) if to is v_ref else turn(both)
    last = attend(heads)
    for i in (1, 2, 3, 4):
        writes[i].start()
    last = jnp.where(odd == 1, last[spare:], last[:spare])
    start = mine + (1 - odd) * whole
    attended_ref[pl.ds(pl.multiple_of(start, 16), spare)] = last
    copy = attended_copy(heads, start, spare)
    copies += [copy(1), copy(0), copy(2)]
    for one in copies[-3:]:
        one.start()

    for i in range(3):
        for j in range(3):
            out_chip(i, j, chips[j]).wait_recv()
        out_core(i, core).start()
    for i in range(3):
        from_z = (z + 3 - i) % 4
        from_odd = from_z % 2
        for h in range(heads):
            attended_copy(h, from_z * quarter + from_odd * spare + h * HEAD_DIM, HEAD_DIM)(i).wait_recv()
        attended_copy(heads, from_z * quarter + (1 - from_odd) * whole, spare)(i).wait_recv()
        out_core(i, other).wait_recv()
    writes[5].start()
    writes[6].start()
    attended = attended_ref[...].T
    residual = x_ref[...].astype(f32) + nt(attended, out_ref[...].reshape(width, width))
    residual_ref[...] = residual
    rms2 = lax.rsqrt(jnp.sum(residual * residual, axis=-1, keepdims=True) * (1.0 / width) + EPS)
    normed2_ref[...] = (residual * rms2 * gain_ref[1:2]).astype(bf16)
    for write in writes:
        write.wait()
    for one in (trade, *out_z, *copies):
        one.wait_send()
    for i in range(3):
        for j in range(3):
            out_chip(i, j, chip).wait_send()
        out_core(i, core).wait_send()


def front(x, gains, wq, wk, wv, wo, doc, tables):
    rows, width = x.shape
    quarter = wq.shape[0]
    heads = -(-quarter // HEAD_DIM)
    spare = quarter % HEAD_DIM
    vmem = pl.BlockSpec(memory_space=pltpu.VMEM)
    dma = pltpu.SemaphoreType.DMA
    low = lambda *shape: jax.ShapeDtypeStruct(shape, bf16)
    early = [
        low(rows, width),
        *[low(heads, HEAD_DIM, rows)] * 3,
        jax.ShapeDtypeStruct((heads, rows, rows), f32),
        low(width, rows),
        low(4, quarter, width),
    ]
    return pl.pallas_call(
        front_kernel,
        in_specs=[vmem] * 9,
        out_specs=[pl.BlockSpec(memory_space=pl.ANY)] * len(early) + [vmem] * 2,
        out_shape=[*early, jax.ShapeDtypeStruct((rows, width), f32), low(rows, width)],
        scratch_shapes=[
            *[pltpu.VMEM(a.shape, a.dtype) for a in early],
            dma((len(early),)),
            pltpu.VMEM((3 * spare, width), bf16),
            pltpu.VMEM((3 * spare, width), bf16),
            dma,
            dma,
            dma((heads, 3)),
            dma((heads, 3)),
            dma((3,)),
            dma((3,)),
            dma((9,)),
            dma((9,)),
            dma((3,)),
            dma((3,)),
        ],
        compiler_params=pltpu.CompilerParams(
            vmem_limit_bytes=VMEM_LIMIT, collective_id=1, has_side_effects=True
        ),
        cost_estimate=takes(50),
        name="front",
    )(x, gains, wq, wk, wv, wo, doc, *tables)


def collect_sum_kernel(
    y_ref,
    slot_ref,
    gsw_ref,
    normed_in,
    grad_in,
    gate_in,
    up_in,
    down_in,
    out_ref,
    sum_ref,
    forward_ref,
    normed_ref,
    grad_ref,
    gate_ref,
    up_ref,
    down_ref,
    loaded,
    mine,
    pick,
    ybuf,
    stage,
    given,
    sums,
    relay,
    land,
    zland,
    copied,
    core_send,
    core_recv,
    send,
    recv,
    zsend,
    zrecv,
    grads,
    *more,
):
    chip, core, z, cx, cy, cd = places()
    other = 1 - core
    x_peer, y_peer, c_peer = (cx, core, z), (cy, core, z), (chip, other, z)
    z_peers = [(chip, core, (z + i) % 4) for i in (1, 2, 3)]
    local, rows = slot_ref.shape[1:]
    tall = out_ref.shape[0]
    me = chip * 2 + core
    number = lax.broadcasted_iota(jnp.int32, (CAP, rows), 0)
    row = lax.broadcasted_iota(jnp.int32, (EXTRA, rows), 0)

    greet([x_peer, y_peer, c_peer, (cd, core, z), *z_peers])

    def turn(t):
        theirs = (t % 2) * (1 - t // 7) + (7 - t) // 7
        return theirs * ((t + 1) // 2) + (1 - theirs) * (t // 2 - 1 + t // 7), theirs

    def sequence(t):
        p, theirs = turn(t)
        x, y = (chip % 2 + 1 + p // 2) % 2, (chip // 2 + 1 + p % 2) % 2
        return (y * 2 + x) * 2 + (core + theirs) % 2

    def in_copy(t):
        return pltpu.make_async_copy(y_ref.at[sequence(t)], ybuf.at[t % 2], copied.at[t % 2])

    def to_core(p):
        return remote(stage.at[p % 2], given.at[p], core_send.at[p], core_recv.at[p], c_peer)

    starts = (*SUM_STARTS, tall)
    units = len(starts) - 1
    sizes = [starts[u + 1] - starts[u] for u in range(units)]

    def top(u):
        return pl.ds(starts[u], sizes[u] // 2)

    def low(u):
        return pl.ds(starts[u] + sizes[u] // 2, sizes[u] // 2)

    def first(u, of):
        return pl.ds(0, sizes[u] // of)

    def over(u, number, src, dst, peer):
        return remote(src, dst, send.at[u, number], recv.at[u, number], peer)

    far_top = [over(u, 0, sums.at[0, top(u)], relay.at[u, 0, first(u, 2)], x_peer) for u in range(units)]
    far_low = [over(u, 1, sums.at[0, low(u)], relay.at[u, 1, first(u, 2)], y_peer) for u in range(units)]
    x_top = [over(u, 2, sums.at[1, top(u)], land.at[0, top(u)], x_peer) for u in range(units)]
    x_low = [over(u, 3, sums.at[1, low(u)], land.at[0, low(u)], x_peer) for u in range(units)]
    y_low = [over(u, 4, sums.at[2, low(u)], land.at[1, low(u)], y_peer) for u in range(units)]
    y_top = [over(u, 5, sums.at[2, top(u)], land.at[1, top(u)], y_peer) for u in range(units)]

    in_copy(0).start()
    late = (normed_in, grad_in, gate_in, up_in, down_in)
    held = (normed_ref, grad_ref, gate_ref, up_ref, down_ref)
    loads = [pltpu.make_async_copy(a, b, loaded.at[i]) for i, (a, b) in enumerate(zip(late, held))]
    for load in loads:
        load.start()
    start, share, _, end, total = weight_sum(grads, *more[:3], None, *more[3:])

    def shared_expert():
        for load in loads:
            load.wait()
        normed, grad_t = normed_ref[...], grad_ref[...]
        size = gate_ref.shape[0]
        gate, up = nt(gate_ref[...], normed), nt(up_ref[...], normed)
        sig = 1.0 / (1.0 + jnp.exp(-gate))
        act = gate * sig
        hidden = (act * up).astype(bf16)
        forward_ref[...] = tn(hidden, down_ref[...]).astype(bf16)
        grad_hidden = nn(down_ref[...], grad_t)
        grad_gate = (grad_hidden * up * sig * (1.0 + gate * (1.0 - sig))).astype(bf16)
        grad_up = (grad_hidden * act).astype(bf16)
        grads[:size] = nn(grad_gate, normed).astype(bf16)
        grads[size : 2 * size] = nn(grad_up, normed).astype(bf16)
        grads[2 * size : 3 * size] = nt(hidden, grad_t).astype(bf16)
        grads[3 * size :] = jnp.zeros((grads.shape[0] - 3 * size, grads.shape[1]), bf16)
        start()
        mine[...] = (tn(grad_gate, gate_ref[...]) + tn(grad_up, up_ref[...])).astype(bf16)

    def step(t, carry):
        @pl.when(t < 7)
        def _():
            in_copy(t + 1).start()

        (p, theirs), s = turn(t), sequence(t)
        probs = jnp.zeros((EXTRA, rows), f32)
        for e in range(local):
            mask = slot_ref[s, e : e + 1, :] == number
            pick[e * CAP : (e + 1) * CAP, :] = mask.astype(f32).astype(bf16)
            column = gsw_ref[e, pl.ds(pl.multiple_of(s * CAP, 8), CAP), :]
            line = jnp.sum(jnp.where(mask, column, 0.0), axis=0, keepdims=True)
            probs = jnp.where(row == me * local + e, line, probs)
        in_copy(t).wait()
        back = tn(pick[...], ybuf[t % 2].reshape(local * CAP, -1))

        @pl.when(theirs == 1)
        def _():
            @pl.when(p >= 2)
            def _():
                to_core(p - 2).wait_send()

            stage[p % 2, :rows] = back.astype(bf16)
            stage[p % 2, rows:] = jnp.zeros((tall - rows, back.shape[1]), bf16)
            stage[p % 2, rows:, :rows] = probs.astype(bf16)
            to_core(p).start()

        @pl.when(theirs == 0)
        def _():
            to_core(p).wait_recv()
            sums[p, :rows] = (back + given[p, :rows].astype(f32)).astype(bf16)
            sums[p, rows:] = given[p, rows:]
            sums[p, rows:, :rows] = (probs + given[p, rows:, :rows].astype(f32)).astype(bf16)

        @pl.when(t == 2)
        def _():
            far_top[0].start()
            far_low[0].start()

        @pl.when(t == 4)
        def _():
            x_top[0].start()

        @pl.when(t == 6)
        def _():
            y_low[0].start()
            far_top[1].start()
            far_low[1].start()

        return carry

    lax.fori_loop(0, 8, step, 0)
    def relayed(u):
        far_low[u].wait_recv()
        at = low(u)
        sums[1, at] = (sums[1, at].astype(f32) + relay[u, 1, first(u, 2)].astype(f32)).astype(bf16)
        x_low[u].start()
        far_top[u].wait_recv()
        at = top(u)
        sums[2, at] = (sums[2, at].astype(f32) + relay[u, 0, first(u, 2)].astype(f32)).astype(bf16)
        y_top[u].start()

    def block_of(u, q):
        part = sizes[u] // 4
        return pl.ds(pl.multiple_of(starts[u] + q * part, 16), part)

    def z_sems(u, number):
        return zsend.at[u, number], zrecv.at[u, number]

    scatter = [
        [
            remote(
                sums.at[3, block_of(u, (z + i) % 4)],
                zland.at[u, i - 1, first(u, 4)],
                *z_sems(u, i - 1),
                z_peers[i - 1],
            )
            for i in (1, 2, 3)
        ]
        for u in range(units)
    ]

    def back_copy(u, q, i):
        at = out_ref.at[block_of(u, q)]
        return remote(at, at, *z_sems(u, 2 + i), z_peers[i - 1])

    def landed(u):
        for copy in (x_top[u], y_top[u], x_low[u], y_low[u]):
            copy.wait_recv()
        at = slice(starts[u], starts[u + 1])
        added = sums[3, at].astype(f32) + land[0, at].astype(f32) + land[1, at].astype(f32)
        ours = min(rows, starts[u + 1]) - starts[u]
        if ours == sizes[u]:
            sums[3, at] = (added + mine[at].astype(f32)).astype(bf16)
        else:
            here = slice(starts[u], starts[u] + ours)
            sums[3, here] = (added[:ours] + mine[here].astype(f32)).astype(bf16)
            sums[3, starts[u] + ours : starts[u + 1]] = added[ours:].astype(bf16)
        for i in (1, 0, 2):
            scatter[u][i].start()

    def summed(u):
        done = sums[3, block_of(u, z)].astype(f32)
        for i in range(3):
            scatter[u][i].wait_recv()
            done = done + zland[u, i, first(u, 4)].astype(f32)
        out_ref[block_of(u, z)] = done.astype(bf16)
        for i in (2, 1, 3):
            back_copy(u, z, i).start()

    for u in range(units):
        relayed(u)
        if u < units - 1:
            x_top[u + 1].start()
            y_low[u + 1].start()
        if u < units - 2:
            far_top[u + 2].start()
            far_low[u + 2].start()
        if u == 0:
            shared_expert()
        if u == units - 1:
            share()
        if u < units - 1:
            landed(u)
        if 1 <= u < units - 1:
            summed(u - 1)
    landed(units - 1)
    summed(units - 2)
    sum_ref[...] = total().astype(bf16)
    end()
    summed(units - 1)
    for u in range(units):
        for i in (1, 2, 3):
            back_copy(u, (z + 4 - i) % 4, i).wait_recv()
    for u in range(units):
        for copy in (far_top[u], far_low[u], x_top[u], x_low[u], y_low[u], y_top[u], *scatter[u]):
            copy.wait_send()
        for i in (1, 2, 3):
            back_copy(u, z, i).wait_send()
    for p in (2, 3):
        to_core(p).wait_send()


def collect_sum(y, slot, gsw, normed, grad_t, *shared):
    s, local, cap, width = y.shape
    rows = slot.shape[2]
    tall = rows + EXTRA
    dma = pltpu.SemaphoreType.DMA
    units = len(SUM_STARTS)
    most = max(b - a for a, b in zip(SUM_STARTS, (*SUM_STARTS[1:], tall)))
    weights = 128 * (-(-sum(a.shape[0] for a in shared) // 128))
    vmem = pl.BlockSpec(memory_space=pltpu.VMEM)
    whole = pl.BlockSpec(memory_space=pl.ANY)
    return pl.pallas_call(
        collect_sum_kernel,
        in_specs=[whole, vmem, vmem] + [whole] * 5,
        out_specs=[vmem, vmem, vmem],
        out_shape=[
            jax.ShapeDtypeStruct((tall, width), bf16),
            jax.ShapeDtypeStruct((weights // 8, width), bf16),
            jax.ShapeDtypeStruct((rows, width), bf16),
        ],
        scratch_shapes=[
            *[pltpu.VMEM(a.shape, a.dtype) for a in (normed, grad_t, *shared)],
            dma((5,)),
            pltpu.VMEM((rows, width), bf16),
            pltpu.VMEM((local * cap, rows), bf16),
            pltpu.VMEM((2, local, cap, width), bf16),
            pltpu.VMEM((2, tall, width), bf16),
            pltpu.VMEM((4, tall, width), bf16),
            pltpu.VMEM((4, tall, width), bf16),
            pltpu.VMEM((units, 2, most // 2, width), bf16),
            pltpu.VMEM((2, tall, width), bf16),
            pltpu.VMEM((units, 3, most // 4, width), bf16),
            dma((2,)),
            dma((4,)),
            dma((4,)),
            dma((units, 6)),
            dma((units, 6)),
            dma((units, 6)),
            dma((units, 6)),
            *weight_sum_scratch(weights, width),
        ],
        compiler_params=pltpu.CompilerParams(
            vmem_limit_bytes=VMEM_LIMIT, collective_id=2, has_side_effects=True
        ),
        cost_estimate=takes(131),
        name="collect_sum",
    )(y, slot, gsw, normed, grad_t, *shared)


def back_kernel(
    sums_ref,
    residual_ref,
    normed2_ref,
    grad_ref,
    router_ref,
    gain_ref,
    cos_ref,
    sin_ref,
    piece_ref,
    *refs,
):
    late, outs, rest = refs[:11], refs[11:17], refs[17:]
    held, sems, rest = rest[:11], rest[11], rest[12:]
    loads = [pltpu.make_async_copy(a, b, sems.at[i]) for i, (a, b) in enumerate(zip(late, held))]
    for load in loads:
        load.start()
    back_steps(
        loads,
        sums_ref,
        residual_ref,
        normed2_ref,
        grad_ref,
        router_ref,
        gain_ref,
        cos_ref,
        sin_ref,
        piece_ref,
        *held,
        *outs,
        *rest,
    )


def back_steps(
    loads,
    sums_ref,
    residual_ref,
    normed2_ref,
    grad_ref,
    router_ref,
    gain_ref,
    cos_ref,
    sin_ref,
    piece_ref,
    out_ref,
    q_ref,
    k_ref,
    v_ref,
    probs_ref,
    wq_ref,
    wk_ref,
    wv_ref,
    attended_ref,
    x_ref,
    normed_ref,
    tokens_ref,
    early_ref,
    first_ref,
    second_ref,
    shared_ref,
    shared_sum_ref,
    dq_ref,
    dk_ref,
    dv_ref,
    x_t,
    gain_column,
    back_t,
    low_t,
    part,
    low_part,
    zland,
    mine,
    theirs,
    zsend,
    zrecv,
    lsend,
    lrecv,
    *more,
):
    chip, core, z, cx, cy, cd = places()
    odd = z % 2
    c_peer = (chip, 1 - core, z)
    z_peers = [(chip, core, (z + i) % 4) for i in (1, 2, 3)]
    quarter, width = wq_ref.shape
    rows = x_ref.shape[0]
    groups = [
        weight_sum(*more[8 * i : 8 * i + 4], ref, *more[8 * i + 4 : 8 * i + 8])
        for i, ref in enumerate((early_ref, first_ref, second_ref, shared_ref))
    ]
    early, *by_head = [more[8 * i] for i in range(4)]
    START, SHARE, GIVE_BACK, END = range(4)
    experts = router_ref.shape[0]
    whole = HEAD_DIM * (quarter // HEAD_DIM)
    spare = quarter - whole
    heads = whole // HEAD_DIM
    greet([c_peer, *[(c, core, z) for c in (cx, cy, cd)], *z_peers])
    put, gathered = weight_gather(shared_sum_ref, *more[32:])
    put(piece_ref[...])

    logits = nt(router_ref[...], normed2_ref[...])
    raised = jnp.exp(logits - jnp.max(logits, axis=0, keepdims=True))
    gates = raised / jnp.sum(raised, axis=0, keepdims=True)
    grad_probs = sums_ref[rows:, :rows].astype(f32)
    grad_logits = gates * (grad_probs - jnp.sum(grad_probs * gates, axis=0, keepdims=True))
    grad_logits = grad_logits.astype(bf16)
    grad_router = nn(grad_logits, normed2_ref[...])
    grad_normed2 = sums_ref[:rows].astype(f32) + tn(grad_logits, router_ref[...])
    residual = residual_ref[...]
    rms2 = lax.rsqrt(jnp.sum(residual * residual, axis=-1, keepdims=True) * (1.0 / width) + EPS)
    grad_ffn = jnp.sum(grad_normed2 * residual * rms2, axis=0, keepdims=True)
    u = grad_normed2 * gain_ref[1:2]
    mean2 = jnp.sum(u * residual, axis=-1, keepdims=True) * (1.0 / width)
    added = rms2 * u - residual * (rms2 * rms2 * rms2 * mean2)
    back_t[...] = added.T + grad_ref[...].astype(f32)
    low_t[...] = back_t[...].astype(bf16)
    own = block(z, quarter)

    cosine, sine = cos_ref[...], sin_ref[...]
    half_dim = HEAD_DIM // 2
    scale = 1.0 / math.sqrt(HEAD_DIM)

    def turn_back(v):
        a, b = v[:half_dim] * scale, v[half_dim:] * scale
        turned = [a * cosine + b * sine, b * cosine - a * sine]
        return jnp.concatenate(turned, axis=0).astype(bf16)

    for i in range(5):
        loads[i].wait()
    first_lane = z * quarter + odd * spare
    shared_lane = z * quarter + (1 - odd) * whole - odd * spare
    for h in range(heads + 1):
        lane = first_lane + h * HEAD_DIM if h < heads else shared_lane
        lane = pl.ds(pl.multiple_of(lane, HEAD_DIM), HEAD_DIM)
        grad_attended = tn(out_ref[:, lane], low_t[...]).astype(bf16)
        probs = probs_ref[h]
        grad_p = tn(grad_attended, v_ref[h])
        grad_v = nn(grad_attended, probs.astype(bf16)).astype(bf16)
        delta = jnp.sum(probs * grad_p, axis=-1, keepdims=True)
        grad_s = (probs * (grad_p - delta)).astype(bf16)
        grad_q = turn_back(nt(k_ref[h], grad_s))
        grad_k = turn_back(nn(q_ref[h], grad_s))
        for ref, value in ((dq_ref, grad_q), (dk_ref, grad_k), (dv_ref, grad_v)):
            if h < heads:
                at = pl.ds(pl.multiple_of(odd * spare + h * HEAD_DIM, 16), HEAD_DIM)
                ref[at] = value
            else:
                at = pl.ds(pl.multiple_of((1 - odd) * whole, 16), spare)
                ref[at] = jnp.where(odd == 1, value[spare:], value[:spare])

    for i in (5, 6, 7):
        loads[i].wait()
    part[...] = tn(wq_ref[...], dq_ref[...])
    part[...] += tn(wk_ref[...], dk_ref[...])
    part[...] += tn(wv_ref[...], dv_ref[...])
    low_part[...] = part[...].astype(bf16)
    to_z = [
        remote(
            low_part.at[block((z + i) % 4, quarter)],
            zland.at[i - 1],
            zsend.at[i - 1],
            zrecv.at[i - 1],
            z_peers[i - 1],
        )
        for i in (1, 2, 3)
    ]
    few_to_z = [
        remote(mine, theirs.at[i], lsend.at[i], lrecv.at[i], peer) for i, peer in enumerate(z_peers)
    ]
    loads[9].wait()
    x_t[...] = x_ref[...].T
    gain_column[...] = jnp.broadcast_to(gain_ref[0:1], (8, width)).T
    x_all = x_t[...].astype(f32)
    rms1 = lax.rsqrt(jnp.sum(x_all * x_all, axis=0, keepdims=True) * (1.0 / width) + EPS)
    along = part[...] * x_all
    mine[...] = jnp.zeros(mine.shape, f32)
    mine[0:1, :rows] = jnp.sum(along * gain_column[:, 0:1], axis=0, keepdims=True)
    mine[:, rows:] = nt(jnp.ones((8, rows), bf16), (along * rms1).astype(bf16))
    for copy in few_to_z:
        copy.start()
    for i in (1, 0, 2):
        to_z[i].start()

    loads[8].wait()
    loads[10].wait()
    early[:quarter] = nt(low_t[own], attended_ref[...]).astype(bf16)
    early[quarter:] = grad_router.astype(bf16)
    groups[0][START]()
    normed = normed_ref[...]
    for h in range(heads + 1):
        if h < heads:
            size, at = HEAD_DIM, odd * spare + h * HEAD_DIM
        else:
            size, at = spare, (1 - odd) * whole
        at = pl.ds(pl.multiple_of(at, 16), size)
        for i, ref in enumerate((dq_ref, dk_ref, dv_ref)):
            by_head[h][i * size : (i + 1) * size] = nn(ref[at], normed).astype(bf16)
        if h < heads:
            groups[1 + h][START]()
            groups[h][SHARE]()
    at = 3 * spare
    late = by_head[heads]
    for copy in few_to_z:
        copy.wait_recv()
    few = mine[...] + theirs[0] + theirs[1] + theirs[2]
    late[at:] = jnp.zeros((late.shape[0] - at, width), bf16)
    line = lax.broadcasted_iota(jnp.int32, (16, width), 0)
    gains = jnp.where(line == 0, few[0:1, rows:], jnp.where(line == 1, grad_ffn, 0.0))
    late[at : at + 16] = gains.astype(bf16)
    groups[3][START]()
    groups[2][SHARE]()
    groups[0][GIVE_BACK]()
    groups[3][SHARE]()
    groups[1][GIVE_BACK]()

    total = part[own]
    for i in range(3):
        to_z[i].wait_recv()
        total = total + zland[i].astype(f32)
    x = x_t[own].astype(f32)
    mean = few[0:1, :rows] * (1.0 / width)
    tokens_ref[...] = back_t[own] + rms1 * gain_column[own, 0:1] * total - x * (rms1 * rms1 * rms1 * mean)

    groups[2][GIVE_BACK]()
    groups[3][GIVE_BACK]()
    gathered()
    for group in groups:
        group[END]()
    for copy in (*to_z, *few_to_z):
        copy.wait_send()


def back(now, late):
    quarter, width = late[5].shape
    rows = now[1].shape[0]
    spare = quarter % HEAD_DIM
    tall = [quarter + now[4].shape[0], 3 * HEAD_DIM, 3 * HEAD_DIM, 3 * spare + 64]
    shared = 8 * now[8].shape[0]
    vmem = pl.BlockSpec(memory_space=pltpu.VMEM)
    dma = pltpu.SemaphoreType.DMA
    return pl.pallas_call(
        back_kernel,
        in_specs=[vmem] * len(now) + [pl.BlockSpec(memory_space=pl.ANY)] * len(late),
        out_specs=[vmem] * 6,
        out_shape=[
            jax.ShapeDtypeStruct((quarter, rows), f32),
            *[jax.ShapeDtypeStruct((lines, width), bf16) for lines in (*tall, shared)],
        ],
        scratch_shapes=[
            *[pltpu.VMEM(a.shape, a.dtype) for a in late],
            dma((len(late),)),
            *[pltpu.VMEM((quarter, rows), bf16)] * 3,
            pltpu.VMEM((width, rows), bf16),
            pltpu.VMEM((width, 8), f32),
            pltpu.VMEM((width, rows), f32),
            pltpu.VMEM((width, rows), bf16),
            pltpu.VMEM((width, rows), f32),
            pltpu.VMEM((width, rows), bf16),
            pltpu.VMEM((3, quarter, rows), bf16),
            pltpu.VMEM((8, rows + width), f32),
            pltpu.VMEM((3, 8, rows + width), f32),
            dma((3,)),
            dma((3,)),
            dma((3,)),
            dma((3,)),
            *[one for lines in tall for one in weight_sum_scratch(lines, width)],
            dma((5,)),
            dma((5,)),
            dma((6,)),
            dma((6,)),
        ],
        compiler_params=pltpu.CompilerParams(
            vmem_limit_bytes=VMEM_LIMIT, collective_id=3, has_side_effects=True
        ),
        cost_estimate=takes(90),
        name="back",
    )(*now, *late)


def widen_kernel(early_ref, first_ref, second_ref, last_ref, shared_ref, *out_refs):
    quarter = out_refs[0].shape[0]
    odd = lax.axis_index("hs") % 2
    whole = HEAD_DIM * (quarter // HEAD_DIM)
    spare = quarter - whole
    for i in range(3):
        for h, ref in enumerate((first_ref, second_ref)):
            at = pl.ds(pl.multiple_of(odd * spare + h * HEAD_DIM, 8), HEAD_DIM)
            out_refs[i][at] = ref[i * HEAD_DIM : (i + 1) * HEAD_DIM].astype(f32)
        at = pl.ds(pl.multiple_of((1 - odd) * whole, 8), spare)
        out_refs[i][at] = last_ref[i * spare : (i + 1) * spare].astype(f32)
    out_refs[3][...] = early_ref[:quarter].astype(f32)
    out_refs[4][...] = early_ref[quarter:].astype(f32)
    out_refs[5][...] = last_ref[3 * spare : 3 * spare + 16].astype(f32)
    size = out_refs[6].shape[0]
    for i in range(3):
        out_refs[6 + i][...] = shared_ref[i * size : (i + 1) * size].astype(f32)


def widen(sums, quarter, hidden_units):
    width = sums[0].shape[1]
    step = width // 5
    tall = [quarter] * 4 + [sums[0].shape[0] - quarter, 16] + [hidden_units] * 3
    blocks = lambda lines: pl.BlockSpec((lines, step), lambda i: (0, i))
    return pl.pallas_call(
        widen_kernel,
        grid=(width // step,),
        in_specs=[blocks(a.shape[0]) for a in sums],
        out_specs=[blocks(lines) for lines in tall],
        out_shape=[jax.ShapeDtypeStruct((lines, width), f32) for lines in tall],
        compiler_params=pltpu.CompilerParams(vmem_limit_bytes=VMEM_LIMIT),
        cost_estimate=takes(8),
        name="widen",
    )(*sums)


def plain_front(
    tokens, attn_gain, query_t, key_t, value_t, attn_out, ffn_gain, documents, tables
):
    rows, width = tokens.shape
    quarter = query_t.shape[0]
    hs, hs_count = lax.axis_index("hs"), lax.axis_size("hs")
    odd = (hs % 2) == 1
    spare = -quarter % HEAD_DIM
    heads = (quarter + spare) // HEAD_DIM

    def outer(w):
        return jnp.where(odd, w[:spare], w[quarter - spare :])

    sent = jnp.concatenate([outer(query_t), outer(key_t), outer(value_t)], axis=0)
    got = lax.ppermute(sent, "hs", [(i, i ^ 1) for i in range(hs_count)])

    def widened(w, extra):
        return jnp.where(
            odd, jnp.concatenate([extra, w], axis=0), jnp.concatenate([w, extra], axis=0)
        )

    x = tokens.astype(f32)
    rms1 = lax.rsqrt(jnp.mean(x * x, axis=-1, keepdims=True) + EPS)
    normed1 = (x * rms1 * attn_gain).astype(bf16)
    shape3 = (heads, HEAD_DIM, rows)
    q, k, v = [
        ein("cd,td->ct", widened(w, got[i * spare : (i + 1) * spare]), normed1).reshape(shape3)
        for i, w in enumerate((query_t, key_t, value_t))
    ]
    q, k, v = rope(q, *tables).astype(bf16), rope(k, *tables).astype(bf16), v.astype(bf16)
    positions = jnp.arange(rows, dtype=jnp.int32)
    doc = documents[0]
    allowed = (positions[:, None] >= positions[None, :]) & (doc[:, None] == doc[None, :])
    scale = 1.0 / math.sqrt(HEAD_DIM)
    scores = jnp.where(allowed[None], ein("hdq,hdk->hqk", q, k) * scale, -1e30)
    raised = jnp.exp(scores - jnp.max(scores, axis=-1, keepdims=True))
    probs = raised / jnp.sum(raised, axis=-1, keepdims=True)
    attended = ein("hdk,hqk->hdq", v, probs.astype(bf16)).astype(bf16).reshape(-1, rows)
    attended = jnp.where(odd, attended[spare:], attended[:quarter])
    attended_t = lax.all_gather(attended, "hs", axis=0, tiled=True)
    out_t = lax.all_gather(attn_out.T, "hs", axis=0, tiled=True)
    residual = x + ein("ct,oc->to", attended_t, out_t)
    rms2 = lax.rsqrt(jnp.mean(residual * residual, axis=-1, keepdims=True) + EPS)
    normed2 = (residual * rms2 * ffn_gain).astype(bf16)
    return normed1, q, k, v, probs, attended_t, out_t, residual, normed2


def over_ep(a):
    return lax.psum(a.astype(bf16), EP).astype(f32)


def plain_back(
    sums,
    residual,
    normed2,
    grad_t,
    router_t,
    ffn_gain,
    out_t,
    q,
    k,
    v,
    probs,
    tables,
    query_t,
    key_t,
    value_t,
    normed1,
    attended_t,
    tokens,
    attn_gain,
):
    rows, width = tokens.shape
    quarter = query_t.shape[0]
    hs = lax.axis_index("hs")
    odd = (hs % 2) == 1
    spare = -quarter % HEAD_DIM
    held = quarter + spare
    col0 = hs * quarter

    def own(v):
        v = v.astype(bf16).reshape(held, rows)
        return jnp.where(odd, v[spare:], v[:quarter])

    gates = jax.nn.softmax(nt(normed2, router_t), axis=-1)
    grad_probs = sums[rows:, :rows].T.astype(f32)
    grad_logits = (
        gates * (grad_probs - jnp.sum(grad_probs * gates, axis=-1, keepdims=True))
    ).astype(bf16)
    grad_router = tn(grad_logits, normed2)
    grad_normed2 = sums[:rows].astype(f32) + dot(grad_logits, router_t)
    rms2 = lax.rsqrt(jnp.mean(residual * residual, axis=-1, keepdims=True) + EPS)
    grad_ffn_gain = jnp.sum(grad_normed2 * residual * rms2, axis=0)
    u = grad_normed2 * ffn_gain
    grad_residual = (
        grad_t.T.astype(f32)
        + rms2 * u
        - residual * rms2**3 * jnp.mean(u * residual, axis=-1, keepdims=True)
    )
    back_t = grad_residual.T
    low_t = back_t.astype(bf16)
    out_held = lax.dynamic_slice_in_dim(out_t, jnp.where(odd, col0 - spare, col0), held, 1)
    grad_attended = tn(out_held, low_t).astype(bf16).reshape(-1, HEAD_DIM, rows)
    grad_p = ein("hdq,hdk->hqk", grad_attended, v)
    grad_v = own(ein("hdq,hqk->hdk", grad_attended, probs.astype(bf16)))
    grad_s = (probs * (grad_p - jnp.sum(probs * grad_p, axis=-1, keepdims=True))).astype(bf16)
    scale = 1.0 / math.sqrt(HEAD_DIM)
    grad_q = own(rope_back(ein("hdk,hqk->hdq", k, grad_s) * scale, *tables))
    grad_k = own(rope_back(ein("hdq,hqk->hdk", q, grad_s) * scale, *tables))
    own_rows = lambda a: lax.dynamic_slice_in_dim(a, col0, quarter, 0)
    heads_sums = [
        over_ep(dot(grad_q, normed1)),
        over_ep(dot(grad_k, normed1)),
        over_ep(dot(grad_v, normed1)),
        over_ep(nt(own_rows(low_t), attended_t)),
    ]
    part = tn(query_t, grad_q) + tn(key_t, grad_k) + tn(value_t, grad_v)
    grad_n1 = lax.psum_scatter(part.astype(bf16), "hs", scatter_dimension=0, tiled=True)
    grad_n1 = grad_n1.astype(f32)
    x = tokens.T.astype(f32)
    x_own = own_rows(x)
    rms_t = lax.rsqrt(jnp.mean(x * x, axis=0, keepdims=True) + EPS)
    w1 = grad_n1 * own_rows(attn_gain)[:, None]
    mean1 = lax.psum(jnp.sum(w1 * x_own, axis=0, keepdims=True), "hs") / width
    grad_tokens = own_rows(back_t) + rms_t * w1 - x_own * rms_t**3 * mean1
    gain_own = jnp.sum(grad_n1 * x_own * rms_t, axis=1)
    gain_part = lax.dynamic_update_slice_in_dim(jnp.zeros((width,), f32), gain_own, col0, 0)
    grad_attn_gain = lax.psum(gain_part, (*EP, "hs"))
    return (
        grad_tokens,
        heads_sums,
        over_ep(grad_router),
        grad_attn_gain,
        lax.psum(grad_ffn_gain, EP),
    )


def shards(
    tokens,
    attn_gain,
    attn_query,
    attn_key,
    attn_value,
    attn_out,
    ffn_gain,
    router,
    shared_gate,
    shared_up,
    shared_down,
    expert_gate,
    expert_up,
    expert_down,
    routes,
    documents,
    out_grad,
):
    rows, width = tokens.shape
    quarter = out_grad.shape[1]
    hs = lax.axis_index("hs")
    ep_count = lax.axis_size("xy") * lax.axis_size("core")
    ep = lax.axis_index("xy") * lax.axis_size("core") + lax.axis_index("core")
    local = expert_gate.shape[0]
    experts = router.shape[1]
    small = ep_count == 8 and lax.axis_size("hs") == 4

    query_t, key_t, value_t, router_t = attn_query.T, attn_key.T, attn_value.T, router.T
    positions = jnp.arange(rows, dtype=jnp.int32)
    below = (positions[:, None] > positions[None, :]).astype(bf16)
    chosen = jnp.any(
        routes[:, :, None] == jnp.arange(experts, dtype=jnp.int32)[None, None, :], axis=1
    )
    own_slots = jnp.where(chosen, dot(below, chosen.astype(bf16)), -1.0).T.astype(bf16)
    tables = rope_tables(rows)

    if small:
        both_gains = jnp.stack([attn_gain, ffn_gain])
        ahead = front(
            tokens, both_gains, query_t, key_t, value_t, attn_out.T, documents, tables
        )
    else:
        ahead = plain_front(
            tokens, attn_gain, query_t, key_t, value_t, attn_out, ffn_gain, documents, tables
        )
    normed1, q, k, v, probs, attended_t, out_t, residual, normed2 = ahead
    out_t = out_t.reshape(width, width)

    first = ep * local
    rolled = jnp.roll(router_t, -first, axis=0)
    gate_t, up_t = expert_gate.swapaxes(1, 2), expert_up.swapaxes(1, 2)
    weights = gate_t, up_t, expert_down
    if small:
        ex_in, slot_weight, slot, grad_t = gather_spread(
            normed2, own_slots, rolled, out_grad.T, local, ep_count
        )
        ex_out, ex_gate, ex_up, near = experts_forward(ex_in, slot_weight, *weights, grad_t)
        out_part, far, given = collect_sending(ex_out, slot, grad_t, near)
        ex_grad = spread_grad(grad_t, near, far, given, slot)
    else:
        grad_all_t = lax.all_gather(out_grad.T, (*EP, "hs"), axis=0, tiled=True)
        grad_all_t = grad_all_t.reshape(ep_count, width, rows)
        grad_t = lax.dynamic_index_in_dim(grad_all_t, ep, 0, keepdims=False)
        slot = lax.dynamic_slice_in_dim(
            lax.all_gather(own_slots, EP, axis=0), first, local, 1
        ).astype(jnp.int32)
        normed_all = lax.all_gather(normed2, EP, axis=0, tiled=True)
        ex_in, slot_weight = spread(normed_all, slot, rolled)
        ex_out, ex_gate, ex_up = experts_forward(ex_in, slot_weight, *weights)
        out_part = collect(ex_out, slot)
        ex_grad = spread(grad_all_t, slot)
    out_part = out_part.reshape(ep_count * rows, width)
    ex_back, grad_gate_t, grad_up_t, grad_expert_down, grad_slot_weight = experts_backward(
        ex_in, ex_grad, ex_gate, ex_up, slot_weight, *weights
    )

    if small:
        back_sums, shared_piece, shared_part = collect_sum(
            ex_back, slot, grad_slot_weight, normed2, grad_t, shared_gate.T, shared_up.T, shared_down
        )
        grad_tokens, *sums = back(
            (back_sums, residual, normed2, grad_t, router_t, both_gains, *tables, shared_piece),
            (out_t, q, k, v, probs, query_t, key_t, value_t, attended_t, tokens, normed1),
        )
        *heads_sums, grad_router, gains, sum_gate, sum_up, sum_down = widen(
            sums, quarter, shared_down.shape[0]
        )
        shared_sums = sum_gate, sum_up, sum_down
        grad_attn_gain, grad_ffn_gain = gains[0], gains[1]
    else:
        sh_gate = dot(normed2, shared_gate)
        sh_up = dot(normed2, shared_up)
        sh_sig = jax.nn.sigmoid(sh_gate)
        sh_act = sh_gate * sh_sig
        sh_hidden = (sh_act * sh_up).astype(bf16)
        shared_part = dot(sh_hidden, shared_down)
        grad_sh = ein("dt,fd->tf", grad_t, shared_down)
        grad_sh_gate = (grad_sh * sh_up * sh_sig * (1 + sh_gate * (1 - sh_sig))).astype(bf16)
        grad_sh_up = (grad_sh * sh_act).astype(bf16)
        shared_grads = [
            ein("tf,td->fd", grad_sh_gate, normed2).astype(bf16),
            ein("tf,td->fd", grad_sh_up, normed2).astype(bf16),
            ein("tf,dt->fd", sh_hidden, grad_t).astype(bf16),
        ]
        shared_back = ein("tf,df->td", grad_sh_gate, shared_gate) + ein(
            "tf,df->td", grad_sh_up, shared_up
        )
        back_part = collect(ex_back, slot, grad_slot_weight, first, experts).reshape(-1, width)
        back_rows = lax.psum_scatter(back_part, EP, scatter_dimension=0, tiled=True).astype(f32)
        back_rows = jnp.concatenate([back_rows[:rows] + shared_back, back_rows[rows:]], axis=0)
        back_sums = lax.psum(back_rows.astype(bf16), "hs")
        shared_sums = [over_ep(a) for a in shared_grads]
        grad_tokens, heads_sums, grad_router, grad_attn_gain, grad_ffn_gain = plain_back(
            back_sums,
            residual,
            normed2,
            grad_t,
            router_t,
            ffn_gain,
            out_t,
            q,
            k,
            v,
            probs,
            tables,
            query_t,
            key_t,
            value_t,
            normed1,
            attended_t,
            tokens,
            attn_gain,
        )

    rows_major = Layout(major_to_minor=(0, 1))
    out_part = with_layout_constraint(out_part, rows_major)
    out_rows = lax.psum_scatter(out_part, EP, scatter_dimension=0, tiled=True)
    out_rows = with_layout_constraint(out_rows, rows_major)
    out_rows = (out_rows.astype(f32) + shared_part.astype(f32)).astype(bf16)
    out_quarter = lax.psum_scatter(out_rows, "hs", scatter_dimension=1, tiled=True)
    residual_quarter = lax.dynamic_slice_in_dim(residual, hs * quarter, quarter, 1)
    output = (residual_quarter + out_quarter.astype(f32)).astype(bf16)

    return (
        output,
        grad_tokens.T,
        grad_attn_gain,
        *[a.T for a in heads_sums],
        grad_ffn_gain,
        grad_router.T,
        shared_sums[0].T,
        shared_sums[1].T,
        shared_sums[2],
        grad_gate_t.swapaxes(1, 2),
        grad_up_t.swapaxes(1, 2),
        grad_expert_down,
    )


def solution(mesh):
    ep_count, hs_count = mesh.devices.shape
    cut = Mesh(mesh.devices.reshape(ep_count // 2, 2, hs_count), ("xy", "core", "hs"))
    return jax.shard_map(
        shards,
        mesh=cut,
        in_specs=(
            P(EP, None),
            P(),
            P(None, "hs"),
            P(None, "hs"),
            P(None, "hs"),
            P(None, "hs"),
            P(),
            P(),
            P(None, "hs"),
            P(None, "hs"),
            P("hs", None),
            P(EP, None, "hs"),
            P(EP, None, "hs"),
            P(EP, "hs", None),
            P(EP, None),
            P(EP, None),
            P(EP, "hs"),
        ),
        out_specs=(
            P(EP, "hs"),
            P(EP, "hs"),
            P(),
            P(None, "hs"),
            P(None, "hs"),
            P(None, "hs"),
            P(None, "hs"),
            P(),
            P(),
            P(None, "hs"),
            P(None, "hs"),
            P("hs", None),
            P(EP, None, "hs"),
            P(EP, None, "hs"),
            P(EP, "hs", None),
        ),
        check_vma=False,
    )
```
